32 devices in a mesh: groups: 2 (over y), blk: 4 (over z), head: 4 (over x, core).
Axes of the slice: x: 2, y: 2, z: 4, core: 2. Of those that a mesh axis runs over, the one named last changes fastest.
Arguments:
- ctx_query: bfloat16 [4096, 8192], P(('groups', 'blk'), 'head'), parts along dimension 0, may hold values from -5 to 5
- ctx_key: bfloat16 [4096, 1024], P(('groups', 'blk'), 'head'), parts along dimension 0, may hold values from -5 to 5
- ctx_value: bfloat16 [4096, 1024], P(('groups', 'blk'), 'head'), parts along dimension 0, may hold values from -4.5 to 4.5
- opt_query: bfloat16 [128, 8192], P(('groups', 'blk'), 'head'), parts along dimension 0, may hold values from -5 to 5
- opt_owner: int32 [128], P('groups'), parts along dimension 0, may hold values from 0 to 3, as said below
- opt_slot: int32 [128], P('groups'), parts along dimension 0, may hold values from 0 to 31, as said below
- opt_length: int32 [128], P('groups'), parts along dimension 0, may hold values from 512 to 2048
Outputs:
- ctx_out: bfloat16 [4096, 8192], P(('groups', 'blk'), 'head'), parts along dimension 0
- opt_out: bfloat16 [256, 8192], P(('groups', 'blk'), 'head'), parts along dimension 0
The draws below stay inside these ranges and needn't reach their ends.
There are 2 independent parts, one for each index of `groups`. The reference program is written for one: setup_inputs(seed, part) draws one part's arguments, and reference() takes and returns one part's arrays. A program takes and returns all parts, laid end to end along the dimension named above; each array names one. Nothing has to cross between parts.
Inputs may be any that keep to these rules, and one draw needn't show every extreme that they name: `opt_owner`: each option token has its own pair of owner block and slot; no block owns more than 32 option tokens, and one block owns exactly 32. `opt_slot`: slots of one owner are distinct.
All inputs are finite; a program needn't handle non-finite values.
Results may differ from the reference program's by a relative error of at most 0.017.
Values may be sent and summed in bfloat16 or wider, within the bound.
No kernel may reach another device: no remote copies, remote signals or barrier semaphores. Data moves between devices by JAX's collectives and lax.ppermute only.
A program may use at most 64 MiB of HBM per device.

```python
import jax
import jax.numpy as jnp
from jax import lax

HD = 128
HQ = 64
KVH = 8
BLK = 512
CAP = 32
CTX = 2048
OPTS = 64
N_BLK = 4


def base_values(key, rows, cols):
    return jnp.clip(jax.random.normal(key, (rows, cols), jnp.float32), -4.5, 4.5)


def draw_ctx_key(key, part):
    values = base_values(jax.random.fold_in(key, 11), CTX, KVH * HD)
    return values.astype(jnp.bfloat16)


def draw_ctx_query(key, part):
    values = base_values(jax.random.fold_in(key, 12), CTX, HQ * HD)
    return values.astype(jnp.bfloat16)


def draw_opt_query(key, part):
    values = jax.random.uniform(jax.random.fold_in(key, 13), (OPTS, HQ * HD), jnp.float32, -5.0, 5.0)
    return values.astype(jnp.bfloat16)


def option_places(key):
    base = jax.random.fold_in(key, 21)
    slot_count = N_BLK * CAP
    full_owner = jax.random.randint(jax.random.fold_in(base, 1), (), 0, N_BLK)
    owner_bias = jax.random.randint(jax.random.fold_in(base, 2), (N_BLK,), 0, 3)
    noise = jax.random.randint(jax.random.fold_in(base, 3), (slot_count,), 0, 65536)
    slot_ids = jnp.arange(slot_count, dtype=jnp.int32)
    owners = slot_ids // CAP
    score = noise + owner_bias[owners] * 32768 + (owners == full_owner).astype(jnp.int32) * 262144
    ranked = jnp.argsort(-(score * slot_count + slot_ids))
    chosen = ranked[:OPTS].astype(jnp.int32)
    shuffle = jax.random.permutation(jax.random.fold_in(base, 4), OPTS)
    chosen = chosen[shuffle]
    return ((chosen // CAP).astype(jnp.int32), (chosen % CAP).astype(jnp.int32))


def draw_opt_owner(key, part):
    return option_places(key)[0]


def draw_opt_slot(key, part):
    return option_places(key)[1]


def place_ends(drawn, own_key, low, high):
    place = [jax.random.randint(jax.random.fold_in(own_key, axis), (), 0, length) for axis, length in enumerate(drawn.shape)]
    main_axis = drawn.shape.index(max(drawn.shape))
    beside = place[:main_axis] + [(place[main_axis] + 1) % drawn.shape[main_axis]] + place[main_axis + 1:]
    return drawn.at[tuple(place)].set(low).at[tuple(beside)].set(high)


def levels(stream_key, shape, pieces, low, high):
    level, own = 1.0, jax.random.fold_in(stream_key, 6)
    for axis_at, blocks in pieces:
        draws = jnp.exp(jax.random.uniform(jax.random.fold_in(own, axis_at), (blocks,), jnp.float32, low / len(pieces), high / len(pieces)))
        level = level * jnp.repeat(draws, shape[axis_at] // blocks).reshape([-1 if axis == axis_at else 1 for axis in range(len(shape))])
    return level


def normal_values(rng, extent, deviation, limit, split=(), held_as=jnp.bfloat16):
    values = deviation * jax.random.normal(rng, extent, jnp.float32)
    if split:
        values = values * levels(rng, extent, split, -0.22, 0.18)
    return jnp.clip(values, -limit, limit).astype(held_as)


def setup_inputs(seed: int = 0, part: int = 0) -> dict:
    key_list = jax.random.split(jax.random.key(seed), 8)
    own_keys = jax.random.split(jax.random.fold_in(key_list[7], part), 8)
    return {
        "ctx_query": draw_ctx_query(jax.random.fold_in(jax.random.fold_in(key_list[7], part), 71), part),
        "ctx_key": draw_ctx_key(jax.random.fold_in(jax.random.fold_in(key_list[7], part), 71), part),
        "ctx_value": normal_values(own_keys[2], (CTX, KVH * HD), 1.0, 4.5, ((0, 4), (1, 4))),
        "opt_query": draw_opt_query(jax.random.fold_in(jax.random.fold_in(key_list[7], part), 71), part),
        "opt_owner": draw_opt_owner(jax.random.fold_in(jax.random.fold_in(key_list[7], part), 71), part),
        "opt_slot": draw_opt_slot(jax.random.fold_in(jax.random.fold_in(key_list[7], part), 71), part),
        "opt_length": place_ends(jax.random.randint(own_keys[6], (OPTS,), BLK, CTX + 1), jax.random.fold_in(own_keys[6], 1), BLK, CTX).astype(jnp.int32),
    }


def reference(ctx_query, ctx_key, ctx_value, opt_query, opt_owner, opt_slot, opt_length):
    group_size = HQ // KVH
    scale = HD ** -0.5
    high = lax.Precision.HIGHEST
    query_all = ctx_query.reshape(N_BLK, BLK, HQ, HD)
    key_all = ctx_key.reshape(N_BLK, BLK, KVH, HD)
    value_all = ctx_value.reshape(N_BLK, BLK, KVH, HD)
    anchor_key = jnp.repeat(key_all[0], group_size, axis=1).astype(jnp.float32)
    anchor_value = jnp.repeat(value_all[0], group_size, axis=1).astype(jnp.float32)
    spots = jnp.arange(BLK, dtype=jnp.int32)
    causal = spots[:, None] >= spots[None, :]

    def first_phase(index):
        query_blk = query_all[index].astype(jnp.float32)
        key_blk = jnp.repeat(key_all[index], group_size, axis=1).astype(jnp.float32)
        value_blk = jnp.repeat(value_all[index], group_size, axis=1).astype(jnp.float32)
        local = jnp.einsum('thd,shd->hts', query_blk, key_blk, precision=high) * scale
        local = jnp.where(causal[None], local, -1e30)
        remote = jnp.einsum('thd,shd->hts', query_blk, anchor_key, precision=high) * scale
        remote = jnp.where(index > 0, remote, -1e30)
        top = jnp.maximum(jnp.max(local, axis=2), jnp.max(remote, axis=2))
        e_local = jnp.exp(local - top[..., None])
        e_remote = jnp.exp(remote - top[..., None])
        total = jnp.sum(e_local, axis=2) + jnp.sum(e_remote, axis=2)
        acc = jnp.einsum('hts,shd->thd', e_local.astype(jnp.bfloat16).astype(jnp.float32), value_blk, precision=high)
        acc = acc + jnp.einsum('hts,shd->thd', e_remote.astype(jnp.bfloat16).astype(jnp.float32), anchor_value, precision=high)
        return (acc / total.T[:, :, None]).astype(jnp.bfloat16)

    ctx_out = lax.map(first_phase, jnp.arange(N_BLK, dtype=jnp.int32)).reshape(CTX, HQ * HD)

    option_q = opt_query.reshape(OPTS, HQ, HD).astype(jnp.float32)

    def second_phase(index):
        key_blk = jnp.repeat(key_all[index], group_size, axis=1).astype(jnp.float32)
        value_blk = jnp.repeat(value_all[index], group_size, axis=1).astype(jnp.float32)
        scores = jnp.einsum('ihd,shd->his', option_q, key_blk, precision=high) * scale
        count = jnp.clip(opt_length - index * BLK, 0, BLK)
        visible = spots[None, :] < count[:, None]
        scores = jnp.where(visible[None], scores, -1e30)
        top = jnp.max(scores, axis=2)
        expo = jnp.exp(scores - top[..., None])
        total = jnp.sum(expo, axis=2)
        acc = jnp.einsum('his,shd->ihd', expo.astype(jnp.bfloat16).astype(jnp.float32), value_blk, precision=high)
        live = count > 0
        part = jnp.where(live[:, None, None], acc / total.T[:, :, None], 0.0).astype(jnp.bfloat16)
        stat = jnp.where(live[:, None], (top + jnp.log(total)).T, -1e30)
        return part, stat

    parts, stats = lax.map(second_phase, jnp.arange(N_BLK, dtype=jnp.int32))
    top_all = jnp.max(stats, axis=0)
    weight = jnp.exp(stats - top_all[None])
    merged = jnp.sum(weight[..., None] * parts.astype(jnp.float32), axis=0) / jnp.sum(weight, axis=0)[..., None]
    where_to = (opt_owner * CAP + opt_slot).astype(jnp.int32)
    opt_out = jnp.zeros((CAP * N_BLK, HQ * HD), jnp.bfloat16).at[where_to].set(merged.reshape(OPTS, HQ * HD).astype(jnp.bfloat16))
    return ctx_out, opt_out
```

```python
import functools
import math

import jax
import jax.numpy as jnp
from jax import lax
from jax.experimental import pallas as pl
from jax.experimental.pallas import tpu as pltpu
from jax.sharding import PartitionSpec as P

HD = 128
HQ = 64
KVH = 8
CAP = 32
GROUP = HQ // KVH
SCALE = HD ** (-0.5)
LOG2E = math.log2(math.e)
NEG = -1e30
TILE = 256
VMEM = pl.BlockSpec(memory_space=pltpu.VMEM)
SMEM = pl.BlockSpec(memory_space=pltpu.SMEM)


def nt(a, b):
    return lax.dot_general(a, b, (((1,), (1,)), ((), ())), preferred_element_type=jnp.float32)


def nn(a, b):
    return jnp.dot(a, b, preferred_element_type=jnp.float32)


def params(mib):
    return pltpu.CompilerParams(vmem_limit_bytes=mib * 1024 * 1024)


def split_kernel(heads, k_ref, v_ref, *outs):
    for g in range(heads):
        outs[2 * g][...] = k_ref[:, g * HD : (g + 1) * HD]
        outs[2 * g + 1][...] = v_ref[:, g * HD : (g + 1) * HD]


def split_heads(key, value):
    rows, heads = key.shape[0], key.shape[1] // HD
    shape = jax.ShapeDtypeStruct((rows, HD), key.dtype)
    outs = pl.pallas_call(
        functools.partial(split_kernel, heads),
        out_shape=[shape] * (2 * heads),
        in_specs=[VMEM] * 2,
        out_specs=[VMEM] * (2 * heads),
        compiler_params=params(16),
        name="split_heads",
    )(key, value)
    return [(outs[2 * g], outs[2 * g + 1]) for g in range(heads)]


def ctx_kernel(count, blk_ref, q_ref, k_ref, v_ref, *refs):
    cand = refs[:count]
    o_ref = refs[-4]
    ve, ka, vae = refs[-3:]
    rows = q_ref.shape[0]
    blk = blk_ref[0]

    @pl.when(pl.program_id(0) == 0)
    def _():
        ve[:, :HD] = v_ref[...]
        ve[:, HD:] = jnp.ones((rows, HD), jnp.bfloat16)
        vae[:, HD:] = jnp.ones((rows, HD), jnp.bfloat16)
        if count == 2:
            ka[...] = cand[0][...]
            vae[:, :HD] = cand[1][...]
        else:
            first_k, first_v, up, down = cand

            @pl.when(blk == 1)
            def _():
                ka[...] = down[...]
                vae[:, :HD] = up[...]

            @pl.when(blk == 2)
            def _():
                ka[...] = first_k[...]
                vae[:, :HD] = down[...]

            @pl.when(blk == 3)
            def _():
                ka[...] = up[...]
                vae[:, :HD] = first_v[...]

    row = lax.broadcasted_iota(jnp.int32, (TILE, TILE), 0)
    col = lax.broadcasted_iota(jnp.int32, (TILE, TILE), 1)

    def attend(anchor):
        for at in range(0, rows, TILE):
            q = q_ref[at : at + TILE, :]
            diag = jnp.where(row >= col, nt(q, k_ref[at : at + TILE, :]), NEG)
            scores = [(diag, ve[at : at + TILE, :])]
            if at:
                scores.append((nt(q, k_ref[:at, :]), ve[:at, :]))
            if anchor:
                scores.append((nt(q, ka[...]), vae[...]))
            top = functools.reduce(jnp.maximum, [jnp.max(s, axis=1, keepdims=True) for s, _ in scores])
            total = None
            for s, v in scores:
                p = jnp.exp2((s - top) * (SCALE * LOG2E)).astype(jnp.bfloat16)
                part = nn(p, v)
                total = part if total is None else total + part
            o_ref[at : at + TILE, :] = (total[:, :HD] / total[:, HD:]).astype(jnp.bfloat16)

    pl.when(blk == 0)(lambda: attend(False))
    pl.when(blk > 0)(lambda: attend(True))


def ctx_attention(blk, query, key, value, anchors, g, prior):
    rows = query.shape[0]
    whole = pl.BlockSpec((rows, HD), lambda h: (0, 0))
    column = pl.BlockSpec((rows, HD), lambda h: (0, g * GROUP + h))
    args = [blk, query, key, value, *anchors]
    specs = [SMEM, column] + [whole] * (2 + len(anchors))
    alias = {}
    if prior is not None:
        alias = {len(args): 0}
        args.append(prior)
        specs.append(pl.BlockSpec(memory_space=pl.ANY))
    flops = 4 * GROUP * rows * rows * HD * 2
    return pl.pallas_call(
        functools.partial(ctx_kernel, len(anchors)),
        grid=(GROUP,),
        out_shape=jax.ShapeDtypeStruct(query.shape, query.dtype),
        in_specs=specs,
        out_specs=column,
        scratch_shapes=[
            pltpu.VMEM((rows, 2 * HD), jnp.bfloat16),
            pltpu.VMEM((rows, HD), jnp.bfloat16),
            pltpu.VMEM((rows, 2 * HD), jnp.bfloat16),
        ],
        input_output_aliases=alias,
        compiler_params=params(32),
        cost_estimate=pl.CostEstimate(flops=flops, bytes_accessed=4 * GROUP * rows * HD, transcendentals=2 * GROUP * rows * rows),
        name="ctx_attention",
    )(*args)


def option_kernel(n, heads, blk_ref, owner_ref, slot_ref, length_ref, k_ref, v_ref, *refs):
    queries, outs, (q_all, part) = refs[:n], refs[n : 2 * n], refs[2 * n :]
    blk = blk_ref[0]
    rows = k_ref.shape[0]
    each = queries[0].shape[0]
    options = n * each
    for d in range(n):
        at = lax.rem(blk + n - d, n) * each
        q_all[pl.ds(pl.multiple_of(at, each), each), :] = queries[d][...]
    eye = lax.broadcasted_iota(jnp.int32, (options, options), 0) == lax.broadcasted_iota(jnp.int32, (options, options), 1)
    length = jnp.sum(jnp.where(eye, length_ref[...].astype(jnp.float32), 0.0), axis=1, keepdims=True)
    seen = length - (blk * rows).astype(jnp.float32)
    lane = lax.broadcasted_iota(jnp.int32, (options, HD), 1)
    logs = jnp.zeros((options, HD), jnp.float32)
    stack = max(1, min(GROUP, 512 // options))
    spots = lax.broadcasted_iota(jnp.int32, (options * stack, rows), 1).astype(jnp.float32)
    seen_all = jnp.concatenate([seen] * stack, axis=0)
    for first in range(0, heads, stack):
        g = first // GROUP
        q = jnp.concatenate([q_all[:, h * HD : (h + 1) * HD] for h in range(first, first + stack)], axis=0)
        s = nt(q, k_ref[:, g * HD : (g + 1) * HD])
        s = jnp.where(spots < seen_all, s, NEG)
        top = jnp.max(s, axis=1, keepdims=True)
        e = jnp.exp2((s - top) * (SCALE * LOG2E))
        z = jnp.sum(e, axis=1, keepdims=True)
        o = nn(e.astype(jnp.bfloat16), v_ref[:, g * HD : (g + 1) * HD]) / z
        live = seen_all > 0
        o = jnp.where(live, o, 0.0).astype(jnp.bfloat16)
        log = jnp.where(live, top * SCALE + jnp.log(z), NEG)
        for j in range(stack):
            h = first + j
            part[:, h * HD : (h + 1) * HD] = o[j * options : (j + 1) * options]
            logs = jnp.where(lax.rem(lane, heads) == h, log[j * options : (j + 1) * options], logs)
    high = logs.astype(jnp.bfloat16)
    rest = logs - high.astype(jnp.float32)
    mid = rest.astype(jnp.bfloat16)
    low = (rest - mid.astype(jnp.float32)).astype(jnp.bfloat16)
    part[:, heads * HD :] = jnp.where(
        lane < heads,
        high.astype(jnp.float32),
        jnp.where(lane < 2 * heads, mid.astype(jnp.float32), jnp.where(lane < 3 * heads, low.astype(jnp.float32), 0.0)),
    ).astype(jnp.bfloat16)
    slot = lax.broadcasted_iota(jnp.int32, (CAP, options), 0)
    for d in range(n):
        target = lax.rem(blk + d, n)
        pick = (owner_ref[...] == target) & (slot_ref[...] == slot)
        outs[d][...] = nn(jnp.where(pick, 1.0, 0.0).astype(jnp.bfloat16), part[...]).astype(jnp.bfloat16)


def option_partials(blk, owner, slot, length, key, value, queries):
    n, heads = len(queries), queries[0].shape[1] // HD
    options = n * queries[0].shape[0]
    width = (heads + 1) * HD
    row = lambda x: x.reshape(1, options)
    return pl.pallas_call(
        functools.partial(option_kernel, n, heads),
        out_shape=[jax.ShapeDtypeStruct((CAP, width), jnp.bfloat16)] * n,
        in_specs=[SMEM] + [VMEM] * (5 + n),
        out_specs=[VMEM] * n,
        scratch_shapes=[
            pltpu.VMEM((options, heads * HD), jnp.bfloat16),
            pltpu.VMEM((options, width), jnp.bfloat16),
        ],
        compiler_params=params(32),
        cost_estimate=pl.CostEstimate(
            flops=4 * options * heads * key.shape[0] * HD, bytes_accessed=1 << 20, transcendentals=options * heads * key.shape[0]
        ),
        name="option_partials",
    )(blk, row(owner), row(slot), row(length), key, value, *queries)


def merge_kernel(heads, *refs):
    parts, o_ref = refs[:-1], refs[-1]
    width = heads * HD
    lane = lax.broadcasted_iota(jnp.int32, (HD, width), 0)
    head = lax.broadcasted_iota(jnp.int32, (HD, width), 1) // HD
    pick = jnp.where((lax.rem(lane, heads) == head) & (lane < 3 * heads), 1.0, 0.0).astype(jnp.bfloat16)
    logs = [nn(p[:, width:], pick) for p in parts]
    top = functools.reduce(jnp.maximum, logs)
    weights = [jnp.exp(log - top) for log in logs]
    total = sum(weights[1:], weights[0])
    merged = sum(w * p[:, :width].astype(jnp.float32) for w, p in zip(weights, parts))
    o_ref[...] = (merged / total).astype(jnp.bfloat16)


def merge(parts):
    heads = parts[0].shape[1] // HD - 1
    return pl.pallas_call(
        functools.partial(merge_kernel, heads),
        out_shape=jax.ShapeDtypeStruct((CAP, heads * HD), jnp.bfloat16),
        in_specs=[VMEM] * len(parts),
        out_specs=VMEM,
        compiler_params=params(32),
        name="merge",
    )(*parts)


def shifted(x, n, d):
    return lax.ppermute(x, "blk", [(i, (i + d) % n) for i in range(n)])


def from_root(x, blk):
    return lax.psum(jnp.where(blk == 0, x, jnp.zeros_like(x)), "blk")


def body(ctx_query, ctx_key, ctx_value, opt_query, opt_owner, opt_slot, opt_length):
    n = lax.axis_size("blk")
    blk = lax.axis_index("blk")
    blk_arr = blk.astype(jnp.int32).reshape(1)
    queries = [opt_query] + [shifted(opt_query, n, d) for d in range(1, n)]
    local = split_heads(ctx_key, ctx_value)
    if n == 4:
        anchors = []
        for key, value in local:
            first_k = lax.ppermute(key, "blk", [(0, 2)])
            first_v = lax.ppermute(value, "blk", [(0, 3)])
            held = jnp.where(blk == 2, first_k, first_v)
            up = lax.ppermute(held, "blk", [(2, 3), (3, 1)])
            down = lax.ppermute(held, "blk", [(2, 1), (3, 2)])
            anchors.append((first_k, first_v, up, down))
    else:
        anchors = [(from_root(key, blk), from_root(value, blk)) for key, value in local]
    sends = option_partials(blk_arr, opt_owner, opt_slot, opt_length, ctx_key, ctx_value, queries)
    parts = [sends[0]] + [shifted(sends[d], n, d) for d in range(1, n)]
    ctx_out = None
    for g, (key, value) in enumerate(local):
        ctx_out = ctx_attention(blk_arr, ctx_query, key, value, anchors[g], g, ctx_out)
    opt_out = merge(parts)
    return (ctx_out, opt_out)


def solution(mesh):
    spread = P(("groups", "blk"), "head")
    return jax.shard_map(
        body,
        mesh=mesh,
        in_specs=(spread, spread, spread, spread, P("groups"), P("groups"), P("groups")),
        out_specs=(spread, spread),
        check_vma=False,
    )
```

```python
import functools
import math

import jax
import jax.numpy as jnp
from jax import lax
from jax.experimental import pallas as pl
from jax.experimental.pallas import tpu as pltpu
from jax.sharding import PartitionSpec as P

HD = 128
HQ = 64
KVH = 8
CAP = 32
GROUP = HQ // KVH
SCALE = HD ** (-0.5)
C2 = SCALE * math.log2(math.e)
NEG = -1e30
TILE = 256
PAIR = 2
VMEM = pl.BlockSpec(memory_space=pltpu.VMEM)
SMEM = pl.BlockSpec(memory_space=pltpu.SMEM)
HBM = pl.BlockSpec(memory_space=pltpu.HBM)
ANY = pl.BlockSpec(memory_space=pl.ANY)


def nt(a, b):
    return lax.dot_general(a, b, (((1,), (1,)), ((), ())), preferred_element_type=jnp.float32)


def nn(a, b):
    return jnp.dot(a, b, preferred_element_type=jnp.float32)


def params(mib):
    return pltpu.CompilerParams(vmem_limit_bytes=mib * 1024 * 1024)


def fold(op, items):
    return functools.reduce(op, items)


def prep_kernel(heads, k_ref, v_ref, *refs):
    smalls = (len(refs) - heads - 1) // 2
    small_in, kv = refs[:smalls], refs[smalls : smalls + heads]
    small_out, sem = refs[smalls + heads : -1], refs[-1]
    copies = []
    for g in range(heads):
        for ref, at in ((k_ref, 0), (v_ref, HD)):
            copies.append((ref.at[:, g * HD : (g + 1) * HD], kv[g].at[:, at : at + HD]))
    copies += list(zip(small_in, small_out))
    started = [pltpu.make_async_copy(a, b, sem.at[i]) for i, (a, b) in enumerate(copies)]
    for copy in started:
        copy.start()
    for copy in started:
        copy.wait()


def prep(key, value, smalls):
    rows, heads = key.shape[0], key.shape[1] // HD
    outs = pl.pallas_call(
        functools.partial(prep_kernel, heads),
        out_shape=[jax.ShapeDtypeStruct((rows, 2 * HD), key.dtype)] * heads
        + [jax.ShapeDtypeStruct(s.shape, s.dtype) for s in smalls],
        in_specs=[HBM] * (2 + len(smalls)),
        out_specs=[VMEM] * (heads + len(smalls)),
        scratch_shapes=[pltpu.SemaphoreType.DMA((2 * heads + len(smalls),))],
        compiler_params=params(16),
        name="prep",
    )(key, value, *smalls)
    return outs[:heads], outs[heads:]


def pipelined(tasks, scores, finish):
    ahead = scores(tasks[0])
    for i, task in enumerate(tasks):
        now = ahead
        if i + 1 < len(tasks):
            ahead = scores(tasks[i + 1])
        finish(task, now)


def local_kernel(q_ref, kv_ref, o_ref, l_ref, ve):
    step = pl.program_id(0)
    rows = q_ref.shape[0]

    @pl.when(step == 0)
    def _():
        ve[:, :HD] = kv_ref[:, HD:]
        ve[:, HD:] = jnp.ones((rows, HD), jnp.bfloat16)
        l_ref[...] = jnp.zeros(l_ref.shape, jnp.float32)

    lane = lax.broadcasted_iota(jnp.int32, (TILE, HD), 1)
    seen = lax.broadcasted_iota(jnp.int32, (TILE, TILE), 0) >= lax.broadcasted_iota(jnp.int32, (TILE, TILE), 1)

    def scores(task):
        j, at = task
        q = q_ref[at : at + TILE, j * HD : (j + 1) * HD]
        parts = [nt(q, kv_ref[:at, :HD])] if at else []
        parts.append(jnp.where(seen, nt(q, kv_ref[at : at + TILE, :HD]), NEG))
        return parts

    def finish(task, parts):
        j, at = task
        top = fold(jnp.maximum, [jnp.max(s, axis=1, keepdims=True) for s in parts])
        total = None
        for s, start in zip(parts, [0, at] if at else [at]):
            p = jnp.exp2((s - top) * C2).astype(jnp.bfloat16)
            part = nn(p, ve[start : start + s.shape[1], :])
            total = part if total is None else total + part
        z = total[:, HD:]
        o_ref[at : at + TILE, j * HD : (j + 1) * HD] = total[:, :HD] / z
        log = top * C2 + jnp.log2(z)
        l_ref[at : at + TILE, :] = jnp.where(lane == step * PAIR + j, log, l_ref[at : at + TILE, :])

    pipelined([(j, at) for j in range(PAIR) for at in range(0, rows, TILE)], scores, finish)


def local_attention(query, kv, g):
    rows = query.shape[0]
    steps = GROUP // PAIR
    whole = pl.BlockSpec((rows, 2 * HD), lambda h: (0, 0))
    return pl.pallas_call(
        local_kernel,
        grid=(steps,),
        out_shape=[
            jax.ShapeDtypeStruct((rows, GROUP * HD), jnp.float32),
            jax.ShapeDtypeStruct((rows, HD), jnp.float32),
        ],
        in_specs=[pl.BlockSpec((rows, PAIR * HD), lambda h: (0, g * steps + h)), whole],
        out_specs=[
            pl.BlockSpec((rows, PAIR * HD), lambda h: (0, h)),
            pl.BlockSpec((rows, HD), lambda h: (0, 0)),
        ],
        scratch_shapes=[pltpu.VMEM((rows, 2 * HD), jnp.bfloat16)],
        compiler_params=params(24),
        cost_estimate=pl.CostEstimate(
            flops=8 * GROUP * rows * rows * HD, bytes_accessed=6 * GROUP * rows * HD, transcendentals=GROUP * rows * rows
        ),
        name="local_attention",
    )(query, kv)


def anchor_kernel(count, blk_ref, q_ref, o_in, l_ref, *refs):
    cand, (o_ref, ka, vae) = refs[:count], refs[-3:]
    step = pl.program_id(0)
    rows = q_ref.shape[0]
    blk = blk_ref[0]

    @pl.when(step == 0)
    def _():
        vae[:, HD:] = jnp.ones((rows, HD), jnp.bfloat16)

        def take(ref):
            ka[...] = ref[:, :HD]
            vae[:, :HD] = ref[:, HD:]

        if count == 1:
            take(cand[0])
        else:
            pl.when(blk == 1)(lambda: take(cand[1]))
            pl.when(blk == 2)(lambda: take(cand[0]))
            pl.when(blk == 3)(lambda: take(cand[2]))

    lane = lax.broadcasted_iota(jnp.int32, (TILE, HD), 1)

    def scores(task):
        j, at = task
        return nt(q_ref[at : at + TILE, j * HD : (j + 1) * HD], ka[...])

    def finish(task, s):
        j, at = task
        log = jnp.sum(jnp.where(lane == step * PAIR + j, l_ref[at : at + TILE, :], 0.0), axis=1, keepdims=True)
        top = jnp.maximum(jnp.max(s, axis=1, keepdims=True) * C2, log)
        p = jnp.exp2(s * C2 - top).astype(jnp.bfloat16)
        total = nn(p, vae[...])
        w = jnp.exp2(log - top)
        o = o_in[at : at + TILE, j * HD : (j + 1) * HD]
        out = (total[:, :HD] + w * o) / (total[:, HD:] + w)
        o_ref[at : at + TILE, j * HD : (j + 1) * HD] = out.astype(jnp.bfloat16)

    @pl.when(blk > 0)
    def _():
        pipelined([(j, at) for j in range(PAIR) for at in range(0, rows, TILE)], scores, finish)

    @pl.when(blk == 0)
    def _():
        o_ref[...] = o_in[...].astype(jnp.bfloat16)


def anchor_attention(blk, query, state, cands, g, prior):
    rows = query.shape[0]
    steps = GROUP // PAIR
    block = (rows, PAIR * HD)
    column = pl.BlockSpec(block, lambda h: (0, g * steps + h))
    args = [blk, query, *state, *cands]
    specs = [SMEM, column, pl.BlockSpec(block, lambda h: (0, h)), pl.BlockSpec((rows, HD), lambda h: (0, 0))]
    specs += [pl.BlockSpec((rows, 2 * HD), lambda h: (0, 0))] * len(cands)
    alias = {}
    if prior is not None:
        alias = {len(args): 0}
        args.append(prior)
        specs.append(ANY)
    return pl.pallas_call(
        functools.partial(anchor_kernel, len(cands)),
        grid=(steps,),
        out_shape=jax.ShapeDtypeStruct(query.shape, query.dtype),
        in_specs=specs,
        out_specs=column,
        scratch_shapes=[pltpu.VMEM((rows, HD), jnp.bfloat16), pltpu.VMEM((rows, 2 * HD), jnp.bfloat16)],
        input_output_aliases=alias,
        compiler_params=params(24),
        cost_estimate=pl.CostEstimate(
            flops=8 * GROUP * rows * rows * HD, bytes_accessed=8 * GROUP * rows * HD, transcendentals=GROUP * rows * rows
        ),
        name="anchor_attention",
    )(*args)


def fold_order(n):
    bits = n.bit_length() - 1
    return sorted(range(n), key=lambda x: int(format(x, "0%db" % bits)[::-1], 2))


def option_kernel(masks, heads, blk_ref, owner_ref, slot_ref, length_ref, *refs):
    n = len(masks)
    kv_heads = heads // GROUP
    kv, queries = refs[:kv_heads], refs[kv_heads : kv_heads + n]
    keep, send, q_all, part = refs[kv_heads + n :]
    blk = blk_ref[0]
    rows = kv[0].shape[0]
    each = queries[0].shape[0]
    options = n * each
    for mask, query in zip(masks, queries):
        at = jnp.bitwise_xor(blk, mask) * each
        q_all[pl.ds(pl.multiple_of(at, each), each), :] = query[...]
    eye = lax.broadcasted_iota(jnp.int32, (options, options), 0) == lax.broadcasted_iota(jnp.int32, (options, options), 1)
    length = jnp.sum(jnp.where(eye, length_ref[...].astype(jnp.float32), 0.0), axis=1, keepdims=True)
    seen = length - (blk * rows).astype(jnp.float32)
    lane = lax.broadcasted_iota(jnp.int32, (options, HD), 1)
    logs = jnp.zeros((options, HD), jnp.float32)
    stack = max(1, min(GROUP, 512 // options))
    spots = lax.broadcasted_iota(jnp.int32, (options * stack, rows), 1).astype(jnp.float32)
    seen_all = jnp.concatenate([seen] * stack, axis=0)
    for first in range(0, heads, stack):
        g = first // GROUP
        q = jnp.concatenate([q_all[:, h * HD : (h + 1) * HD] for h in range(first, first + stack)], axis=0)
        s = nt(q, kv[g][:, :HD])
        s = jnp.where(spots < seen_all, s, NEG)
        top = jnp.max(s, axis=1, keepdims=True)
        e = jnp.exp2((s - top) * C2)
        z = jnp.sum(e, axis=1, keepdims=True)
        o = nn(e.astype(jnp.bfloat16), kv[g][:, HD:]) / z
        live = seen_all > 0
        o = jnp.where(live, o, 0.0).astype(jnp.bfloat16)
        log = jnp.where(live, top * SCALE + jnp.log(z), NEG)
        for j in range(stack):
            h = first + j
            part[:, h * HD : (h + 1) * HD] = o[j * options : (j + 1) * options]
            logs = jnp.where(lax.rem(lane, heads) == h, log[j * options : (j + 1) * options], logs)
    part[:, heads * HD :] = summands(logs, heads)
    slot = lax.broadcasted_iota(jnp.int32, (CAP, options), 0)
    order = fold_order(n)
    for half, out in ((order[: n // 2], keep), (order[n // 2 :], send)):
        for i, mask in enumerate(half):
            pick = (owner_ref[...] == jnp.bitwise_xor(blk, mask)) & (slot_ref[...] == slot)
            pick = jnp.where(pick, 1.0, 0.0).astype(jnp.bfloat16)
            out[i * CAP : (i + 1) * CAP, :] = nn(pick, part[...]).astype(jnp.bfloat16)


def summands(logs, heads):
    lane = lax.broadcasted_iota(jnp.int32, logs.shape, 1)
    high = logs.astype(jnp.bfloat16).astype(jnp.float32)
    rest = logs - high
    mid = rest.astype(jnp.bfloat16).astype(jnp.float32)
    low = rest - mid
    low = jnp.where(lane < 3 * heads, low, 0.0)
    return jnp.where(lane < heads, high, jnp.where(lane < 2 * heads, mid, low)).astype(jnp.bfloat16)


def option_partials(blk, owner, slot, length, kvs, masks, queries):
    n, heads = len(queries), queries[0].shape[1] // HD
    options = n * queries[0].shape[0]
    width = (heads + 1) * HD
    rows = kvs[0].shape[0]
    return pl.pallas_call(
        functools.partial(option_kernel, masks, heads),
        out_shape=[jax.ShapeDtypeStruct((n // 2 * CAP, width), jnp.bfloat16)] * 2,
        in_specs=[SMEM] + [VMEM] * (3 + len(kvs) + n),
        out_specs=[VMEM] * 2,
        scratch_shapes=[
            pltpu.VMEM((options, heads * HD), jnp.bfloat16),
            pltpu.VMEM((options, width), jnp.bfloat16),
        ],
        compiler_params=params(32),
        cost_estimate=pl.CostEstimate(
            flops=4 * options * heads * rows * HD, bytes_accessed=1 << 20, transcendentals=options * heads * rows
        ),
        name="option_partials",
    )(blk, owner, slot, length, *kvs, *queries)


def merge_kernel(heads, a, b, *outs):
    width = heads * HD
    lane = lax.broadcasted_iota(jnp.int32, (HD, width), 0)
    head = lax.broadcasted_iota(jnp.int32, (HD, width), 1) // HD
    pick = jnp.where((lax.rem(lane, heads) == head) & (lane < 3 * heads), 1.0, 0.0).astype(jnp.bfloat16)
    logs = [nn(x[:, width:], pick) for x in (a, b)]
    top = jnp.maximum(*logs)
    weights = [jnp.exp(log - top) for log in logs]
    total = weights[0] + weights[1]
    merged = (weights[0] * a[:, :width].astype(jnp.float32) + weights[1] * b[:, :width].astype(jnp.float32)) / total
    merged = merged.astype(jnp.bfloat16)
    if len(outs) == 1:
        outs[0][...] = merged
        return
    log = top + jnp.log(total)
    lane = lax.broadcasted_iota(jnp.int32, (a.shape[0], HD), 1)
    packed = jnp.zeros((a.shape[0], HD), jnp.float32)
    for h in range(heads):
        packed = jnp.where(lax.rem(lane, heads) == h, log[:, h * HD : (h + 1) * HD], packed)
    packed = summands(packed, heads)
    half = a.shape[0] // 2
    for i, out in enumerate(outs):
        out[:, :width] = merged[i * half : (i + 1) * half]
        out[:, width:] = packed[i * half : (i + 1) * half]


def merge(a, b, last):
    rows, width = a.shape
    heads = width // HD - 1
    if last:
        shapes = [jax.ShapeDtypeStruct((rows, heads * HD), jnp.bfloat16)]
    else:
        shapes = [jax.ShapeDtypeStruct((rows // 2, width), jnp.bfloat16)] * 2
    return pl.pallas_call(
        functools.partial(merge_kernel, heads),
        out_shape=shapes,
        in_specs=[VMEM] * 2,
        out_specs=[VMEM] * len(shapes),
        compiler_params=params(32),
        name="merge",
    )(a, b)


def swap(x, n, mask):
    return lax.ppermute(x, "blk", [(i, i ^ mask) for i in range(n)])


def from_root(x, blk):
    return lax.psum(jnp.where(blk == 0, x, jnp.zeros_like(x)), "blk")


def body(ctx_query, ctx_key, ctx_value, opt_query, opt_owner, opt_slot, opt_length):
    n = lax.axis_size("blk")
    blk = lax.axis_index("blk")
    blk_arr = blk.astype(jnp.int32).reshape(1)
    options = opt_owner.shape[0]
    rounds = n.bit_length() - 1

    masks, queries = [0], [opt_query]
    for bit in reversed(range(rounds)):
        queries = queries + [swap(q, n, 1 << bit) for q in queries]
        masks = masks + [m | (1 << bit) for m in masks]
    row = lambda x: x.reshape(1, options)
    kvs, smalls = prep(ctx_key, ctx_value, [row(opt_owner), row(opt_slot), row(opt_length), opt_query])
    queries[0] = smalls[3]

    if n == 4:
        first = [lax.ppermute(kv, "blk", [(0, 2)]) for kv in kvs]
        anchors = [(x, lax.ppermute(x, "blk", [(2, 1)]), lax.ppermute(x, "blk", [(2, 3)])) for x in first]
    else:
        anchors = [(from_root(kv, blk),) for kv in kvs]

    states = [local_attention(ctx_query, kv, g) for g, kv in enumerate(kvs)]
    keep, send = option_partials(blk_arr, *smalls[:3], kvs, masks, queries)
    for bit in range(rounds):
        got = swap(send, n, 1 << bit)
        last = bit == rounds - 1
        outs = merge(keep, got, last)
        if last:
            opt_out = outs[0]
        else:
            keep, send = outs
    ctx_out = None
    for g, state in enumerate(states):
        ctx_out = anchor_attention(blk_arr, ctx_query, state, anchors[g], g, ctx_out)
    return (ctx_out, opt_out)


def solution(mesh):
    spread = P(("groups", "blk"), "head")
    return jax.shard_map(
        body,
        mesh=mesh,
        in_specs=(spread, spread, spread, spread, P("groups"), P("groups"), P("groups")),
        out_specs=(spread, spread),
        check_vma=False,
    )
```

```python
import functools
import math

import jax
import jax.numpy as jnp
from jax import lax
from jax.experimental import pallas as pl
from jax.experimental.pallas import tpu as pltpu
from jax.sharding import PartitionSpec as P

HD = 128
HQ = 64
KVH = 8
CAP = 32
GROUP = HQ // KVH
SCALE = HD ** (-0.5)
C2 = SCALE * math.log2(math.e)
NEG = -1e30
TILE = 256
PAIR = 2
VMEM = pl.BlockSpec(memory_space=pltpu.VMEM)
SMEM = pl.BlockSpec(memory_space=pltpu.SMEM)
HBM = pl.BlockSpec(memory_space=pltpu.HBM)
ANY = pl.BlockSpec(memory_space=pl.ANY)
BRIEF = pl.CostEstimate(flops=1, bytes_accessed=1, transcendentals=0)


def nt(a, b):
    return lax.dot_general(a, b, (((1,), (1,)), ((), ())), preferred_element_type=jnp.float32)


def nn(a, b):
    return jnp.dot(a, b, preferred_element_type=jnp.float32)


def params(mib):
    return pltpu.CompilerParams(vmem_limit_bytes=mib * 1024 * 1024)


def fold(op, items):
    return functools.reduce(op, items)


def prep_kernel(heads, k_ref, v_ref, *refs):
    smalls = (len(refs) - heads - 1) // 2
    small_in, kv = refs[:smalls], refs[smalls : smalls + heads]
    small_out, sem = refs[smalls + heads : -1], refs[-1]
    copies = []
    for g in range(heads):
        for ref, at in ((k_ref, 0), (v_ref, HD)):
            copies.append((ref.at[:, g * HD : (g + 1) * HD], kv[g].at[:, at : at + HD]))
    copies += list(zip(small_in, small_out))
    started = [pltpu.make_async_copy(a, b, sem.at[i]) for i, (a, b) in enumerate(copies)]
    for copy in started:
        copy.start()
    for copy in started:
        copy.wait()


def prep(key, value, smalls):
    rows, heads = key.shape[0], key.shape[1] // HD
    outs = pl.pallas_call(
        functools.partial(prep_kernel, heads),
        out_shape=[jax.ShapeDtypeStruct((rows, 2 * HD), key.dtype)] * heads
        + [jax.ShapeDtypeStruct(s.shape, s.dtype) for s in smalls],
        in_specs=[HBM] * (2 + len(smalls)),
        out_specs=[VMEM] * (heads + len(smalls)),
        scratch_shapes=[pltpu.SemaphoreType.DMA((2 * heads + len(smalls),))],
        compiler_params=params(16),
        cost_estimate=BRIEF,
        name="prep",
    )(*[pltpu.with_memory_space_constraint(x, pltpu.HBM) for x in (key, value, *smalls)])
    return outs[:heads], outs[heads:]


def pipelined(tasks, scores, finish):
    ahead = scores(tasks[0])
    for i, task in enumerate(tasks):
        now = ahead
        if i + 1 < len(tasks):
            ahead = scores(tasks[i + 1])
        finish(task, now)


def local_kernel(q_ref, kv_ref, o_ref, l_ref, ve):
    step = pl.program_id(0)
    rows = q_ref.shape[0]

    @pl.when(step == 0)
    def _():
        ve[:, :HD] = kv_ref[:, HD:]
        ve[:, HD:] = jnp.ones((rows, HD), jnp.bfloat16)
        l_ref[...] = jnp.zeros(l_ref.shape, jnp.float32)

    lane = lax.broadcasted_iota(jnp.int32, (TILE, HD), 1)
    seen = lax.broadcasted_iota(jnp.int32, (TILE, TILE), 0) >= lax.broadcasted_iota(jnp.int32, (TILE, TILE), 1)

    def scores(task):
        j, at = task
        q = q_ref[at : at + TILE, j * HD : (j + 1) * HD]
        parts = [nt(q, kv_ref[:at, :HD])] if at else []
        parts.append(jnp.where(seen, nt(q, kv_ref[at : at + TILE, :HD]), NEG))
        return parts

    def finish(task, parts):
        j, at = task
        top = fold(jnp.maximum, [jnp.max(s, axis=1, keepdims=True) for s in parts])
        total = None
        for s, start in zip(parts, [0, at] if at else [at]):
            p = jnp.exp2((s - top) * C2).astype(jnp.bfloat16)
            part = nn(p, ve[start : start + s.shape[1], :])
            total = part if total is None else total + part
        z = total[:, HD:]
        o_ref[at : at + TILE, j * HD : (j + 1) * HD] = total[:, :HD] / z
        log = top * C2 + jnp.log2(z)
        l_ref[at : at + TILE, :] = jnp.where(lane == step * PAIR + j, log, l_ref[at : at + TILE, :])

    pipelined([(j, at) for j in range(PAIR) for at in range(0, rows, TILE)], scores, finish)


def local_attention(query, kv, g):
    rows = query.shape[0]
    steps = GROUP // PAIR
    whole = pl.BlockSpec((rows, 2 * HD), lambda h: (0, 0))
    return pl.pallas_call(
        local_kernel,
        grid=(steps,),
        out_shape=[
            jax.ShapeDtypeStruct((rows, GROUP * HD), jnp.float32),
            jax.ShapeDtypeStruct((rows, HD), jnp.float32),
        ],
        in_specs=[pl.BlockSpec((rows, PAIR * HD), lambda h: (0, g * steps + h)), whole],
        out_specs=[
            pl.BlockSpec((rows, PAIR * HD), lambda h: (0, h)),
            pl.BlockSpec((rows, HD), lambda h: (0, 0)),
        ],
        scratch_shapes=[pltpu.VMEM((rows, 2 * HD), jnp.bfloat16)],
        compiler_params=params(24),
        cost_estimate=BRIEF,
        name="local_attention",
    )(pltpu.with_memory_space_constraint(query, pltpu.HBM), kv)


def anchor_kernel(count, blk_ref, q_ref, o_in, l_ref, *refs):
    cand, (o_ref, ka, vae) = refs[:count], refs[-3:]
    step = pl.program_id(0)
    rows = q_ref.shape[0]
    blk = blk_ref[0]

    @pl.when(step == 0)
    def _():
        vae[:, HD:] = jnp.ones((rows, HD), jnp.bfloat16)

        def take(ref):
            ka[...] = ref[:, :HD]
            vae[:, :HD] = ref[:, HD:]

        if count == 1:
            take(cand[0])
        else:
            pl.when(blk == 1)(lambda: take(cand[1]))
            pl.when(blk == 2)(lambda: take(cand[0]))
            pl.when(blk == 3)(lambda: take(cand[2]))

    lane = lax.broadcasted_iota(jnp.int32, (TILE, HD), 1)

    def scores(task):
        j, at = task
        return nt(q_ref[at : at + TILE, j * HD : (j + 1) * HD], ka[...])

    def finish(task, s):
        j, at = task
        log = jnp.sum(jnp.where(lane == step * PAIR + j, l_ref[at : at + TILE, :], 0.0), axis=1, keepdims=True)
        top = jnp.maximum(jnp.max(s, axis=1, keepdims=True) * C2, log)
        p = jnp.exp2(s * C2 - top).astype(jnp.bfloat16)
        total = nn(p, vae[...])
        w = jnp.exp2(log - top)
        o = o_in[at : at + TILE, j * HD : (j + 1) * HD]
        out = (total[:, :HD] + w * o) / (total[:, HD:] + w)
        o_ref[at : at + TILE, j * HD : (j + 1) * HD] = out.astype(jnp.bfloat16)

    @pl.when(blk > 0)
    def _():
        pipelined([(j, at) for j in range(PAIR) for at in range(0, rows, TILE)], scores, finish)

    @pl.when(blk == 0)
    def _():
        o_ref[...] = o_in[...].astype(jnp.bfloat16)


def anchor_attention(blk, query, state, cands, g, prior):
    rows = query.shape[0]
    steps = GROUP // PAIR
    block = (rows, PAIR * HD)
    column = pl.BlockSpec(block, lambda h: (0, g * steps + h))
    args = [blk, query, *state, *cands]
    specs = [SMEM, column, pl.BlockSpec(block, lambda h: (0, h)), pl.BlockSpec((rows, HD), lambda h: (0, 0))]
    specs += [pl.BlockSpec((rows, 2 * HD), lambda h: (0, 0))] * len(cands)
    alias = {}
    if prior is not None:
        alias = {len(args): 0}
        args.append(prior)
        specs.append(ANY)
    return pl.pallas_call(
        functools.partial(anchor_kernel, len(cands)),
        grid=(steps,),
        out_shape=jax.ShapeDtypeStruct(query.shape, query.dtype),
        in_specs=specs,
        out_specs=column,
        scratch_shapes=[pltpu.VMEM((rows, HD), jnp.bfloat16), pltpu.VMEM((rows, 2 * HD), jnp.bfloat16)],
        input_output_aliases=alias,
        compiler_params=params(24),
        cost_estimate=BRIEF,
        name="anchor_attention",
    )(*args)


def fold_order(n):
    bits = n.bit_length() - 1
    return sorted(range(n), key=lambda x: int(format(x, "0%db" % bits)[::-1], 2))


def option_kernel(n, heads, blk_ref, owner_ref, slot_ref, length_ref, *refs):
    kv_heads = heads // GROUP
    kv, queries = refs[:kv_heads], refs[kv_heads : kv_heads + n]
    keep, send, q_all, part = refs[kv_heads + n + 1 :]
    blk = blk_ref[0]
    rows = kv[0].shape[0]
    each = queries[0].shape[0]
    options = n * each
    for mask, query in enumerate(queries):
        at = jnp.bitwise_xor(blk, mask) * each
        q_all[pl.ds(pl.multiple_of(at, each), each), :] = query[...]
    eye = lax.broadcasted_iota(jnp.int32, (options, options), 0) == lax.broadcasted_iota(jnp.int32, (options, options), 1)
    length = jnp.sum(jnp.where(eye, length_ref[...].astype(jnp.float32), 0.0), axis=1, keepdims=True)
    seen = length - (blk * rows).astype(jnp.float32)
    lane = lax.broadcasted_iota(jnp.int32, (options, HD), 1)
    logs = jnp.zeros((options, HD), jnp.float32)
    stack = max(1, min(GROUP, 512 // options))
    spots = lax.broadcasted_iota(jnp.int32, (options * stack, rows), 1).astype(jnp.float32)
    seen_all = jnp.concatenate([seen] * stack, axis=0)
    for first in range(0, heads, stack):
        g = first // GROUP
        q = jnp.concatenate([q_all[:, h * HD : (h + 1) * HD] for h in range(first, first + stack)], axis=0)
        s = nt(q, kv[g][:, :HD])
        s = jnp.where(spots < seen_all, s, NEG)
        top = jnp.max(s, axis=1, keepdims=True)
        e = jnp.exp2((s - top) * C2)
        z = jnp.sum(e, axis=1, keepdims=True)
        o = nn(e.astype(jnp.bfloat16), kv[g][:, HD:]) / z
        live = seen_all > 0
        o = jnp.where(live, o, 0.0).astype(jnp.bfloat16)
        log = jnp.where(live, top * SCALE + jnp.log(z), NEG)
        for j in range(stack):
            h = first + j
            part[:, h * HD : (h + 1) * HD] = o[j * options : (j + 1) * options]
            logs = jnp.where(lax.rem(lane, heads) == h, log[j * options : (j + 1) * options], logs)
    part[:, heads * HD :] = summands(logs, heads)
    slot = lax.broadcasted_iota(jnp.int32, (CAP, options), 0)
    order = fold_order(n)
    for half, out in ((order[: n // 2], keep), (order[n // 2 :], send)):
        for i, mask in enumerate(half):
            pick = (owner_ref[...] == jnp.bitwise_xor(blk, mask)) & (slot_ref[...] == slot)
            pick = jnp.where(pick, 1.0, 0.0).astype(jnp.bfloat16)
            out[i * CAP : (i + 1) * CAP, :] = nn(pick, part[...]).astype(jnp.bfloat16)


def summands(logs, heads):
    lane = lax.broadcasted_iota(jnp.int32, logs.shape, 1)
    high = logs.astype(jnp.bfloat16).astype(jnp.float32)
    rest = logs - high
    mid = rest.astype(jnp.bfloat16).astype(jnp.float32)
    low = rest - mid
    low = jnp.where(lane < 3 * heads, low, 0.0)
    return jnp.where(lane < heads, high, jnp.where(lane < 2 * heads, mid, low)).astype(jnp.bfloat16)


def option_partials(blk, owner, slot, length, kvs, queries, after):
    n, heads = len(queries), queries[0].shape[1] // HD
    options = n * queries[0].shape[0]
    width = (heads + 1) * HD
    rows = kvs[0].shape[0]
    return pl.pallas_call(
        functools.partial(option_kernel, n, heads),
        out_shape=[jax.ShapeDtypeStruct((n // 2 * CAP, width), jnp.bfloat16)] * 2,
        in_specs=[SMEM] + [VMEM] * (3 + len(kvs) + n) + [ANY],
        out_specs=[VMEM] * 2,
        scratch_shapes=[
            pltpu.VMEM((options, heads * HD), jnp.bfloat16),
            pltpu.VMEM((options, width), jnp.bfloat16),
        ],
        compiler_params=params(32),
        cost_estimate=BRIEF,
        name="option_partials",
    )(blk, owner, slot, length, *kvs, *queries, after)


def merge_kernel(heads, a, b, after, *outs):
    width = heads * HD
    lane = lax.broadcasted_iota(jnp.int32, (HD, width), 0)
    head = lax.broadcasted_iota(jnp.int32, (HD, width), 1) // HD
    pick = jnp.where((lax.rem(lane, heads) == head) & (lane < 3 * heads), 1.0, 0.0).astype(jnp.bfloat16)
    logs = [nn(x[:, width:], pick) for x in (a, b)]
    top = jnp.maximum(*logs)
    weights = [jnp.exp(log - top) for log in logs]
    total = weights[0] + weights[1]
    merged = (weights[0] * a[:, :width].astype(jnp.float32) + weights[1] * b[:, :width].astype(jnp.float32)) / total
    merged = merged.astype(jnp.bfloat16)
    if len(outs) == 1:
        outs[0][...] = merged
        return
    log = top + jnp.log(total)
    lane = lax.broadcasted_iota(jnp.int32, (a.shape[0], HD), 1)
    packed = jnp.zeros((a.shape[0], HD), jnp.float32)
    for h in range(heads):
        packed = jnp.where(lax.rem(lane, heads) == h, log[:, h * HD : (h + 1) * HD], packed)
    packed = summands(packed, heads)
    half = a.shape[0] // 2
    for i, out in enumerate(outs):
        out[:, :width] = merged[i * half : (i + 1) * half]
        out[:, width:] = packed[i * half : (i + 1) * half]


def merge(a, b, last, after):
    rows, width = a.shape
    heads = width // HD - 1
    if last:
        shapes = [jax.ShapeDtypeStruct((rows, heads * HD), jnp.bfloat16)]
    else:
        shapes = [jax.ShapeDtypeStruct((rows // 2, width), jnp.bfloat16)] * 2
    return pl.pallas_call(
        functools.partial(merge_kernel, heads),
        out_shape=shapes,
        in_specs=[VMEM] * 2 + [ANY],
        out_specs=[VMEM] * len(shapes),
        compiler_params=params(32),
        cost_estimate=BRIEF,
        name="merge",
    )(a, b, after)


def swap(x, n, mask):
    return lax.ppermute(x, "blk", [(i, i ^ mask) for i in range(n)])


def from_root(x, blk):
    return lax.psum(jnp.where(blk == 0, x, jnp.zeros_like(x)), "blk")


def body(ctx_query, ctx_key, ctx_value, opt_query, opt_owner, opt_slot, opt_length):
    n = lax.axis_size("blk")
    blk = lax.axis_index("blk")
    blk_arr = blk.astype(jnp.int32).reshape(1)
    options = opt_owner.shape[0]
    rounds = n.bit_length() - 1

    queries = [opt_query] + [swap(opt_query, n, mask) for mask in range(1, n)]
    row = lambda x: x.reshape(1, options)
    kvs, smalls = prep(ctx_key, ctx_value, [row(opt_owner), row(opt_slot), row(opt_length), opt_query])
    queries[0] = smalls[3]

    states = [local_attention(ctx_query, kvs[0], 0)]
    queries, kvs, states = lax.optimization_barrier((queries, kvs, states))
    states += [local_attention(ctx_query, kv, g) for g, kv in enumerate(kvs) if g]
    if n == 4:
        first = [lax.ppermute(kv, "blk", [(0, 2)]) for kv in kvs]
        first[1:], states = lax.optimization_barrier((first[1:], states))
        anchors = [(x, lax.ppermute(x, "blk", [(2, 1)]), lax.ppermute(x, "blk", [(2, 3)])) for x in first]
    else:
        anchors = [(from_root(kv, blk),) for kv in kvs]

    keep, send = option_partials(blk_arr, *smalls[:3], kvs, queries, states[0][1])
    for bit in range(rounds):
        got = swap(send, n, 1 << bit)
        last = bit == rounds - 1
        outs = merge(keep, got, last, states[-1][1])
        if last:
            opt_out = outs[0]
        else:
            keep, send = outs
    ctx_out = None
    for g, state in enumerate(states):
        ctx_out = anchor_attention(blk_arr, ctx_query, state, anchors[g], g, ctx_out)
    return (ctx_out, opt_out)


def solution(mesh):
    spread = P(("groups", "blk"), "head")
    return jax.shard_map(
        body,
        mesh=mesh,
        in_specs=(spread, spread, spread, spread, P("groups"), P("groups"), P("groups")),
        out_specs=(spread, spread),
        check_vma=False,
    )
```

```python
import functools
import math

import jax
import jax.numpy as jnp
from jax import lax
from jax.experimental import pallas as pl
from jax.experimental.pallas import tpu as pltpu
from jax.sharding import PartitionSpec as P

HD = 128
HQ = 64
KVH = 8
CAP = 32
GROUP = HQ // KVH
SCALE = HD ** (-0.5)
C2 = SCALE * math.log2(math.e)
NEG = -1e30
TILE = 256
PAIR = 2
VMEM = pl.BlockSpec(memory_space=pltpu.VMEM)
SMEM = pl.BlockSpec(memory_space=pltpu.SMEM)
HBM = pl.BlockSpec(memory_space=pltpu.HBM)
ANY = pl.BlockSpec(memory_space=pl.ANY)
BRIEF = pl.CostEstimate(flops=1, bytes_accessed=1, transcendentals=0)


def nt(a, b):
    return lax.dot_general(a, b, (((1,), (1,)), ((), ())), preferred_element_type=jnp.float32)


def nn(a, b):
    return jnp.dot(a, b, preferred_element_type=jnp.float32)


def params(mib):
    return pltpu.CompilerParams(vmem_limit_bytes=mib * 1024 * 1024)


def fold(op, items):
    return functools.reduce(op, items)


def prep_kernel(heads, k_ref, v_ref, *refs):
    smalls = (len(refs) - heads - 1) // 2
    small_in, kv = refs[:smalls], refs[smalls : smalls + heads]
    small_out, sem = refs[smalls + heads : -1], refs[-1]
    copies = []
    for g in range(heads):
        for ref, at in ((k_ref, 0), (v_ref, HD)):
            copies.append((ref.at[:, g * HD : (g + 1) * HD], kv[g].at[:, at : at + HD]))
    copies += list(zip(small_in, small_out))
    started = [pltpu.make_async_copy(a, b, sem.at[i]) for i, (a, b) in enumerate(copies)]
    for copy in started:
        copy.start()
    for copy in started:
        copy.wait()


def prep(key, value, smalls):
    rows, heads = key.shape[0], key.shape[1] // HD
    outs = pl.pallas_call(
        functools.partial(prep_kernel, heads),
        out_shape=[jax.ShapeDtypeStruct((rows, 2 * HD), key.dtype)] * heads
        + [jax.ShapeDtypeStruct(s.shape, s.dtype) for s in smalls],
        in_specs=[HBM] * (2 + len(smalls)),
        out_specs=[VMEM] * (heads + len(smalls)),
        scratch_shapes=[pltpu.SemaphoreType.DMA((2 * heads + len(smalls),))],
        compiler_params=params(16),
        cost_estimate=BRIEF,
        name="prep",
    )(*[pltpu.with_memory_space_constraint(x, pltpu.HBM) for x in (key, value, *smalls)])
    return list(outs[:heads]), list(outs[heads:])


def pipelined(tasks, scores, finish):
    ahead = scores(tasks[0])
    for i, task in enumerate(tasks):
        now = ahead
        if i + 1 < len(tasks):
            ahead = scores(tasks[i + 1])
        finish(task, now)


def local_kernel(q_ref, kv_ref, o_ref, l_ref, ve):
    step = pl.program_id(0)
    rows = q_ref.shape[0]

    @pl.when(step == 0)
    def _():
        ve[:, :HD] = kv_ref[:, HD:]
        ve[:, HD:] = jnp.ones((rows, HD), jnp.bfloat16)
        l_ref[...] = jnp.zeros(l_ref.shape, jnp.float32)

    lane = lax.broadcasted_iota(jnp.int32, (TILE, HD), 1)
    seen = lax.broadcasted_iota(jnp.int32, (TILE, TILE), 0) >= lax.broadcasted_iota(jnp.int32, (TILE, TILE), 1)

    def scores(task):
        j, at = task
        q = q_ref[at : at + TILE, j * HD : (j + 1) * HD]
        parts = [nt(q, kv_ref[:at, :HD])] if at else []
        parts.append(jnp.where(seen, nt(q, kv_ref[at : at + TILE, :HD]), NEG))
        return parts

    def finish(task, parts):
        j, at = task
        top = fold(jnp.maximum, [jnp.max(s, axis=1, keepdims=True) for s in parts])
        total = None
        for s, start in zip(parts, [0, at] if at else [at]):
            p = jnp.exp2((s - top) * C2).astype(jnp.bfloat16)
            part = nn(p, ve[start : start + s.shape[1], :])
            total = part if total is None else total + part
        z = total[:, HD:]
        o_ref[at : at + TILE, j * HD : (j + 1) * HD] = total[:, :HD] / z
        log = top * C2 + jnp.log2(z)
        l_ref[at : at + TILE, :] = jnp.where(lane == step * PAIR + j, log, l_ref[at : at + TILE, :])

    pipelined([(j, at) for j in range(PAIR) for at in range(0, rows, TILE)], scores, finish)


def local_attention(query, kv, g):
    rows = query.shape[0]
    steps = GROUP // PAIR
    whole = pl.BlockSpec((rows, 2 * HD), lambda h: (0, 0))
    return pl.pallas_call(
        local_kernel,
        grid=(steps,),
        out_shape=[
            jax.ShapeDtypeStruct((rows, GROUP * HD), jnp.float32),
            jax.ShapeDtypeStruct((rows, HD), jnp.float32),
        ],
        in_specs=[pl.BlockSpec((rows, PAIR * HD), lambda h: (0, g * steps + h)), whole],
        out_specs=[
            pl.BlockSpec((rows, PAIR * HD), lambda h: (0, h)),
            pl.BlockSpec((rows, HD), lambda h: (0, 0)),
        ],
        scratch_shapes=[pltpu.VMEM((rows, 2 * HD), jnp.bfloat16)],
        compiler_params=params(24),
        cost_estimate=BRIEF,
        name="local_attention",
    )(query, kv)


def anchor_kernel(count, blk_ref, q_ref, o_in, l_ref, *refs):
    cand, (o_ref, ka, vae) = refs[:count], refs[-3:]
    step = pl.program_id(0)
    rows = q_ref.shape[0]
    blk = blk_ref[0]

    @pl.when(step == 0)
    def _():
        vae[:, HD:] = jnp.ones((rows, HD), jnp.bfloat16)

        def take(ref):
            ka[...] = ref[:, :HD]
            vae[:, :HD] = ref[:, HD:]

        if count == 1:
            take(cand[0])
        else:
            pl.when(blk == 1)(lambda: take(cand[1]))
            pl.when(blk == 2)(lambda: take(cand[0]))
            pl.when(blk == 3)(lambda: take(cand[2]))

    lane = lax.broadcasted_iota(jnp.int32, (TILE, HD), 1)

    def scores(task):
        j, at = task
        return nt(q_ref[at : at + TILE, j * HD : (j + 1) * HD], ka[...])

    def finish(task, s):
        j, at = task
        log = jnp.sum(jnp.where(lane == step * PAIR + j, l_ref[at : at + TILE, :], 0.0), axis=1, keepdims=True)
        top = jnp.maximum(jnp.max(s, axis=1, keepdims=True) * C2, log)
        p = jnp.exp2(s * C2 - top).astype(jnp.bfloat16)
        total = nn(p, vae[...])
        w = jnp.exp2(log - top)
        o = o_in[at : at + TILE, j * HD : (j + 1) * HD]
        out = (total[:, :HD] + w * o) / (total[:, HD:] + w)
        o_ref[at : at + TILE, j * HD : (j + 1) * HD] = out.astype(jnp.bfloat16)

    @pl.when(blk > 0)
    def _():
        pipelined([(j, at) for j in range(PAIR) for at in range(0, rows, TILE)], scores, finish)

    @pl.when(blk == 0)
    def _():
        o_ref[...] = o_in[...].astype(jnp.bfloat16)


def anchor_attention(blk, query, state, cands, g, prior):
    rows = query.shape[0]
    steps = GROUP // PAIR
    block = (rows, PAIR * HD)
    column = pl.BlockSpec(block, lambda h: (0, g * steps + h))
    args = [blk, query, *state, *cands]
    specs = [SMEM, column, pl.BlockSpec(block, lambda h: (0, h)), pl.BlockSpec((rows, HD), lambda h: (0, 0))]
    specs += [pl.BlockSpec((rows, 2 * HD), lambda h: (0, 0))] * len(cands)
    alias = {}
    if prior is not None:
        alias = {len(args): 0}
        args.append(prior)
        specs.append(ANY)
    return pl.pallas_call(
        functools.partial(anchor_kernel, len(cands)),
        grid=(steps,),
        out_shape=jax.ShapeDtypeStruct(query.shape, query.dtype),
        in_specs=specs,
        out_specs=column,
        scratch_shapes=[pltpu.VMEM((rows, HD), jnp.bfloat16), pltpu.VMEM((rows, 2 * HD), jnp.bfloat16)],
        input_output_aliases=alias,
        compiler_params=params(24),
        cost_estimate=BRIEF,
        name="anchor_attention",
    )(*args)


def fold_order(n):
    bits = n.bit_length() - 1
    return sorted(range(n), key=lambda x: int(format(x, "0%db" % bits)[::-1], 2))


def option_kernel(n, heads, blk_ref, owner_ref, slot_ref, length_ref, *refs):
    kv_heads = heads // GROUP
    kv, queries = refs[:kv_heads], refs[kv_heads : kv_heads + n]
    keep, send, q_all, part = refs[kv_heads + n + 1 :]
    blk = blk_ref[0]
    rows = kv[0].shape[0]
    each = queries[0].shape[0]
    options = n * each
    for mask, query in enumerate(queries):
        at = jnp.bitwise_xor(blk, mask) * each
        q_all[pl.ds(pl.multiple_of(at, each), each), :] = query[...]
    eye = lax.broadcasted_iota(jnp.int32, (options, options), 0) == lax.broadcasted_iota(jnp.int32, (options, options), 1)
    length = jnp.sum(jnp.where(eye, length_ref[...].astype(jnp.float32), 0.0), axis=1, keepdims=True)
    seen = length - (blk * rows).astype(jnp.float32)
    lane = lax.broadcasted_iota(jnp.int32, (options, HD), 1)
    logs = jnp.zeros((options, HD), jnp.float32)
    stack = max(1, min(GROUP, 512 // options))
    spots = lax.broadcasted_iota(jnp.int32, (options * stack, rows), 1).astype(jnp.float32)
    seen_all = jnp.concatenate([seen] * stack, axis=0)
    for first in range(0, heads, stack):
        g = first // GROUP
        q = jnp.concatenate([q_all[:, h * HD : (h + 1) * HD] for h in range(first, first + stack)], axis=0)
        s = nt(q, kv[g][:, :HD])
        s = jnp.where(spots < seen_all, s, NEG)
        top = jnp.max(s, axis=1, keepdims=True)
        e = jnp.exp2((s - top) * C2)
        z = jnp.sum(e, axis=1, keepdims=True)
        o = nn(e.astype(jnp.bfloat16), kv[g][:, HD:]) / z
        live = seen_all > 0
        o = jnp.where(live, o, 0.0).astype(jnp.bfloat16)
        log = jnp.where(live, top * SCALE + jnp.log(z), NEG)
        for j in range(stack):
            h = first + j
            part[:, h * HD : (h + 1) * HD] = o[j * options : (j + 1) * options]
            logs = jnp.where(lax.rem(lane, heads) == h, log[j * options : (j + 1) * options], logs)
    part[:, heads * HD :] = summands(logs, heads)
    slot = lax.broadcasted_iota(jnp.int32, (CAP, options), 0)
    order = fold_order(n)
    for half, out in ((order[: n // 2], keep), (order[n // 2 :], send)):
        for i, mask in enumerate(half):
            pick = (owner_ref[...] == jnp.bitwise_xor(blk, mask)) & (slot_ref[...] == slot)
            pick = jnp.where(pick, 1.0, 0.0).astype(jnp.bfloat16)
            out[i * CAP : (i + 1) * CAP, :] = nn(pick, part[...]).astype(jnp.bfloat16)


def summands(logs, heads):
    lane = lax.broadcasted_iota(jnp.int32, logs.shape, 1)
    high = logs.astype(jnp.bfloat16).astype(jnp.float32)
    rest = logs - high
    mid = rest.astype(jnp.bfloat16).astype(jnp.float32)
    low = rest - mid
    low = jnp.where(lane < 3 * heads, low, 0.0)
    return jnp.where(lane < heads, high, jnp.where(lane < 2 * heads, mid, low)).astype(jnp.bfloat16)


def option_partials(blk, owner, slot, length, kvs, queries, after):
    n, heads = len(queries), queries[0].shape[1] // HD
    options = n * queries[0].shape[0]
    width = (heads + 1) * HD
    rows = kvs[0].shape[0]
    return pl.pallas_call(
        functools.partial(option_kernel, n, heads),
        out_shape=[jax.ShapeDtypeStruct((n // 2 * CAP, width), jnp.bfloat16)] * 2,
        in_specs=[SMEM] + [VMEM] * (3 + len(kvs) + n) + [ANY],
        out_specs=[VMEM] * 2,
        scratch_shapes=[
            pltpu.VMEM((options, heads * HD), jnp.bfloat16),
            pltpu.VMEM((options, width), jnp.bfloat16),
        ],
        compiler_params=params(32),
        cost_estimate=BRIEF,
        name="option_partials",
    )(blk, owner, slot, length, *kvs, *queries, after)


def merge_kernel(heads, a, b, after, *outs):
    width = heads * HD
    lane = lax.broadcasted_iota(jnp.int32, (HD, width), 0)
    head = lax.broadcasted_iota(jnp.int32, (HD, width), 1) // HD
    pick = jnp.where((lax.rem(lane, heads) == head) & (lane < 3 * heads), 1.0, 0.0).astype(jnp.bfloat16)
    logs = [nn(x[:, width:], pick) for x in (a, b)]
    top = jnp.maximum(*logs)
    weights = [jnp.exp(log - top) for log in logs]
    total = weights[0] + weights[1]
    merged = (weights[0] * a[:, :width].astype(jnp.float32) + weights[1] * b[:, :width].astype(jnp.float32)) / total
    merged = merged.astype(jnp.bfloat16)
    if len(outs) == 1:
        outs[0][...] = merged
        return
    log = top + jnp.log(total)
    lane = lax.broadcasted_iota(jnp.int32, (a.shape[0], HD), 1)
    packed = jnp.zeros((a.shape[0], HD), jnp.float32)
    for h in range(heads):
        packed = jnp.where(lax.rem(lane, heads) == h, log[:, h * HD : (h + 1) * HD], packed)
    packed = summands(packed, heads)
    half = a.shape[0] // 2
    for i, out in enumerate(outs):
        out[:, :width] = merged[i * half : (i + 1) * half]
        out[:, width:] = packed[i * half : (i + 1) * half]


def merge(a, b, last, after):
    rows, width = a.shape
    heads = width // HD - 1
    if last:
        shapes = [jax.ShapeDtypeStruct((rows, heads * HD), jnp.bfloat16)]
    else:
        shapes = [jax.ShapeDtypeStruct((rows // 2, width), jnp.bfloat16)] * 2
    return pl.pallas_call(
        functools.partial(merge_kernel, heads),
        out_shape=shapes,
        in_specs=[VMEM] * 2 + [ANY],
        out_specs=[VMEM] * len(shapes),
        compiler_params=params(32),
        cost_estimate=BRIEF,
        name="merge",
    )(a, b, after)


def swap(x, n, mask):
    return lax.ppermute(x, "blk", [(i, i ^ mask) for i in range(n)])


def from_root(x, blk):
    return lax.psum(jnp.where(blk == 0, x, jnp.zeros_like(x)), "blk")


def body(ctx_query, ctx_key, ctx_value, opt_query, opt_owner, opt_slot, opt_length):
    n = lax.axis_size("blk")
    blk = lax.axis_index("blk")
    blk_arr = blk.astype(jnp.int32).reshape(1)
    options = opt_owner.shape[0]
    rounds = n.bit_length() - 1

    queries = [opt_query] + [swap(opt_query, n, mask) for mask in range(1, n)]
    row = lambda x: x.reshape(1, options)
    kvs, smalls = prep(ctx_key, ctx_value, [row(opt_owner), row(opt_slot), row(opt_length), opt_query, ctx_query])
    queries[0], ctx_query = smalls[3:]

    states = [local_attention(ctx_query, kvs[0], 0)]
    keep, send = option_partials(blk_arr, *smalls[:3], kvs, queries, states[0][1])
    if n == 4:
        first = [lax.ppermute(kv, "blk", [(0, 2)]) for kv in kvs]
        first[0], kvs[1:] = lax.optimization_barrier((first[0], kvs[1:]))
    states += [local_attention(ctx_query, kv, g) for g, kv in enumerate(kvs) if g]
    if n == 4:
        first[1:], states = lax.optimization_barrier((first[1:], states))
        anchors = [(x, lax.ppermute(x, "blk", [(2, 1)]), lax.ppermute(x, "blk", [(2, 3)])) for x in first]
    else:
        anchors = [(from_root(kv, blk),) for kv in kvs]

    for bit in range(rounds):
        got = swap(send, n, 1 << bit)
        last = bit == rounds - 1
        outs = merge(keep, got, last, states[-1][1])
        if last:
            opt_out = outs[0]
        else:
            keep, send = outs
    ctx_out = None
    for g, state in enumerate(states):
        ctx_out = anchor_attention(blk_arr, ctx_query, state, anchors[g], g, ctx_out)
    return (ctx_out, opt_out)


def solution(mesh):
    spread = P(("groups", "blk"), "head")
    return jax.shard_map(
        body,
        mesh=mesh,
        in_specs=(spread, spread, spread, spread, P("groups"), P("groups"), P("groups")),
        out_specs=(spread, spread),
        check_vma=False,
    )
```

```python
import functools
import math

import jax
import jax.numpy as jnp
from jax import lax
from jax.experimental import pallas as pl
from jax.experimental.pallas import tpu as pltpu
from jax.sharding import PartitionSpec as P

HD = 128
HQ = 64
KVH = 8
CAP = 32
GROUP = HQ // KVH
SCALE = HD ** (-0.5)
C2 = SCALE * math.log2(math.e)
NEG = -1e30
TILE = 256
PAIR = 2
VMEM = pl.BlockSpec(memory_space=pltpu.VMEM)
SMEM = pl.BlockSpec(memory_space=pltpu.SMEM)
HBM = pl.BlockSpec(memory_space=pltpu.HBM)
ANY = pl.BlockSpec(memory_space=pl.ANY)
LONG = pl.CostEstimate(flops=10**11, bytes_accessed=1, transcendentals=0)
BRIEF = pl.CostEstimate(flops=1, bytes_accessed=1, transcendentals=0)


def nt(a, b):
    return lax.dot_general(a, b, (((1,), (1,)), ((), ())), preferred_element_type=jnp.float32)


def nn(a, b):
    return jnp.dot(a, b, preferred_element_type=jnp.float32)


def params(mib):
    return pltpu.CompilerParams(vmem_limit_bytes=mib * 1024 * 1024)


def fold(op, items):
    return functools.reduce(op, items)


def prep_kernel(heads, k_ref, v_ref, *refs):
    smalls = (len(refs) - heads - 1) // 2
    small_in, kv = refs[:smalls], refs[smalls : smalls + heads]
    small_out, sem = refs[smalls + heads : -1], refs[-1]
    copies = []
    for g in range(heads):
        for ref, at in ((k_ref, 0), (v_ref, HD)):
            copies.append((ref.at[:, g * HD : (g + 1) * HD], kv[g].at[:, at : at + HD]))
    copies += list(zip(small_in, small_out))
    started = [pltpu.make_async_copy(a, b, sem.at[i]) for i, (a, b) in enumerate(copies)]
    for copy in started:
        copy.start()
    for copy in started:
        copy.wait()


def prep(key, value, smalls):
    rows, heads = key.shape[0], key.shape[1] // HD
    outs = pl.pallas_call(
        functools.partial(prep_kernel, heads),
        out_shape=[jax.ShapeDtypeStruct((rows, 2 * HD), key.dtype)] * heads
        + [jax.ShapeDtypeStruct(s.shape, s.dtype) for s in smalls],
        in_specs=[HBM] * (2 + len(smalls)),
        out_specs=[VMEM] * (heads + len(smalls)),
        scratch_shapes=[pltpu.SemaphoreType.DMA((2 * heads + len(smalls),))],
        compiler_params=params(16),
        cost_estimate=BRIEF,
        name="prep",
    )(*[pltpu.with_memory_space_constraint(x, pltpu.HBM) for x in (key, value, *smalls)])
    return list(outs[:heads]), list(outs[heads:])


def pipelined(tasks, scores, finish):
    ahead = scores(tasks[0])
    for i, task in enumerate(tasks):
        now = ahead
        if i + 1 < len(tasks):
            ahead = scores(tasks[i + 1])
        finish(task, now)


def head_columns(h):
    return slice(h * HD, (h + 1) * HD)


def local_kernel(g, q_ref, kv_ref, acc_ref, top_ref, sum_ref, ve):
    rows = q_ref.shape[0]
    ve[:, :HD] = kv_ref[:, HD:]
    ve[:, HD:] = jnp.ones((rows, HD), jnp.bfloat16)
    row = lax.broadcasted_iota(jnp.int32, (PAIR * TILE, TILE), 0)
    seen = lax.rem(row, TILE) >= lax.broadcasted_iota(jnp.int32, (PAIR * TILE, TILE), 1)

    def scores(task):
        first, at = task
        q = jnp.concatenate([q_ref[at : at + TILE, head_columns(g * GROUP + first + j)] for j in range(PAIR)], axis=0)
        parts = [nt(q, kv_ref[:at, :HD])] if at else []
        parts.append(jnp.where(seen, nt(q, kv_ref[at : at + TILE, :HD]), NEG))
        return parts

    def finish(task, parts):
        first, at = task
        top = fold(jnp.maximum, [jnp.max(s, axis=1, keepdims=True) for s in parts])
        total = None
        for s, start in zip(parts, [0, at] if at else [at]):
            p = jnp.exp2((s - top) * C2).astype(jnp.bfloat16)
            part = nn(p, ve[start : start + s.shape[1], :])
            total = part if total is None else total + part
        top = jnp.broadcast_to(top * C2, (PAIR * TILE, HD))
        for j in range(PAIR):
            here, at_j = (slice(at, at + TILE), head_columns(first + j)), slice(j * TILE, (j + 1) * TILE)
            acc_ref[here] = total[at_j, :HD]
            sum_ref[here] = total[at_j, HD:]
            top_ref[here] = top[at_j]

    pipelined([(h, at) for h in range(0, GROUP, PAIR) for at in range(0, rows, TILE)], scores, finish)


def local_attention(query, kv, g):
    rows = query.shape[0]
    return pl.pallas_call(
        functools.partial(local_kernel, g),
        out_shape=[jax.ShapeDtypeStruct((rows, GROUP * HD), jnp.float32)] * 3,
        in_specs=[VMEM] * 2,
        out_specs=[VMEM] * 3,
        scratch_shapes=[pltpu.VMEM((rows, 2 * HD), jnp.bfloat16)],
        compiler_params=params(16),
        cost_estimate=LONG,
        name="local_attention",
    )(query, kv)


def anchor_kernel(g, count, prior, blk_ref, q_ref, acc_ref, top_ref, sum_ref, *refs):
    cand, (o_ref, token, ka, vae, out, sem) = refs[:count], refs[count + prior :]
    rows = q_ref.shape[0]
    blk = blk_ref[0]
    token[...] = jnp.zeros(token.shape, jnp.float32)

    def leave(h):
        return pltpu.make_async_copy(out.at[h], o_ref.at[:, head_columns(g * GROUP + h)], sem.at[h])

    def take(ref):
        ka[...] = ref[:, :HD]
        vae[:, :HD] = ref[:, HD:]

    if count == 1:
        take(cand[0])
    else:
        pl.when(blk == 1)(lambda: take(cand[1]))
        pl.when(blk == 2)(lambda: take(cand[0]))
        pl.when(blk == 3)(lambda: take(cand[2]))

    def scores(h):
        return nt(q_ref[:, head_columns(g * GROUP + h)], ka[...])

    def finish(h, s):
        held = (slice(None), head_columns(h))
        before = top_ref[held]
        top = jnp.maximum(jnp.max(s, axis=1, keepdims=True) * C2, before)
        p = [jnp.exp2(s[:, at : at + HD] * C2 - top).astype(jnp.bfloat16) for at in range(0, rows, HD)]
        total = nn(jnp.concatenate(p, axis=1), vae[...])
        w = jnp.exp2(before - top)
        o = (total[:, :HD] + w * acc_ref[held]) * inverse(total[:, HD:] + w * sum_ref[held])
        out[h] = o.astype(jnp.bfloat16)
        leave(h).start()

    @pl.when(blk > 0)
    def _():
        vae[:, HD:] = jnp.ones((rows, HD), jnp.bfloat16)
        pipelined(list(range(GROUP)), scores, finish)

    @pl.when(blk == 0)
    def _():
        for h in range(GROUP):
            held = (slice(None), head_columns(h))
            out[h] = (acc_ref[held] * inverse(sum_ref[held])).astype(jnp.bfloat16)
            leave(h).start()

    for h in range(GROUP):
        leave(h).wait()


def inverse(x):
    guess = pl.reciprocal(x, approx=True)
    return guess * (2.0 - x * guess)


def anchor_attention(blk, query, state, cands, g, prior):
    rows = query.shape[0]
    args = [blk, query, *state, *cands]
    specs = [SMEM] + [VMEM] * (4 + len(cands))
    alias = {}
    if prior is not None:
        alias = {len(args): 0}
        args.append(prior)
        specs.append(ANY)
    return pl.pallas_call(
        functools.partial(anchor_kernel, g, len(cands), len(alias)),
        out_shape=[jax.ShapeDtypeStruct(query.shape, query.dtype), jax.ShapeDtypeStruct((8, HD), jnp.float32)],
        in_specs=specs,
        out_specs=[ANY, VMEM],
        scratch_shapes=[
            pltpu.VMEM((rows, HD), jnp.bfloat16),
            pltpu.VMEM((rows, 2 * HD), jnp.bfloat16),
            pltpu.VMEM((GROUP, rows, HD), jnp.bfloat16),
            pltpu.SemaphoreType.DMA((GROUP,)),
        ],
        input_output_aliases=alias,
        compiler_params=params(16),
        cost_estimate=BRIEF,
        name="anchor_attention",
    )(*args)


def fold_order(n):
    bits = n.bit_length() - 1
    return sorted(range(n), key=lambda x: int(format(x, "0%db" % bits)[::-1], 2))


def option_kernel(n, heads, blk_ref, owner_ref, slot_ref, length_ref, *refs):
    kv_heads = heads // GROUP
    kv, queries = refs[:kv_heads], refs[kv_heads : kv_heads + n]
    keep, send, q_all, part = refs[kv_heads + n + 1 :]
    blk = blk_ref[0]
    rows = kv[0].shape[0]
    each = queries[0].shape[0]
    options = n * each
    for mask, query in enumerate(queries):
        at = jnp.bitwise_xor(blk, mask) * each
        q_all[pl.ds(pl.multiple_of(at, each), each), :] = query[...]
    eye = lax.broadcasted_iota(jnp.int32, (options, options), 0) == lax.broadcasted_iota(jnp.int32, (options, options), 1)
    length = jnp.sum(jnp.where(eye, length_ref[...].astype(jnp.float32), 0.0), axis=1, keepdims=True)
    seen = length - (blk * rows).astype(jnp.float32)
    lane = lax.broadcasted_iota(jnp.int32, (options, HD), 1)
    logs = jnp.zeros((options, HD), jnp.float32)
    stack = max(1, min(GROUP, 512 // options))
    spots = lax.broadcasted_iota(jnp.int32, (options * stack, rows), 1).astype(jnp.float32)
    seen_all = jnp.concatenate([seen] * stack, axis=0)
    for first in range(0, heads, stack):
        g = first // GROUP
        q = jnp.concatenate([q_all[:, h * HD : (h + 1) * HD] for h in range(first, first + stack)], axis=0)
        s = nt(q, kv[g][:, :HD])
        s = jnp.where(spots < seen_all, s, NEG)
        top = jnp.max(s, axis=1, keepdims=True)
        e = jnp.exp2((s - top) * C2)
        z = jnp.sum(e, axis=1, keepdims=True)
        o = nn(e.astype(jnp.bfloat16), kv[g][:, HD:]) / z
        live = seen_all > 0
        o = jnp.where(live, o, 0.0).astype(jnp.bfloat16)
        log = jnp.where(live, top * SCALE + jnp.log(z), NEG)
        for j in range(stack):
            h = first + j
            part[:, h * HD : (h + 1) * HD] = o[j * options : (j + 1) * options]
            logs = jnp.where(lax.rem(lane, heads) == h, log[j * options : (j + 1) * options], logs)
    part[:, heads * HD :] = summands(logs, heads)
    slot = lax.broadcasted_iota(jnp.int32, (CAP, options), 0)
    order = fold_order(n)
    for half, out in ((order[: n // 2], keep), (order[n // 2 :], send)):
        for i, mask in enumerate(half):
            pick = (owner_ref[...] == jnp.bitwise_xor(blk, mask)) & (slot_ref[...] == slot)
            pick = jnp.where(pick, 1.0, 0.0).astype(jnp.bfloat16)
            out[i * CAP : (i + 1) * CAP, :] = nn(pick, part[...]).astype(jnp.bfloat16)


def summands(logs, heads):
    lane = lax.broadcasted_iota(jnp.int32, logs.shape, 1)
    high = logs.astype(jnp.bfloat16).astype(jnp.float32)
    rest = logs - high
    mid = rest.astype(jnp.bfloat16).astype(jnp.float32)
    low = rest - mid
    low = jnp.where(lane < 3 * heads, low, 0.0)
    return jnp.where(lane < heads, high, jnp.where(lane < 2 * heads, mid, low)).astype(jnp.bfloat16)


def option_partials(blk, owner, slot, length, kvs, queries, after):
    n, heads = len(queries), queries[0].shape[1] // HD
    options = n * queries[0].shape[0]
    width = (heads + 1) * HD
    rows = kvs[0].shape[0]
    return pl.pallas_call(
        functools.partial(option_kernel, n, heads),
        out_shape=[jax.ShapeDtypeStruct((n // 2 * CAP, width), jnp.bfloat16)] * 2,
        in_specs=[SMEM] + [VMEM] * (3 + len(kvs) + n) + [ANY],
        out_specs=[VMEM] * 2,
        scratch_shapes=[
            pltpu.VMEM((options, heads * HD), jnp.bfloat16),
            pltpu.VMEM((options, width), jnp.bfloat16),
        ],
        compiler_params=params(16),
        cost_estimate=BRIEF,
        name="option_partials",
    )(blk, owner, slot, length, *kvs, *queries, after)


def merge_kernel(heads, a, b, after, *outs):
    width = heads * HD
    lane = lax.broadcasted_iota(jnp.int32, (HD, width), 0)
    head = lax.broadcasted_iota(jnp.int32, (HD, width), 1) // HD
    pick = jnp.where((lax.rem(lane, heads) == head) & (lane < 3 * heads), 1.0, 0.0).astype(jnp.bfloat16)
    logs = [nn(x[:, width:], pick) for x in (a, b)]
    top = jnp.maximum(*logs)
    weights = [jnp.exp(log - top) for log in logs]
    total = weights[0] + weights[1]
    merged = (weights[0] * a[:, :width].astype(jnp.float32) + weights[1] * b[:, :width].astype(jnp.float32)) / total
    merged = merged.astype(jnp.bfloat16)
    if len(outs) == 1:
        outs[0][...] = merged
        return
    log = top + jnp.log(total)
    lane = lax.broadcasted_iota(jnp.int32, (a.shape[0], HD), 1)
    packed = jnp.zeros((a.shape[0], HD), jnp.float32)
    for h in range(heads):
        packed = jnp.where(lax.rem(lane, heads) == h, log[:, h * HD : (h + 1) * HD], packed)
    packed = summands(packed, heads)
    half = a.shape[0] // 2
    for i, out in enumerate(outs):
        out[:, :width] = merged[i * half : (i + 1) * half]
        out[:, width:] = packed[i * half : (i + 1) * half]


def merge(a, b, last, after):
    rows, width = a.shape
    heads = width // HD - 1
    if last:
        shapes = [jax.ShapeDtypeStruct((rows, heads * HD), jnp.bfloat16)]
    else:
        shapes = [jax.ShapeDtypeStruct((rows // 2, width), jnp.bfloat16)] * 2
    return pl.pallas_call(
        functools.partial(merge_kernel, heads),
        out_shape=shapes,
        in_specs=[VMEM] * 2 + [ANY],
        out_specs=[VMEM] * len(shapes),
        compiler_params=params(16),
        cost_estimate=BRIEF,
        name="merge",
    )(a, b, after)


def swap(x, n, mask):
    return lax.ppermute(x, "blk", [(i, i ^ mask) for i in range(n)])


def from_root(x, blk):
    return lax.psum(jnp.where(blk == 0, x, jnp.zeros_like(x)), "blk")


def body(ctx_query, ctx_key, ctx_value, opt_query, opt_owner, opt_slot, opt_length):
    n = lax.axis_size("blk")
    blk = lax.axis_index("blk")
    blk_arr = blk.astype(jnp.int32).reshape(1)
    options = opt_owner.shape[0]
    rounds = n.bit_length() - 1

    queries = [opt_query] + [swap(opt_query, n, mask) for mask in range(1, n)]
    row = lambda x: x.reshape(1, options)
    kvs, smalls = prep(ctx_key, ctx_value, [row(opt_owner), row(opt_slot), row(opt_length), opt_query, ctx_query])
    queries[0], ctx_query = smalls[3:]

    hold = lax.optimization_barrier
    states = [local_attention(ctx_query, kvs[0], 0)]
    keep, send = option_partials(blk_arr, *smalls[:3], kvs, queries, states[0][1])
    if n == 4:
        first = [lax.ppermute(kv, "blk", [(0, 2)]) for kv in kvs]
        first[0], keep, kvs[1:] = hold((first[0], keep, kvs[1:]))
    states += [local_attention(ctx_query, kv, g) for g, kv in enumerate(kvs) if g]
    if n == 4:
        first[1:], states = hold((first[1:], states))
        anchors = [[x, lax.ppermute(x, "blk", [(2, 1)]), lax.ppermute(x, "blk", [(2, 3)])] for x in first]
        anchors[0], first[1:] = hold((anchors[0], first[1:]))
    else:
        anchors = [[from_root(kv, blk)] for kv in kvs]
    ctx_out, tokens = None, []
    for g, state in enumerate(states):
        ctx_out, token = anchor_attention(blk_arr, ctx_query, state, anchors[g], g, ctx_out)
        tokens.append(token)
    for bit in range(rounds):
        got = swap(send, n, 1 << bit)
        last = bit == rounds - 1
        outs = merge(keep, got, last, tokens[-1 if last else 0])
        if last:
            opt_out = outs[0]
        else:
            keep, send = outs
    return (ctx_out, opt_out)


def solution(mesh):
    spread = P(("groups", "blk"), "head")
    return jax.shard_map(
        body,
        mesh=mesh,
        in_specs=(spread, spread, spread, spread, P("groups"), P("groups"), P("groups")),
        out_specs=(spread, spread),
        check_vma=False,
    )
```

```python
import functools
import math

import jax
import jax.numpy as jnp
from jax import lax
from jax.experimental import pallas as pl
from jax.experimental.pallas import tpu as pltpu
from jax.sharding import PartitionSpec as P

HD = 128
HQ = 64
KVH = 8
CAP = 32
GROUP = HQ // KVH
SCALE = HD ** (-0.5)
C2 = SCALE * math.log2(math.e)
NEG = -1e30
TILE = 256
PAIR = 2
VMEM = pl.BlockSpec(memory_space=pltpu.VMEM)
SMEM = pl.BlockSpec(memory_space=pltpu.SMEM)
HBM = pl.BlockSpec(memory_space=pltpu.HBM)
ANY = pl.BlockSpec(memory_space=pl.ANY)
LONG = pl.CostEstimate(flops=10**11, bytes_accessed=1, transcendentals=0)
BRIEF = pl.CostEstimate(flops=1, bytes_accessed=1, transcendentals=0)


def nt(a, b):
    return lax.dot_general(a, b, (((1,), (1,)), ((), ())), preferred_element_type=jnp.float32)


def nn(a, b):
    return jnp.dot(a, b, preferred_element_type=jnp.float32)


def params(mib):
    return pltpu.CompilerParams(vmem_limit_bytes=mib * 1024 * 1024)


def fold(op, items):
    return functools.reduce(op, items)


def copy_all(copies, sem):
    started = [pltpu.make_async_copy(a, b, sem.at[i]) for i, (a, b) in enumerate(copies)]
    for copy in started:
        copy.start()
    for copy in started:
        copy.wait()


def in_hbm(x):
    return pltpu.with_memory_space_constraint(x, pltpu.HBM)


def gather_kernel(heads, k_ref, v_ref, *refs):
    others = (len(refs) - heads - 1) // 2
    plain, kv, outs, sem = refs[:others], refs[others : others + heads], refs[others + heads : -1], refs[-1]
    copies = []
    for g in range(heads):
        for ref, at in ((k_ref, 0), (v_ref, HD)):
            copies.append((ref.at[:, g * HD : (g + 1) * HD], kv[g].at[:, at : at + HD]))
    copy_all(copies + list(zip(plain, outs)), sem)


def gather(key, value, others, name):
    rows, heads = key.shape[0], key.shape[1] // HD
    shapes = [((rows, 2 * HD), key.dtype)] * heads + [(x.shape, x.dtype) for x in others]
    outs = pl.pallas_call(
        functools.partial(gather_kernel, heads),
        out_shape=[pltpu.VMEM(*x) if others else jax.ShapeDtypeStruct(*x) for x in shapes],
        in_specs=[HBM] * (2 + len(others)),
        out_specs=[VMEM if others else ANY] * len(shapes),
        scratch_shapes=[pltpu.SemaphoreType.DMA((2 * heads + len(others),))],
        compiler_params=params(2),
        cost_estimate=BRIEF,
        name=name,
    )(*[in_hbm(x) for x in (key, value, *others)])
    return list(outs[:heads]), list(outs[heads:])


def pipelined(tasks, scores, finish):
    ahead = scores(tasks[0])
    for i, task in enumerate(tasks):
        now = ahead
        if i + 1 < len(tasks):
            ahead = scores(tasks[i + 1])
        finish(task, now)


def head_columns(h):
    return slice(h * HD, (h + 1) * HD)


def local_kernel(g, q_ref, kv_ref, acc_ref, top_ref, sum_ref, ve):
    rows = q_ref.shape[0]
    ve[:, :HD] = kv_ref[:, HD:]
    ve[:, HD:] = jnp.ones((rows, HD), jnp.bfloat16)
    row = lax.broadcasted_iota(jnp.int32, (PAIR * TILE, TILE), 0)
    seen = lax.rem(row, TILE) >= lax.broadcasted_iota(jnp.int32, (PAIR * TILE, TILE), 1)

    def scores(task):
        first, at = task
        q = jnp.concatenate([q_ref[at : at + TILE, head_columns(g * GROUP + first + j)] for j in range(PAIR)], axis=0)
        parts = [nt(q, kv_ref[:at, :HD])] if at else []
        parts.append(jnp.where(seen, nt(q, kv_ref[at : at + TILE, :HD]), NEG))
        return parts

    def finish(task, parts):
        first, at = task
        top = fold(jnp.maximum, [jnp.max(s, axis=1, keepdims=True) for s in parts])
        total = None
        for s, start in zip(parts, [0, at] if at else [at]):
            p = jnp.exp2((s - top) * C2).astype(jnp.bfloat16)
            part = nn(p, ve[start : start + s.shape[1], :])
            total = part if total is None else total + part
        top = jnp.broadcast_to(top * C2, (PAIR * TILE, HD))
        for j in range(PAIR):
            here, at_j = (slice(at, at + TILE), head_columns(first + j)), slice(j * TILE, (j + 1) * TILE)
            acc_ref[here] = total[at_j, :HD]
            sum_ref[here] = total[at_j, HD:]
            top_ref[here] = top[at_j]

    pipelined([(h, at) for h in range(0, GROUP, PAIR) for at in range(0, rows, TILE)], scores, finish)


def local_attention(query, kv, g):
    rows = query.shape[0]
    return pl.pallas_call(
        functools.partial(local_kernel, g),
        out_shape=[pltpu.VMEM((rows, GROUP * HD), jnp.float32)] * 3,
        in_specs=[VMEM] * 2,
        out_specs=[VMEM] * 3,
        scratch_shapes=[pltpu.VMEM((rows, 2 * HD), jnp.bfloat16)],
        compiler_params=params(6),
        cost_estimate=LONG,
        name="local_attention",
    )(query, kv)


def anchor_kernel(g, count, prior, blk_ref, q_ref, acc_ref, top_ref, sum_ref, *refs):
    cand, (o_ref, token, ka, vae, out, sem) = refs[:count], refs[count + prior :]
    rows = q_ref.shape[0]
    blk = blk_ref[0]
    token[...] = jnp.zeros(token.shape, jnp.float32)

    def leave(h):
        return pltpu.make_async_copy(out.at[h], o_ref.at[:, head_columns(g * GROUP + h)], sem.at[h])

    def take(ref):
        ka[...] = ref[:, :HD]
        vae[:, :HD] = ref[:, HD:]

    if count == 1:
        take(cand[0])
    else:
        pl.when(blk == 1)(lambda: take(cand[0]))
        pl.when(blk == 2)(lambda: take(cand[1]))
        pl.when(blk == 3)(lambda: take(cand[2]))

    def scores(h):
        return nt(q_ref[:, head_columns(g * GROUP + h)], ka[...])

    def finish(h, s):
        held = (slice(None), head_columns(h))
        before = top_ref[held]
        top = jnp.maximum(jnp.max(s, axis=1, keepdims=True) * C2, before)
        p = [jnp.exp2(s[:, at : at + HD] * C2 - top).astype(jnp.bfloat16) for at in range(0, rows, HD)]
        total = nn(jnp.concatenate(p, axis=1), vae[...])
        w = jnp.exp2(before - top)
        o = (total[:, :HD] + w * acc_ref[held]) * inverse(total[:, HD:] + w * sum_ref[held])
        out[h] = o.astype(jnp.bfloat16)
        leave(h).start()

    @pl.when(blk > 0)
    def _():
        vae[:, HD:] = jnp.ones((rows, HD), jnp.bfloat16)
        pipelined(list(range(GROUP)), scores, finish)

    @pl.when(blk == 0)
    def _():
        for h in range(GROUP):
            held = (slice(None), head_columns(h))
            out[h] = (acc_ref[held] * inverse(sum_ref[held])).astype(jnp.bfloat16)
            leave(h).start()

    for h in range(GROUP):
        leave(h).wait()


def inverse(x):
    guess = pl.reciprocal(x, approx=True)
    return guess * (2.0 - x * guess)


def anchor_attention(blk, query, state, cands, g, prior):
    rows = query.shape[0]
    args = [blk, query, *state, *cands]
    specs = [SMEM] + [VMEM] * (4 + len(cands))
    alias = {}
    if prior is not None:
        alias = {len(args): 0}
        args.append(prior)
        specs.append(ANY)
    return pl.pallas_call(
        functools.partial(anchor_kernel, g, len(cands), len(alias)),
        out_shape=[jax.ShapeDtypeStruct(query.shape, query.dtype), jax.ShapeDtypeStruct((8, HD), jnp.float32)],
        in_specs=specs,
        out_specs=[ANY, VMEM],
        scratch_shapes=[
            pltpu.VMEM((rows, HD), jnp.bfloat16),
            pltpu.VMEM((rows, 2 * HD), jnp.bfloat16),
            pltpu.VMEM((GROUP, rows, HD), jnp.bfloat16),
            pltpu.SemaphoreType.DMA((GROUP,)),
        ],
        input_output_aliases=alias,
        compiler_params=params(6),
        cost_estimate=BRIEF,
        name="anchor_attention",
    )(*args)


def fold_order(n):
    bits = n.bit_length() - 1
    return sorted(range(n), key=lambda x: int(format(x, "0%db" % bits)[::-1], 2))


def option_kernel(n, heads, blk_ref, owner_ref, slot_ref, length_ref, *refs):
    kv_heads = heads // GROUP
    kv, queries = refs[:kv_heads], refs[kv_heads : kv_heads + n]
    keep, send, q_all, part = refs[kv_heads + n + 1 :]
    blk = blk_ref[0]
    rows = kv[0].shape[0]
    each = queries[0].shape[0]
    options = n * each
    for mask, query in enumerate(queries):
        at = jnp.bitwise_xor(blk, mask) * each
        q_all[pl.ds(pl.multiple_of(at, each), each), :] = query[...]
    eye = lax.broadcasted_iota(jnp.int32, (options, options), 0) == lax.broadcasted_iota(jnp.int32, (options, options), 1)
    length = jnp.sum(jnp.where(eye, length_ref[...].astype(jnp.float32), 0.0), axis=1, keepdims=True)
    seen = length - (blk * rows).astype(jnp.float32)
    lane = lax.broadcasted_iota(jnp.int32, (options, HD), 1)
    logs = jnp.zeros((options, HD), jnp.float32)
    stack = max(1, min(GROUP, 512 // options))
    spots = lax.broadcasted_iota(jnp.int32, (options * stack, rows), 1).astype(jnp.float32)
    seen_all = jnp.concatenate([seen] * stack, axis=0)
    for first in range(0, heads, stack):
        g = first // GROUP
        q = jnp.concatenate([q_all[:, h * HD : (h + 1) * HD] for h in range(first, first + stack)], axis=0)
        s = nt(q, kv[g][:, :HD])
        s = jnp.where(spots < seen_all, s, NEG)
        top = jnp.max(s, axis=1, keepdims=True)
        e = jnp.exp2((s - top) * C2)
        z = jnp.sum(e, axis=1, keepdims=True)
        o = nn(e.astype(jnp.bfloat16), kv[g][:, HD:]) / z
        live = seen_all > 0
        o = jnp.where(live, o, 0.0).astype(jnp.bfloat16)
        log = jnp.where(live, top * SCALE + jnp.log(z), NEG)
        for j in range(stack):
            h = first + j
            part[:, h * HD : (h + 1) * HD] = o[j * options : (j + 1) * options]
            logs = jnp.where(lax.rem(lane, heads) == h, log[j * options : (j + 1) * options], logs)
    part[:, heads * HD :] = summands(logs, heads)
    slot = lax.broadcasted_iota(jnp.int32, (CAP, options), 0)
    order = fold_order(n)
    for half, out in ((order[: n // 2], keep), (order[n // 2 :], send)):
        for i, mask in enumerate(half):
            pick = (owner_ref[...] == jnp.bitwise_xor(blk, mask)) & (slot_ref[...] == slot)
            pick = jnp.where(pick, 1.0, 0.0).astype(jnp.bfloat16)
            out[i * CAP : (i + 1) * CAP, :] = nn(pick, part[...]).astype(jnp.bfloat16)


def summands(logs, heads):
    lane = lax.broadcasted_iota(jnp.int32, logs.shape, 1)
    high = logs.astype(jnp.bfloat16).astype(jnp.float32)
    rest = logs - high
    mid = rest.astype(jnp.bfloat16).astype(jnp.float32)
    low = rest - mid
    low = jnp.where(lane < 3 * heads, low, 0.0)
    return jnp.where(lane < heads, high, jnp.where(lane < 2 * heads, mid, low)).astype(jnp.bfloat16)


def option_partials(blk, owner, slot, length, kvs, queries, after):
    n, heads = len(queries), queries[0].shape[1] // HD
    options = n * queries[0].shape[0]
    width = (heads + 1) * HD
    rows = kvs[0].shape[0]
    return pl.pallas_call(
        functools.partial(option_kernel, n, heads),
        out_shape=[jax.ShapeDtypeStruct((n // 2 * CAP, width), jnp.bfloat16)] * 2,
        in_specs=[SMEM] + [VMEM] * (3 + len(kvs) + n) + [ANY],
        out_specs=[VMEM] * 2,
        scratch_shapes=[
            pltpu.VMEM((options, heads * HD), jnp.bfloat16),
            pltpu.VMEM((options, width), jnp.bfloat16),
        ],
        compiler_params=params(4 + options // 32),
        cost_estimate=LONG,
        name="option_partials",
    )(blk, owner, slot, length, *kvs, *queries, after)


def merge_kernel(heads, a, b, after, *outs):
    width = heads * HD
    lane = lax.broadcasted_iota(jnp.int32, (HD, width), 0)
    head = lax.broadcasted_iota(jnp.int32, (HD, width), 1) // HD
    pick = jnp.where((lax.rem(lane, heads) == head) & (lane < 3 * heads), 1.0, 0.0).astype(jnp.bfloat16)
    logs = [nn(x[:, width:], pick) for x in (a, b)]
    top = jnp.maximum(*logs)
    weights = [jnp.exp(log - top) for log in logs]
    total = weights[0] + weights[1]
    merged = (weights[0] * a[:, :width].astype(jnp.float32) + weights[1] * b[:, :width].astype(jnp.float32)) / total
    merged = merged.astype(jnp.bfloat16)
    if len(outs) == 1:
        outs[0][...] = merged
        return
    log = top + jnp.log(total)
    lane = lax.broadcasted_iota(jnp.int32, (a.shape[0], HD), 1)
    packed = jnp.zeros((a.shape[0], HD), jnp.float32)
    for h in range(heads):
        packed = jnp.where(lax.rem(lane, heads) == h, log[:, h * HD : (h + 1) * HD], packed)
    packed = summands(packed, heads)
    half = a.shape[0] // 2
    for i, out in enumerate(outs):
        out[:, :width] = merged[i * half : (i + 1) * half]
        out[:, width:] = packed[i * half : (i + 1) * half]


def merge(a, b, last, after):
    rows, width = a.shape
    heads = width // HD - 1
    if last:
        shapes = [jax.ShapeDtypeStruct((rows, heads * HD), jnp.bfloat16)]
    else:
        shapes = [jax.ShapeDtypeStruct((rows // 2, width), jnp.bfloat16)] * 2
    return pl.pallas_call(
        functools.partial(merge_kernel, heads),
        out_shape=shapes,
        in_specs=[VMEM] * 2 + [ANY],
        out_specs=[VMEM] * len(shapes),
        compiler_params=params(6),
        cost_estimate=BRIEF,
        name="merge",
    )(a, b, after)


def swap(x, n, mask):
    return lax.ppermute(x, "blk", [(i, i ^ mask) for i in range(n)])


def from_root(x, blk):
    return lax.psum(jnp.where(blk == 0, x, jnp.zeros_like(x)), "blk")


def body(ctx_query, ctx_key, ctx_value, opt_query, opt_owner, opt_slot, opt_length):
    n = lax.axis_size("blk")
    blk = lax.axis_index("blk")
    blk_arr = blk.astype(jnp.int32).reshape(1)
    options = opt_owner.shape[0]
    rounds = n.bit_length() - 1

    hold = lax.optimization_barrier
    row = lambda x: x.reshape(1, options)

    queries = [opt_query] + [swap(opt_query, n, mask) for mask in range(1, n)]
    sent, _ = gather(ctx_key, ctx_value, [], "anchor_parts")
    if n == 4:
        on = lambda x: lax.ppermute(x, "blk", [(0, 2), (2, 1), (1, 0), (3, 3)])
        up = lambda x: lax.ppermute(x, "blk", [(2, 3), (3, 2), (0, 0), (1, 1)])
        got = on(sent[0])
    plain = [row(opt_owner), row(opt_slot), row(opt_length), opt_query, ctx_query]
    kvs, (*smalls, queries[0], ctx_query) = gather(ctx_key, ctx_value, plain, "load")

    states = [local_attention(ctx_query, kvs[0], 0)]
    keep, send = option_partials(blk_arr, *smalls, kvs, queries, states[0][1])
    if n == 4:
        anchors = []
        got, keep, kvs[1:] = hold((got, keep, kvs[1:]))
        for g in range(len(kvs)):
            after = on(jnp.where(blk == 0, sent[g + 1], got) if g + 1 < len(kvs) else got)
            anchors.append([after, got, up(got)])
            if g + 1 < len(kvs):
                states.append(local_attention(ctx_query, kvs[g + 1], g + 1))
                after, states = hold((after, states))
            got = after
    else:
        states += [local_attention(ctx_query, kv, g) for g, kv in enumerate(kvs) if g]
        anchors = [[from_root(kv, blk)] for kv in sent]
    ctx_out, tokens = None, []
    for g, state in enumerate(states):
        ctx_out, token = anchor_attention(blk_arr, ctx_query, state, anchors[g], g, ctx_out)
        tokens.append(token)
    for bit in range(rounds):
        got = swap(send, n, 1 << bit)
        last = bit == rounds - 1
        outs = merge(keep, got, last, tokens[-1 if last else 0])
        if last:
            opt_out = outs[0]
        else:
            keep, send = outs
    return (ctx_out, opt_out)


def solution(mesh):
    spread = P(("groups", "blk"), "head")
    return jax.shard_map(
        body,
        mesh=mesh,
        in_specs=(spread, spread, spread, spread, P("groups"), P("groups"), P("groups")),
        out_specs=(spread, spread),
        check_vma=False,
    )
```

```python
import functools
import math

import jax
import jax.numpy as jnp
from jax import lax
from jax.experimental import pallas as pl
from jax.experimental.pallas import tpu as pltpu
from jax.sharding import PartitionSpec as P

HD = 128
HQ = 64
KVH = 8
CAP = 32
GROUP = HQ // KVH
SCALE = HD ** (-0.5)
C2 = SCALE * math.log2(math.e)
NEG = -1e30
TILE = 256
PAIR = 2
VMEM = pl.BlockSpec(memory_space=pltpu.VMEM)
SMEM = pl.BlockSpec(memory_space=pltpu.SMEM)
HBM = pl.BlockSpec(memory_space=pltpu.HBM)
ANY = pl.BlockSpec(memory_space=pl.ANY)
LONG = pl.CostEstimate(flops=10**11, bytes_accessed=1, transcendentals=0)
BRIEF = pl.CostEstimate(flops=1, bytes_accessed=1, transcendentals=0)


def nt(a, b):
    return lax.dot_general(a, b, (((1,), (1,)), ((), ())), preferred_element_type=jnp.float32)


def nn(a, b):
    return jnp.dot(a, b, preferred_element_type=jnp.float32)


def params(mib):
    return pltpu.CompilerParams(vmem_limit_bytes=mib * 1024 * 1024)


def fold(op, items):
    return functools.reduce(op, items)


def start_all(copies, sem):
    started = [pltpu.make_async_copy(a, b, sem.at[i]) for i, (a, b) in enumerate(copies)]
    for copy in started:
        copy.start()
    return started


def in_hbm(x):
    return pltpu.with_memory_space_constraint(x, pltpu.HBM)


def parts_kernel(heads, k_ref, v_ref, *refs):
    kv, sem = refs[:heads], refs[heads]
    copies = []
    for g in range(heads):
        for ref, at in ((k_ref, 0), (v_ref, HD)):
            copies.append((ref.at[:, g * HD : (g + 1) * HD], kv[g].at[:, at : at + HD]))
    for copy in start_all(copies, sem):
        copy.wait()


def parts(key, value):
    rows, heads = key.shape[0], key.shape[1] // HD
    outs = pl.pallas_call(
        functools.partial(parts_kernel, heads),
        out_shape=[pltpu.VMEM((rows, 2 * HD), key.dtype)] * heads,
        in_specs=[HBM] * 2,
        out_specs=[VMEM] * heads,
        scratch_shapes=[pltpu.SemaphoreType.DMA((2 * heads,))],
        compiler_params=params(2),
        cost_estimate=BRIEF,
        name="parts",
    )(in_hbm(key), in_hbm(value))
    return list(outs)


def pipelined(tasks, scores, finish):
    ahead = scores(tasks[0])
    for i, task in enumerate(tasks):
        now = ahead
        if i + 1 < len(tasks):
            ahead = scores(tasks[i + 1])
        finish(task, now)


def head_columns(h):
    return slice(h * HD, (h + 1) * HD)


def local_kernel(g, loads, kv_ref, *refs):
    ins = max(loads, 1)
    sources, (acc_ref, top_ref, sum_ref) = refs[:ins], refs[ins : ins + 3]
    held, ve = refs[ins + 3 : ins + 3 + loads] or sources, refs[ins + 3 + loads]
    q_ref, rows = held[0], kv_ref.shape[0]
    queries, others = {}, []
    if loads:
        sem = refs[-1]
        order = list(range(g * GROUP, g * GROUP + GROUP)) + [h for h in range(q_ref.shape[1] // HD) if h // GROUP != g]
        spots = [slice(h * HD, (h + PAIR) * HD) for h in order[::PAIR]]
        copies = [(sources[0].at[:, spot], q_ref.at[:, spot]) for spot in spots]
        copies += list(zip(sources[1:], held[1:]))
        copies = start_all(copies, sem)
        queries = dict(zip(order[:GROUP:PAIR], copies))
        others = copies[GROUP // PAIR :]
    ve[:, :HD] = kv_ref[:, HD:]
    ve[:, HD:] = jnp.ones((rows, HD), jnp.bfloat16)
    row = lax.broadcasted_iota(jnp.int32, (PAIR * TILE, TILE), 0)
    seen = lax.rem(row, TILE) >= lax.broadcasted_iota(jnp.int32, (PAIR * TILE, TILE), 1)

    def scores(task):
        first, at = task
        if at == 0 and loads:
            queries[g * GROUP + first].wait()
        q = jnp.concatenate([q_ref[at : at + TILE, head_columns(g * GROUP + first + j)] for j in range(PAIR)], axis=0)
        parts = [nt(q, kv_ref[:at, :HD])] if at else []
        parts.append(jnp.where(seen, nt(q, kv_ref[at : at + TILE, :HD]), NEG))
        return parts

    def finish(task, parts):
        first, at = task
        top = fold(jnp.maximum, [jnp.max(s, axis=1, keepdims=True) for s in parts])
        total = None
        for s, start in zip(parts, [0, at] if at else [at]):
            p = jnp.exp2((s - top) * C2).astype(jnp.bfloat16)
            part = nn(p, ve[start : start + s.shape[1], :])
            total = part if total is None else total + part
        top = jnp.broadcast_to(top * C2, (PAIR * TILE, HD))
        for j in range(PAIR):
            here, at_j = (slice(at, at + TILE), head_columns(first + j)), slice(j * TILE, (j + 1) * TILE)
            acc_ref[here] = total[at_j, :HD]
            sum_ref[here] = total[at_j, HD:]
            top_ref[here] = top[at_j]

    pipelined([(h, at) for h in range(0, GROUP, PAIR) for at in range(0, rows, TILE)], scores, finish)
    for copy in others:
        copy.wait()


def local_attention(kv, g, query, loads=()):
    rows = kv.shape[0]
    sources = [in_hbm(x) for x in (query, *loads)] if loads else [query]
    held = [pltpu.VMEM(x.shape, x.dtype) for x in sources] if loads else []
    count = len(held)
    outs = pl.pallas_call(
        functools.partial(local_kernel, g, count),
        out_shape=[pltpu.VMEM((rows, GROUP * HD), jnp.float32)] * 3 + held,
        in_specs=[VMEM] + [HBM if loads else VMEM] * len(sources),
        out_specs=[VMEM] * (3 + count),
        scratch_shapes=[pltpu.VMEM((rows, 2 * HD), jnp.bfloat16)]
        + ([pltpu.SemaphoreType.DMA((query.shape[1] // HD // PAIR + len(loads),))] if loads else []),
        compiler_params=params(6),
        cost_estimate=LONG if loads else BRIEF,
        name="local_attention",
    )(kv, *sources)
    return list(outs[:3]), list(outs[3:])


def anchor_kernel(g, count, prior, blk_ref, q_ref, acc_ref, top_ref, sum_ref, *refs):
    cand, (o_ref, token, ka, vae, out, sem) = refs[:count], refs[count + prior :]
    rows = q_ref.shape[0]
    blk = blk_ref[0]
    token[...] = jnp.zeros(token.shape, jnp.float32)

    def leave(h):
        return pltpu.make_async_copy(out.at[h], o_ref.at[:, head_columns(g * GROUP + h)], sem.at[h])

    def take(ref):
        ka[...] = ref[:, :HD]
        vae[:, :HD] = ref[:, HD:]

    if count == 1:
        take(cand[0])
    else:
        pl.when(blk == 1)(lambda: take(cand[0]))
        pl.when(blk == 2)(lambda: take(cand[1]))
        pl.when(blk == 3)(lambda: take(cand[2]))

    def scores(h):
        return nt(q_ref[:, head_columns(g * GROUP + h)], ka[...])

    def finish(h, s):
        held = (slice(None), head_columns(h))
        before = top_ref[held]
        top = jnp.maximum(jnp.max(s, axis=1, keepdims=True) * C2, before)
        p = [jnp.exp2(s[:, at : at + HD] * C2 - top).astype(jnp.bfloat16) for at in range(0, rows, HD)]
        total = nn(jnp.concatenate(p, axis=1), vae[...])
        w = jnp.exp2(before - top)
        o = (total[:, :HD] + w * acc_ref[held]) * inverse(total[:, HD:] + w * sum_ref[held])
        out[h] = o.astype(jnp.bfloat16)
        leave(h).start()

    @pl.when(blk > 0)
    def _():
        vae[:, HD:] = jnp.ones((rows, HD), jnp.bfloat16)
        pipelined(list(range(GROUP)), scores, finish)

    @pl.when(blk == 0)
    def _():
        for h in range(GROUP):
            held = (slice(None), head_columns(h))
            out[h] = (acc_ref[held] * inverse(sum_ref[held])).astype(jnp.bfloat16)
            leave(h).start()

    for h in range(GROUP):
        leave(h).wait()


def inverse(x):
    guess = pl.reciprocal(x, approx=True)
    return guess * (2.0 - x * guess)


def anchor_attention(blk, query, state, cands, g, prior):
    rows = query.shape[0]
    args = [blk, query, *state, *cands]
    specs = [SMEM] + [VMEM] * (4 + len(cands))
    alias = {}
    if prior is not None:
        alias = {len(args): 0}
        args.append(prior)
        specs.append(ANY)
    return pl.pallas_call(
        functools.partial(anchor_kernel, g, len(cands), len(alias)),
        out_shape=[jax.ShapeDtypeStruct(query.shape, query.dtype), jax.ShapeDtypeStruct((8, HD), jnp.float32)],
        in_specs=specs,
        out_specs=[ANY, VMEM],
        scratch_shapes=[
            pltpu.VMEM((rows, HD), jnp.bfloat16),
            pltpu.VMEM((rows, 2 * HD), jnp.bfloat16),
            pltpu.VMEM((GROUP, rows, HD), jnp.bfloat16),
            pltpu.SemaphoreType.DMA((GROUP,)),
        ],
        input_output_aliases=alias,
        compiler_params=params(6),
        cost_estimate=BRIEF,
        name="anchor_attention",
    )(*args)


def fold_order(n):
    bits = n.bit_length() - 1
    return sorted(range(n), key=lambda x: int(format(x, "0%db" % bits)[::-1], 2))


def option_kernel(n, heads, blk_ref, owner_ref, slot_ref, length_ref, *refs):
    kv_heads = heads // GROUP
    kv, queries = refs[:kv_heads], refs[kv_heads : kv_heads + n]
    keep, send, q_all, part = refs[kv_heads + n + 1 :]
    blk = blk_ref[0]
    rows = kv[0].shape[0]
    each = queries[0].shape[0]
    options = n * each
    for mask, query in enumerate(queries):
        at = jnp.bitwise_xor(blk, mask) * each
        q_all[pl.ds(pl.multiple_of(at, each), each), :] = query[...]
    eye = lax.broadcasted_iota(jnp.int32, (options, options), 0) == lax.broadcasted_iota(jnp.int32, (options, options), 1)
    length = jnp.sum(jnp.where(eye, length_ref[...].astype(jnp.float32), 0.0), axis=1, keepdims=True)
    seen = length - (blk * rows).astype(jnp.float32)
    lane = lax.broadcasted_iota(jnp.int32, (options, HD), 1)
    logs = jnp.zeros((options, HD), jnp.float32)
    stack = max(1, min(GROUP, 512 // options))
    spots = lax.broadcasted_iota(jnp.int32, (options * stack, rows), 1).astype(jnp.float32)
    seen_all = jnp.concatenate([seen] * stack, axis=0)
    for first in range(0, heads, stack):
        g = first // GROUP
        q = jnp.concatenate([q_all[:, h * HD : (h + 1) * HD] for h in range(first, first + stack)], axis=0)
        s = nt(q, kv[g][:, :HD])
        s = jnp.where(spots < seen_all, s, NEG)
        top = jnp.max(s, axis=1, keepdims=True)
        e = jnp.exp2((s - top) * C2)
        z = jnp.sum(e, axis=1, keepdims=True)
        o = nn(e.astype(jnp.bfloat16), kv[g][:, HD:]) / z
        live = seen_all > 0
        o = jnp.where(live, o, 0.0).astype(jnp.bfloat16)
        log = jnp.where(live, top * SCALE + jnp.log(z), NEG)
        for j in range(stack):
            h = first + j
            part[:, h * HD : (h + 1) * HD] = o[j * options : (j + 1) * options]
            logs = jnp.where(lax.rem(lane, heads) == h, log[j * options : (j + 1) * options], logs)
    part[:, heads * HD :] = summands(logs, heads)
    slot = lax.broadcasted_iota(jnp.int32, (CAP, options), 0)
    order = fold_order(n)
    for half, out in ((order[: n // 2], keep), (order[n // 2 :], send)):
        for i, mask in enumerate(half):
            pick = (owner_ref[...] == jnp.bitwise_xor(blk, mask)) & (slot_ref[...] == slot)
            pick = jnp.where(pick, 1.0, 0.0).astype(jnp.bfloat16)
            out[i * CAP : (i + 1) * CAP, :] = nn(pick, part[...]).astype(jnp.bfloat16)


def summands(logs, heads):
    lane = lax.broadcasted_iota(jnp.int32, logs.shape, 1)
    high = logs.astype(jnp.bfloat16).astype(jnp.float32)
    rest = logs - high
    mid = rest.astype(jnp.bfloat16).astype(jnp.float32)
    low = rest - mid
    low = jnp.where(lane < 3 * heads, low, 0.0)
    return jnp.where(lane < heads, high, jnp.where(lane < 2 * heads, mid, low)).astype(jnp.bfloat16)


def option_partials(blk, owner, slot, length, kvs, queries, after):
    n, heads = len(queries), queries[0].shape[1] // HD
    options = n * queries[0].shape[0]
    width = (heads + 1) * HD
    rows = kvs[0].shape[0]
    return pl.pallas_call(
        functools.partial(option_kernel, n, heads),
        out_shape=[jax.ShapeDtypeStruct((n // 2 * CAP, width), jnp.bfloat16)] * 2,
        in_specs=[SMEM] + [VMEM] * (3 + len(kvs) + n) + [ANY],
        out_specs=[VMEM] * 2,
        scratch_shapes=[
            pltpu.VMEM((options, heads * HD), jnp.bfloat16),
            pltpu.VMEM((options, width), jnp.bfloat16),
        ],
        compiler_params=params(4 + options // 32),
        cost_estimate=LONG,
        name="option_partials",
    )(blk, owner, slot, length, *kvs, *queries, after)


def merge_kernel(heads, a, b, after, *outs):
    width = heads * HD
    lane = lax.broadcasted_iota(jnp.int32, (HD, width), 0)
    head = lax.broadcasted_iota(jnp.int32, (HD, width), 1) // HD
    pick = jnp.where((lax.rem(lane, heads) == head) & (lane < 3 * heads), 1.0, 0.0).astype(jnp.bfloat16)
    logs = [nn(x[:, width:], pick) for x in (a, b)]
    top = jnp.maximum(*logs)
    weights = [jnp.exp(log - top) for log in logs]
    total = weights[0] + weights[1]
    merged = (weights[0] * a[:, :width].astype(jnp.float32) + weights[1] * b[:, :width].astype(jnp.float32)) / total
    merged = merged.astype(jnp.bfloat16)
    if len(outs) == 1:
        outs[0][...] = merged
        return
    log = top + jnp.log(total)
    lane = lax.broadcasted_iota(jnp.int32, (a.shape[0], HD), 1)
    packed = jnp.zeros((a.shape[0], HD), jnp.float32)
    for h in range(heads):
        packed = jnp.where(lax.rem(lane, heads) == h, log[:, h * HD : (h + 1) * HD], packed)
    packed = summands(packed, heads)
    half = a.shape[0] // 2
    for i, out in enumerate(outs):
        out[:, :width] = merged[i * half : (i + 1) * half]
        out[:, width:] = packed[i * half : (i + 1) * half]


def merge(a, b, last, after):
    rows, width = a.shape
    heads = width // HD - 1
    if last:
        shapes = [jax.ShapeDtypeStruct((rows, heads * HD), jnp.bfloat16)]
    else:
        shapes = [jax.ShapeDtypeStruct((rows // 2, width), jnp.bfloat16)] * 2
    return pl.pallas_call(
        functools.partial(merge_kernel, heads),
        out_shape=shapes,
        in_specs=[VMEM] * 2 + [ANY],
        out_specs=[VMEM] * len(shapes),
        compiler_params=params(6),
        cost_estimate=BRIEF,
        name="merge",
    )(a, b, after)


def swap(x, n, mask):
    return lax.ppermute(x, "blk", [(i, i ^ mask) for i in range(n)])


def from_root(x, blk):
    return lax.psum(jnp.where(blk == 0, x, jnp.zeros_like(x)), "blk")


def body(ctx_query, ctx_key, ctx_value, opt_query, opt_owner, opt_slot, opt_length):
    n = lax.axis_size("blk")
    blk = lax.axis_index("blk")
    blk_arr = blk.astype(jnp.int32).reshape(1)
    options = opt_owner.shape[0]
    rounds = n.bit_length() - 1

    hold = lax.optimization_barrier
    row = lambda x: x.reshape(1, options)

    blk_arr, ctx_key = hold((blk_arr, ctx_key))
    kvs = parts(ctx_key, ctx_value)
    queries = [opt_query] + [swap(opt_query, n, mask) for mask in range(1, n)]
    state, (ctx_query, *smalls, queries[0]) = local_attention(
        kvs[0], 0, ctx_query, [row(opt_owner), row(opt_slot), row(opt_length), opt_query]
    )
    states = [state]
    keep, send = option_partials(blk_arr, *smalls, kvs, queries, state[1])
    if n == 4:
        anchors = []
        first = [lax.ppermute(kvs[0], "blk", [(0, 2)])]
        kvs, states = hold((kvs, states))
        first += [lax.ppermute(kv, "blk", [(0, 2)]) for kv in kvs[1:]]
        first[0], keep, kvs = hold((first[0], keep, kvs))
        for g, got in enumerate(first):
            anchors.append([lax.ppermute(got, "blk", [(2, 1)]), got, lax.ppermute(got, "blk", [(2, 3)])])
            if g + 1 < len(kvs):
                states.append(local_attention(kvs[g + 1], g + 1, ctx_query)[0])
                first[g + 1], states = hold((first[g + 1], states))
        anchors[0], first = hold((anchors[0], first))
    else:
        states += [local_attention(kv, g, ctx_query)[0] for g, kv in enumerate(kvs) if g]
        anchors = [[from_root(kv, blk)] for kv in kvs]
    ctx_out, tokens = None, []
    for g, state in enumerate(states):
        ctx_out, token = anchor_attention(blk_arr, ctx_query, state, anchors[g], g, ctx_out)
        tokens.append(token)
    for bit in range(rounds):
        got = swap(send, n, 1 << bit)
        last = bit == rounds - 1
        outs = merge(keep, got, last, tokens[-1 if last else 0])
        if last:
            opt_out = outs[0]
        else:
            keep, send = outs
    return (ctx_out, opt_out)


def solution(mesh):
    spread = P(("groups", "blk"), "head")
    return jax.shard_map(
        body,
        mesh=mesh,
        in_specs=(spread, spread, spread, spread, P("groups"), P("groups"), P("groups")),
        out_specs=(spread, spread),
        check_vma=False,
    )
```

```python
import functools
import math

import jax
import jax.numpy as jnp
from jax import lax
from jax.experimental import pallas as pl
from jax.experimental.pallas import tpu as pltpu
from jax.sharding import PartitionSpec as P

HD = 128
HQ = 64
KVH = 8
CAP = 32
GROUP = HQ // KVH
SCALE = HD ** (-0.5)
C2 = SCALE * math.log2(math.e)
NEG = -1e30
TILE = 256
PAIR = 2
VMEM = pl.BlockSpec(memory_space=pltpu.VMEM)
SMEM = pl.BlockSpec(memory_space=pltpu.SMEM)
HBM = pl.BlockSpec(memory_space=pltpu.HBM)
ANY = pl.BlockSpec(memory_space=pl.ANY)
LONG = pl.CostEstimate(flops=10**9, bytes_accessed=1, transcendentals=0)
BRIEF = pl.CostEstimate(flops=1, bytes_accessed=1, transcendentals=0)


def nt(a, b):
    return lax.dot_general(a, b, (((1,), (1,)), ((), ())), preferred_element_type=jnp.float32)


def nn(a, b):
    return jnp.dot(a, b, preferred_element_type=jnp.float32)


def params(mib):
    return pltpu.CompilerParams(vmem_limit_bytes=mib * 1024 * 1024)


def fold(op, items):
    return functools.reduce(op, items)


def start_all(copies, sem):
    started = [pltpu.make_async_copy(a, b, sem.at[i]) for i, (a, b) in enumerate(copies)]
    for copy in started:
        copy.start()
    return started


def in_hbm(x):
    return pltpu.with_memory_space_constraint(x, pltpu.HBM)


def parts_kernel(heads, k_ref, v_ref, *refs):
    kv, sem = refs[:heads], refs[heads]
    copies = []
    for g in range(heads):
        for ref, at in ((k_ref, 0), (v_ref, HD)):
            copies.append((ref.at[:, g * HD : (g + 1) * HD], kv[g].at[:, at : at + HD]))
    for copy in start_all(copies, sem):
        copy.wait()


def parts(key, value):
    rows, heads = key.shape[0], key.shape[1] // HD
    outs = pl.pallas_call(
        functools.partial(parts_kernel, heads),
        out_shape=[pltpu.VMEM((rows, 2 * HD), key.dtype)] * heads,
        in_specs=[HBM] * 2,
        out_specs=[VMEM] * heads,
        scratch_shapes=[pltpu.SemaphoreType.DMA((2 * heads,))],
        compiler_params=params(2),
        cost_estimate=BRIEF,
        name="parts",
    )(in_hbm(key), in_hbm(value))
    return list(outs)


def pipelined(tasks, scores, finish):
    ahead = scores(tasks[0])
    for i, task in enumerate(tasks):
        now = ahead
        if i + 1 < len(tasks):
            ahead = scores(tasks[i + 1])
        finish(task, now)


def head_columns(h):
    return slice(h * HD, (h + 1) * HD)


def local_kernel(g, loads, kv_ref, *refs):
    ins = max(loads, 1)
    sources, (acc_ref, top_ref, sum_ref) = refs[:ins], refs[ins : ins + 3]
    held, ve = refs[ins + 3 : ins + 3 + loads] or sources, refs[ins + 3 + loads]
    q_ref, rows = held[0], kv_ref.shape[0]
    queries, others = {}, []
    if loads:
        sem = refs[-1]
        order = list(range(g * GROUP, g * GROUP + GROUP)) + [h for h in range(q_ref.shape[1] // HD) if h // GROUP != g]
        spots = [slice(h * HD, (h + PAIR) * HD) for h in order[::PAIR]]
        copies = [(sources[0].at[:, spot], q_ref.at[:, spot]) for spot in spots]
        copies += list(zip(sources[1:], held[1:]))
        copies = start_all(copies, sem)
        queries = dict(zip(order[:GROUP:PAIR], copies))
        others = copies[GROUP // PAIR :]
    ve[:, :HD] = kv_ref[:, HD:]
    ve[:, HD:] = jnp.ones((rows, HD), jnp.bfloat16)
    row = lax.broadcasted_iota(jnp.int32, (PAIR * TILE, TILE), 0)
    seen = lax.rem(row, TILE) >= lax.broadcasted_iota(jnp.int32, (PAIR * TILE, TILE), 1)

    def scores(task):
        first, at = task
        if at == 0 and loads:
            queries[g * GROUP + first].wait()
        q = jnp.concatenate([q_ref[at : at + TILE, head_columns(g * GROUP + first + j)] for j in range(PAIR)], axis=0)
        parts = [nt(q, kv_ref[:at, :HD])] if at else []
        parts.append(jnp.where(seen, nt(q, kv_ref[at : at + TILE, :HD]), NEG))
        return parts

    def finish(task, parts):
        first, at = task
        top = fold(jnp.maximum, [jnp.max(s, axis=1, keepdims=True) for s in parts])
        total = None
        for s, start in zip(parts, [0, at] if at else [at]):
            p = jnp.exp2((s - top) * C2).astype(jnp.bfloat16)
            part = nn(p, ve[start : start + s.shape[1], :])
            total = part if total is None else total + part
        top = jnp.broadcast_to(top * C2, (PAIR * TILE, HD))
        for j in range(PAIR):
            here, at_j = (slice(at, at + TILE), head_columns(first + j)), slice(j * TILE, (j + 1) * TILE)
            acc_ref[here] = total[at_j, :HD]
            sum_ref[here] = total[at_j, HD:]
            top_ref[here] = top[at_j]

    pipelined([(h, at) for h in range(0, GROUP, PAIR) for at in range(0, rows, TILE)], scores, finish)
    for copy in others:
        copy.wait()


def local_attention(kv, g, query, loads=()):
    rows = kv.shape[0]
    sources = [in_hbm(x) for x in (query, *loads)] if loads else [query]
    held = [pltpu.VMEM(x.shape, x.dtype) for x in sources] if loads else []
    count = len(held)
    outs = pl.pallas_call(
        functools.partial(local_kernel, g, count),
        out_shape=[pltpu.VMEM((rows, GROUP * HD), jnp.float32)] * 3 + held,
        in_specs=[VMEM] + [HBM if loads else VMEM] * len(sources),
        out_specs=[VMEM] * (3 + count),
        scratch_shapes=[pltpu.VMEM((rows, 2 * HD), jnp.bfloat16)]
        + ([pltpu.SemaphoreType.DMA((query.shape[1] // HD // PAIR + len(loads),))] if loads else []),
        compiler_params=params(6),
        cost_estimate=LONG if loads else BRIEF,
        name="local_attention",
    )(kv, *sources)
    return list(outs[:3]), list(outs[3:])


def anchor_kernel(g, count, prior, blk_ref, q_ref, acc_ref, top_ref, sum_ref, *refs):
    cand, (o_ref, token, ka, vae, out, sem) = refs[:count], refs[count + prior :]
    rows = q_ref.shape[0]
    blk = blk_ref[0]
    token[...] = jnp.zeros(token.shape, jnp.float32)

    def leave(h):
        return pltpu.make_async_copy(out.at[h], o_ref.at[:, head_columns(g * GROUP + h)], sem.at[h])

    def take(ref):
        ka[...] = ref[:, :HD]
        vae[:, :HD] = ref[:, HD:]

    if count == 1:
        take(cand[0])
    else:
        pl.when(blk == 1)(lambda: take(cand[0]))
        pl.when(blk == 2)(lambda: take(cand[1]))
        pl.when(blk == 3)(lambda: take(cand[2]))

    def scores(h):
        return nt(q_ref[:, head_columns(g * GROUP + h)], ka[...])

    def finish(h, s):
        held = (slice(None), head_columns(h))
        before = top_ref[held]
        top = jnp.maximum(jnp.max(s, axis=1, keepdims=True) * C2, before)
        p = [jnp.exp2(s[:, at : at + HD] * C2 - top).astype(jnp.bfloat16) for at in range(0, rows, HD)]
        total = nn(jnp.concatenate(p, axis=1), vae[...])
        w = jnp.exp2(before - top)
        o = (total[:, :HD] + w * acc_ref[held]) * inverse(total[:, HD:] + w * sum_ref[held])
        out[h] = o.astype(jnp.bfloat16)
        leave(h).start()

    @pl.when(blk > 0)
    def _():
        vae[:, HD:] = jnp.ones((rows, HD), jnp.bfloat16)
        pipelined(list(range(GROUP)), scores, finish)

    @pl.when(blk == 0)
    def _():
        for h in range(GROUP):
            held = (slice(None), head_columns(h))
            out[h] = (acc_ref[held] * inverse(sum_ref[held])).astype(jnp.bfloat16)
            leave(h).start()

    for h in range(GROUP):
        leave(h).wait()


def inverse(x):
    guess = pl.reciprocal(x, approx=True)
    return guess * (2.0 - x * guess)


def anchor_attention(blk, query, state, cands, g, prior):
    rows = query.shape[0]
    args = [blk, query, *state, *cands]
    specs = [SMEM] + [VMEM] * (4 + len(cands))
    alias = {}
    if prior is not None:
        alias = {len(args): 0}
        args.append(prior)
        specs.append(ANY)
    return pl.pallas_call(
        functools.partial(anchor_kernel, g, len(cands), len(alias)),
        out_shape=[jax.ShapeDtypeStruct(query.shape, query.dtype), jax.ShapeDtypeStruct((8, HD), jnp.float32)],
        in_specs=specs,
        out_specs=[ANY, VMEM],
        scratch_shapes=[
            pltpu.VMEM((rows, HD), jnp.bfloat16),
            pltpu.VMEM((rows, 2 * HD), jnp.bfloat16),
            pltpu.VMEM((GROUP, rows, HD), jnp.bfloat16),
            pltpu.SemaphoreType.DMA((GROUP,)),
        ],
        input_output_aliases=alias,
        compiler_params=params(6),
        cost_estimate=BRIEF,
        name="anchor_attention",
    )(*args)


def fold_order(n):
    bits = n.bit_length() - 1
    return sorted(range(n), key=lambda x: int(format(x, "0%db" % bits)[::-1], 2))


def option_kernel(n, heads, blk_ref, owner_ref, slot_ref, length_ref, *refs):
    kv_heads = heads // GROUP
    kv, queries = refs[:kv_heads], refs[kv_heads : kv_heads + n]
    keep, send, q_all, part = refs[kv_heads + n + 1 :]
    blk = blk_ref[0]
    rows = kv[0].shape[0]
    each = queries[0].shape[0]
    options = n * each
    for mask, query in enumerate(queries):
        at = jnp.bitwise_xor(blk, mask) * each
        q_all[pl.ds(pl.multiple_of(at, each), each), :] = query[...]
    eye = lax.broadcasted_iota(jnp.int32, (options, options), 0) == lax.broadcasted_iota(jnp.int32, (options, options), 1)
    length = jnp.sum(jnp.where(eye, length_ref[...].astype(jnp.float32), 0.0), axis=1, keepdims=True)
    seen = length - (blk * rows).astype(jnp.float32)
    lane = lax.broadcasted_iota(jnp.int32, (options, HD), 1)
    logs = jnp.zeros((options, HD), jnp.float32)
    stack = max(1, min(GROUP, 512 // options))
    spots = lax.broadcasted_iota(jnp.int32, (options * stack, rows), 1).astype(jnp.float32)
    seen_all = jnp.concatenate([seen] * stack, axis=0)
    for first in range(0, heads, stack):
        g = first // GROUP
        q = jnp.concatenate([q_all[:, h * HD : (h + 1) * HD] for h in range(first, first + stack)], axis=0)
        s = nt(q, kv[g][:, :HD])
        s = jnp.where(spots < seen_all, s, NEG)
        top = jnp.max(s, axis=1, keepdims=True)
        e = jnp.exp2((s - top) * C2)
        z = jnp.sum(e, axis=1, keepdims=True)
        o = nn(e.astype(jnp.bfloat16), kv[g][:, HD:]) / z
        live = seen_all > 0
        o = jnp.where(live, o, 0.0).astype(jnp.bfloat16)
        log = jnp.where(live, top * SCALE + jnp.log(z), NEG)
        for j in range(stack):
            h = first + j
            part[:, h * HD : (h + 1) * HD] = o[j * options : (j + 1) * options]
            logs = jnp.where(lax.rem(lane, heads) == h, log[j * options : (j + 1) * options], logs)
    part[:, heads * HD :] = summands(logs, heads)
    slot = lax.broadcasted_iota(jnp.int32, (CAP, options), 0)
    order = fold_order(n)
    for half, out in ((order[: n // 2], keep), (order[n // 2 :], send)):
        for i, mask in enumerate(half):
            pick = (owner_ref[...] == jnp.bitwise_xor(blk, mask)) & (slot_ref[...] == slot)
            pick = jnp.where(pick, 1.0, 0.0).astype(jnp.bfloat16)
            out[i * CAP : (i + 1) * CAP, :] = nn(pick, part[...]).astype(jnp.bfloat16)


def summands(logs, heads):
    lane = lax.broadcasted_iota(jnp.int32, logs.shape, 1)
    high = logs.astype(jnp.bfloat16).astype(jnp.float32)
    rest = logs - high
    mid = rest.astype(jnp.bfloat16).astype(jnp.float32)
    low = rest - mid
    low = jnp.where(lane < 3 * heads, low, 0.0)
    return jnp.where(lane < heads, high, jnp.where(lane < 2 * heads, mid, low)).astype(jnp.bfloat16)


def option_partials(blk, owner, slot, length, kvs, queries, after):
    n, heads = len(queries), queries[0].shape[1] // HD
    options = n * queries[0].shape[0]
    width = (heads + 1) * HD
    rows = kvs[0].shape[0]
    return pl.pallas_call(
        functools.partial(option_kernel, n, heads),
        out_shape=[jax.ShapeDtypeStruct((n // 2 * CAP, width), jnp.bfloat16)] * 2,
        in_specs=[SMEM] + [VMEM] * (3 + len(kvs) + n) + [ANY],
        out_specs=[VMEM] * 2,
        scratch_shapes=[
            pltpu.VMEM((options, heads * HD), jnp.bfloat16),
            pltpu.VMEM((options, width), jnp.bfloat16),
        ],
        compiler_params=params(4 + options // 32),
        cost_estimate=LONG,
        name="option_partials",
    )(blk, owner, slot, length, *kvs, *queries, after)


def merge_kernel(heads, a, b, after, *outs):
    width = heads * HD
    lane = lax.broadcasted_iota(jnp.int32, (HD, width), 0)
    head = lax.broadcasted_iota(jnp.int32, (HD, width), 1) // HD
    pick = jnp.where((lax.rem(lane, heads) == head) & (lane < 3 * heads), 1.0, 0.0).astype(jnp.bfloat16)
    logs = [nn(x[:, width:], pick) for x in (a, b)]
    top = jnp.maximum(*logs)
    weights = [jnp.exp(log - top) for log in logs]
    total = weights[0] + weights[1]
    merged = (weights[0] * a[:, :width].astype(jnp.float32) + weights[1] * b[:, :width].astype(jnp.float32)) / total
    merged = merged.astype(jnp.bfloat16)
    if len(outs) == 1:
        outs[0][...] = merged
        return
    log = top + jnp.log(total)
    lane = lax.broadcasted_iota(jnp.int32, (a.shape[0], HD), 1)
    packed = jnp.zeros((a.shape[0], HD), jnp.float32)
    for h in range(heads):
        packed = jnp.where(lax.rem(lane, heads) == h, log[:, h * HD : (h + 1) * HD], packed)
    packed = summands(packed, heads)
    half = a.shape[0] // 2
    for i, out in enumerate(outs):
        out[:, :width] = merged[i * half : (i + 1) * half]
        out[:, width:] = packed[i * half : (i + 1) * half]


def merge(a, b, last, after):
    rows, width = a.shape
    heads = width // HD - 1
    if last:
        shapes = [jax.ShapeDtypeStruct((rows, heads * HD), jnp.bfloat16)]
    else:
        shapes = [jax.ShapeDtypeStruct((rows // 2, width), jnp.bfloat16)] * 2
    return pl.pallas_call(
        functools.partial(merge_kernel, heads),
        out_shape=shapes,
        in_specs=[VMEM] * 2 + [ANY],
        out_specs=[VMEM] * len(shapes),
        compiler_params=params(6),
        cost_estimate=BRIEF,
        name="merge",
    )(a, b, after)


def swap(x, n, mask):
    return lax.ppermute(x, "blk", [(i, i ^ mask) for i in range(n)])


def from_root(x, blk):
    return lax.psum(jnp.where(blk == 0, x, jnp.zeros_like(x)), "blk")


def body(ctx_query, ctx_key, ctx_value, opt_query, opt_owner, opt_slot, opt_length):
    n = lax.axis_size("blk")
    blk = lax.axis_index("blk")
    blk_arr = blk.astype(jnp.int32).reshape(1)
    options = opt_owner.shape[0]
    rounds = n.bit_length() - 1

    hold = lax.optimization_barrier
    row = lambda x: x.reshape(1, options)

    blk_arr, ctx_key = hold((blk_arr, ctx_key))
    kvs = parts(ctx_key, ctx_value)
    kvs, opt_query = hold((kvs, opt_query))
    queries = [opt_query] + [swap(opt_query, n, mask) for mask in range(1, n)]
    state, (ctx_query, *smalls, queries[0]) = local_attention(
        kvs[0], 0, ctx_query, [row(opt_owner), row(opt_slot), row(opt_length), opt_query]
    )
    states = [state]
    keep, send = option_partials(blk_arr, *smalls, kvs, queries, state[1])
    if n == 4:
        anchors = []
        first = [lax.ppermute(kvs[0], "blk", [(0, 2)])]
        kvs, states = hold((kvs, states))
        first += [lax.ppermute(kv, "blk", [(0, 2)]) for kv in kvs[1:]]
        first[0], keep, kvs = hold((first[0], keep, kvs))
        for g, got in enumerate(first):
            anchors.append([lax.ppermute(got, "blk", [(2, 1)]), got, lax.ppermute(got, "blk", [(2, 3)])])
            if g + 1 < len(kvs):
                states.append(local_attention(kvs[g + 1], g + 1, ctx_query)[0])
                first[g + 1], states = hold((first[g + 1], states))
        anchors[0], first = hold((anchors[0], first))
    else:
        states += [local_attention(kv, g, ctx_query)[0] for g, kv in enumerate(kvs) if g]
        anchors = [[from_root(kv, blk)] for kv in kvs]
    ctx_out, tokens = None, []
    for g, state in enumerate(states):
        ctx_out, token = anchor_attention(blk_arr, ctx_query, state, anchors[g], g, ctx_out)
        tokens.append(token)
    for bit in range(rounds):
        got = swap(send, n, 1 << bit)
        last = bit == rounds - 1
        outs = merge(keep, got, last, tokens[-1 if last else 0])
        if last:
            opt_out = outs[0]
        else:
            keep, send = outs
    return (ctx_out, opt_out)


def solution(mesh):
    spread = P(("groups", "blk"), "head")
    return jax.shard_map(
        body,
        mesh=mesh,
        in_specs=(spread, spread, spread, spread, P("groups"), P("groups"), P("groups")),
        out_specs=(spread, spread),
        check_vma=False,
    )
```

```python
import functools
import math

import jax
import jax.numpy as jnp
from jax import lax
from jax.experimental import pallas as pl
from jax.experimental.pallas import tpu as pltpu
from jax.sharding import PartitionSpec as P

HD = 128
HQ = 64
KVH = 8
CAP = 32
GROUP = HQ // KVH
SCALE = HD ** (-0.5)
C2 = SCALE * math.log2(math.e)
NEG = -1e30
TILE = 256
PAIR = 2
VMEM = pl.BlockSpec(memory_space=pltpu.VMEM)
SMEM = pl.BlockSpec(memory_space=pltpu.SMEM)
HBM = pl.BlockSpec(memory_space=pltpu.HBM)
ANY = pl.BlockSpec(memory_space=pl.ANY)
LONG = pl.CostEstimate(flops=10**9, bytes_accessed=1, transcendentals=0)
BRIEF = pl.CostEstimate(flops=1, bytes_accessed=1, transcendentals=0)


def nt(a, b):
    return lax.dot_general(a, b, (((1,), (1,)), ((), ())), preferred_element_type=jnp.float32)


def nn(a, b):
    return jnp.dot(a, b, preferred_element_type=jnp.float32)


def params(mib):
    return pltpu.CompilerParams(vmem_limit_bytes=mib * 1024 * 1024)


def fold(op, items):
    return functools.reduce(op, items)


def start_all(copies, sem):
    started = [pltpu.make_async_copy(a, b, sem.at[i]) for i, (a, b) in enumerate(copies)]
    for copy in started:
        copy.start()
    return started


def in_hbm(x):
    return pltpu.with_memory_space_constraint(x, pltpu.HBM)


def parts_kernel(heads, k_ref, v_ref, *refs):
    kv, sem = refs[:heads], refs[heads]
    copies = []
    for g in range(heads):
        for ref, at in ((k_ref, 0), (v_ref, HD)):
            copies.append((ref.at[:, g * HD : (g + 1) * HD], kv[g].at[:, at : at + HD]))
    for copy in start_all(copies, sem):
        copy.wait()


def parts(key, value):
    rows, heads = key.shape[0], key.shape[1] // HD
    outs = pl.pallas_call(
        functools.partial(parts_kernel, heads),
        out_shape=[pltpu.VMEM((rows, 2 * HD), key.dtype)] * heads,
        in_specs=[HBM] * 2,
        out_specs=[VMEM] * heads,
        scratch_shapes=[pltpu.SemaphoreType.DMA((2 * heads,))],
        compiler_params=params(2),
        cost_estimate=BRIEF,
        name="parts",
    )(in_hbm(key), in_hbm(value))
    return list(outs)


def pipelined(tasks, scores, finish):
    ahead = scores(tasks[0])
    for i, task in enumerate(tasks):
        now = ahead
        if i + 1 < len(tasks):
            ahead = scores(tasks[i + 1])
        finish(task, now)


def head_columns(h):
    return slice(h * HD, (h + 1) * HD)


def local_pass(g, q_ref, kv_ref, ve, arrived, emit):
    rows = kv_ref.shape[0]
    ve[:, :HD] = kv_ref[:, HD:]
    ve[:, HD:] = jnp.ones((rows, HD), jnp.bfloat16)
    row = lax.broadcasted_iota(jnp.int32, (PAIR * TILE, TILE), 0)
    seen = lax.rem(row, TILE) >= lax.broadcasted_iota(jnp.int32, (PAIR * TILE, TILE), 1)

    def scores(task):
        first, at = task
        if at == 0:
            arrived(first)
        q = jnp.concatenate([q_ref[at : at + TILE, head_columns(g * GROUP + first + j)] for j in range(PAIR)], axis=0)
        parts = [nt(q, kv_ref[:at, :HD])] if at else []
        parts.append(jnp.where(seen, nt(q, kv_ref[at : at + TILE, :HD]), NEG))
        return parts

    def finish(task, parts):
        first, at = task
        top = fold(jnp.maximum, [jnp.max(s, axis=1, keepdims=True) for s in parts])
        total = None
        for s, start in zip(parts, [0, at] if at else [at]):
            p = jnp.exp2((s - top) * C2).astype(jnp.bfloat16)
            part = nn(p, ve[start : start + s.shape[1], :])
            total = part if total is None else total + part
        for j in range(PAIR):
            mine = slice(j * TILE, (j + 1) * TILE)
            emit(slice(at, at + TILE), first + j, total[mine, :HD], total[mine, HD:], top[mine] * C2)

    pipelined([(h, at) for h in range(0, GROUP, PAIR) for at in range(0, rows, TILE)], scores, finish)


def local_kernel(g, loads, joined, blk_ref, kv_ref, *refs):
    ins = max(loads + joined, 1)
    sources, (acc_ref, top_ref, sum_ref) = refs[:ins], refs[ins : ins + 3]
    held = refs[ins + 3 : ins + 3 + loads + (joined > 0)] or sources
    ve = refs[ins + 3 + loads + (joined > 0)]
    q_ref, queries, others = held[0], {}, []
    if loads:
        order = list(range(g * GROUP, g * GROUP + GROUP)) + [h for h in range(q_ref.shape[1] // HD) if h // GROUP != g]
        spots = [slice(h * HD, (h + PAIR) * HD) for h in order[::PAIR]]
        copies = [(sources[0].at[:, spot], q_ref.at[:, spot]) for spot in spots]
        copies += list(zip(sources[1:loads], held[1:loads]))
        each = sources[loads].shape[0]
        copies += [(x, held[loads].at[i * each : (i + 1) * each]) for i, x in enumerate(sources[loads:])]
        copies = start_all(copies, refs[-1])
        queries = dict(zip(range(0, GROUP, PAIR), copies))
        others = copies[GROUP // PAIR :]

    def arrived(first):
        if loads:
            queries[first].wait()

    def emit(rows, h, total, z, top):
        here = (rows, head_columns(h))
        acc_ref[here], sum_ref[here], top_ref[here] = total, z, jnp.broadcast_to(top, total.shape)

    @pl.when(blk_ref[0] > 0)
    def _():
        local_pass(g, q_ref, kv_ref, ve, arrived, emit)

    @pl.when(blk_ref[0] == 0)
    def _():
        for copy in queries.values():
            copy.wait()

    for copy in others:
        copy.wait()


def local_attention(blk, kv, g, query, loads=(), joined=()):
    rows = kv.shape[0]
    sources, held = [query], []
    if loads:
        sources = [in_hbm(x) for x in (query, *loads)]
        height, width = joined[0].shape
        held = [pltpu.VMEM(x.shape, x.dtype) for x in sources]
        held.append(pltpu.VMEM((len(joined) * height, width), joined[0].dtype))
        sources += [in_hbm(joined[0]), *joined[1:]]
    semaphores = query.shape[1] // HD // PAIR + len(loads) + len(joined)
    outs = pl.pallas_call(
        functools.partial(local_kernel, g, len(loads) + 1 if loads else 0, len(joined)),
        out_shape=[pltpu.VMEM((rows, GROUP * HD), jnp.float32)] * 3 + held,
        in_specs=[SMEM, VMEM] + ([HBM] * (len(loads) + 1) + [ANY] * len(joined) if loads else [VMEM]),
        out_specs=[VMEM] * (3 + len(held)),
        scratch_shapes=[pltpu.VMEM((rows, 2 * HD), jnp.bfloat16)]
        + ([pltpu.SemaphoreType.DMA((semaphores,))] if loads else []),
        compiler_params=params(6),
        cost_estimate=LONG,
        name="local_attention",
    )(blk, kv, *sources)
    return list(outs[:3]), list(outs[3:])


def anchor_kernel(g, count, prior, blk_ref, q_ref, kv_ref, acc_ref, top_ref, sum_ref, *refs):
    cand, (o_ref, token, ka, vae, out, sem) = refs[:count], refs[count + prior :]
    rows = q_ref.shape[0]
    blk = blk_ref[0]
    token[...] = jnp.zeros(token.shape, jnp.float32)

    def leave(h):
        return pltpu.make_async_copy(out.at[h], o_ref.at[:, head_columns(g * GROUP + h)], sem.at[h])

    def take(ref):
        ka[...] = ref[:, :HD]
        vae[:, :HD] = ref[:, HD:]

    def scores(h):
        return nt(q_ref[:, head_columns(g * GROUP + h)], ka[...])

    def finish(h, s):
        held = (slice(None), head_columns(h))
        before = top_ref[held]
        top = jnp.maximum(jnp.max(s, axis=1, keepdims=True) * C2, before)
        p = [jnp.exp2(s[:, at : at + HD] * C2 - top).astype(jnp.bfloat16) for at in range(0, rows, HD)]
        total = nn(jnp.concatenate(p, axis=1), vae[...])
        w = jnp.exp2(before - top)
        o = (total[:, :HD] + w * acc_ref[held]) * inverse(total[:, HD:] + w * sum_ref[held])
        out[h] = o.astype(jnp.bfloat16)
        leave(h).start()

    @pl.when(blk > 0)
    def _():
        if count == 1:
            take(cand[0])
        else:
            for i, ref in enumerate(cand):
                pl.when(blk == i + 1)(functools.partial(take, ref))
        vae[:, HD:] = jnp.ones((rows, HD), jnp.bfloat16)
        pipelined(list(range(GROUP)), scores, finish)

    def emit(here, h, total, z, top):
        out[h, here, :] = (total * inverse(z)).astype(jnp.bfloat16)
        if here.stop == rows:
            leave(h).start()

    @pl.when(blk == 0)
    def _():
        local_pass(g, q_ref, kv_ref, vae, lambda first: None, emit)

    for h in range(GROUP):
        leave(h).wait()


def inverse(x):
    guess = pl.reciprocal(x, approx=True)
    return guess * (2.0 - x * guess)


def anchor_attention(blk, query, kv, state, cands, g, prior):
    rows = query.shape[0]
    args = [blk, query, kv, *state, *cands]
    specs = [SMEM] + [VMEM] * (5 + len(cands))
    alias = {}
    if prior is not None:
        alias = {len(args): 0}
        args.append(prior)
        specs.append(ANY)
    return pl.pallas_call(
        functools.partial(anchor_kernel, g, len(cands), len(alias)),
        out_shape=[jax.ShapeDtypeStruct(query.shape, query.dtype), jax.ShapeDtypeStruct((8, HD), jnp.float32)],
        in_specs=specs,
        out_specs=[ANY, VMEM],
        scratch_shapes=[
            pltpu.VMEM((rows, HD), jnp.bfloat16),
            pltpu.VMEM((rows, 2 * HD), jnp.bfloat16),
            pltpu.VMEM((GROUP, rows, HD), jnp.bfloat16),
            pltpu.SemaphoreType.DMA((GROUP,)),
        ],
        input_output_aliases=alias,
        compiler_params=params(6),
        cost_estimate=LONG,
        name="anchor_attention",
    )(*args)


def fold_order(n):
    bits = n.bit_length() - 1
    return sorted(range(n), key=lambda x: int(format(x, "0%db" % bits)[::-1], 2))


def option_kernel(masks, heads, blk_ref, owner_ref, slot_ref, length_ref, *refs):
    n = len(masks)
    kv_heads = heads // GROUP
    kv, queries = refs[:kv_heads], refs[kv_heads : kv_heads + 2]
    keep, send, q_all, part = refs[kv_heads + 3 :]
    blk = blk_ref[0]
    rows = kv[0].shape[0]
    half = queries[0].shape[0]
    options, each = 2 * half, 2 * half // n
    for i, mask in enumerate(masks):
        at = jnp.bitwise_xor(blk, mask) * each
        here = queries[i * each // half].at[i * each % half : i * each % half + each]
        q_all[pl.ds(pl.multiple_of(at, each), each), :] = here[...]
    eye = lax.broadcasted_iota(jnp.int32, (options, options), 0) == lax.broadcasted_iota(jnp.int32, (options, options), 1)
    length = jnp.sum(jnp.where(eye, length_ref[...].astype(jnp.float32), 0.0), axis=1, keepdims=True)
    seen = length - (blk * rows).astype(jnp.float32)
    lane = lax.broadcasted_iota(jnp.int32, (options, HD), 1)
    logs = jnp.zeros((options, HD), jnp.float32)
    stack = max(1, min(GROUP, 512 // options))
    spots = lax.broadcasted_iota(jnp.int32, (options * stack, rows), 1).astype(jnp.float32)
    seen_all = jnp.concatenate([seen] * stack, axis=0)
    for first in range(0, heads, stack):
        g = first // GROUP
        q = jnp.concatenate([q_all[:, h * HD : (h + 1) * HD] for h in range(first, first + stack)], axis=0)
        s = nt(q, kv[g][:, :HD])
        s = jnp.where(spots < seen_all, s, NEG)
        top = jnp.max(s, axis=1, keepdims=True)
        e = jnp.exp2((s - top) * C2)
        z = jnp.sum(e, axis=1, keepdims=True)
        o = nn(e.astype(jnp.bfloat16), kv[g][:, HD:]) / z
        live = seen_all > 0
        o = jnp.where(live, o, 0.0).astype(jnp.bfloat16)
        log = jnp.where(live, top * SCALE + jnp.log(z), NEG)
        for j in range(stack):
            h = first + j
            part[:, h * HD : (h + 1) * HD] = o[j * options : (j + 1) * options]
            logs = jnp.where(lax.rem(lane, heads) == h, log[j * options : (j + 1) * options], logs)
    part[:, heads * HD :] = summands(logs, heads)
    slot = lax.broadcasted_iota(jnp.int32, (CAP, options), 0)
    order = fold_order(n)
    for half, out in ((order[: n // 2], keep), (order[n // 2 :], send)):
        for i, mask in enumerate(half):
            pick = (owner_ref[...] == jnp.bitwise_xor(blk, mask)) & (slot_ref[...] == slot)
            pick = jnp.where(pick, 1.0, 0.0).astype(jnp.bfloat16)
            out[i * CAP : (i + 1) * CAP, :] = nn(pick, part[...]).astype(jnp.bfloat16)


def summands(logs, heads):
    lane = lax.broadcasted_iota(jnp.int32, logs.shape, 1)
    high = logs.astype(jnp.bfloat16).astype(jnp.float32)
    rest = logs - high
    mid = rest.astype(jnp.bfloat16).astype(jnp.float32)
    low = rest - mid
    low = jnp.where(lane < 3 * heads, low, 0.0)
    return jnp.where(lane < heads, high, jnp.where(lane < 2 * heads, mid, low)).astype(jnp.bfloat16)


def option_partials(blk, owner, slot, length, kvs, masks, queries, after):
    n, heads = len(masks), queries[0].shape[1] // HD
    options = 2 * queries[0].shape[0]
    width = (heads + 1) * HD
    rows = kvs[0].shape[0]
    return pl.pallas_call(
        functools.partial(option_kernel, masks, heads),
        out_shape=[jax.ShapeDtypeStruct((n // 2 * CAP, width), jnp.bfloat16)] * 2,
        in_specs=[SMEM] + [VMEM] * (5 + len(kvs)) + [ANY],
        out_specs=[VMEM] * 2,
        scratch_shapes=[
            pltpu.VMEM((options, heads * HD), jnp.bfloat16),
            pltpu.VMEM((options, width), jnp.bfloat16),
        ],
        compiler_params=params(4 + options // 32),
        cost_estimate=BRIEF,
        name="option_partials",
    )(blk, owner, slot, length, *kvs, *queries, after)


def merge_kernel(heads, a, b, after, *outs):
    width = heads * HD
    lane = lax.broadcasted_iota(jnp.int32, (HD, width), 0)
    head = lax.broadcasted_iota(jnp.int32, (HD, width), 1) // HD
    pick = jnp.where((lax.rem(lane, heads) == head) & (lane < 3 * heads), 1.0, 0.0).astype(jnp.bfloat16)
    logs = [nn(x[:, width:], pick) for x in (a, b)]
    top = jnp.maximum(*logs)
    weights = [jnp.exp(log - top) for log in logs]
    total = weights[0] + weights[1]
    merged = (weights[0] * a[:, :width].astype(jnp.float32) + weights[1] * b[:, :width].astype(jnp.float32)) / total
    merged = merged.astype(jnp.bfloat16)
    if len(outs) == 1:
        outs[0][...] = merged
        return
    log = top + jnp.log(total)
    lane = lax.broadcasted_iota(jnp.int32, (a.shape[0], HD), 1)
    packed = jnp.zeros((a.shape[0], HD), jnp.float32)
    for h in range(heads):
        packed = jnp.where(lax.rem(lane, heads) == h, log[:, h * HD : (h + 1) * HD], packed)
    packed = summands(packed, heads)
    half = a.shape[0] // 2
    for i, out in enumerate(outs):
        out[:, :width] = merged[i * half : (i + 1) * half]
        out[:, width:] = packed[i * half : (i + 1) * half]


def merge(a, b, last, after):
    rows, width = a.shape
    heads = width // HD - 1
    if last:
        shapes = [jax.ShapeDtypeStruct((rows, heads * HD), jnp.bfloat16)]
    else:
        shapes = [jax.ShapeDtypeStruct((rows // 2, width), jnp.bfloat16)] * 2
    return pl.pallas_call(
        functools.partial(merge_kernel, heads),
        out_shape=shapes,
        in_specs=[VMEM] * 2 + [ANY],
        out_specs=[VMEM] * len(shapes),
        compiler_params=params(6),
        cost_estimate=BRIEF,
        name="merge",
    )(a, b, after)


def swap(x, n, mask):
    return lax.ppermute(x, "blk", [(i, i ^ mask) for i in range(n)])


def from_root(x, blk):
    return lax.psum(jnp.where(blk == 0, x, jnp.zeros_like(x)), "blk")


def body(ctx_query, ctx_key, ctx_value, opt_query, opt_owner, opt_slot, opt_length):
    n = lax.axis_size("blk")
    blk = lax.axis_index("blk")
    blk_arr = blk.astype(jnp.int32).reshape(1)
    options = opt_owner.shape[0]
    rounds = n.bit_length() - 1

    hold = lax.optimization_barrier
    row = lambda x: x.reshape(1, options)

    blk_arr, ctx_key = hold((blk_arr, ctx_key))
    masks, shards = [0], [opt_query]
    for bit in reversed(range(1, rounds)):
        mine = shards[0] if len(shards) == 1 else jnp.concatenate(shards, axis=0)
        shards = [mine, swap(mine, n, 1 << bit)]
        masks = masks + [mask | 1 << bit for mask in masks]
    masks = masks + [mask | 1 for mask in masks]
    kvs = parts(ctx_key, ctx_value)
    if n == 4:
        first = [lax.ppermute(kvs[0], "blk", [(0, 2)])]
    small = [row(opt_owner), row(opt_slot), row(opt_length)]
    state, (ctx_query, *small, mine) = local_attention(blk_arr, kvs[0], 0, ctx_query, small, shards)
    queries = [mine, swap(mine, n, 1)]
    kvs, states = hold((kvs, [state]))
    if n == 4:
        first += [lax.ppermute(kv, "blk", [(0, 2)]) for kv in kvs[1:]]
    states += [local_attention(blk_arr, kv, g, ctx_query)[0] for g, kv in enumerate(kvs) if g]
    if n == 4:
        first[0], queries, states = hold((first[0], queries, states))
    keep, send = option_partials(blk_arr, *small, kvs, masks, queries, states[-1][1])
    if n == 4:
        first[1:], keep = hold((first[1:], keep))
        anchors = [[lax.ppermute(x, "blk", [(2, 1)]), x, lax.ppermute(x, "blk", [(2, 3)])] for x in first]
        anchors[0], first = hold((anchors[0], first))
    else:
        anchors = [[from_root(kv, blk)] for kv in kvs]
    ctx_out, tokens = None, []
    for g, state in enumerate(states):
        ctx_out, token = anchor_attention(blk_arr, ctx_query, kvs[g], state, anchors[g], g, ctx_out)
        tokens.append(token)
    for bit in range(rounds):
        got = swap(send, n, 1 << bit)
        last = bit == rounds - 1
        outs = merge(keep, got, last, tokens[-1 if last else 0])
        if last:
            opt_out = outs[0]
        else:
            keep, send = outs
    return (ctx_out, opt_out)


def solution(mesh):
    spread = P(("groups", "blk"), "head")
    return jax.shard_map(
        body,
        mesh=mesh,
        in_specs=(spread, spread, spread, spread, P("groups"), P("groups"), P("groups")),
        out_specs=(spread, spread),
        check_vma=False,
    )
```

```python
import functools
import math

import jax
import jax.numpy as jnp
from jax import lax
from jax.experimental import pallas as pl
from jax.experimental.pallas import tpu as pltpu
from jax.sharding import PartitionSpec as P

HD = 128
HQ = 64
KVH = 8
CAP = 32
GROUP = HQ // KVH
SCALE = HD ** (-0.5)
C2 = SCALE * math.log2(math.e)
NEG = -1e30
TILE = 256
PAIR = 2
VMEM = pl.BlockSpec(memory_space=pltpu.VMEM)
SMEM = pl.BlockSpec(memory_space=pltpu.SMEM)
HBM = pl.BlockSpec(memory_space=pltpu.HBM)
ANY = pl.BlockSpec(memory_space=pl.ANY)


def cost(flops):
    return pl.CostEstimate(flops=flops, bytes_accessed=1, transcendentals=0)


BRIEF = cost(1)


def nt(a, b):
    return lax.dot_general(a, b, (((1,), (1,)), ((), ())), preferred_element_type=jnp.float32)


def nn(a, b):
    return jnp.dot(a, b, preferred_element_type=jnp.float32)


def params(mib):
    return pltpu.CompilerParams(vmem_limit_bytes=mib * 1024 * 1024)


def fold(op, items):
    return functools.reduce(op, items)


def start_all(copies, sem):
    started = [pltpu.make_async_copy(a, b, sem.at[i]) for i, (a, b) in enumerate(copies)]
    for copy in started:
        copy.start()
    return started


def in_hbm(x):
    return pltpu.with_memory_space_constraint(x, pltpu.HBM)


def parts_kernel(heads, k_ref, v_ref, *refs):
    kv, sem = refs[:heads], refs[heads]
    copies = []
    for g in range(heads):
        for ref, at in ((k_ref, 0), (v_ref, HD)):
            copies.append((ref.at[:, g * HD : (g + 1) * HD], kv[g].at[:, at : at + HD]))
    for copy in start_all(copies, sem):
        copy.wait()


def parts(key, value):
    rows, heads = key.shape[0], key.shape[1] // HD
    outs = pl.pallas_call(
        functools.partial(parts_kernel, heads),
        out_shape=[pltpu.VMEM((rows, 2 * HD), key.dtype)] * heads,
        in_specs=[HBM] * 2,
        out_specs=[VMEM] * heads,
        scratch_shapes=[pltpu.SemaphoreType.DMA((2 * heads,))],
        compiler_params=params(2),
        cost_estimate=BRIEF,
        name="parts",
    )(in_hbm(key), in_hbm(value))
    return list(outs)


def pipelined(tasks, scores, finish):
    ahead = scores(tasks[0])
    for i, task in enumerate(tasks):
        now = ahead
        if i + 1 < len(tasks):
            ahead = scores(tasks[i + 1])
        finish(task, now)


def head_columns(h):
    return slice(h * HD, (h + 1) * HD)


def local_pass(g, q_ref, kv_ref, ve, arrived, emit):
    rows = kv_ref.shape[0]
    ve[:, :HD] = kv_ref[:, HD:]
    ve[:, HD:] = jnp.ones((rows, HD), jnp.bfloat16)
    row = lax.broadcasted_iota(jnp.int32, (PAIR * TILE, TILE), 0)
    seen = lax.rem(row, TILE) >= lax.broadcasted_iota(jnp.int32, (PAIR * TILE, TILE), 1)

    def scores(task):
        first, at = task
        if at == 0:
            arrived(first)
        q = jnp.concatenate([q_ref[at : at + TILE, head_columns(g * GROUP + first + j)] for j in range(PAIR)], axis=0)
        parts = [nt(q, kv_ref[:at, :HD])] if at else []
        parts.append(jnp.where(seen, nt(q, kv_ref[at : at + TILE, :HD]), NEG))
        return parts

    def finish(task, parts):
        first, at = task
        top = fold(jnp.maximum, [jnp.max(s, axis=1, keepdims=True) for s in parts])
        total = None
        for s, start in zip(parts, [0, at] if at else [at]):
            p = jnp.exp2((s - top) * C2).astype(jnp.bfloat16)
            part = nn(p, ve[start : start + s.shape[1], :])
            total = part if total is None else total + part
        for j in range(PAIR):
            mine = slice(j * TILE, (j + 1) * TILE)
            emit(slice(at, at + TILE), first + j, total[mine, :HD], total[mine, HD:], top[mine] * C2)

    pipelined([(h, at) for h in range(0, GROUP, PAIR) for at in range(0, rows, TILE)], scores, finish)


def local_kernel(g, loads, joined, blk_ref, kv_ref, *refs):
    ins = max(loads + joined, 1)
    sources, (acc_ref, top_ref, sum_ref) = refs[:ins], refs[ins : ins + 3]
    held = refs[ins + 3 : ins + 3 + loads + (joined > 0)] or sources
    ve = refs[ins + 3 + loads + (joined > 0)]
    q_ref, queries, others = held[0], {}, []
    if loads:
        order = list(range(g * GROUP, g * GROUP + GROUP)) + [h for h in range(q_ref.shape[1] // HD) if h // GROUP != g]
        spots = [slice(h * HD, (h + PAIR) * HD) for h in order[::PAIR]]
        copies = [(sources[0].at[:, spot], q_ref.at[:, spot]) for spot in spots]
        copies += list(zip(sources[1:loads], held[1:loads]))
        each = sources[loads].shape[0]
        copies += [(x, held[loads].at[i * each : (i + 1) * each]) for i, x in enumerate(sources[loads:])]
        copies = start_all(copies, refs[-1])
        queries = dict(zip(range(0, GROUP, PAIR), copies))
        others = copies[GROUP // PAIR :]

    def arrived(first):
        if loads:
            queries[first].wait()

    def emit(rows, h, total, z, top):
        here = (rows, head_columns(h))
        acc_ref[here], sum_ref[here], top_ref[here] = total, z, jnp.broadcast_to(top, total.shape)

    @pl.when(blk_ref[0] > 0)
    def _():
        local_pass(g, q_ref, kv_ref, ve, arrived, emit)

    @pl.when(blk_ref[0] == 0)
    def _():
        for copy in queries.values():
            copy.wait()

    for copy in others:
        copy.wait()


def local_attention(blk, kv, g, query, loads=(), joined=()):
    rows = kv.shape[0]
    sources, held = [query], []
    if loads:
        sources = [in_hbm(x) for x in (query, *loads)]
        height, width = joined[0].shape
        held = [pltpu.VMEM(x.shape, x.dtype) for x in sources]
        held.append(pltpu.VMEM((len(joined) * height, width), joined[0].dtype))
        sources += [in_hbm(joined[0]), *joined[1:]]
    semaphores = query.shape[1] // HD // PAIR + len(loads) + len(joined)
    outs = pl.pallas_call(
        functools.partial(local_kernel, g, len(loads) + 1 if loads else 0, len(joined)),
        out_shape=[pltpu.VMEM((rows, GROUP * HD), jnp.float32)] * 3 + held,
        in_specs=[SMEM, VMEM] + ([HBM] * (len(loads) + 1) + [ANY] * len(joined) if loads else [VMEM]),
        out_specs=[VMEM] * (3 + len(held)),
        scratch_shapes=[pltpu.VMEM((rows, 2 * HD), jnp.bfloat16)]
        + ([pltpu.SemaphoreType.DMA((semaphores,))] if loads else []),
        compiler_params=params(6),
        cost_estimate=cost(1000000000 if loads else 1000000000),
        name="local_attention",
    )(blk, kv, *sources)
    return list(outs[:3]), list(outs[3:])


def anchor_kernel(g, count, prior, blk_ref, q_ref, kv_ref, acc_ref, top_ref, sum_ref, *refs):
    cand, (o_ref, token, ka, vae, out, sem) = refs[:count], refs[count + prior :]
    rows = q_ref.shape[0]
    blk = blk_ref[0]
    token[...] = jnp.zeros(token.shape, jnp.float32)

    def leave(h):
        return pltpu.make_async_copy(out.at[h], o_ref.at[:, head_columns(g * GROUP + h)], sem.at[h])

    def take(ref):
        ka[...] = ref[:, :HD]
        vae[:, :HD] = ref[:, HD:]

    def scores(h):
        return nt(q_ref[:, head_columns(g * GROUP + h)], ka[...])

    def finish(h, s):
        held = (slice(None), head_columns(h))
        before = top_ref[held]
        top = jnp.maximum(jnp.max(s, axis=1, keepdims=True) * C2, before)
        p = [jnp.exp2(s[:, at : at + HD] * C2 - top).astype(jnp.bfloat16) for at in range(0, rows, HD)]
        total = nn(jnp.concatenate(p, axis=1), vae[...])
        w = jnp.exp2(before - top)
        o = (total[:, :HD] + w * acc_ref[held]) * inverse(total[:, HD:] + w * sum_ref[held])
        out[h] = o.astype(jnp.bfloat16)
        leave(h).start()

    @pl.when(blk > 0)
    def _():
        if count == 1:
            take(cand[0])
        else:
            for i, ref in enumerate(cand):
                pl.when(blk == i + 1)(functools.partial(take, ref))
        vae[:, HD:] = jnp.ones((rows, HD), jnp.bfloat16)
        pipelined(list(range(GROUP)), scores, finish)

    def emit(here, h, total, z, top):
        out[h, here, :] = (total * inverse(z)).astype(jnp.bfloat16)
        if here.stop == rows:
            leave(h).start()

    @pl.when(blk == 0)
    def _():
        local_pass(g, q_ref, kv_ref, vae, lambda first: None, emit)

    for h in range(GROUP):
        leave(h).wait()


def inverse(x):
    guess = pl.reciprocal(x, approx=True)
    return guess * (2.0 - x * guess)


def anchor_attention(blk, query, kv, state, cands, g, prior):
    rows = query.shape[0]
    args = [blk, query, kv, *state, *cands]
    specs = [SMEM] + [VMEM] * (5 + len(cands))
    alias = {}
    if prior is not None:
        alias = {len(args): 0}
        args.append(prior)
        specs.append(ANY)
    return pl.pallas_call(
        functools.partial(anchor_kernel, g, len(cands), len(alias)),
        out_shape=[jax.ShapeDtypeStruct(query.shape, query.dtype), jax.ShapeDtypeStruct((8, HD), jnp.float32)],
        in_specs=specs,
        out_specs=[ANY, VMEM],
        scratch_shapes=[
            pltpu.VMEM((rows, HD), jnp.bfloat16),
            pltpu.VMEM((rows, 2 * HD), jnp.bfloat16),
            pltpu.VMEM((GROUP, rows, HD), jnp.bfloat16),
            pltpu.SemaphoreType.DMA((GROUP,)),
        ],
        input_output_aliases=alias,
        compiler_params=params(6),
        cost_estimate=cost(1000000000),
        name="anchor_attention",
    )(*args)


def fold_order(n):
    bits = n.bit_length() - 1
    return sorted(range(n), key=lambda x: int(format(x, "0%db" % bits)[::-1], 2))


def option_kernel(masks, heads, blk_ref, owner_ref, slot_ref, length_ref, *refs):
    n = len(masks)
    kv_heads = heads // GROUP
    kv, queries = refs[:kv_heads], refs[kv_heads : kv_heads + 2]
    keep, send, q_all, part = refs[kv_heads + 3 :]
    blk = blk_ref[0]
    rows = kv[0].shape[0]
    half = queries[0].shape[0]
    options, each = 2 * half, 2 * half // n
    for i, mask in enumerate(masks):
        at = jnp.bitwise_xor(blk, mask) * each
        here = queries[i * each // half].at[i * each % half : i * each % half + each]
        q_all[pl.ds(pl.multiple_of(at, each), each), :] = here[...]
    eye = lax.broadcasted_iota(jnp.int32, (options, options), 0) == lax.broadcasted_iota(jnp.int32, (options, options), 1)
    length = jnp.sum(jnp.where(eye, length_ref[...].astype(jnp.float32), 0.0), axis=1, keepdims=True)
    seen = length - (blk * rows).astype(jnp.float32)
    lane = lax.broadcasted_iota(jnp.int32, (options, HD), 1)
    logs = jnp.zeros((options, HD), jnp.float32)
    stack = max(1, min(GROUP, 512 // options))
    spots = lax.broadcasted_iota(jnp.int32, (options * stack, rows), 1).astype(jnp.float32)
    seen_all = jnp.concatenate([seen] * stack, axis=0)
    for first in range(0, heads, stack):
        g = first // GROUP
        q = jnp.concatenate([q_all[:, h * HD : (h + 1) * HD] for h in range(first, first + stack)], axis=0)
        s = nt(q, kv[g][:, :HD])
        s = jnp.where(spots < seen_all, s, NEG)
        top = jnp.max(s, axis=1, keepdims=True)
        e = jnp.exp2((s - top) * C2)
        z = jnp.sum(e, axis=1, keepdims=True)
        o = nn(e.astype(jnp.bfloat16), kv[g][:, HD:]) / z
        live = seen_all > 0
        o = jnp.where(live, o, 0.0).astype(jnp.bfloat16)
        log = jnp.where(live, top * SCALE + jnp.log(z), NEG)
        for j in range(stack):
            h = first + j
            part[:, h * HD : (h + 1) * HD] = o[j * options : (j + 1) * options]
            logs = jnp.where(lax.rem(lane, heads) == h, log[j * options : (j + 1) * options], logs)
    part[:, heads * HD :] = summands(logs, heads)
    slot = lax.broadcasted_iota(jnp.int32, (CAP, options), 0)
    order = fold_order(n)
    for half, out in ((order[: n // 2], keep), (order[n // 2 :], send)):
        for i, mask in enumerate(half):
            pick = (owner_ref[...] == jnp.bitwise_xor(blk, mask)) & (slot_ref[...] == slot)
            pick = jnp.where(pick, 1.0, 0.0).astype(jnp.bfloat16)
            out[i * CAP : (i + 1) * CAP, :] = nn(pick, part[...]).astype(jnp.bfloat16)


def summands(logs, heads):
    lane = lax.broadcasted_iota(jnp.int32, logs.shape, 1)
    high = logs.astype(jnp.bfloat16).astype(jnp.float32)
    rest = logs - high
    mid = rest.astype(jnp.bfloat16).astype(jnp.float32)
    low = rest - mid
    low = jnp.where(lane < 3 * heads, low, 0.0)
    return jnp.where(lane < heads, high, jnp.where(lane < 2 * heads, mid, low)).astype(jnp.bfloat16)


def option_partials(blk, owner, slot, length, kvs, masks, queries, after):
    n, heads = len(masks), queries[0].shape[1] // HD
    options = 2 * queries[0].shape[0]
    width = (heads + 1) * HD
    rows = kvs[0].shape[0]
    return pl.pallas_call(
        functools.partial(option_kernel, masks, heads),
        out_shape=[jax.ShapeDtypeStruct((n // 2 * CAP, width), jnp.bfloat16)] * 2,
        in_specs=[SMEM] + [VMEM] * (5 + len(kvs)) + [ANY],
        out_specs=[VMEM] * 2,
        scratch_shapes=[
            pltpu.VMEM((options, heads * HD), jnp.bfloat16),
            pltpu.VMEM((options, width), jnp.bfloat16),
        ],
        compiler_params=params(4 + options // 32),
        cost_estimate=cost(1000000000),
        name="option_partials",
    )(blk, owner, slot, length, *kvs, *queries, after)


def merge_kernel(heads, a, b, after, *outs):
    width = heads * HD
    lane = lax.broadcasted_iota(jnp.int32, (HD, width), 0)
    head = lax.broadcasted_iota(jnp.int32, (HD, width), 1) // HD
    pick = jnp.where((lax.rem(lane, heads) == head) & (lane < 3 * heads), 1.0, 0.0).astype(jnp.bfloat16)
    logs = [nn(x[:, width:], pick) for x in (a, b)]
    top = jnp.maximum(*logs)
    weights = [jnp.exp(log - top) for log in logs]
    total = weights[0] + weights[1]
    merged = (weights[0] * a[:, :width].astype(jnp.float32) + weights[1] * b[:, :width].astype(jnp.float32)) / total
    merged = merged.astype(jnp.bfloat16)
    if len(outs) == 1:
        outs[0][...] = merged
        return
    log = top + jnp.log(total)
    lane = lax.broadcasted_iota(jnp.int32, (a.shape[0], HD), 1)
    packed = jnp.zeros((a.shape[0], HD), jnp.float32)
    for h in range(heads):
        packed = jnp.where(lax.rem(lane, heads) == h, log[:, h * HD : (h + 1) * HD], packed)
    packed = summands(packed, heads)
    half = a.shape[0] // 2
    for i, out in enumerate(outs):
        out[:, :width] = merged[i * half : (i + 1) * half]
        out[:, width:] = packed[i * half : (i + 1) * half]


def merge(a, b, last, after):
    rows, width = a.shape
    heads = width // HD - 1
    if last:
        shapes = [jax.ShapeDtypeStruct((rows, heads * HD), jnp.bfloat16)]
    else:
        shapes = [jax.ShapeDtypeStruct((rows // 2, width), jnp.bfloat16)] * 2
    return pl.pallas_call(
        functools.partial(merge_kernel, heads),
        out_shape=shapes,
        in_specs=[VMEM] * 2 + [ANY],
        out_specs=[VMEM] * len(shapes),
        compiler_params=params(6),
        cost_estimate=BRIEF,
        name="merge",
    )(a, b, after)


def swap(x, n, mask):
    return lax.ppermute(x, "blk", [(i, i ^ mask) for i in range(n)])


def from_root(x, blk):
    return lax.psum(jnp.where(blk == 0, x, jnp.zeros_like(x)), "blk")


def body(ctx_query, ctx_key, ctx_value, opt_query, opt_owner, opt_slot, opt_length):
    n = lax.axis_size("blk")
    blk = lax.axis_index("blk")
    blk_arr = blk.astype(jnp.int32).reshape(1)
    options = opt_owner.shape[0]
    rounds = n.bit_length() - 1

    hold = lax.optimization_barrier
    row = lambda x: x.reshape(1, options)

    blk_arr, ctx_key = hold((blk_arr, ctx_key))
    masks, shards = [0], [opt_query]
    for bit in reversed(range(1, rounds)):
        mine = shards[0] if len(shards) == 1 else jnp.concatenate(shards, axis=0)
        shards = [mine, swap(mine, n, 1 << bit)]
        masks = masks + [mask | 1 << bit for mask in masks]
    masks = masks + [mask | 1 for mask in masks]
    kvs = parts(ctx_key, ctx_value)
    if n == 4:
        first = [lax.ppermute(kvs[0], "blk", [(0, 2)])]
    small = [row(opt_owner), row(opt_slot), row(opt_length)]
    state, (ctx_query, *small, mine) = local_attention(blk_arr, kvs[0], 0, ctx_query, small, shards)
    queries = [mine, swap(mine, n, 1)]
    kvs, states = hold((kvs, [state]))
    if n == 4:
        first += [lax.ppermute(kv, "blk", [(0, 2)]) for kv in kvs[1:]]
        first[0], kvs = hold((first[0], kvs))
    keep, send = option_partials(blk_arr, *small, kvs, masks, queries, state[1])
    keep, kvs = hold((keep, kvs))
    states += [local_attention(blk_arr, kv, g, ctx_query)[0] for g, kv in enumerate(kvs) if g]
    if n == 4:
        first[1:], states = hold((first[1:], states))
        anchors = [[lax.ppermute(x, "blk", [(2, 1)]), x, lax.ppermute(x, "blk", [(2, 3)])] for x in first]
        anchors[0], first = hold((anchors[0], first))
    else:
        anchors = [[from_root(kv, blk)] for kv in kvs]
    ctx_out, tokens = None, []
    for g, state in enumerate(states):
        ctx_out, token = anchor_attention(blk_arr, ctx_query, kvs[g], state, anchors[g], g, ctx_out)
        tokens.append(token)
    for bit in range(rounds):
        got = swap(send, n, 1 << bit)
        last = bit == rounds - 1
        outs = merge(keep, got, last, tokens[-1 if last else 0])
        if last:
            opt_out = outs[0]
        else:
            keep, send = outs
    return (ctx_out, opt_out)


def solution(mesh):
    spread = P(("groups", "blk"), "head")
    return jax.shard_map(
        body,
        mesh=mesh,
        in_specs=(spread, spread, spread, spread, P("groups"), P("groups"), P("groups")),
        out_specs=(spread, spread),
        check_vma=False,
    )
```

```python
import functools
import math

import jax
import jax.numpy as jnp
from jax import lax
from jax.experimental import pallas as pl
from jax.experimental.pallas import tpu as pltpu
from jax.sharding import PartitionSpec as P

HD = 128
HQ = 64
KVH = 8
CAP = 32
GROUP = HQ // KVH
SCALE = HD ** (-0.5)
C2 = SCALE * math.log2(math.e)
NEG = -1e30
TILE = 256
PAIR = 2
VMEM = pl.BlockSpec(memory_space=pltpu.VMEM)
SMEM = pl.BlockSpec(memory_space=pltpu.SMEM)
HBM = pl.BlockSpec(memory_space=pltpu.HBM)
ANY = pl.BlockSpec(memory_space=pl.ANY)


def cost(flops):
    return pl.CostEstimate(flops=flops, bytes_accessed=1, transcendentals=0)


BRIEF = cost(1)


def nt(a, b):
    return lax.dot_general(a, b, (((1,), (1,)), ((), ())), preferred_element_type=jnp.float32)


def nn(a, b):
    return jnp.dot(a, b, preferred_element_type=jnp.float32)


def params(mib):
    return pltpu.CompilerParams(vmem_limit_bytes=mib * 1024 * 1024)


def fold(op, items):
    return functools.reduce(op, items)


def start_all(copies, sem):
    started = [pltpu.make_async_copy(a, b, sem.at[i]) for i, (a, b) in enumerate(copies)]
    for copy in started:
        copy.start()
    return started


def in_hbm(x):
    return pltpu.with_memory_space_constraint(x, pltpu.HBM)


def parts_kernel(heads, k_ref, v_ref, *refs):
    kv, sem = refs[:heads], refs[heads]
    copies = []
    for g in range(heads):
        for ref, at in ((k_ref, 0), (v_ref, HD)):
            copies.append((ref.at[:, g * HD : (g + 1) * HD], kv[g].at[:, at : at + HD]))
    for copy in start_all(copies, sem):
        copy.wait()


def parts(key, value):
    rows, heads = key.shape[0], key.shape[1] // HD
    outs = pl.pallas_call(
        functools.partial(parts_kernel, heads),
        out_shape=[pltpu.VMEM((rows, 2 * HD), key.dtype)] * heads,
        in_specs=[HBM] * 2,
        out_specs=[VMEM] * heads,
        scratch_shapes=[pltpu.SemaphoreType.DMA((2 * heads,))],
        compiler_params=params(2),
        cost_estimate=BRIEF,
        name="parts",
    )(in_hbm(key), in_hbm(value))
    return list(outs)


def pipelined(tasks, scores, finish):
    ahead = scores(tasks[0])
    for i, task in enumerate(tasks):
        now = ahead
        if i + 1 < len(tasks):
            ahead = scores(tasks[i + 1])
        finish(task, now)


def head_columns(h):
    return slice(h * HD, (h + 1) * HD)


def local_pass(g, q_ref, kv_ref, ve, arrived, emit):
    rows = kv_ref.shape[0]
    ve[:, :HD] = kv_ref[:, HD:]
    ve[:, HD:] = jnp.ones((rows, HD), jnp.bfloat16)
    row = lax.broadcasted_iota(jnp.int32, (PAIR * TILE, TILE), 0)
    seen = lax.rem(row, TILE) >= lax.broadcasted_iota(jnp.int32, (PAIR * TILE, TILE), 1)

    def scores(task):
        first, at = task
        if at == 0:
            arrived(first)
        q = jnp.concatenate([q_ref[at : at + TILE, head_columns(g * GROUP + first + j)] for j in range(PAIR)], axis=0)
        parts = [nt(q, kv_ref[:at, :HD])] if at else []
        parts.append(jnp.where(seen, nt(q, kv_ref[at : at + TILE, :HD]), NEG))
        return parts

    def finish(task, parts):
        first, at = task
        top = fold(jnp.maximum, [jnp.max(s, axis=1, keepdims=True) for s in parts])
        total = None
        for s, start in zip(parts, [0, at] if at else [at]):
            p = jnp.exp2((s - top) * C2).astype(jnp.bfloat16)
            part = nn(p, ve[start : start + s.shape[1], :])
            total = part if total is None else total + part
        for j in range(PAIR):
            mine = slice(j * TILE, (j + 1) * TILE)
            emit(slice(at, at + TILE), first + j, total[mine, :HD], total[mine, HD:], top[mine] * C2)

    pipelined([(h, at) for h in range(0, GROUP, PAIR) for at in range(0, rows, TILE)], scores, finish)


def local_kernel(g, loads, blk_ref, kv_ref, *refs):
    ins = max(loads, 1)
    sources, (acc_ref, top_ref, sum_ref) = refs[:ins], refs[ins : ins + 3]
    held, ve = refs[ins + 3 : ins + 3 + loads] or sources, refs[ins + 3 + loads]
    q_ref, queries, others = held[0], {}, []
    if loads:
        order = list(range(g * GROUP, g * GROUP + GROUP)) + [h for h in range(q_ref.shape[1] // HD) if h // GROUP != g]
        spots = [slice(h * HD, (h + PAIR) * HD) for h in order[::PAIR]]
        copies = [(sources[0].at[:, spot], q_ref.at[:, spot]) for spot in spots]
        copies += list(zip(sources[1:], held[1:]))
        copies = start_all(copies, refs[-1])
        queries = dict(zip(range(0, GROUP, PAIR), copies))
        others = copies[GROUP // PAIR :]

    def arrived(first):
        if loads:
            queries[first].wait()

    def emit(rows, h, total, z, top):
        here = (rows, head_columns(h))
        acc_ref[here], sum_ref[here], top_ref[here] = total, z, jnp.broadcast_to(top, total.shape)

    @pl.when(blk_ref[0] > 0)
    def _():
        local_pass(g, q_ref, kv_ref, ve, arrived, emit)

    @pl.when(blk_ref[0] == 0)
    def _():
        for copy in queries.values():
            copy.wait()

    for copy in others:
        copy.wait()


def local_attention(blk, kv, g, query, loads=()):
    rows = kv.shape[0]
    sources, held = [query], []
    if loads:
        sources = [in_hbm(x) for x in (query, *loads)]
        held = [pltpu.VMEM(x.shape, x.dtype) for x in sources]
    semaphores = query.shape[1] // HD // PAIR + len(loads)
    outs = pl.pallas_call(
        functools.partial(local_kernel, g, len(held)),
        out_shape=[pltpu.VMEM((rows, GROUP * HD), jnp.float32)] * 3 + held,
        in_specs=[SMEM, VMEM] + [HBM if loads else VMEM] * len(sources),
        out_specs=[VMEM] * (3 + len(held)),
        scratch_shapes=[pltpu.VMEM((rows, 2 * HD), jnp.bfloat16)]
        + ([pltpu.SemaphoreType.DMA((semaphores,))] if loads else []),
        compiler_params=params(6),
        cost_estimate=cost(2 * 10**9 if loads else 10**9),
        name="local_attention",
    )(blk, kv, *sources)
    return list(outs[:3]), list(outs[3:])


def anchor_kernel(g, count, prior, blk_ref, q_ref, kv_ref, acc_ref, top_ref, sum_ref, *refs):
    cand, (o_ref, token, ka, vae, out, sem) = refs[:count], refs[count + prior :]
    rows = q_ref.shape[0]
    blk = blk_ref[0]
    token[...] = jnp.zeros(token.shape, jnp.float32)

    def leave(h):
        return pltpu.make_async_copy(out.at[h], o_ref.at[:, head_columns(g * GROUP + h)], sem.at[h])

    def take(ref):
        ka[...] = ref[:, :HD]
        vae[:, :HD] = ref[:, HD:]

    def scores(h):
        return nt(q_ref[:, head_columns(g * GROUP + h)], ka[...])

    def finish(h, s):
        held = (slice(None), head_columns(h))
        before = top_ref[held]
        top = jnp.maximum(jnp.max(s, axis=1, keepdims=True) * C2, before)
        p = [jnp.exp2(s[:, at : at + HD] * C2 - top).astype(jnp.bfloat16) for at in range(0, rows, HD)]
        total = nn(jnp.concatenate(p, axis=1), vae[...])
        w = jnp.exp2(before - top)
        o = (total[:, :HD] + w * acc_ref[held]) * inverse(total[:, HD:] + w * sum_ref[held])
        out[h] = o.astype(jnp.bfloat16)
        leave(h).start()

    @pl.when(blk > 0)
    def _():
        if count == 1:
            take(cand[0])
        else:
            for i, ref in enumerate(cand):
                pl.when(blk == i + 1)(functools.partial(take, ref))
        vae[:, HD:] = jnp.ones((rows, HD), jnp.bfloat16)
        pipelined(list(range(GROUP)), scores, finish)

    def emit(here, h, total, z, top):
        out[h, here, :] = (total * inverse(z)).astype(jnp.bfloat16)
        if here.stop == rows:
            leave(h).start()

    @pl.when(blk == 0)
    def _():
        local_pass(g, q_ref, kv_ref, vae, lambda first: None, emit)

    for h in range(GROUP):
        leave(h).wait()


def inverse(x):
    guess = pl.reciprocal(x, approx=True)
    return guess * (2.0 - x * guess)


def anchor_attention(blk, query, kv, state, cands, g, prior):
    rows = query.shape[0]
    args = [blk, query, kv, *state, *cands]
    specs = [SMEM] + [VMEM] * (5 + len(cands))
    alias = {}
    if prior is not None:
        alias = {len(args): 0}
        args.append(prior)
        specs.append(ANY)
    return pl.pallas_call(
        functools.partial(anchor_kernel, g, len(cands), len(alias)),
        out_shape=[jax.ShapeDtypeStruct(query.shape, query.dtype), jax.ShapeDtypeStruct((8, HD), jnp.float32)],
        in_specs=specs,
        out_specs=[ANY, VMEM],
        scratch_shapes=[
            pltpu.VMEM((rows, HD), jnp.bfloat16),
            pltpu.VMEM((rows, 2 * HD), jnp.bfloat16),
            pltpu.VMEM((GROUP, rows, HD), jnp.bfloat16),
            pltpu.SemaphoreType.DMA((GROUP,)),
        ],
        input_output_aliases=alias,
        compiler_params=params(6),
        cost_estimate=cost(1000000000),
        name="anchor_attention",
    )(*args)


def fold_order(n):
    bits = n.bit_length() - 1
    return sorted(range(n), key=lambda x: int(format(x, "0%db" % bits)[::-1], 2))


def join_kernel(*refs):
    at = 0
    for ref in refs[:-1]:
        refs[-1][at : at + ref.shape[0], :] = ref[...]
        at += ref.shape[0]


def join(arrays):
    height, width = sum(x.shape[0] for x in arrays), arrays[0].shape[1]
    return pl.pallas_call(
        join_kernel,
        out_shape=pltpu.VMEM((height, width), arrays[0].dtype),
        in_specs=[VMEM] * len(arrays),
        out_specs=VMEM,
        compiler_params=params(2),
        cost_estimate=BRIEF,
        name="join",
    )(*arrays)


def option_kernel(masks, heads, blk_ref, owner_ref, slot_ref, length_ref, *refs):
    n = len(masks)
    kv_heads = heads // GROUP
    kv, queries = refs[:kv_heads], refs[kv_heads : kv_heads + 2]
    keep, send, q_all, part = refs[kv_heads + 3 :]
    blk = blk_ref[0]
    rows = kv[0].shape[0]
    half = queries[0].shape[0]
    options, each = 2 * half, 2 * half // n
    for i, mask in enumerate(masks):
        at = jnp.bitwise_xor(blk, mask) * each
        here = queries[i * each // half].at[i * each % half : i * each % half + each]
        q_all[pl.ds(pl.multiple_of(at, each), each), :] = here[...]
    eye = lax.broadcasted_iota(jnp.int32, (options, options), 0) == lax.broadcasted_iota(jnp.int32, (options, options), 1)
    length = jnp.sum(jnp.where(eye, length_ref[...].astype(jnp.float32), 0.0), axis=1, keepdims=True)
    seen = length - (blk * rows).astype(jnp.float32)
    lane = lax.broadcasted_iota(jnp.int32, (options, HD), 1)
    logs = jnp.zeros((options, HD), jnp.float32)
    stack = max(1, min(GROUP, 512 // options))
    spots = lax.broadcasted_iota(jnp.int32, (options * stack, rows), 1).astype(jnp.float32)
    seen_all = jnp.concatenate([seen] * stack, axis=0)
    for first in range(0, heads, stack):
        g = first // GROUP
        q = jnp.concatenate([q_all[:, h * HD : (h + 1) * HD] for h in range(first, first + stack)], axis=0)
        s = nt(q, kv[g][:, :HD])
        s = jnp.where(spots < seen_all, s, NEG)
        top = jnp.max(s, axis=1, keepdims=True)
        e = jnp.exp2((s - top) * C2)
        z = jnp.sum(e, axis=1, keepdims=True)
        o = nn(e.astype(jnp.bfloat16), kv[g][:, HD:]) / z
        live = seen_all > 0
        o = jnp.where(live, o, 0.0).astype(jnp.bfloat16)
        log = jnp.where(live, top * SCALE + jnp.log(z), NEG)
        for j in range(stack):
            h = first + j
            part[:, h * HD : (h + 1) * HD] = o[j * options : (j + 1) * options]
            logs = jnp.where(lax.rem(lane, heads) == h, log[j * options : (j + 1) * options], logs)
    part[:, heads * HD :] = summands(logs, heads)
    slot = lax.broadcasted_iota(jnp.int32, (CAP, options), 0)
    order = fold_order(n)
    for half, out in ((order[: n // 2], keep), (order[n // 2 :], send)):
        for i, mask in enumerate(half):
            pick = (owner_ref[...] == jnp.bitwise_xor(blk, mask)) & (slot_ref[...] == slot)
            pick = jnp.where(pick, 1.0, 0.0).astype(jnp.bfloat16)
            out[i * CAP : (i + 1) * CAP, :] = nn(pick, part[...]).astype(jnp.bfloat16)


def summands(logs, heads):
    lane = lax.broadcasted_iota(jnp.int32, logs.shape, 1)
    high = logs.astype(jnp.bfloat16).astype(jnp.float32)
    rest = logs - high
    mid = rest.astype(jnp.bfloat16).astype(jnp.float32)
    low = rest - mid
    low = jnp.where(lane < 3 * heads, low, 0.0)
    return jnp.where(lane < heads, high, jnp.where(lane < 2 * heads, mid, low)).astype(jnp.bfloat16)


def option_partials(blk, owner, slot, length, kvs, masks, queries, after):
    n, heads = len(masks), queries[0].shape[1] // HD
    options = 2 * queries[0].shape[0]
    width = (heads + 1) * HD
    rows = kvs[0].shape[0]
    return pl.pallas_call(
        functools.partial(option_kernel, masks, heads),
        out_shape=[jax.ShapeDtypeStruct((n // 2 * CAP, width), jnp.bfloat16)] * 2,
        in_specs=[SMEM] + [VMEM] * (5 + len(kvs)) + [ANY],
        out_specs=[VMEM] * 2,
        scratch_shapes=[
            pltpu.VMEM((options, heads * HD), jnp.bfloat16),
            pltpu.VMEM((options, width), jnp.bfloat16),
        ],
        compiler_params=params(4 + options // 32),
        cost_estimate=cost(1000000000),
        name="option_partials",
    )(blk, owner, slot, length, *kvs, *queries, after)


def merge_kernel(heads, a, b, after, *outs):
    width = heads * HD
    lane = lax.broadcasted_iota(jnp.int32, (HD, width), 0)
    head = lax.broadcasted_iota(jnp.int32, (HD, width), 1) // HD
    pick = jnp.where((lax.rem(lane, heads) == head) & (lane < 3 * heads), 1.0, 0.0).astype(jnp.bfloat16)
    logs = [nn(x[:, width:], pick) for x in (a, b)]
    top = jnp.maximum(*logs)
    weights = [jnp.exp(log - top) for log in logs]
    total = weights[0] + weights[1]
    merged = (weights[0] * a[:, :width].astype(jnp.float32) + weights[1] * b[:, :width].astype(jnp.float32)) / total
    merged = merged.astype(jnp.bfloat16)
    if len(outs) == 1:
        outs[0][...] = merged
        return
    log = top + jnp.log(total)
    lane = lax.broadcasted_iota(jnp.int32, (a.shape[0], HD), 1)
    packed = jnp.zeros((a.shape[0], HD), jnp.float32)
    for h in range(heads):
        packed = jnp.where(lax.rem(lane, heads) == h, log[:, h * HD : (h + 1) * HD], packed)
    packed = summands(packed, heads)
    half = a.shape[0] // 2
    for i, out in enumerate(outs):
        out[:, :width] = merged[i * half : (i + 1) * half]
        out[:, width:] = packed[i * half : (i + 1) * half]


def merge(a, b, last, after):
    rows, width = a.shape
    heads = width // HD - 1
    if last:
        shapes = [jax.ShapeDtypeStruct((rows, heads * HD), jnp.bfloat16)]
    else:
        shapes = [jax.ShapeDtypeStruct((rows // 2, width), jnp.bfloat16)] * 2
    return pl.pallas_call(
        functools.partial(merge_kernel, heads),
        out_shape=shapes,
        in_specs=[VMEM] * 2 + [ANY],
        out_specs=[VMEM] * len(shapes),
        compiler_params=params(6),
        cost_estimate=BRIEF,
        name="merge",
    )(a, b, after)


def swap(x, n, mask):
    return lax.ppermute(x, "blk", [(i, i ^ mask) for i in range(n)])


def from_root(x, blk):
    return lax.psum(jnp.where(blk == 0, x, jnp.zeros_like(x)), "blk")


def body(ctx_query, ctx_key, ctx_value, opt_query, opt_owner, opt_slot, opt_length):
    n = lax.axis_size("blk")
    blk = lax.axis_index("blk")
    blk_arr = blk.astype(jnp.int32).reshape(1)
    options = opt_owner.shape[0]
    rounds = n.bit_length() - 1

    hold = lax.optimization_barrier
    row = lambda x: x.reshape(1, options)

    blk_arr, ctx_key = hold((blk_arr, ctx_key))
    masks, shards = [0], [opt_query]
    for bit in reversed(range(1, rounds)):
        mine = shards[0] if len(shards) == 1 else jnp.concatenate(shards, axis=0)
        shards = [mine, swap(mine, n, 1 << bit)]
        masks = masks + [mask | 1 << bit for mask in masks]
    masks = masks + [mask | 1 for mask in masks]
    kvs = parts(ctx_key, ctx_value)
    if n == 4:
        first = [lax.ppermute(kvs[0], "blk", [(0, 2)])]
    small = [row(opt_owner), row(opt_slot), row(opt_length)]
    state, (ctx_query, *small, own) = local_attention(blk_arr, kvs[0], 0, ctx_query, small + shards[:1])
    kvs, states, shards = hold((kvs, [state], shards))
    mine = join([own, *shards[1:]])
    queries = [mine, swap(mine, n, 1)]
    if n == 4:
        first += [lax.ppermute(kv, "blk", [(0, 2)]) for kv in kvs[1:]]
        first[0], kvs = hold((first[0], kvs))
    keep, send = option_partials(blk_arr, *small, kvs, masks, queries, state[1])
    keep, kvs = hold((keep, kvs))
    states += [local_attention(blk_arr, kv, g, ctx_query)[0] for g, kv in enumerate(kvs) if g]
    if n == 4:
        first[1:], states = hold((first[1:], states))
        anchors = [[lax.ppermute(x, "blk", [(2, 1)]), x, lax.ppermute(x, "blk", [(2, 3)])] for x in first]
        anchors[0], first = hold((anchors[0], first))
    else:
        anchors = [[from_root(kv, blk)] for kv in kvs]
    ctx_out, tokens = None, []
    for g, state in enumerate(states):
        ctx_out, token = anchor_attention(blk_arr, ctx_query, kvs[g], state, anchors[g], g, ctx_out)
        tokens.append(token)
    for bit in range(rounds):
        got = swap(send, n, 1 << bit)
        last = bit == rounds - 1
        outs = merge(keep, got, last, tokens[-1 if last else 0])
        if last:
            opt_out = outs[0]
        else:
            keep, send = outs
    return (ctx_out, opt_out)


def solution(mesh):
    spread = P(("groups", "blk"), "head")
    return jax.shard_map(
        body,
        mesh=mesh,
        in_specs=(spread, spread, spread, spread, P("groups"), P("groups"), P("groups")),
        out_specs=(spread, spread),
        check_vma=False,
    )
```

```python
import functools
import math

import jax
import jax.numpy as jnp
from jax import lax
from jax.experimental import pallas as pl
from jax.experimental.pallas import tpu as pltpu
from jax.sharding import PartitionSpec as P

HD = 128
HQ = 64
KVH = 8
CAP = 32
GROUP = HQ // KVH
SCALE = HD ** (-0.5)
C2 = SCALE * math.log2(math.e)
NEG = -1e30
TILE = 256
PAIR = 2
VMEM = pl.BlockSpec(memory_space=pltpu.VMEM)
SMEM = pl.BlockSpec(memory_space=pltpu.SMEM)
HBM = pl.BlockSpec(memory_space=pltpu.HBM)
ANY = pl.BlockSpec(memory_space=pl.ANY)


def cost(flops):
    return pl.CostEstimate(flops=flops, bytes_accessed=1, transcendentals=0)


BRIEF = cost(1)


def nt(a, b):
    return lax.dot_general(a, b, (((1,), (1,)), ((), ())), preferred_element_type=jnp.float32)


def nn(a, b):
    return jnp.dot(a, b, preferred_element_type=jnp.float32)


def params(mib):
    return pltpu.CompilerParams(vmem_limit_bytes=mib * 1024 * 1024)


def fold(op, items):
    return functools.reduce(op, items)


def start_all(copies, sem):
    started = [pltpu.make_async_copy(a, b, sem.at[i]) for i, (a, b) in enumerate(copies)]
    for copy in started:
        copy.start()
    return started


def in_hbm(x):
    return pltpu.with_memory_space_constraint(x, pltpu.HBM)


def parts_kernel(heads, k_ref, v_ref, *refs):
    kv, sem = refs[:heads], refs[heads]
    copies = []
    for g in range(heads):
        for ref, at in ((k_ref, 0), (v_ref, HD)):
            copies.append((ref.at[:, g * HD : (g + 1) * HD], kv[g].at[:, at : at + HD]))
    for copy in start_all(copies, sem):
        copy.wait()


def parts(key, value):
    rows, heads = key.shape[0], key.shape[1] // HD
    outs = pl.pallas_call(
        functools.partial(parts_kernel, heads),
        out_shape=[pltpu.VMEM((rows, 2 * HD), key.dtype)] * heads,
        in_specs=[HBM] * 2,
        out_specs=[VMEM] * heads,
        scratch_shapes=[pltpu.SemaphoreType.DMA((2 * heads,))],
        compiler_params=params(2),
        cost_estimate=BRIEF,
        name="parts",
    )(in_hbm(key), in_hbm(value))
    return list(outs)


def pipelined(tasks, scores, finish):
    ahead = scores(tasks[0])
    for i, task in enumerate(tasks):
        now = ahead
        if i + 1 < len(tasks):
            ahead = scores(tasks[i + 1])
        finish(task, now)


def head_columns(h):
    return slice(h * HD, (h + 1) * HD)


def local_pass(g, q_ref, kv_ref, ve, arrived, emit):
    rows = kv_ref.shape[0]
    ve[:, :HD] = kv_ref[:, HD:]
    ve[:, HD:] = jnp.ones((rows, HD), jnp.bfloat16)
    row = lax.broadcasted_iota(jnp.int32, (PAIR * TILE, TILE), 0)
    seen = lax.rem(row, TILE) >= lax.broadcasted_iota(jnp.int32, (PAIR * TILE, TILE), 1)

    def scores(task):
        first, at = task
        if at == 0:
            arrived(first)
        q = jnp.concatenate([q_ref[at : at + TILE, head_columns(g * GROUP + first + j)] for j in range(PAIR)], axis=0)
        parts = [nt(q, kv_ref[:at, :HD])] if at else []
        parts.append(jnp.where(seen, nt(q, kv_ref[at : at + TILE, :HD]), NEG))
        return parts

    def finish(task, parts):
        first, at = task
        top = fold(jnp.maximum, [jnp.max(s, axis=1, keepdims=True) for s in parts])
        total = None
        for s, start in zip(parts, [0, at] if at else [at]):
            p = jnp.exp2((s - top) * C2).astype(jnp.bfloat16)
            part = nn(p, ve[start : start + s.shape[1], :])
            total = part if total is None else total + part
        for j in range(PAIR):
            mine = slice(j * TILE, (j + 1) * TILE)
            emit(slice(at, at + TILE), first + j, total[mine, :HD], total[mine, HD:], top[mine] * C2)

    pipelined([(h, at) for h in range(0, GROUP, PAIR) for at in range(0, rows, TILE)], scores, finish)


def local_kernel(g, loads, blk_ref, kv_ref, *refs):
    ins = max(loads, 1)
    sources, (acc_ref, top_ref, sum_ref) = refs[:ins], refs[ins : ins + 3]
    held, ve = refs[ins + 3 : ins + 3 + loads] or sources, refs[ins + 3 + loads]
    q_ref, queries, others = held[0], {}, []
    if loads:
        order = list(range(g * GROUP, g * GROUP + GROUP)) + [h for h in range(q_ref.shape[1] // HD) if h // GROUP != g]
        spots = [slice(h * HD, (h + PAIR) * HD) for h in order[::PAIR]]
        copies = [(sources[0].at[:, spot], q_ref.at[:, spot]) for spot in spots]
        copies += list(zip(sources[1:], held[1:]))
        copies = start_all(copies, refs[-1])
        queries = dict(zip(range(0, GROUP, PAIR), copies))
        others = copies[GROUP // PAIR :]

    def arrived(first):
        if loads:
            queries[first].wait()

    def emit(rows, h, total, z, top):
        here = (rows, head_columns(h))
        acc_ref[here], sum_ref[here], top_ref[here] = total, z, jnp.broadcast_to(top, total.shape)

    @pl.when(blk_ref[0] > 0)
    def _():
        local_pass(g, q_ref, kv_ref, ve, arrived, emit)

    @pl.when(blk_ref[0] == 0)
    def _():
        for copy in queries.values():
            copy.wait()

    for copy in others:
        copy.wait()


def local_attention(blk, kv, g, query, loads=()):
    rows = kv.shape[0]
    sources, held = [query], []
    if loads:
        sources = [in_hbm(x) for x in (query, *loads)]
        held = [pltpu.VMEM(x.shape, x.dtype) for x in sources]
    semaphores = query.shape[1] // HD // PAIR + len(loads)
    outs = pl.pallas_call(
        functools.partial(local_kernel, g, len(held)),
        out_shape=[pltpu.VMEM((rows, GROUP * HD), jnp.float32)] * 3 + held,
        in_specs=[SMEM, VMEM] + [HBM if loads else VMEM] * len(sources),
        out_specs=[VMEM] * (3 + len(held)),
        scratch_shapes=[pltpu.VMEM((rows, 2 * HD), jnp.bfloat16)]
        + ([pltpu.SemaphoreType.DMA((semaphores,))] if loads else []),
        compiler_params=params(6),
        cost_estimate=cost(2 * 10**9 if loads else 10**9),
        name="local_attention",
    )(blk, kv, *sources)
    return list(outs[:3]), list(outs[3:])


def anchor_kernel(g, count, prior, blk_ref, q_ref, kv_ref, acc_ref, top_ref, sum_ref, *refs):
    cand, (o_ref, token, ka, vae, out, sem) = refs[:count], refs[count + prior :]
    rows = q_ref.shape[0]
    blk = blk_ref[0]
    token[...] = jnp.zeros(token.shape, jnp.float32)

    def leave(h):
        return pltpu.make_async_copy(out.at[h], o_ref.at[:, head_columns(g * GROUP + h)], sem.at[h])

    def take(ref):
        ka[...] = ref[:, :HD]
        vae[:, :HD] = ref[:, HD:]

    def scores(h):
        return nt(q_ref[:, head_columns(g * GROUP + h)], ka[...])

    def finish(h, s):
        held = (slice(None), head_columns(h))
        before = top_ref[held]
        top = jnp.maximum(jnp.max(s, axis=1, keepdims=True) * C2, before)
        p = [jnp.exp2(s[:, at : at + HD] * C2 - top).astype(jnp.bfloat16) for at in range(0, rows, HD)]
        total = nn(jnp.concatenate(p, axis=1), vae[...])
        w = jnp.exp2(before - top)
        o = (total[:, :HD] + w * acc_ref[held]) * inverse(total[:, HD:] + w * sum_ref[held])
        out[h] = o.astype(jnp.bfloat16)
        leave(h).start()

    @pl.when(blk > 0)
    def _():
        if count == 1:
            take(cand[0])
        else:
            for i, ref in enumerate(cand):
                pl.when(blk == i + 1)(functools.partial(take, ref))
        vae[:, HD:] = jnp.ones((rows, HD), jnp.bfloat16)
        pipelined(list(range(GROUP)), scores, finish)

    def emit(here, h, total, z, top):
        out[h, here, :] = (total * inverse(z)).astype(jnp.bfloat16)
        if here.stop == rows:
            leave(h).start()

    @pl.when(blk == 0)
    def _():
        local_pass(g, q_ref, kv_ref, vae, lambda first: None, emit)

    for h in range(GROUP):
        leave(h).wait()


def inverse(x):
    guess = pl.reciprocal(x, approx=True)
    return guess * (2.0 - x * guess)


def anchor_attention(blk, query, kv, state, cands, g, prior):
    rows = query.shape[0]
    args = [blk, query, kv, *state, *cands]
    specs = [SMEM] + [VMEM] * (5 + len(cands))
    alias = {}
    if prior is not None:
        alias = {len(args): 0}
        args.append(prior)
        specs.append(ANY)
    return pl.pallas_call(
        functools.partial(anchor_kernel, g, len(cands), len(alias)),
        out_shape=[jax.ShapeDtypeStruct(query.shape, query.dtype), jax.ShapeDtypeStruct((8, HD), jnp.float32)],
        in_specs=specs,
        out_specs=[ANY, VMEM],
        scratch_shapes=[
            pltpu.VMEM((rows, HD), jnp.bfloat16),
            pltpu.VMEM((rows, 2 * HD), jnp.bfloat16),
            pltpu.VMEM((GROUP, rows, HD), jnp.bfloat16),
            pltpu.SemaphoreType.DMA((GROUP,)),
        ],
        input_output_aliases=alias,
        compiler_params=params(6),
        cost_estimate=cost(1000000000),
        name="anchor_attention",
    )(*args)


def fold_order(n):
    bits = n.bit_length() - 1
    return sorted(range(n), key=lambda x: int(format(x, "0%db" % bits)[::-1], 2))


def join_kernel(*refs):
    at = 0
    for ref in refs[:-1]:
        refs[-1][at : at + ref.shape[0], :] = ref[...]
        at += ref.shape[0]


def join(arrays):
    height, width = sum(x.shape[0] for x in arrays), arrays[0].shape[1]
    return pl.pallas_call(
        join_kernel,
        out_shape=pltpu.VMEM((height, width), arrays[0].dtype),
        in_specs=[VMEM] * len(arrays),
        out_specs=VMEM,
        compiler_params=params(2),
        cost_estimate=BRIEF,
        name="join",
    )(*arrays)


def option_kernel(masks, heads, blk_ref, owner_ref, slot_ref, length_ref, *refs):
    n = len(masks)
    kv_heads = heads // GROUP
    kv, queries = refs[:kv_heads], refs[kv_heads : kv_heads + 2]
    keep, send, q_all, part = refs[kv_heads + 3 :]
    blk = blk_ref[0]
    rows = kv[0].shape[0]
    half = queries[0].shape[0]
    options, each = 2 * half, 2 * half // n
    for i, mask in enumerate(masks):
        at = jnp.bitwise_xor(blk, mask) * each
        here = queries[i * each // half].at[i * each % half : i * each % half + each]
        q_all[pl.ds(pl.multiple_of(at, each), each), :] = here[...]
    eye = lax.broadcasted_iota(jnp.int32, (options, options), 0) == lax.broadcasted_iota(jnp.int32, (options, options), 1)
    length = jnp.sum(jnp.where(eye, length_ref[...].astype(jnp.float32), 0.0), axis=1, keepdims=True)
    seen = length - (blk * rows).astype(jnp.float32)
    lane = lax.broadcasted_iota(jnp.int32, (options, HD), 1)
    logs = jnp.zeros((options, HD), jnp.float32)
    stack = max(1, min(GROUP, 512 // options))
    spots = lax.broadcasted_iota(jnp.int32, (options * stack, rows), 1).astype(jnp.float32)
    seen_all = jnp.concatenate([seen] * stack, axis=0)
    for first in range(0, heads, stack):
        g = first // GROUP
        q = jnp.concatenate([q_all[:, h * HD : (h + 1) * HD] for h in range(first, first + stack)], axis=0)
        s = nt(q, kv[g][:, :HD])
        s = jnp.where(spots < seen_all, s, NEG)
        top = jnp.max(s, axis=1, keepdims=True)
        e = jnp.exp2((s - top) * C2)
        z = jnp.sum(e, axis=1, keepdims=True)
        o = nn(e.astype(jnp.bfloat16), kv[g][:, HD:]) / z
        live = seen_all > 0
        o = jnp.where(live, o, 0.0).astype(jnp.bfloat16)
        log = jnp.where(live, top * SCALE + jnp.log(z), NEG)
        for j in range(stack):
            h = first + j
            part[:, h * HD : (h + 1) * HD] = o[j * options : (j + 1) * options]
            logs = jnp.where(lax.rem(lane, heads) == h, log[j * options : (j + 1) * options], logs)
    part[:, heads * HD :] = summands(logs, heads)
    slot = lax.broadcasted_iota(jnp.int32, (CAP, options), 0)
    order = fold_order(n)
    for half, out in ((order[: n // 2], keep), (order[n // 2 :], send)):
        for i, mask in enumerate(half):
            pick = (owner_ref[...] == jnp.bitwise_xor(blk, mask)) & (slot_ref[...] == slot)
            pick = jnp.where(pick, 1.0, 0.0).astype(jnp.bfloat16)
            out[i * CAP : (i + 1) * CAP, :] = nn(pick, part[...]).astype(jnp.bfloat16)


def summands(logs, heads):
    lane = lax.broadcasted_iota(jnp.int32, logs.shape, 1)
    high = logs.astype(jnp.bfloat16).astype(jnp.float32)
    rest = logs - high
    mid = rest.astype(jnp.bfloat16).astype(jnp.float32)
    low = rest - mid
    low = jnp.where(lane < 3 * heads, low, 0.0)
    return jnp.where(lane < heads, high, jnp.where(lane < 2 * heads, mid, low)).astype(jnp.bfloat16)


def option_partials(blk, owner, slot, length, kvs, masks, queries, after):
    n, heads = len(masks), queries[0].shape[1] // HD
    options = 2 * queries[0].shape[0]
    width = (heads + 1) * HD
    rows = kvs[0].shape[0]
    return pl.pallas_call(
        functools.partial(option_kernel, masks, heads),
        out_shape=[jax.ShapeDtypeStruct((n // 2 * CAP, width), jnp.bfloat16)] * 2,
        in_specs=[SMEM] + [VMEM] * (5 + len(kvs)) + [ANY],
        out_specs=[VMEM] * 2,
        scratch_shapes=[
            pltpu.VMEM((options, heads * HD), jnp.bfloat16),
            pltpu.VMEM((options, width), jnp.bfloat16),
        ],
        compiler_params=params(4 + options // 32),
        cost_estimate=cost(1000000000),
        name="option_partials",
    )(blk, owner, slot, length, *kvs, *queries, after)


def merge_kernel(heads, a, b, after, *outs):
    width = heads * HD
    lane = lax.broadcasted_iota(jnp.int32, (HD, width), 0)
    head = lax.broadcasted_iota(jnp.int32, (HD, width), 1) // HD
    pick = jnp.where((lax.rem(lane, heads) == head) & (lane < 3 * heads), 1.0, 0.0).astype(jnp.bfloat16)
    logs = [nn(x[:, width:], pick) for x in (a, b)]
    top = jnp.maximum(*logs)
    weights = [jnp.exp(log - top) for log in logs]
    total = weights[0] + weights[1]
    merged = (weights[0] * a[:, :width].astype(jnp.float32) + weights[1] * b[:, :width].astype(jnp.float32)) / total
    merged = merged.astype(jnp.bfloat16)
    if len(outs) == 1:
        outs[0][...] = merged
        return
    log = top + jnp.log(total)
    lane = lax.broadcasted_iota(jnp.int32, (a.shape[0], HD), 1)
    packed = jnp.zeros((a.shape[0], HD), jnp.float32)
    for h in range(heads):
        packed = jnp.where(lax.rem(lane, heads) == h, log[:, h * HD : (h + 1) * HD], packed)
    packed = summands(packed, heads)
    half = a.shape[0] // 2
    for i, out in enumerate(outs):
        out[:, :width] = merged[i * half : (i + 1) * half]
        out[:, width:] = packed[i * half : (i + 1) * half]


def merge(a, b, last, after):
    rows, width = a.shape
    heads = width // HD - 1
    if last:
        shapes = [jax.ShapeDtypeStruct((rows, heads * HD), jnp.bfloat16)]
    else:
        shapes = [jax.ShapeDtypeStruct((rows // 2, width), jnp.bfloat16)] * 2
    return pl.pallas_call(
        functools.partial(merge_kernel, heads),
        out_shape=shapes,
        in_specs=[VMEM] * 2 + [ANY],
        out_specs=[VMEM] * len(shapes),
        compiler_params=params(6),
        cost_estimate=BRIEF,
        name="merge",
    )(a, b, after)


def swap(x, n, mask):
    return lax.ppermute(x, "blk", [(i, i ^ mask) for i in range(n)])


def from_root(x, blk):
    return lax.psum(jnp.where(blk == 0, x, jnp.zeros_like(x)), "blk")


def body(ctx_query, ctx_key, ctx_value, opt_query, opt_owner, opt_slot, opt_length):
    n = lax.axis_size("blk")
    blk = lax.axis_index("blk")
    blk_arr = blk.astype(jnp.int32).reshape(1)
    options = opt_owner.shape[0]
    rounds = n.bit_length() - 1

    hold = lax.optimization_barrier
    row = lambda x: x.reshape(1, options)

    blk_arr, ctx_key = hold((blk_arr, ctx_key))
    masks, shards = [0], [opt_query]
    for bit in reversed(range(1, rounds)):
        mine = shards[0] if len(shards) == 1 else jnp.concatenate(shards, axis=0)
        shards = [mine, swap(mine, n, 1 << bit)]
        masks = masks + [mask | 1 << bit for mask in masks]
    masks = masks + [mask | 1 for mask in masks]
    kvs = parts(ctx_key, ctx_value)
    if n == 4:
        first = [lax.ppermute(kvs[0], "blk", [(0, 2)])]
    small = [row(opt_owner), row(opt_slot), row(opt_length)]
    state, (ctx_query, *small, own) = local_attention(blk_arr, kvs[0], 0, ctx_query, small + shards[:1])
    kvs, states, shards = hold((kvs, [state], shards))
    mine = join([own, *shards[1:]])
    queries = [mine, swap(mine, n, 1)]
    if n == 4:
        first += [lax.ppermute(kv, "blk", [(0, 2)]) for kv in kvs[1:]]
        first[0], kvs = hold((first[0], kvs))
    keep, send = option_partials(blk_arr, *small, kvs, masks, queries, state[1])
    keep, kvs = hold((keep, kvs))
    states += [local_attention(blk_arr, kv, g, ctx_query)[0] for g, kv in enumerate(kvs) if g]
    if n == 4:
        kvs, states = hold((kvs, states))
        near = [lax.ppermute(first[0], "blk", [(2, 1)])]
        near += [lax.ppermute(kv, "blk", [(0, 1)]) for kv in kvs[1:]]
        first[1:], states = hold((first[1:], states))
        anchors = [[x, y, lax.ppermute(y, "blk", [(2, 3)])] for x, y in zip(near, first)]
        anchors[0], first = hold((anchors[0], first))
    else:
        anchors = [[from_root(kv, blk)] for kv in kvs]
    ctx_out, tokens = None, []
    for g, state in enumerate(states):
        ctx_out, token = anchor_attention(blk_arr, ctx_query, kvs[g], state, anchors[g], g, ctx_out)
        tokens.append(token)
    for bit in range(rounds):
        got = swap(send, n, 1 << bit)
        last = bit == rounds - 1
        outs = merge(keep, got, last, tokens[-1 if last else 0])
        if last:
            opt_out = outs[0]
        else:
            keep, send = outs
    return (ctx_out, opt_out)


def solution(mesh):
    spread = P(("groups", "blk"), "head")
    return jax.shard_map(
        body,
        mesh=mesh,
        in_specs=(spread, spread, spread, spread, P("groups"), P("groups"), P("groups")),
        out_specs=(spread, spread),
        check_vma=False,
    )
```

```python
import functools
import math

import jax
import jax.numpy as jnp
from jax import lax
from jax.experimental import pallas as pl
from jax.experimental.pallas import tpu as pltpu
from jax.sharding import PartitionSpec as P

HD = 128
HQ = 64
KVH = 8
CAP = 32
GROUP = HQ // KVH
SCALE = HD ** (-0.5)
C2 = SCALE * math.log2(math.e)
NEG = -1e30
TILE = 256
PAIR = 2
VMEM = pl.BlockSpec(memory_space=pltpu.VMEM)
SMEM = pl.BlockSpec(memory_space=pltpu.SMEM)
HBM = pl.BlockSpec(memory_space=pltpu.HBM)
ANY = pl.BlockSpec(memory_space=pl.ANY)


def cost(flops):
    return pl.CostEstimate(flops=flops, bytes_accessed=1, transcendentals=0)


BRIEF = cost(1)


def nt(a, b):
    return lax.dot_general(a, b, (((1,), (1,)), ((), ())), preferred_element_type=jnp.float32)


def nn(a, b):
    return jnp.dot(a, b, preferred_element_type=jnp.float32)


def params(mib):
    return pltpu.CompilerParams(vmem_limit_bytes=mib * 1024 * 1024)


def fold(op, items):
    return functools.reduce(op, items)


def start_all(copies, sem):
    started = [pltpu.make_async_copy(a, b, sem.at[i]) for i, (a, b) in enumerate(copies)]
    for copy in started:
        copy.start()
    return started


def in_hbm(x):
    return pltpu.with_memory_space_constraint(x, pltpu.HBM)


def beside(heads, k_ref, v_ref, kv):
    copies = []
    for g in range(heads):
        for ref, at in ((k_ref, 0), (v_ref, HD)):
            copies.append((ref.at[:, g * HD : (g + 1) * HD], kv[g].at[:, at : at + HD]))
    return copies


def parts_kernel(heads, blk_ref, k_ref, v_ref, *refs):
    kv, sem = refs[:heads], refs[heads]

    @pl.when(blk_ref[0] == 0)
    def _():
        for copy in start_all(beside(heads, k_ref, v_ref, kv), sem):
            copy.wait()


def parts(blk, key, value):
    rows, heads = key.shape[0], key.shape[1] // HD
    outs = pl.pallas_call(
        functools.partial(parts_kernel, heads),
        out_shape=[pltpu.VMEM((rows, 2 * HD), key.dtype)] * heads,
        in_specs=[SMEM] + [HBM] * 2,
        out_specs=[VMEM] * heads,
        scratch_shapes=[pltpu.SemaphoreType.DMA((2 * heads,))],
        compiler_params=params(2),
        cost_estimate=BRIEF,
        name="parts",
    )(blk, in_hbm(key), in_hbm(value))
    return list(outs)


def pipelined(tasks, scores, finish):
    ahead = scores(tasks[0])
    for i, task in enumerate(tasks):
        now = ahead
        if i + 1 < len(tasks):
            ahead = scores(tasks[i + 1])
        finish(task, now)


def head_columns(h):
    return slice(h * HD, (h + 1) * HD)


def local_pass(g, q_ref, kv_ref, ve, arrived, emit):
    rows = kv_ref.shape[0]
    ve[:, :HD] = kv_ref[:, HD:]
    ve[:, HD:] = jnp.ones((rows, HD), jnp.bfloat16)
    row = lax.broadcasted_iota(jnp.int32, (PAIR * TILE, TILE), 0)
    seen = lax.rem(row, TILE) >= lax.broadcasted_iota(jnp.int32, (PAIR * TILE, TILE), 1)

    def scores(task):
        first, at = task
        if at == 0:
            arrived(first)
        q = jnp.concatenate([q_ref[at : at + TILE, head_columns(g * GROUP + first + j)] for j in range(PAIR)], axis=0)
        parts = [nt(q, kv_ref[:at, :HD])] if at else []
        parts.append(jnp.where(seen, nt(q, kv_ref[at : at + TILE, :HD]), NEG))
        return parts

    def finish(task, parts):
        first, at = task
        top = fold(jnp.maximum, [jnp.max(s, axis=1, keepdims=True) for s in parts])
        total = None
        for s, start in zip(parts, [0, at] if at else [at]):
            p = jnp.exp2((s - top) * C2).astype(jnp.bfloat16)
            part = nn(p, ve[start : start + s.shape[1], :])
            total = part if total is None else total + part
        for j in range(PAIR):
            mine = slice(j * TILE, (j + 1) * TILE)
            emit(slice(at, at + TILE), first + j, total[mine, :HD], total[mine, HD:], top[mine] * C2)

    pipelined([(h, at) for h in range(0, GROUP, PAIR) for at in range(0, rows, TILE)], scores, finish)


def first_kernel(heads, blk_ref, k_ref, v_ref, *refs):
    count = (len(refs) - heads - 5) // 2
    sources, state, kv = refs[:count], refs[count : count + 3], refs[count + 3 : count + 3 + heads]
    held, (ve, sem) = refs[count + 3 + heads : -2], refs[-2:]
    q_ref = held[0]
    spots = [slice(h * HD, (h + PAIR) * HD) for h in range(0, q_ref.shape[1] // HD, PAIR)]
    copies = beside(heads, k_ref, v_ref, kv)[:2] + [(sources[0].at[:, x], q_ref.at[:, x]) for x in spots]
    copies += beside(heads, k_ref, v_ref, kv)[2:] + list(zip(sources[1:], held[1:]))
    copies = start_all(copies, sem)
    ahead = 2 + GROUP // PAIR

    @pl.when(blk_ref[0] > 0)
    def _():
        for copy in copies[:2]:
            copy.wait()
        local_pass(0, q_ref, kv[0], ve, lambda h: copies[2 + h // PAIR].wait(), keep_in(state))

    @pl.when(blk_ref[0] == 0)
    def _():
        for copy in copies[:ahead]:
            copy.wait()

    for copy in copies[ahead:]:
        copy.wait()


def first_attention(blk, key, value, query, others):
    rows, heads = key.shape[0], key.shape[1] // HD
    sources = [query, *others]
    outs = pl.pallas_call(
        functools.partial(first_kernel, heads),
        out_shape=[pltpu.VMEM((rows, GROUP * HD), jnp.float32)] * 3
        + [pltpu.VMEM((rows, 2 * HD), key.dtype)] * heads
        + [pltpu.VMEM(x.shape, x.dtype) for x in sources],
        in_specs=[SMEM] + [HBM] * (2 + len(sources)),
        out_specs=[VMEM] * (3 + heads + len(sources)),
        scratch_shapes=[
            pltpu.VMEM((rows, 2 * HD), jnp.bfloat16),
            pltpu.SemaphoreType.DMA((2 * heads + query.shape[1] // HD // PAIR + len(others),)),
        ],
        compiler_params=params(6),
        cost_estimate=cost(2 * 10**9),
        name="local_attention",
    )(blk, *[in_hbm(x) for x in (key, value, *sources)])
    return list(outs[:3]), list(outs[3 : 3 + heads]), list(outs[3 + heads :])


def keep_in(state):
    acc_ref, top_ref, sum_ref = state

    def emit(rows, h, total, z, top):
        here = (rows, head_columns(h))
        acc_ref[here], sum_ref[here], top_ref[here] = total, z, jnp.broadcast_to(top, total.shape)

    return emit


def local_kernel(g, blk_ref, kv_ref, q_ref, *refs):
    @pl.when(blk_ref[0] > 0)
    def _():
        local_pass(g, q_ref, kv_ref, refs[3], lambda h: None, keep_in(refs[:3]))


def local_attention(blk, kv, g, query):
    rows = kv.shape[0]
    return list(
        pl.pallas_call(
            functools.partial(local_kernel, g),
            out_shape=[pltpu.VMEM((rows, GROUP * HD), jnp.float32)] * 3,
            in_specs=[SMEM, VMEM, VMEM],
            out_specs=[VMEM] * 3,
            scratch_shapes=[pltpu.VMEM((rows, 2 * HD), jnp.bfloat16)],
            compiler_params=params(6),
            cost_estimate=cost(10**9),
            name="local_attention",
        )(blk, kv, query)
    )


def anchor_kernel(g, count, prior, blk_ref, q_ref, kv_ref, acc_ref, top_ref, sum_ref, *refs):
    cand, (o_ref, token, ka, vae, out, sem) = refs[:count], refs[count + prior :]
    rows = q_ref.shape[0]
    blk = blk_ref[0]
    token[...] = jnp.zeros(token.shape, jnp.float32)

    def leave(h):
        return pltpu.make_async_copy(out.at[h], o_ref.at[:, head_columns(g * GROUP + h)], sem.at[h])

    def take(ref):
        ka[...] = ref[:, :HD]
        vae[:, :HD] = ref[:, HD:]

    def scores(h):
        return nt(q_ref[:, head_columns(g * GROUP + h)], ka[...])

    def finish(h, s):
        held = (slice(None), head_columns(h))
        before = top_ref[held]
        top = jnp.maximum(jnp.max(s, axis=1, keepdims=True) * C2, before)
        p = [jnp.exp2(s[:, at : at + HD] * C2 - top).astype(jnp.bfloat16) for at in range(0, rows, HD)]
        total = nn(jnp.concatenate(p, axis=1), vae[...])
        w = jnp.exp2(before - top)
        o = (total[:, :HD] + w * acc_ref[held]) * inverse(total[:, HD:] + w * sum_ref[held])
        out[h] = o.astype(jnp.bfloat16)
        leave(h).start()

    @pl.when(blk > 0)
    def _():
        if count == 1:
            take(cand[0])
        else:
            for i, ref in enumerate(cand):
                pl.when(blk == i + 1)(functools.partial(take, ref))
        vae[:, HD:] = jnp.ones((rows, HD), jnp.bfloat16)
        pipelined(list(range(GROUP)), scores, finish)

    def emit(here, h, total, z, top):
        out[h, here, :] = (total * inverse(z)).astype(jnp.bfloat16)
        if here.stop == rows:
            leave(h).start()

    @pl.when(blk == 0)
    def _():
        local_pass(g, q_ref, kv_ref, vae, lambda first: None, emit)

    for h in range(GROUP):
        leave(h).wait()


def inverse(x):
    guess = pl.reciprocal(x, approx=True)
    return guess * (2.0 - x * guess)


def anchor_attention(blk, query, kv, state, cands, g, prior):
    rows = query.shape[0]
    args = [blk, query, kv, *state, *cands]
    specs = [SMEM] + [VMEM] * (5 + len(cands))
    alias = {}
    if prior is not None:
        alias = {len(args): 0}
        args.append(prior)
        specs.append(ANY)
    return pl.pallas_call(
        functools.partial(anchor_kernel, g, len(cands), len(alias)),
        out_shape=[jax.ShapeDtypeStruct(query.shape, query.dtype), jax.ShapeDtypeStruct((8, HD), jnp.float32)],
        in_specs=specs,
        out_specs=[ANY, VMEM],
        scratch_shapes=[
            pltpu.VMEM((rows, HD), jnp.bfloat16),
            pltpu.VMEM((rows, 2 * HD), jnp.bfloat16),
            pltpu.VMEM((GROUP, rows, HD), jnp.bfloat16),
            pltpu.SemaphoreType.DMA((GROUP,)),
        ],
        input_output_aliases=alias,
        compiler_params=params(6),
        cost_estimate=cost(1000000000),
        name="anchor_attention",
    )(*args)


def fold_order(n):
    bits = n.bit_length() - 1
    return sorted(range(n), key=lambda x: int(format(x, "0%db" % bits)[::-1], 2))


def join_kernel(*refs):
    at = 0
    for ref in refs[:-1]:
        refs[-1][at : at + ref.shape[0], :] = ref[...]
        at += ref.shape[0]


def join(arrays):
    height, width = sum(x.shape[0] for x in arrays), arrays[0].shape[1]
    return pl.pallas_call(
        join_kernel,
        out_shape=pltpu.VMEM((height, width), arrays[0].dtype),
        in_specs=[VMEM] * len(arrays),
        out_specs=VMEM,
        compiler_params=params(2),
        cost_estimate=BRIEF,
        name="join",
    )(*arrays)


def option_kernel(masks, heads, blk_ref, owner_ref, slot_ref, length_ref, *refs):
    n = len(masks)
    kv_heads = heads // GROUP
    kv, queries = refs[:kv_heads], refs[kv_heads : kv_heads + 2]
    keep, send, q_all, part = refs[kv_heads + 3 :]
    blk = blk_ref[0]
    rows = kv[0].shape[0]
    half = queries[0].shape[0]
    options, each = 2 * half, 2 * half // n
    for i, mask in enumerate(masks):
        at = jnp.bitwise_xor(blk, mask) * each
        here = queries[i * each // half].at[i * each % half : i * each % half + each]
        q_all[pl.ds(pl.multiple_of(at, each), each), :] = here[...]
    eye = lax.broadcasted_iota(jnp.int32, (options, options), 0) == lax.broadcasted_iota(jnp.int32, (options, options), 1)
    length = jnp.sum(jnp.where(eye, length_ref[...].astype(jnp.float32), 0.0), axis=1, keepdims=True)
    seen = length - (blk * rows).astype(jnp.float32)
    lane = lax.broadcasted_iota(jnp.int32, (options, HD), 1)
    logs = jnp.zeros((options, HD), jnp.float32)
    stack = max(1, min(GROUP, 512 // options))
    spots = lax.broadcasted_iota(jnp.int32, (options * stack, rows), 1).astype(jnp.float32)
    seen_all = jnp.concatenate([seen] * stack, axis=0)
    for first in range(0, heads, stack):
        g = first // GROUP
        q = jnp.concatenate([q_all[:, h * HD : (h + 1) * HD] for h in range(first, first + stack)], axis=0)
        s = nt(q, kv[g][:, :HD])
        s = jnp.where(spots < seen_all, s, NEG)
        top = jnp.max(s, axis=1, keepdims=True)
        e = jnp.exp2((s - top) * C2)
        z = jnp.sum(e, axis=1, keepdims=True)
        o = nn(e.astype(jnp.bfloat16), kv[g][:, HD:]) / z
        live = seen_all > 0
        o = jnp.where(live, o, 0.0).astype(jnp.bfloat16)
        log = jnp.where(live, top * SCALE + jnp.log(z), NEG)
        for j in range(stack):
            h = first + j
            part[:, h * HD : (h + 1) * HD] = o[j * options : (j + 1) * options]
            logs = jnp.where(lax.rem(lane, heads) == h, log[j * options : (j + 1) * options], logs)
    part[:, heads * HD :] = summands(logs, heads)
    slot = lax.broadcasted_iota(jnp.int32, (CAP, options), 0)
    order = fold_order(n)
    for half, out in ((order[: n // 2], keep), (order[n // 2 :], send)):
        for i, mask in enumerate(half):
            pick = (owner_ref[...] == jnp.bitwise_xor(blk, mask)) & (slot_ref[...] == slot)
            pick = jnp.where(pick, 1.0, 0.0).astype(jnp.bfloat16)
            out[i * CAP : (i + 1) * CAP, :] = nn(pick, part[...]).astype(jnp.bfloat16)


def summands(logs, heads):
    lane = lax.broadcasted_iota(jnp.int32, logs.shape, 1)
    high = logs.astype(jnp.bfloat16).astype(jnp.float32)
    rest = logs - high
    mid = rest.astype(jnp.bfloat16).astype(jnp.float32)
    low = rest - mid
    low = jnp.where(lane < 3 * heads, low, 0.0)
    return jnp.where(lane < heads, high, jnp.where(lane < 2 * heads, mid, low)).astype(jnp.bfloat16)


def option_partials(blk, owner, slot, length, kvs, masks, queries, after):
    n, heads = len(masks), queries[0].shape[1] // HD
    options = 2 * queries[0].shape[0]
    width = (heads + 1) * HD
    rows = kvs[0].shape[0]
    return pl.pallas_call(
        functools.partial(option_kernel, masks, heads),
        out_shape=[jax.ShapeDtypeStruct((n // 2 * CAP, width), jnp.bfloat16)] * 2,
        in_specs=[SMEM] + [VMEM] * (5 + len(kvs)) + [ANY],
        out_specs=[VMEM] * 2,
        scratch_shapes=[
            pltpu.VMEM((options, heads * HD), jnp.bfloat16),
            pltpu.VMEM((options, width), jnp.bfloat16),
        ],
        compiler_params=params(4 + options // 32),
        cost_estimate=cost(1000000000),
        name="option_partials",
    )(blk, owner, slot, length, *kvs, *queries, after)


def merge_kernel(heads, a, b, after, *outs):
    width = heads * HD
    lane = lax.broadcasted_iota(jnp.int32, (HD, width), 0)
    head = lax.broadcasted_iota(jnp.int32, (HD, width), 1) // HD
    pick = jnp.where((lax.rem(lane, heads) == head) & (lane < 3 * heads), 1.0, 0.0).astype(jnp.bfloat16)
    logs = [nn(x[:, width:], pick) for x in (a, b)]
    top = jnp.maximum(*logs)
    weights = [jnp.exp(log - top) for log in logs]
    total = weights[0] + weights[1]
    merged = (weights[0] * a[:, :width].astype(jnp.float32) + weights[1] * b[:, :width].astype(jnp.float32)) / total
    merged = merged.astype(jnp.bfloat16)
    if len(outs) == 1:
        outs[0][...] = merged
        return
    log = top + jnp.log(total)
    lane = lax.broadcasted_iota(jnp.int32, (a.shape[0], HD), 1)
    packed = jnp.zeros((a.shape[0], HD), jnp.float32)
    for h in range(heads):
        packed = jnp.where(lax.rem(lane, heads) == h, log[:, h * HD : (h + 1) * HD], packed)
    packed = summands(packed, heads)
    half = a.shape[0] // 2
    for i, out in enumerate(outs):
        out[:, :width] = merged[i * half : (i + 1) * half]
        out[:, width:] = packed[i * half : (i + 1) * half]


def merge(a, b, last, after):
    rows, width = a.shape
    heads = width // HD - 1
    if last:
        shapes = [jax.ShapeDtypeStruct((rows, heads * HD), jnp.bfloat16)]
    else:
        shapes = [jax.ShapeDtypeStruct((rows // 2, width), jnp.bfloat16)] * 2
    return pl.pallas_call(
        functools.partial(merge_kernel, heads),
        out_shape=shapes,
        in_specs=[VMEM] * 2 + [ANY],
        out_specs=[VMEM] * len(shapes),
        compiler_params=params(6),
        cost_estimate=BRIEF,
        name="merge",
    )(a, b, after)


def swap(x, n, mask):
    return lax.ppermute(x, "blk", [(i, i ^ mask) for i in range(n)])


def from_root(x, blk):
    return lax.psum(jnp.where(blk == 0, x, jnp.zeros_like(x)), "blk")


def body(ctx_query, ctx_key, ctx_value, opt_query, opt_owner, opt_slot, opt_length):
    n = lax.axis_size("blk")
    blk = lax.axis_index("blk")
    blk_arr = blk.astype(jnp.int32).reshape(1)
    options = opt_owner.shape[0]
    rounds = n.bit_length() - 1

    hold = lax.optimization_barrier
    row = lambda x: x.reshape(1, options)

    blk_arr, ctx_key = hold((blk_arr, ctx_key))
    sent = parts(blk_arr, ctx_key, ctx_value)
    sent, opt_query = hold((sent, opt_query))
    shards = [opt_query]
    masks = [0]
    for bit in reversed(range(1, rounds)):
        mine = shards[0] if len(shards) == 1 else jnp.concatenate(shards, axis=0)
        shards = [mine, swap(mine, n, 1 << bit)]
        masks = masks + [mask | 1 << bit for mask in masks]
    masks = masks + [mask | 1 for mask in masks]
    if n == 4:
        first = [lax.ppermute(sent[0], "blk", [(0, 2)])]
    small = [row(opt_owner), row(opt_slot), row(opt_length), shards[0]]
    state, kvs, (ctx_query, *small, own) = first_attention(blk_arr, ctx_key, ctx_value, ctx_query, small)
    kvs, state, sent, shards = hold((kvs, state, sent, shards))
    mine = join([own, *shards[1:]])
    queries = [mine, swap(mine, n, 1)]
    states = [state]
    if n == 4:
        first += [lax.ppermute(x, "blk", [(0, 2)]) for x in sent[1:]]
    states += [local_attention(blk_arr, kv, g, ctx_query) for g, kv in enumerate(kvs) if g]
    if n == 4:
        first[0], states = hold((first[0], states))
    keep, send = option_partials(blk_arr, *small, kvs, masks, queries, states[-1][1])
    if n == 4:
        near = [lax.ppermute(first[0], "blk", [(2, 1)])]
        sent, keep = hold((sent, keep))
        near += [lax.ppermute(x, "blk", [(0, 1)]) for x in sent[1:]]
        first[1:], keep = hold((first[1:], keep))
        anchors = [[x, y, lax.ppermute(y, "blk", [(2, 3)])] for x, y in zip(near, first)]
        anchors[0], first = hold((anchors[0], first))
    else:
        anchors = [[from_root(x, blk)] for x in sent]
    ctx_out, tokens = None, []
    for g, state in enumerate(states):
        ctx_out, token = anchor_attention(blk_arr, ctx_query, kvs[g], state, anchors[g], g, ctx_out)
        tokens.append(token)
    for bit in range(rounds):
        got = swap(send, n, 1 << bit)
        last = bit == rounds - 1
        outs = merge(keep, got, last, tokens[-1 if last else 0])
        if last:
            opt_out = outs[0]
        else:
            keep, send = outs
    return (ctx_out, opt_out)


def solution(mesh):
    spread = P(("groups", "blk"), "head")
    return jax.shard_map(
        body,
        mesh=mesh,
        in_specs=(spread, spread, spread, spread, P("groups"), P("groups"), P("groups")),
        out_specs=(spread, spread),
        check_vma=False,
    )
```

```python
import functools
import math

import jax
import jax.numpy as jnp
from jax import lax
from jax.experimental import pallas as pl
from jax.experimental.pallas import tpu as pltpu
from jax.sharding import PartitionSpec as P

HD = 128
HQ = 64
KVH = 8
CAP = 32
GROUP = HQ // KVH
SCALE = HD ** (-0.5)
C2 = SCALE * math.log2(math.e)
NEG = -1e30
TILE = 256
PAIR = 2
VMEM = pl.BlockSpec(memory_space=pltpu.VMEM)
SMEM = pl.BlockSpec(memory_space=pltpu.SMEM)
HBM = pl.BlockSpec(memory_space=pltpu.HBM)
ANY = pl.BlockSpec(memory_space=pl.ANY)


def cost(flops):
    return pl.CostEstimate(flops=flops, bytes_accessed=1, transcendentals=0)


BRIEF = cost(1)


def nt(a, b):
    return lax.dot_general(a, b, (((1,), (1,)), ((), ())), preferred_element_type=jnp.float32)


def nn(a, b):
    return jnp.dot(a, b, preferred_element_type=jnp.float32)


def params(mib):
    return pltpu.CompilerParams(vmem_limit_bytes=mib * 1024 * 1024)


def fold(op, items):
    return functools.reduce(op, items)


def start_all(copies, sem):
    started = [pltpu.make_async_copy(a, b, sem.at[i]) for i, (a, b) in enumerate(copies)]
    for copy in started:
        copy.start()
    return started


def in_hbm(x):
    return pltpu.with_memory_space_constraint(x, pltpu.HBM)


def beside(heads, k_ref, v_ref, kv):
    copies = []
    for g in range(heads):
        for ref, at in ((k_ref, 0), (v_ref, HD)):
            copies.append((ref.at[:, g * HD : (g + 1) * HD], kv[g].at[:, at : at + HD]))
    return copies


def parts_kernel(heads, k_ref, v_ref, *refs):
    kv, sem = refs[:heads], refs[heads]
    for copy in start_all(beside(heads, k_ref, v_ref, kv), sem):
        copy.wait()


def parts(key, value):
    rows, heads = key.shape[0], key.shape[1] // HD
    outs = pl.pallas_call(
        functools.partial(parts_kernel, heads),
        out_shape=[pltpu.VMEM((rows, 2 * HD), key.dtype)] * heads,
        in_specs=[HBM] * 2,
        out_specs=[VMEM] * heads,
        scratch_shapes=[pltpu.SemaphoreType.DMA((2 * heads,))],
        compiler_params=params(2),
        cost_estimate=BRIEF,
        name="parts",
    )(in_hbm(key), in_hbm(value))
    return list(outs)


def pipelined(tasks, scores, finish):
    ahead = scores(tasks[0])
    for i, task in enumerate(tasks):
        now = ahead
        if i + 1 < len(tasks):
            ahead = scores(tasks[i + 1])
        finish(task, now)


def head_columns(h):
    return slice(h * HD, (h + 1) * HD)


def local_pass(g, q_ref, kv_ref, ve, arrived, emit):
    rows = kv_ref.shape[0]
    ve[:, :HD] = kv_ref[:, HD:]
    ve[:, HD:] = jnp.ones((rows, HD), jnp.bfloat16)
    row = lax.broadcasted_iota(jnp.int32, (PAIR * TILE, TILE), 0)
    seen = lax.rem(row, TILE) >= lax.broadcasted_iota(jnp.int32, (PAIR * TILE, TILE), 1)

    def scores(task):
        first, at = task
        if at == 0:
            arrived(first)
        q = jnp.concatenate([q_ref[at : at + TILE, head_columns(g * GROUP + first + j)] for j in range(PAIR)], axis=0)
        parts = [nt(q, kv_ref[:at, :HD])] if at else []
        parts.append(jnp.where(seen, nt(q, kv_ref[at : at + TILE, :HD]), NEG))
        return parts

    def finish(task, parts):
        first, at = task
        top = fold(jnp.maximum, [jnp.max(s, axis=1, keepdims=True) for s in parts])
        total = None
        for s, start in zip(parts, [0, at] if at else [at]):
            p = jnp.exp2((s - top) * C2).astype(jnp.bfloat16)
            part = nn(p, ve[start : start + s.shape[1], :])
            total = part if total is None else total + part
        for j in range(PAIR):
            mine = slice(j * TILE, (j + 1) * TILE)
            emit(slice(at, at + TILE), first + j, total[mine, :HD], total[mine, HD:], top[mine] * C2)

    pipelined([(h, at) for h in range(0, GROUP, PAIR) for at in range(0, rows, TILE)], scores, finish)


def first_kernel(blk_ref, kv_ref, *refs):
    count = (len(refs) - 5) // 2
    sources, state, held, (ve, sem) = refs[:count], refs[count : count + 3], refs[count + 3 : -2], refs[-2:]
    q_ref = held[0]
    spots = [slice(h * HD, (h + PAIR) * HD) for h in range(0, q_ref.shape[1] // HD, PAIR)]
    copies = [(sources[0].at[:, x], q_ref.at[:, x]) for x in spots] + list(zip(sources[1:], held[1:]))
    copies = start_all(copies, sem)
    ahead = GROUP // PAIR

    @pl.when(blk_ref[0] > 0)
    def _():
        local_pass(0, q_ref, kv_ref, ve, lambda h: copies[h // PAIR].wait(), keep_in(state))

    @pl.when(blk_ref[0] == 0)
    def _():
        for copy in copies[:ahead]:
            copy.wait()

    for copy in copies[ahead:]:
        copy.wait()


def first_attention(blk, kv, query, others):
    rows = kv.shape[0]
    sources = [query, *others]
    outs = pl.pallas_call(
        first_kernel,
        out_shape=[pltpu.VMEM((rows, GROUP * HD), jnp.float32)] * 3 + [pltpu.VMEM(x.shape, x.dtype) for x in sources],
        in_specs=[SMEM, VMEM] + [HBM] * len(sources),
        out_specs=[VMEM] * (3 + len(sources)),
        scratch_shapes=[
            pltpu.VMEM((rows, 2 * HD), jnp.bfloat16),
            pltpu.SemaphoreType.DMA((query.shape[1] // HD // PAIR + len(others),)),
        ],
        compiler_params=params(6),
        cost_estimate=cost(2 * 10**9),
        name="local_attention",
    )(blk, kv, *[in_hbm(x) for x in sources])
    return list(outs[:3]), list(outs[3:])


def keep_in(state):
    acc_ref, top_ref, sum_ref = state

    def emit(rows, h, total, z, top):
        here = (rows, head_columns(h))
        acc_ref[here], sum_ref[here], top_ref[here] = total, z, jnp.broadcast_to(top, total.shape)

    return emit


def local_kernel(g, blk_ref, kv_ref, q_ref, *refs):
    @pl.when(blk_ref[0] > 0)
    def _():
        local_pass(g, q_ref, kv_ref, refs[3], lambda h: None, keep_in(refs[:3]))


def local_attention(blk, kv, g, query):
    rows = kv.shape[0]
    return list(
        pl.pallas_call(
            functools.partial(local_kernel, g),
            out_shape=[pltpu.VMEM((rows, GROUP * HD), jnp.float32)] * 3,
            in_specs=[SMEM, VMEM, VMEM],
            out_specs=[VMEM] * 3,
            scratch_shapes=[pltpu.VMEM((rows, 2 * HD), jnp.bfloat16)],
            compiler_params=params(6),
            cost_estimate=cost(10**9),
            name="local_attention",
        )(blk, kv, query)
    )


def anchor_kernel(g, count, prior, blk_ref, q_ref, kv_ref, acc_ref, top_ref, sum_ref, *refs):
    cand, (o_ref, token, ka, vae, out, sem) = refs[:count], refs[count + prior :]
    rows = q_ref.shape[0]
    blk = blk_ref[0]
    token[...] = jnp.zeros(token.shape, jnp.float32)

    def leave(h):
        return pltpu.make_async_copy(out.at[h], o_ref.at[:, head_columns(g * GROUP + h)], sem.at[h])

    def take(ref):
        ka[...] = ref[:, :HD]
        vae[:, :HD] = ref[:, HD:]

    def scores(h):
        return nt(q_ref[:, head_columns(g * GROUP + h)], ka[...])

    def finish(h, s):
        held = (slice(None), head_columns(h))
        before = top_ref[held]
        top = jnp.maximum(jnp.max(s, axis=1, keepdims=True) * C2, before)
        p = [jnp.exp2(s[:, at : at + HD] * C2 - top).astype(jnp.bfloat16) for at in range(0, rows, HD)]
        total = nn(jnp.concatenate(p, axis=1), vae[...])
        w = jnp.exp2(before - top)
        o = (total[:, :HD] + w * acc_ref[held]) * inverse(total[:, HD:] + w * sum_ref[held])
        out[h] = o.astype(jnp.bfloat16)
        leave(h).start()

    @pl.when(blk > 0)
    def _():
        if count == 1:
            take(cand[0])
        else:
            for i, ref in enumerate(cand):
                pl.when(blk == i + 1)(functools.partial(take, ref))
        vae[:, HD:] = jnp.ones((rows, HD), jnp.bfloat16)
        pipelined(list(range(GROUP)), scores, finish)

    def emit(here, h, total, z, top):
        out[h, here, :] = (total * inverse(z)).astype(jnp.bfloat16)
        if here.stop == rows:
            leave(h).start()

    @pl.when(blk == 0)
    def _():
        local_pass(g, q_ref, kv_ref, vae, lambda first: None, emit)

    for h in range(GROUP):
        leave(h).wait()


def inverse(x):
    guess = pl.reciprocal(x, approx=True)
    return guess * (2.0 - x * guess)


def anchor_attention(blk, query, kv, state, cands, g, prior):
    rows = query.shape[0]
    args = [blk, query, kv, *state, *cands]
    specs = [SMEM] + [VMEM] * (5 + len(cands))
    alias = {}
    if prior is not None:
        alias = {len(args): 0}
        args.append(prior)
        specs.append(ANY)
    return pl.pallas_call(
        functools.partial(anchor_kernel, g, len(cands), len(alias)),
        out_shape=[jax.ShapeDtypeStruct(query.shape, query.dtype), jax.ShapeDtypeStruct((8, HD), jnp.float32)],
        in_specs=specs,
        out_specs=[ANY, VMEM],
        scratch_shapes=[
            pltpu.VMEM((rows, HD), jnp.bfloat16),
            pltpu.VMEM((rows, 2 * HD), jnp.bfloat16),
            pltpu.VMEM((GROUP, rows, HD), jnp.bfloat16),
            pltpu.SemaphoreType.DMA((GROUP,)),
        ],
        input_output_aliases=alias,
        compiler_params=params(6),
        cost_estimate=cost(1000000000),
        name="anchor_attention",
    )(*args)


def fold_order(n):
    bits = n.bit_length() - 1
    return sorted(range(n), key=lambda x: int(format(x, "0%db" % bits)[::-1], 2))


def join_kernel(*refs):
    at = 0
    for ref in refs[:-1]:
        refs[-1][at : at + ref.shape[0], :] = ref[...]
        at += ref.shape[0]


def join(arrays):
    height, width = sum(x.shape[0] for x in arrays), arrays[0].shape[1]
    return pl.pallas_call(
        join_kernel,
        out_shape=pltpu.VMEM((height, width), arrays[0].dtype),
        in_specs=[VMEM] * len(arrays),
        out_specs=VMEM,
        compiler_params=params(2),
        cost_estimate=BRIEF,
        name="join",
    )(*arrays)


def option_kernel(masks, heads, blk_ref, owner_ref, slot_ref, length_ref, *refs):
    n = len(masks)
    kv_heads = heads // GROUP
    kv, queries = refs[:kv_heads], refs[kv_heads : kv_heads + 2]
    keep, send, q_all, part = refs[kv_heads + 3 :]
    blk = blk_ref[0]
    rows = kv[0].shape[0]
    half = queries[0].shape[0]
    options, each = 2 * half, 2 * half // n
    for i, mask in enumerate(masks):
        at = jnp.bitwise_xor(blk, mask) * each
        here = queries[i * each // half].at[i * each % half : i * each % half + each]
        q_all[pl.ds(pl.multiple_of(at, each), each), :] = here[...]
    eye = lax.broadcasted_iota(jnp.int32, (options, options), 0) == lax.broadcasted_iota(jnp.int32, (options, options), 1)
    length = jnp.sum(jnp.where(eye, length_ref[...].astype(jnp.float32), 0.0), axis=1, keepdims=True)
    seen = length - (blk * rows).astype(jnp.float32)
    lane = lax.broadcasted_iota(jnp.int32, (options, HD), 1)
    logs = jnp.zeros((options, HD), jnp.float32)
    stack = max(1, min(GROUP, 512 // options))
    spots = lax.broadcasted_iota(jnp.int32, (options * stack, rows), 1).astype(jnp.float32)
    seen_all = jnp.concatenate([seen] * stack, axis=0)
    for first in range(0, heads, stack):
        g = first // GROUP
        q = jnp.concatenate([q_all[:, h * HD : (h + 1) * HD] for h in range(first, first + stack)], axis=0)
        s = nt(q, kv[g][:, :HD])
        s = jnp.where(spots < seen_all, s, NEG)
        top = jnp.max(s, axis=1, keepdims=True)
        e = jnp.exp2((s - top) * C2)
        z = jnp.sum(e, axis=1, keepdims=True)
        o = nn(e.astype(jnp.bfloat16), kv[g][:, HD:]) / z
        live = seen_all > 0
        o = jnp.where(live, o, 0.0).astype(jnp.bfloat16)
        log = jnp.where(live, top * SCALE + jnp.log(z), NEG)
        for j in range(stack):
            h = first + j
            part[:, h * HD : (h + 1) * HD] = o[j * options : (j + 1) * options]
            logs = jnp.where(lax.rem(lane, heads) == h, log[j * options : (j + 1) * options], logs)
    part[:, heads * HD :] = summands(logs, heads)
    slot = lax.broadcasted_iota(jnp.int32, (CAP, options), 0)
    order = fold_order(n)
    for half, out in ((order[: n // 2], keep), (order[n // 2 :], send)):
        for i, mask in enumerate(half):
            pick = (owner_ref[...] == jnp.bitwise_xor(blk, mask)) & (slot_ref[...] == slot)
            pick = jnp.where(pick, 1.0, 0.0).astype(jnp.bfloat16)
            out[i * CAP : (i + 1) * CAP, :] = nn(pick, part[...]).astype(jnp.bfloat16)


def summands(logs, heads):
    lane = lax.broadcasted_iota(jnp.int32, logs.shape, 1)
    high = logs.astype(jnp.bfloat16).astype(jnp.float32)
    rest = logs - high
    mid = rest.astype(jnp.bfloat16).astype(jnp.float32)
    low = rest - mid
    low = jnp.where(lane < 3 * heads, low, 0.0)
    return jnp.where(lane < heads, high, jnp.where(lane < 2 * heads, mid, low)).astype(jnp.bfloat16)


def option_partials(blk, owner, slot, length, kvs, masks, queries, after):
    n, heads = len(masks), queries[0].shape[1] // HD
    options = 2 * queries[0].shape[0]
    width = (heads + 1) * HD
    rows = kvs[0].shape[0]
    return pl.pallas_call(
        functools.partial(option_kernel, masks, heads),
        out_shape=[jax.ShapeDtypeStruct((n // 2 * CAP, width), jnp.bfloat16)] * 2,
        in_specs=[SMEM] + [VMEM] * (5 + len(kvs)) + [ANY],
        out_specs=[VMEM] * 2,
        scratch_shapes=[
            pltpu.VMEM((options, heads * HD), jnp.bfloat16),
            pltpu.VMEM((options, width), jnp.bfloat16),
        ],
        compiler_params=params(4 + options // 32),
        cost_estimate=cost(1000000000),
        name="option_partials",
    )(blk, owner, slot, length, *kvs, *queries, after)


def merge_kernel(heads, a, b, after, *outs):
    width = heads * HD
    lane = lax.broadcasted_iota(jnp.int32, (HD, width), 0)
    head = lax.broadcasted_iota(jnp.int32, (HD, width), 1) // HD
    pick = jnp.where((lax.rem(lane, heads) == head) & (lane < 3 * heads), 1.0, 0.0).astype(jnp.bfloat16)
    logs = [nn(x[:, width:], pick) for x in (a, b)]
    top = jnp.maximum(*logs)
    weights = [jnp.exp(log - top) for log in logs]
    total = weights[0] + weights[1]
    merged = (weights[0] * a[:, :width].astype(jnp.float32) + weights[1] * b[:, :width].astype(jnp.float32)) / total
    merged = merged.astype(jnp.bfloat16)
    if len(outs) == 1:
        outs[0][...] = merged
        return
    log = top + jnp.log(total)
    lane = lax.broadcasted_iota(jnp.int32, (a.shape[0], HD), 1)
    packed = jnp.zeros((a.shape[0], HD), jnp.float32)
    for h in range(heads):
        packed = jnp.where(lax.rem(lane, heads) == h, log[:, h * HD : (h + 1) * HD], packed)
    packed = summands(packed, heads)
    half = a.shape[0] // 2
    for i, out in enumerate(outs):
        out[:, :width] = merged[i * half : (i + 1) * half]
        out[:, width:] = packed[i * half : (i + 1) * half]


def merge(a, b, last, after):
    rows, width = a.shape
    heads = width // HD - 1
    if last:
        shapes = [jax.ShapeDtypeStruct((rows, heads * HD), jnp.bfloat16)]
    else:
        shapes = [jax.ShapeDtypeStruct((rows // 2, width), jnp.bfloat16)] * 2
    return pl.pallas_call(
        functools.partial(merge_kernel, heads),
        out_shape=shapes,
        in_specs=[VMEM] * 2 + [ANY],
        out_specs=[VMEM] * len(shapes),
        compiler_params=params(6),
        cost_estimate=BRIEF,
        name="merge",
    )(a, b, after)


def swap(x, n, mask):
    return lax.ppermute(x, "blk", [(i, i ^ mask) for i in range(n)])


def from_root(x, blk):
    return lax.psum(jnp.where(blk == 0, x, jnp.zeros_like(x)), "blk")


def body(ctx_query, ctx_key, ctx_value, opt_query, opt_owner, opt_slot, opt_length):
    n = lax.axis_size("blk")
    blk = lax.axis_index("blk")
    blk_arr = blk.astype(jnp.int32).reshape(1)
    options = opt_owner.shape[0]
    rounds = n.bit_length() - 1

    hold = lax.optimization_barrier
    row = lambda x: x.reshape(1, options)

    blk_arr, ctx_key = hold((blk_arr, ctx_key))
    kvs = parts(ctx_key, ctx_value)
    shards = [opt_query]
    masks = [0]
    for bit in reversed(range(1, rounds)):
        mine = shards[0] if len(shards) == 1 else jnp.concatenate(shards, axis=0)
        shards = [mine, swap(mine, n, 1 << bit)]
        masks = masks + [mask | 1 << bit for mask in masks]
    masks = masks + [mask | 1 for mask in masks]
    if n == 4:
        first = [lax.ppermute(kvs[0], "blk", [(0, 2)])]
    small = [row(opt_owner), row(opt_slot), row(opt_length), shards[0]]
    state, (ctx_query, *small, own) = first_attention(blk_arr, kvs[0], ctx_query, small)
    kvs, state, shards = hold((kvs, state, shards))
    mine = join([own, *shards[1:]])
    queries = [mine, swap(mine, n, 1)]
    states = [state]
    if n == 4:
        first += [lax.ppermute(x, "blk", [(0, 2)]) for x in kvs[1:]]
    states += [local_attention(blk_arr, kv, g, ctx_query) for g, kv in enumerate(kvs) if g]
    if n == 4:
        first[0], states = hold((first[0], states))
    keep, send = option_partials(blk_arr, *small, kvs, masks, queries, states[-1][1])
    if n == 4:
        near = [lax.ppermute(first[0], "blk", [(2, 1)])]
        kvs, keep = hold((kvs, keep))
        near += [lax.ppermute(x, "blk", [(0, 1)]) for x in kvs[1:]]
        first[1:], keep = hold((first[1:], keep))
        anchors = [[x, y, lax.ppermute(y, "blk", [(2, 3)])] for x, y in zip(near, first)]
        anchors[0], first = hold((anchors[0], first))
    else:
        anchors = [[from_root(x, blk)] for x in kvs]
    ctx_out, tokens = None, []
    for g, state in enumerate(states):
        ctx_out, token = anchor_attention(blk_arr, ctx_query, kvs[g], state, anchors[g], g, ctx_out)
        tokens.append(token)
    for bit in range(rounds):
        got = swap(send, n, 1 << bit)
        last = bit == rounds - 1
        outs = merge(keep, got, last, tokens[-1 if last else 0])
        if last:
            opt_out = outs[0]
        else:
            keep, send = outs
    return (ctx_out, opt_out)


def solution(mesh):
    spread = P(("groups", "blk"), "head")
    return jax.shard_map(
        body,
        mesh=mesh,
        in_specs=(spread, spread, spread, spread, P("groups"), P("groups"), P("groups")),
        out_specs=(spread, spread),
        check_vma=False,
    )
```

```python
import functools
import math

import jax
import jax.numpy as jnp
from jax import lax
from jax.experimental import pallas as pl
from jax.experimental.pallas import tpu as pltpu
from jax.sharding import PartitionSpec as P

HD = 128
HQ = 64
KVH = 8
CAP = 32
GROUP = HQ // KVH
SCALE = HD ** (-0.5)
C2 = SCALE * math.log2(math.e)
NEG = -1e30
TILE = 256
PAIR = 2
SLAB = 64
VMEM = pl.BlockSpec(memory_space=pltpu.VMEM)
SMEM = pl.BlockSpec(memory_space=pltpu.SMEM)
HBM = pl.BlockSpec(memory_space=pltpu.HBM)
ANY = pl.BlockSpec(memory_space=pl.ANY)


def cost(flops):
    return pl.CostEstimate(flops=flops, bytes_accessed=1, transcendentals=0)


BRIEF = cost(1)


def nt(a, b):
    return lax.dot_general(a, b, (((1,), (1,)), ((), ())), preferred_element_type=jnp.float32)


def nn(a, b):
    return jnp.dot(a, b, preferred_element_type=jnp.float32)


def params(mib):
    return pltpu.CompilerParams(vmem_limit_bytes=mib * 1024 * 1024)


def fold(op, items):
    return functools.reduce(op, items)


def start_all(copies, sem):
    started = [pltpu.make_async_copy(a, b, sem.at[i]) for i, (a, b) in enumerate(copies)]
    for copy in started:
        copy.start()
    return started


def in_hbm(x):
    return pltpu.with_memory_space_constraint(x, pltpu.HBM)


def beside(heads, k_ref, v_ref, kv):
    copies = []
    for g in range(heads):
        for ref, at in ((k_ref, 0), (v_ref, HD)):
            copies.append((ref.at[:, g * HD : (g + 1) * HD], kv[g].at[:, at : at + HD]))
    return copies


def parts_kernel(heads, k_ref, v_ref, *refs):
    kv, sem = refs[:heads], refs[heads]
    for copy in start_all(beside(heads, k_ref, v_ref, kv), sem):
        copy.wait()


def parts(key, value):
    rows, heads = key.shape[0], key.shape[1] // HD
    outs = pl.pallas_call(
        functools.partial(parts_kernel, heads),
        out_shape=[pltpu.VMEM((rows, 2 * HD), key.dtype)] * heads,
        in_specs=[HBM] * 2,
        out_specs=[VMEM] * heads,
        scratch_shapes=[pltpu.SemaphoreType.DMA((2 * heads,))],
        compiler_params=params(2),
        cost_estimate=BRIEF,
        name="parts",
    )(in_hbm(key), in_hbm(value))
    return list(outs)


def pipelined(tasks, scores, finish):
    ahead = scores(tasks[0])
    for i, task in enumerate(tasks):
        now = ahead
        if i + 1 < len(tasks):
            ahead = scores(tasks[i + 1])
        finish(task, now)


def head_columns(h):
    return slice(h * HD, (h + 1) * HD)


def local_pass(g, q_ref, kv_ref, ve, arrived, emit):
    rows = kv_ref.shape[0]
    ve[:, :HD] = kv_ref[:, HD:]
    ve[:, HD:] = jnp.ones((rows, HD), jnp.bfloat16)
    row = lax.broadcasted_iota(jnp.int32, (PAIR * TILE, TILE), 0)
    seen = lax.rem(row, TILE) >= lax.broadcasted_iota(jnp.int32, (PAIR * TILE, TILE), 1)

    def scores(task):
        first, at = task
        if at == 0:
            arrived(first)
        q = jnp.concatenate([q_ref[at : at + TILE, head_columns(g * GROUP + first + j)] for j in range(PAIR)], axis=0)
        parts = [nt(q, kv_ref[:at, :HD])] if at else []
        parts.append(jnp.where(seen, nt(q, kv_ref[at : at + TILE, :HD]), NEG))
        return parts

    def finish(task, parts):
        first, at = task
        top = fold(jnp.maximum, [jnp.max(s, axis=1, keepdims=True) for s in parts])
        total = None
        for s, start in zip(parts, [0, at] if at else [at]):
            p = jnp.exp2((s - top) * C2).astype(jnp.bfloat16)
            part = nn(p, ve[start : start + s.shape[1], :])
            total = part if total is None else total + part
        for j in range(PAIR):
            mine = slice(j * TILE, (j + 1) * TILE)
            emit(slice(at, at + TILE), first + j, total[mine, :HD], total[mine, HD:], top[mine] * C2)

    pipelined([(h, at) for h in range(0, GROUP, PAIR) for at in range(0, rows, TILE)], scores, finish)


def first_kernel(blk_ref, kv_ref, *refs):
    count = (len(refs) - 5) // 2
    sources, state, held, (ve, sem) = refs[:count], refs[count : count + 3], refs[count + 3 : -2], refs[-2:]
    q_ref = held[0]
    spots = [slice(h * HD, (h + PAIR) * HD) for h in range(0, q_ref.shape[1] // HD, PAIR)]
    copies = [(sources[0].at[:, x], q_ref.at[:, x]) for x in spots] + list(zip(sources[1:], held[1:]))
    copies = start_all(copies, sem)
    ahead = GROUP // PAIR

    @pl.when(blk_ref[0] > 0)
    def _():
        local_pass(0, q_ref, kv_ref, ve, lambda h: copies[h // PAIR].wait(), keep_in(state))

    @pl.when(blk_ref[0] == 0)
    def _():
        for copy in copies[:ahead]:
            copy.wait()

    for copy in copies[ahead:]:
        copy.wait()


def first_attention(blk, kv, query, others):
    rows = kv.shape[0]
    sources = [query, *others]
    outs = pl.pallas_call(
        first_kernel,
        out_shape=[pltpu.VMEM((rows, GROUP * HD), jnp.float32)] * 3 + [pltpu.VMEM(x.shape, x.dtype) for x in sources],
        in_specs=[SMEM, VMEM] + [HBM] * len(sources),
        out_specs=[VMEM] * (3 + len(sources)),
        scratch_shapes=[
            pltpu.VMEM((rows, 2 * HD), jnp.bfloat16),
            pltpu.SemaphoreType.DMA((query.shape[1] // HD // PAIR + len(others),)),
        ],
        compiler_params=params(6),
        cost_estimate=cost(2 * 10**9),
        name="local_attention",
    )(blk, kv, *[in_hbm(x) for x in sources])
    return list(outs[:3]), list(outs[3:])


def keep_in(state):
    acc_ref, top_ref, sum_ref = state

    def emit(rows, h, total, z, top):
        here = (rows, head_columns(h))
        acc_ref[here], sum_ref[here], top_ref[here] = total, z, jnp.broadcast_to(top, total.shape)

    return emit


def local_kernel(g, blk_ref, kv_ref, q_ref, *refs):
    @pl.when(blk_ref[0] > 0)
    def _():
        local_pass(g, q_ref, kv_ref, refs[3], lambda h: None, keep_in(refs[:3]))


def local_attention(blk, kv, g, query):
    rows = kv.shape[0]
    return list(
        pl.pallas_call(
            functools.partial(local_kernel, g),
            out_shape=[pltpu.VMEM((rows, GROUP * HD), jnp.float32)] * 3,
            in_specs=[SMEM, VMEM, VMEM],
            out_specs=[VMEM] * 3,
            scratch_shapes=[pltpu.VMEM((rows, 2 * HD), jnp.bfloat16)],
            compiler_params=params(6),
            cost_estimate=cost(10**9),
            name="local_attention",
        )(blk, kv, query)
    )


def anchor_kernel(g, groups, prior, blk_ref, q_ref, kv_ref, acc_ref, top_ref, sum_ref, *refs):
    count = sum(groups)
    cand, (o_ref, token, ka, vae, s_buf, p_buf, w_buf, out, sem) = refs[:count], refs[count + prior :]
    rows = q_ref.shape[0]
    blk = blk_ref[0]
    token[...] = jnp.zeros(token.shape, jnp.float32)

    def leave(h):
        return pltpu.make_async_copy(out.at[h], o_ref.at[:, head_columns(g * GROUP + h)], sem.at[h])

    def take(refs):
        at = 0
        for ref in refs:
            here = slice(at, at + ref.shape[0])
            ka[here, :] = ref[:, :HD]
            vae[here, :HD] = ref[:, HD:]
            at = here.stop

    def scores(h):
        s_buf[h % 2] = nt(q_ref[:, head_columns(g * GROUP + h)], ka[...])

    def finish(h, _):
        mine = head_columns(h)
        for at in range(0, rows, SLAB):
            here = slice(at, at + SLAB)
            s = s_buf[h % 2, here, :]
            before = top_ref[here, mine]
            top = jnp.maximum(jnp.max(s, axis=1, keepdims=True) * C2, before)
            for x in range(0, rows, HD):
                p_buf[h % 2, here, x : x + HD] = jnp.exp2(s[:, x : x + HD] * C2 - top).astype(jnp.bfloat16)
            w_buf[h % 2, here, :] = jnp.exp2(before - top)
        total = nn(p_buf[h % 2], vae[...])
        for at in range(0, rows, SLAB):
            here = slice(at, at + SLAB)
            w = w_buf[h % 2, here, :]
            o = (total[here, :HD] + w * acc_ref[here, mine]) * inverse(total[here, HD:] + w * sum_ref[here, mine])
            out[h, here, :] = o.astype(jnp.bfloat16)
        leave(h).start()

    @pl.when(blk > 0)
    def _():
        if len(groups) == 1:
            take(cand)
        else:
            at = 0
            for i, size in enumerate(groups):
                pl.when(blk == i + 1)(functools.partial(take, cand[at : at + size]))
                at += size
        vae[:, HD:] = jnp.ones((rows, HD), jnp.bfloat16)
        pipelined(list(range(GROUP)), scores, finish)

    def emit(here, h, total, z, top):
        out[h, here, :] = (total * inverse(z)).astype(jnp.bfloat16)
        if here.stop == rows:
            leave(h).start()

    @pl.when(blk == 0)
    def _():
        local_pass(g, q_ref, kv_ref, vae, lambda first: None, emit)

    for h in range(GROUP):
        leave(h).wait()


def inverse(x):
    guess = pl.reciprocal(x, approx=True)
    return guess * (2.0 - x * guess)


def anchor_attention(blk, query, kv, state, cands, g, prior):
    rows = query.shape[0]
    flat = [x for group in cands for x in group]
    args = [blk, query, kv, *state, *flat]
    specs = [SMEM] + [VMEM] * (5 + len(flat))
    alias = {}
    if prior is not None:
        alias = {len(args): 0}
        args.append(prior)
        specs.append(ANY)
    return pl.pallas_call(
        functools.partial(anchor_kernel, g, [len(group) for group in cands], len(alias)),
        out_shape=[jax.ShapeDtypeStruct(query.shape, query.dtype), jax.ShapeDtypeStruct((8, HD), jnp.float32)],
        in_specs=specs,
        out_specs=[ANY, VMEM],
        scratch_shapes=[
            pltpu.VMEM((rows, HD), jnp.bfloat16),
            pltpu.VMEM((rows, 2 * HD), jnp.bfloat16),
            pltpu.VMEM((2, rows, rows), jnp.float32),
            pltpu.VMEM((2, rows, rows), jnp.bfloat16),
            pltpu.VMEM((2, rows, HD), jnp.float32),
            pltpu.VMEM((GROUP, rows, HD), jnp.bfloat16),
            pltpu.SemaphoreType.DMA((GROUP,)),
        ],
        input_output_aliases=alias,
        compiler_params=params(10),
        cost_estimate=cost(1000000000),
        name="anchor_attention",
    )(*args)


def fold_order(n):
    bits = n.bit_length() - 1
    return sorted(range(n), key=lambda x: int(format(x, "0%db" % bits)[::-1], 2))


def join_kernel(*refs):
    at = 0
    for ref in refs[:-1]:
        refs[-1][at : at + ref.shape[0], :] = ref[...]
        at += ref.shape[0]


def join(arrays):
    height, width = sum(x.shape[0] for x in arrays), arrays[0].shape[1]
    return pl.pallas_call(
        join_kernel,
        out_shape=pltpu.VMEM((height, width), arrays[0].dtype),
        in_specs=[VMEM] * len(arrays),
        out_specs=VMEM,
        compiler_params=params(2),
        cost_estimate=BRIEF,
        name="join",
    )(*arrays)


def half_kernel(which, x_ref, o_ref):
    rows = o_ref.shape[0]
    o_ref[...] = x_ref[which * rows : (which + 1) * rows, :]


def half_rows(x, which):
    return pl.pallas_call(
        functools.partial(half_kernel, which),
        out_shape=pltpu.VMEM((x.shape[0] // 2, x.shape[1]), x.dtype),
        in_specs=[VMEM],
        out_specs=VMEM,
        compiler_params=params(2),
        cost_estimate=BRIEF,
        name="half_rows",
    )(x)


def option_kernel(masks, heads, blk_ref, owner_ref, slot_ref, length_ref, *refs):
    n = len(masks)
    kv_heads = heads // GROUP
    kv, queries = refs[:kv_heads], refs[kv_heads : kv_heads + 2]
    keep, send, q_all, part = refs[kv_heads + 3 :]
    blk = blk_ref[0]
    rows = kv[0].shape[0]
    half = queries[0].shape[0]
    options, each = 2 * half, 2 * half // n
    for i, mask in enumerate(masks):
        at = jnp.bitwise_xor(blk, mask) * each
        here = queries[i * each // half].at[i * each % half : i * each % half + each]
        q_all[pl.ds(pl.multiple_of(at, each), each), :] = here[...]
    eye = lax.broadcasted_iota(jnp.int32, (options, options), 0) == lax.broadcasted_iota(jnp.int32, (options, options), 1)
    length = jnp.sum(jnp.where(eye, length_ref[...].astype(jnp.float32), 0.0), axis=1, keepdims=True)
    seen = length - (blk * rows).astype(jnp.float32)
    lane = lax.broadcasted_iota(jnp.int32, (options, HD), 1)
    logs = jnp.zeros((options, HD), jnp.float32)
    stack = max(1, min(GROUP, 512 // options))
    spots = lax.broadcasted_iota(jnp.int32, (options * stack, rows), 1).astype(jnp.float32)
    seen_all = jnp.concatenate([seen] * stack, axis=0)
    for first in range(0, heads, stack):
        g = first // GROUP
        q = jnp.concatenate([q_all[:, h * HD : (h + 1) * HD] for h in range(first, first + stack)], axis=0)
        s = nt(q, kv[g][:, :HD])
        s = jnp.where(spots < seen_all, s, NEG)
        top = jnp.max(s, axis=1, keepdims=True)
        e = jnp.exp2((s - top) * C2)
        z = jnp.sum(e, axis=1, keepdims=True)
        o = nn(e.astype(jnp.bfloat16), kv[g][:, HD:]) / z
        live = seen_all > 0
        o = jnp.where(live, o, 0.0).astype(jnp.bfloat16)
        log = jnp.where(live, top * SCALE + jnp.log(z), NEG)
        for j in range(stack):
            h = first + j
            part[:, h * HD : (h + 1) * HD] = o[j * options : (j + 1) * options]
            logs = jnp.where(lax.rem(lane, heads) == h, log[j * options : (j + 1) * options], logs)
    part[:, heads * HD :] = summands(logs, heads)
    slot = lax.broadcasted_iota(jnp.int32, (CAP, options), 0)
    order = fold_order(n)
    for half, out in ((order[: n // 2], keep), (order[n // 2 :], send)):
        for i, mask in enumerate(half):
            pick = (owner_ref[...] == jnp.bitwise_xor(blk, mask)) & (slot_ref[...] == slot)
            pick = jnp.where(pick, 1.0, 0.0).astype(jnp.bfloat16)
            out[i * CAP : (i + 1) * CAP, :] = nn(pick, part[...]).astype(jnp.bfloat16)


def summands(logs, heads):
    lane = lax.broadcasted_iota(jnp.int32, logs.shape, 1)
    high = logs.astype(jnp.bfloat16).astype(jnp.float32)
    rest = logs - high
    mid = rest.astype(jnp.bfloat16).astype(jnp.float32)
    low = rest - mid
    low = jnp.where(lane < 3 * heads, low, 0.0)
    return jnp.where(lane < heads, high, jnp.where(lane < 2 * heads, mid, low)).astype(jnp.bfloat16)


def option_partials(blk, owner, slot, length, kvs, masks, queries, after):
    n, heads = len(masks), queries[0].shape[1] // HD
    options = 2 * queries[0].shape[0]
    width = (heads + 1) * HD
    rows = kvs[0].shape[0]
    return pl.pallas_call(
        functools.partial(option_kernel, masks, heads),
        out_shape=[jax.ShapeDtypeStruct((n // 2 * CAP, width), jnp.bfloat16)] * 2,
        in_specs=[SMEM] + [VMEM] * (5 + len(kvs)) + [ANY],
        out_specs=[VMEM] * 2,
        scratch_shapes=[
            pltpu.VMEM((options, heads * HD), jnp.bfloat16),
            pltpu.VMEM((options, width), jnp.bfloat16),
        ],
        compiler_params=params(4 + options // 32),
        cost_estimate=cost(1000000000),
        name="option_partials",
    )(blk, owner, slot, length, *kvs, *queries, after)


def merge_kernel(heads, a, b, after, *outs):
    width = heads * HD
    lane = lax.broadcasted_iota(jnp.int32, (HD, width), 0)
    head = lax.broadcasted_iota(jnp.int32, (HD, width), 1) // HD
    pick = jnp.where((lax.rem(lane, heads) == head) & (lane < 3 * heads), 1.0, 0.0).astype(jnp.bfloat16)
    logs = [nn(x[:, width:], pick) for x in (a, b)]
    top = jnp.maximum(*logs)
    weights = [jnp.exp(log - top) for log in logs]
    total = weights[0] + weights[1]
    merged = (weights[0] * a[:, :width].astype(jnp.float32) + weights[1] * b[:, :width].astype(jnp.float32)) / total
    merged = merged.astype(jnp.bfloat16)
    if len(outs) == 1:
        outs[0][...] = merged
        return
    log = top + jnp.log(total)
    lane = lax.broadcasted_iota(jnp.int32, (a.shape[0], HD), 1)
    packed = jnp.zeros((a.shape[0], HD), jnp.float32)
    for h in range(heads):
        packed = jnp.where(lax.rem(lane, heads) == h, log[:, h * HD : (h + 1) * HD], packed)
    packed = summands(packed, heads)
    half = a.shape[0] // 2
    for i, out in enumerate(outs):
        out[:, :width] = merged[i * half : (i + 1) * half]
        out[:, width:] = packed[i * half : (i + 1) * half]


def merge(a, b, last, after):
    rows, width = a.shape
    heads = width // HD - 1
    if last:
        shapes = [jax.ShapeDtypeStruct((rows, heads * HD), jnp.bfloat16)]
    else:
        shapes = [jax.ShapeDtypeStruct((rows // 2, width), jnp.bfloat16)] * 2
    return pl.pallas_call(
        functools.partial(merge_kernel, heads),
        out_shape=shapes,
        in_specs=[VMEM] * 2 + [ANY],
        out_specs=[VMEM] * len(shapes),
        compiler_params=params(6),
        cost_estimate=BRIEF,
        name="merge",
    )(a, b, after)


def swap(x, n, mask):
    return lax.ppermute(x, "blk", [(i, i ^ mask) for i in range(n)])


def from_root(x, blk):
    return lax.psum(jnp.where(blk == 0, x, jnp.zeros_like(x)), "blk")


def body(ctx_query, ctx_key, ctx_value, opt_query, opt_owner, opt_slot, opt_length):
    n = lax.axis_size("blk")
    blk = lax.axis_index("blk")
    blk_arr = blk.astype(jnp.int32).reshape(1)
    options = opt_owner.shape[0]
    rounds = n.bit_length() - 1

    hold = lax.optimization_barrier
    row = lambda x: x.reshape(1, options)

    blk_arr, ctx_key = hold((blk_arr, ctx_key))
    kvs = parts(ctx_key, ctx_value)
    shards = [opt_query]
    masks = [0]
    for bit in reversed(range(1, rounds)):
        mine = shards[0] if len(shards) == 1 else jnp.concatenate(shards, axis=0)
        shards = [mine, swap(mine, n, 1 << bit)]
        masks = masks + [mask | 1 << bit for mask in masks]
    masks = masks + [mask | 1 for mask in masks]
    if n == 4:
        first = [lax.ppermute(kvs[0], "blk", [(0, 2)])]
    small = [row(opt_owner), row(opt_slot), row(opt_length), shards[0]]
    state, (ctx_query, *small, own) = first_attention(blk_arr, kvs[0], ctx_query, small)
    kvs, state, shards = hold((kvs, state, shards))
    mine = join([own, *shards[1:]])
    queries = [mine, swap(mine, n, 1)]
    states = [state]
    if n == 4:
        first += [lax.ppermute(x, "blk", [(0, 2)]) for x in kvs[1:]]
    states += [local_attention(blk_arr, kv, g, ctx_query) for g, kv in enumerate(kvs) if g]
    if n == 4:
        first[0], states = hold((first[0], states))
    keep, send = option_partials(blk_arr, *small, kvs, masks, queries, states[-1][1])
    if n == 4:
        near = [[lax.ppermute(first[0], "blk", [(2, 1)])]]
        kvs, keep = hold((kvs, keep))
        tops = [half_rows(x, 0) for x in kvs[1:]]
        near += [[lax.ppermute(x, "blk", [(0, 1)])] for x in tops]
        first[1:], keep, tops = hold((first[1:], keep, tops))
        for x, y in zip(near[1:], first[1:]):
            x.append(lax.ppermute(half_rows(y, 1), "blk", [(2, 1)]))
        anchors = [[x, [y], [lax.ppermute(y, "blk", [(2, 3)])]] for x, y in zip(near, first)]
        anchors[0], first = hold((anchors[0], first))
    else:
        anchors = [[[from_root(x, blk)]] for x in kvs]
    ctx_out, tokens = None, []
    for g, state in enumerate(states):
        ctx_out, token = anchor_attention(blk_arr, ctx_query, kvs[g], state, anchors[g], g, ctx_out)
        tokens.append(token)
    for bit in range(rounds):
        got = swap(send, n, 1 << bit)
        last = bit == rounds - 1
        outs = merge(keep, got, last, tokens[-1 if last else 0])
        if last:
            opt_out = outs[0]
        else:
            keep, send = outs
    return (ctx_out, opt_out)


def solution(mesh):
    spread = P(("groups", "blk"), "head")
    return jax.shard_map(
        body,
        mesh=mesh,
        in_specs=(spread, spread, spread, spread, P("groups"), P("groups"), P("groups")),
        out_specs=(spread, spread),
        check_vma=False,
    )
```

```python
import functools
import math

import jax
import jax.numpy as jnp
from jax import lax
from jax.experimental import pallas as pl
from jax.experimental.pallas import tpu as pltpu
from jax.sharding import PartitionSpec as P

HD = 128
HQ = 64
KVH = 8
CAP = 32
GROUP = HQ // KVH
SCALE = HD ** (-0.5)
C2 = SCALE * math.log2(math.e)
NEG = -1e30
TILE = 256
PAIR = 2
VMEM = pl.BlockSpec(memory_space=pltpu.VMEM)
SMEM = pl.BlockSpec(memory_space=pltpu.SMEM)
HBM = pl.BlockSpec(memory_space=pltpu.HBM)
ANY = pl.BlockSpec(memory_space=pl.ANY)


def cost(flops):
    return pl.CostEstimate(flops=flops, bytes_accessed=1, transcendentals=0)


BRIEF = cost(1)


def nt(a, b):
    return lax.dot_general(a, b, (((1,), (1,)), ((), ())), preferred_element_type=jnp.float32)


def nn(a, b):
    return jnp.dot(a, b, preferred_element_type=jnp.float32)


def params(mib):
    return pltpu.CompilerParams(vmem_limit_bytes=mib * 1024 * 1024)


def fold(op, items):
    return functools.reduce(op, items)


def start_all(copies, sem):
    started = [pltpu.make_async_copy(a, b, sem.at[i]) for i, (a, b) in enumerate(copies)]
    for copy in started:
        copy.start()
    return started


def in_hbm(x):
    return pltpu.with_memory_space_constraint(x, pltpu.HBM)


def beside(heads, k_ref, v_ref, kv):
    copies = []
    for g in range(heads):
        for ref, at in ((k_ref, 0), (v_ref, HD)):
            copies.append((ref.at[:, g * HD : (g + 1) * HD], kv[g].at[:, at : at + HD]))
    return copies


def parts_kernel(heads, k_ref, v_ref, *refs):
    kv, sem = refs[:heads], refs[heads]
    for copy in start_all(beside(heads, k_ref, v_ref, kv), sem):
        copy.wait()


def parts(key, value):
    rows, heads = key.shape[0], key.shape[1] // HD
    outs = pl.pallas_call(
        functools.partial(parts_kernel, heads),
        out_shape=[pltpu.VMEM((rows, 2 * HD), key.dtype)] * heads,
        in_specs=[HBM] * 2,
        out_specs=[VMEM] * heads,
        scratch_shapes=[pltpu.SemaphoreType.DMA((2 * heads,))],
        compiler_params=params(2),
        cost_estimate=BRIEF,
        name="parts",
    )(in_hbm(key), in_hbm(value))
    return list(outs)


def pipelined(tasks, scores, finish):
    ahead = scores(tasks[0])
    for i, task in enumerate(tasks):
        now = ahead
        if i + 1 < len(tasks):
            ahead = scores(tasks[i + 1])
        finish(task, now)


def head_columns(h):
    return slice(h * HD, (h + 1) * HD)


def local_pass(g, q_ref, kv_ref, ve, arrived, emit):
    rows = kv_ref.shape[0]
    ve[:, :HD] = kv_ref[:, HD:]
    ve[:, HD:] = jnp.ones((rows, HD), jnp.bfloat16)
    row = lax.broadcasted_iota(jnp.int32, (PAIR * TILE, TILE), 0)
    seen = lax.rem(row, TILE) >= lax.broadcasted_iota(jnp.int32, (PAIR * TILE, TILE), 1)

    def scores(task):
        first, at = task
        if at == 0:
            arrived(first)
        q = jnp.concatenate([q_ref[at : at + TILE, head_columns(g * GROUP + first + j)] for j in range(PAIR)], axis=0)
        parts = [nt(q, kv_ref[:at, :HD])] if at else []
        parts.append(jnp.where(seen, nt(q, kv_ref[at : at + TILE, :HD]), NEG))
        return parts

    def finish(task, parts):
        first, at = task
        top = fold(jnp.maximum, [jnp.max(s, axis=1, keepdims=True) for s in parts])
        total = None
        for s, start in zip(parts, [0, at] if at else [at]):
            p = jnp.exp2((s - top) * C2).astype(jnp.bfloat16)
            part = nn(p, ve[start : start + s.shape[1], :])
            total = part if total is None else total + part
        for j in range(PAIR):
            mine = slice(j * TILE, (j + 1) * TILE)
            emit(slice(at, at + TILE), first + j, total[mine, :HD], total[mine, HD:], top[mine] * C2)

    pipelined([(h, at) for h in range(0, GROUP, PAIR) for at in range(0, rows, TILE)], scores, finish)


def first_kernel(blk_ref, kv_ref, *refs):
    count = (len(refs) - 5) // 2
    sources, state, held, (ve, sem) = refs[:count], refs[count : count + 3], refs[count + 3 : -2], refs[-2:]
    q_ref = held[0]
    spots = [slice(h * HD, (h + PAIR) * HD) for h in range(0, q_ref.shape[1] // HD, PAIR)]
    copies = [(sources[0].at[:, x], q_ref.at[:, x]) for x in spots] + list(zip(sources[1:], held[1:]))
    copies = start_all(copies, sem)
    ahead = GROUP // PAIR

    @pl.when(blk_ref[0] > 0)
    def _():
        local_pass(0, q_ref, kv_ref, ve, lambda h: copies[h // PAIR].wait(), keep_in(state))

    @pl.when(blk_ref[0] == 0)
    def _():
        for copy in copies[:ahead]:
            copy.wait()

    for copy in copies[ahead:]:
        copy.wait()


def first_attention(blk, kv, query, others):
    rows = kv.shape[0]
    sources = [query, *others]
    outs = pl.pallas_call(
        first_kernel,
        out_shape=[pltpu.VMEM((rows, GROUP * HD), jnp.float32)] * 3 + [pltpu.VMEM(x.shape, x.dtype) for x in sources],
        in_specs=[SMEM, VMEM] + [HBM] * len(sources),
        out_specs=[VMEM] * (3 + len(sources)),
        scratch_shapes=[
            pltpu.VMEM((rows, 2 * HD), jnp.bfloat16),
            pltpu.SemaphoreType.DMA((query.shape[1] // HD // PAIR + len(others),)),
        ],
        compiler_params=params(6),
        cost_estimate=cost(2 * 10**9),
        name="local_attention",
    )(blk, kv, *[in_hbm(x) for x in sources])
    return list(outs[:3]), list(outs[3:])


def keep_in(state):
    acc_ref, top_ref, sum_ref = state

    def emit(rows, h, total, z, top):
        here = (rows, head_columns(h))
        acc_ref[here], sum_ref[here], top_ref[here] = total, z, jnp.broadcast_to(top, total.shape)

    return emit


def local_kernel(g, blk_ref, kv_ref, q_ref, *refs):
    @pl.when(blk_ref[0] > 0)
    def _():
        local_pass(g, q_ref, kv_ref, refs[3], lambda h: None, keep_in(refs[:3]))


def local_attention(blk, kv, g, query):
    rows = kv.shape[0]
    return list(
        pl.pallas_call(
            functools.partial(local_kernel, g),
            out_shape=[pltpu.VMEM((rows, GROUP * HD), jnp.float32)] * 3,
            in_specs=[SMEM, VMEM, VMEM],
            out_specs=[VMEM] * 3,
            scratch_shapes=[pltpu.VMEM((rows, 2 * HD), jnp.bfloat16)],
            compiler_params=params(6),
            cost_estimate=cost(10**9),
            name="local_attention",
        )(blk, kv, query)
    )


def anchor_kernel(g, count, prior, blk_ref, q_ref, kv_ref, acc_ref, top_ref, sum_ref, *refs):
    cand, (o_ref, token, ka, vae, out, sem) = refs[:count], refs[count + prior :]
    rows = q_ref.shape[0]
    blk = blk_ref[0]
    token[...] = jnp.zeros(token.shape, jnp.float32)

    def leave(h):
        return pltpu.make_async_copy(out.at[h], o_ref.at[:, head_columns(g * GROUP + h)], sem.at[h])

    def take(ref):
        ka[...] = ref[:, :HD]
        vae[:, :HD] = ref[:, HD:]

    def scores(h):
        return nt(q_ref[:, head_columns(g * GROUP + h)], ka[...])

    def finish(h, s):
        held = (slice(None), head_columns(h))
        before = top_ref[held]
        top = jnp.maximum(jnp.max(s, axis=1, keepdims=True) * C2, before)
        p = [jnp.exp2(s[:, at : at + HD] * C2 - top).astype(jnp.bfloat16) for at in range(0, rows, HD)]
        total = nn(jnp.concatenate(p, axis=1), vae[...])
        w = jnp.exp2(before - top)
        o = (total[:, :HD] + w * acc_ref[held]) * inverse(total[:, HD:] + w * sum_ref[held])
        out[h] = o.astype(jnp.bfloat16)
        leave(h).start()

    @pl.when(blk > 0)
    def _():
        if count == 1:
            take(cand[0])
        else:
            for i, ref in enumerate(cand):
                pl.when(blk == i + 1)(functools.partial(take, ref))
        vae[:, HD:] = jnp.ones((rows, HD), jnp.bfloat16)
        pipelined(list(range(GROUP)), scores, finish)

    def emit(here, h, total, z, top):
        out[h, here, :] = (total * inverse(z)).astype(jnp.bfloat16)
        if here.stop == rows:
            leave(h).start()

    @pl.when(blk == 0)
    def _():
        local_pass(g, q_ref, kv_ref, vae, lambda first: None, emit)

    for h in range(GROUP):
        leave(h).wait()


def inverse(x):
    guess = pl.reciprocal(x, approx=True)
    return guess * (2.0 - x * guess)


def anchor_attention(blk, query, kv, state, cands, g, prior):
    rows = query.shape[0]
    args = [blk, query, kv, *state, *cands]
    specs = [SMEM] + [VMEM] * (5 + len(cands))
    alias = {}
    if prior is not None:
        alias = {len(args): 0}
        args.append(prior)
        specs.append(ANY)
    return pl.pallas_call(
        functools.partial(anchor_kernel, g, len(cands), len(alias)),
        out_shape=[jax.ShapeDtypeStruct(query.shape, query.dtype), jax.ShapeDtypeStruct((8, HD), jnp.float32)],
        in_specs=specs,
        out_specs=[ANY, VMEM],
        scratch_shapes=[
            pltpu.VMEM((rows, HD), jnp.bfloat16),
            pltpu.VMEM((rows, 2 * HD), jnp.bfloat16),
            pltpu.VMEM((GROUP, rows, HD), jnp.bfloat16),
            pltpu.SemaphoreType.DMA((GROUP,)),
        ],
        input_output_aliases=alias,
        compiler_params=params(6),
        cost_estimate=cost(1000000000),
        name="anchor_attention",
    )(*args)


def fold_order(n):
    bits = n.bit_length() - 1
    return sorted(range(n), key=lambda x: int(format(x, "0%db" % bits)[::-1], 2))


def join_kernel(*refs):
    at = 0
    for ref in refs[:-1]:
        refs[-1][at : at + ref.shape[0], :] = ref[...]
        at += ref.shape[0]


def join(arrays):
    height, width = sum(x.shape[0] for x in arrays), arrays[0].shape[1]
    return pl.pallas_call(
        join_kernel,
        out_shape=pltpu.VMEM((height, width), arrays[0].dtype),
        in_specs=[VMEM] * len(arrays),
        out_specs=VMEM,
        compiler_params=params(2),
        cost_estimate=BRIEF,
        name="join",
    )(*arrays)


def option_kernel(masks, heads, blk_ref, owner_ref, slot_ref, length_ref, *refs):
    n = len(masks)
    kv_heads = heads // GROUP
    count = len(refs) - kv_heads - 5
    kv, queries = refs[:kv_heads], refs[kv_heads : kv_heads + count]
    keep, send, q_all, part = refs[kv_heads + count + 1 :]
    blk = blk_ref[0]
    rows = kv[0].shape[0]
    half = queries[0].shape[0]
    options, each = 2 * half, 2 * half // n

    def place(ref, masks, flip):
        for i, mask in enumerate(masks):
            at = jnp.bitwise_xor(blk, jnp.bitwise_xor(mask, flip)) * each
            q_all[pl.ds(pl.multiple_of(at, each), each), :] = ref[i * each : (i + 1) * each, :]

    place(queries[0], masks[: n // 2], 0)
    if count == 2:
        place(queries[1], masks[n // 2 :], 0)
    else:
        pl.when(blk < 3)(lambda: place(queries[1], masks[n // 2 :], jnp.where(blk == 1, 2, 0)))
        pl.when(blk == 3)(lambda: place(queries[2], masks[n // 2 :], 0))
    eye = lax.broadcasted_iota(jnp.int32, (options, options), 0) == lax.broadcasted_iota(jnp.int32, (options, options), 1)
    length = jnp.sum(jnp.where(eye, length_ref[...].astype(jnp.float32), 0.0), axis=1, keepdims=True)
    seen = length - (blk * rows).astype(jnp.float32)
    lane = lax.broadcasted_iota(jnp.int32, (options, HD), 1)
    logs = jnp.zeros((options, HD), jnp.float32)
    stack = max(1, min(GROUP, 512 // options))
    spots = lax.broadcasted_iota(jnp.int32, (options * stack, rows), 1).astype(jnp.float32)
    seen_all = jnp.concatenate([seen] * stack, axis=0)
    for first in range(0, heads, stack):
        g = first // GROUP
        q = jnp.concatenate([q_all[:, h * HD : (h + 1) * HD] for h in range(first, first + stack)], axis=0)
        s = nt(q, kv[g][:, :HD])
        s = jnp.where(spots < seen_all, s, NEG)
        top = jnp.max(s, axis=1, keepdims=True)
        e = jnp.exp2((s - top) * C2)
        z = jnp.sum(e, axis=1, keepdims=True)
        o = nn(e.astype(jnp.bfloat16), kv[g][:, HD:]) / z
        live = seen_all > 0
        o = jnp.where(live, o, 0.0).astype(jnp.bfloat16)
        log = jnp.where(live, top * SCALE + jnp.log(z), NEG)
        for j in range(stack):
            h = first + j
            part[:, h * HD : (h + 1) * HD] = o[j * options : (j + 1) * options]
            logs = jnp.where(lax.rem(lane, heads) == h, log[j * options : (j + 1) * options], logs)
    part[:, heads * HD :] = summands(logs, heads)
    slot = lax.broadcasted_iota(jnp.int32, (CAP, options), 0)
    order = fold_order(n)
    for half, out in ((order[: n // 2], keep), (order[n // 2 :], send)):
        for i, mask in enumerate(half):
            pick = (owner_ref[...] == jnp.bitwise_xor(blk, mask)) & (slot_ref[...] == slot)
            pick = jnp.where(pick, 1.0, 0.0).astype(jnp.bfloat16)
            out[i * CAP : (i + 1) * CAP, :] = nn(pick, part[...]).astype(jnp.bfloat16)


def summands(logs, heads):
    lane = lax.broadcasted_iota(jnp.int32, logs.shape, 1)
    high = logs.astype(jnp.bfloat16).astype(jnp.float32)
    rest = logs - high
    mid = rest.astype(jnp.bfloat16).astype(jnp.float32)
    low = rest - mid
    low = jnp.where(lane < 3 * heads, low, 0.0)
    return jnp.where(lane < heads, high, jnp.where(lane < 2 * heads, mid, low)).astype(jnp.bfloat16)


def option_partials(blk, owner, slot, length, kvs, masks, queries, after):
    n, heads = len(masks), queries[0].shape[1] // HD
    options = 2 * queries[0].shape[0]
    width = (heads + 1) * HD
    rows = kvs[0].shape[0]
    return pl.pallas_call(
        functools.partial(option_kernel, masks, heads),
        out_shape=[jax.ShapeDtypeStruct((n // 2 * CAP, width), jnp.bfloat16)] * 2,
        in_specs=[SMEM] + [VMEM] * (3 + len(kvs) + len(queries)) + [ANY],
        out_specs=[VMEM] * 2,
        scratch_shapes=[
            pltpu.VMEM((options, heads * HD), jnp.bfloat16),
            pltpu.VMEM((options, width), jnp.bfloat16),
        ],
        compiler_params=params(4 + options // 32),
        cost_estimate=cost(1000000000),
        name="option_partials",
    )(blk, owner, slot, length, *kvs, *queries, after)


def merge_kernel(heads, a, b, after, *outs):
    width = heads * HD
    lane = lax.broadcasted_iota(jnp.int32, (HD, width), 0)
    head = lax.broadcasted_iota(jnp.int32, (HD, width), 1) // HD
    pick = jnp.where((lax.rem(lane, heads) == head) & (lane < 3 * heads), 1.0, 0.0).astype(jnp.bfloat16)
    logs = [nn(x[:, width:], pick) for x in (a, b)]
    top = jnp.maximum(*logs)
    weights = [jnp.exp(log - top) for log in logs]
    total = weights[0] + weights[1]
    merged = (weights[0] * a[:, :width].astype(jnp.float32) + weights[1] * b[:, :width].astype(jnp.float32)) / total
    merged = merged.astype(jnp.bfloat16)
    if len(outs) == 1:
        outs[0][...] = merged
        return
    log = top + jnp.log(total)
    lane = lax.broadcasted_iota(jnp.int32, (a.shape[0], HD), 1)
    packed = jnp.zeros((a.shape[0], HD), jnp.float32)
    for h in range(heads):
        packed = jnp.where(lax.rem(lane, heads) == h, log[:, h * HD : (h + 1) * HD], packed)
    packed = summands(packed, heads)
    half = a.shape[0] // 2
    for i, out in enumerate(outs):
        out[:, :width] = merged[i * half : (i + 1) * half]
        out[:, width:] = packed[i * half : (i + 1) * half]


def merge(a, b, last, after):
    rows, width = a.shape
    heads = width // HD - 1
    if last:
        shapes = [jax.ShapeDtypeStruct((rows, heads * HD), jnp.bfloat16)]
    else:
        shapes = [jax.ShapeDtypeStruct((rows // 2, width), jnp.bfloat16)] * 2
    return pl.pallas_call(
        functools.partial(merge_kernel, heads),
        out_shape=shapes,
        in_specs=[VMEM] * 2 + [ANY],
        out_specs=[VMEM] * len(shapes),
        compiler_params=params(6),
        cost_estimate=BRIEF,
        name="merge",
    )(a, b, after)


def swap(x, n, mask):
    return lax.ppermute(x, "blk", [(i, i ^ mask) for i in range(n)])


def from_root(x, blk):
    return lax.psum(jnp.where(blk == 0, x, jnp.zeros_like(x)), "blk")


def body(ctx_query, ctx_key, ctx_value, opt_query, opt_owner, opt_slot, opt_length):
    n = lax.axis_size("blk")
    blk = lax.axis_index("blk")
    blk_arr = blk.astype(jnp.int32).reshape(1)
    options = opt_owner.shape[0]
    rounds = n.bit_length() - 1

    hold = lax.optimization_barrier
    row = lambda x: x.reshape(1, options)

    blk_arr, ctx_key = hold((blk_arr, ctx_key))
    kvs = parts(ctx_key, ctx_value)
    shards = [opt_query]
    masks = [0]
    for bit in reversed(range(1, rounds)):
        mine = shards[0] if len(shards) == 1 else jnp.concatenate(shards, axis=0)
        shards = [mine, swap(mine, n, 1 << bit)]
        masks = masks + [mask | 1 << bit for mask in masks]
    masks = masks + [mask | 1 for mask in masks]
    if n == 4:
        first = [lax.ppermute(kvs[0], "blk", [(0, 2)])]
    small = [row(opt_owner), row(opt_slot), row(opt_length), shards[0]]
    state, (ctx_query, *small, own) = first_attention(blk_arr, kvs[0], ctx_query, small)
    kvs, state, shards = hold((kvs, state, shards))
    mine = join([own, *shards[1:]])
    queries = [mine]
    if n == 4:
        queries += [lax.ppermute(mine, "blk", pairs) for pairs in ([(2, 1), (1, 0), (3, 2)], [(2, 3)])]
    else:
        queries.append(swap(mine, n, 1))
    states = [state]
    if n == 4:
        first += [lax.ppermute(x, "blk", [(0, 2)]) for x in kvs[1:]]
    states += [local_attention(blk_arr, kv, g, ctx_query) for g, kv in enumerate(kvs) if g]
    if n == 4:
        first[0], states = hold((first[0], states))
    keep, send = option_partials(blk_arr, *small, kvs, masks, queries, states[-1][1])
    if n == 4:
        near = [lax.ppermute(first[0], "blk", [(2, 1)])]
        kvs, keep = hold((kvs, keep))
        near += [lax.ppermute(x, "blk", [(0, 1)]) for x in kvs[1:]]
        first[1:], keep = hold((first[1:], keep))
        anchors = [[x, y, lax.ppermute(y, "blk", [(2, 3)])] for x, y in zip(near, first)]
        anchors[0], first = hold((anchors[0], first))
    else:
        anchors = [[from_root(x, blk)] for x in kvs]
    ctx_out, tokens = None, []
    for g, state in enumerate(states):
        ctx_out, token = anchor_attention(blk_arr, ctx_query, kvs[g], state, anchors[g], g, ctx_out)
        tokens.append(token)
    for bit in range(rounds):
        got = swap(send, n, 1 << bit)
        last = bit == rounds - 1
        outs = merge(keep, got, last, tokens[-1 if last else 0])
        if last:
            opt_out = outs[0]
        else:
            keep, send = outs
    return (ctx_out, opt_out)


def solution(mesh):
    spread = P(("groups", "blk"), "head")
    return jax.shard_map(
        body,
        mesh=mesh,
        in_specs=(spread, spread, spread, spread, P("groups"), P("groups"), P("groups")),
        out_specs=(spread, spread),
        check_vma=False,
    )
```

```python
import functools
import math

import jax
import jax.numpy as jnp
from jax import lax
from jax.experimental import pallas as pl
from jax.experimental.pallas import tpu as pltpu
from jax.sharding import PartitionSpec as P

HD = 128
HQ = 64
KVH = 8
CAP = 32
GROUP = HQ // KVH
SCALE = HD ** (-0.5)
C2 = SCALE * math.log2(math.e)
NEG = -1e30
TILE = 256
PAIR = 2
VMEM = pl.BlockSpec(memory_space=pltpu.VMEM)
SMEM = pl.BlockSpec(memory_space=pltpu.SMEM)
HBM = pl.BlockSpec(memory_space=pltpu.HBM)
ANY = pl.BlockSpec(memory_space=pl.ANY)


def cost(flops):
    return pl.CostEstimate(flops=flops, bytes_accessed=1, transcendentals=0)


BRIEF = cost(1)


def nt(a, b):
    return lax.dot_general(a, b, (((1,), (1,)), ((), ())), preferred_element_type=jnp.float32)


def nn(a, b):
    return jnp.dot(a, b, preferred_element_type=jnp.float32)


def params(mib):
    return pltpu.CompilerParams(vmem_limit_bytes=mib * 1024 * 1024)


def fold(op, items):
    return functools.reduce(op, items)


def start_all(copies, sem):
    started = [pltpu.make_async_copy(a, b, sem.at[i]) for i, (a, b) in enumerate(copies)]
    for copy in started:
        copy.start()
    return started


def in_hbm(x):
    return pltpu.with_memory_space_constraint(x, pltpu.HBM)


def beside(heads, k_ref, v_ref, kv):
    copies = []
    for g in range(heads):
        for ref, at in ((k_ref, 0), (v_ref, HD)):
            copies.append((ref.at[:, g * HD : (g + 1) * HD], kv[g].at[:, at : at + HD]))
    return copies


def parts_kernel(heads, k_ref, v_ref, *refs):
    kv, sem = refs[:heads], refs[heads]
    for copy in start_all(beside(heads, k_ref, v_ref, kv), sem):
        copy.wait()


def parts(key, value):
    rows, heads = key.shape[0], key.shape[1] // HD
    outs = pl.pallas_call(
        functools.partial(parts_kernel, heads),
        out_shape=[pltpu.VMEM((rows, 2 * HD), key.dtype)] * heads,
        in_specs=[HBM] * 2,
        out_specs=[VMEM] * heads,
        scratch_shapes=[pltpu.SemaphoreType.DMA((2 * heads,))],
        compiler_params=params(2),
        cost_estimate=BRIEF,
        name="parts",
    )(in_hbm(key), in_hbm(value))
    return list(outs)


def pipelined(tasks, scores, finish):
    ahead = scores(tasks[0])
    for i, task in enumerate(tasks):
        now = ahead
        if i + 1 < len(tasks):
            ahead = scores(tasks[i + 1])
        finish(task, now)


def head_columns(h):
    return slice(h * HD, (h + 1) * HD)


def local_pass(g, q_ref, kv_ref, ve, arrived, emit):
    rows = kv_ref.shape[0]
    ve[:, :HD] = kv_ref[:, HD:]
    ve[:, HD:] = jnp.ones((rows, HD), jnp.bfloat16)
    row = lax.broadcasted_iota(jnp.int32, (PAIR * TILE, TILE), 0)
    seen = lax.rem(row, TILE) >= lax.broadcasted_iota(jnp.int32, (PAIR * TILE, TILE), 1)

    def scores(task):
        first, at = task
        if at == 0:
            arrived(first)
        q = jnp.concatenate([q_ref[at : at + TILE, head_columns(g * GROUP + first + j)] for j in range(PAIR)], axis=0)
        parts = [nt(q, kv_ref[:at, :HD])] if at else []
        parts.append(jnp.where(seen, nt(q, kv_ref[at : at + TILE, :HD]), NEG))
        return parts

    def finish(task, parts):
        first, at = task
        top = fold(jnp.maximum, [jnp.max(s, axis=1, keepdims=True) for s in parts])
        total = None
        for s, start in zip(parts, [0, at] if at else [at]):
            p = jnp.exp2((s - top) * C2).astype(jnp.bfloat16)
            part = nn(p, ve[start : start + s.shape[1], :])
            total = part if total is None else total + part
        for j in range(PAIR):
            mine = slice(j * TILE, (j + 1) * TILE)
            emit(slice(at, at + TILE), first + j, total[mine, :HD], total[mine, HD:], top[mine] * C2)

    pipelined([(h, at) for h in range(0, GROUP, PAIR) for at in range(0, rows, TILE)], scores, finish)


def first_kernel(blk_ref, kv_ref, *refs):
    count = (len(refs) - 5) // 2
    sources, state, held, (ve, sem) = refs[:count], refs[count : count + 3], refs[count + 3 : -2], refs[-2:]
    q_ref = held[0]
    spots = [slice(h * HD, (h + PAIR) * HD) for h in range(0, q_ref.shape[1] // HD, PAIR)]
    copies = [(sources[0].at[:, x], q_ref.at[:, x]) for x in spots] + list(zip(sources[1:], held[1:]))
    copies = start_all(copies, sem)
    ahead = GROUP // PAIR

    @pl.when(blk_ref[0] > 0)
    def _():
        local_pass(0, q_ref, kv_ref, ve, lambda h: copies[h // PAIR].wait(), keep_in(state))

    @pl.when(blk_ref[0] == 0)
    def _():
        for copy in copies[:ahead]:
            copy.wait()

    for copy in copies[ahead:]:
        copy.wait()


def first_attention(blk, kv, query, others):
    rows = kv.shape[0]
    sources = [query, *others]
    outs = pl.pallas_call(
        first_kernel,
        out_shape=[pltpu.VMEM((rows, GROUP * HD), jnp.float32)] * 3 + [pltpu.VMEM(x.shape, x.dtype) for x in sources],
        in_specs=[SMEM, VMEM] + [HBM] * len(sources),
        out_specs=[VMEM] * (3 + len(sources)),
        scratch_shapes=[
            pltpu.VMEM((rows, 2 * HD), jnp.bfloat16),
            pltpu.SemaphoreType.DMA((query.shape[1] // HD // PAIR + len(others),)),
        ],
        compiler_params=params(6),
        cost_estimate=cost(2 * 10**9),
        name="local_attention",
    )(blk, kv, *[in_hbm(x) for x in sources])
    return list(outs[:3]), list(outs[3:])


def keep_in(state):
    acc_ref, top_ref, sum_ref = state

    def emit(rows, h, total, z, top):
        here = (rows, head_columns(h))
        acc_ref[here], sum_ref[here], top_ref[here] = total, z, jnp.broadcast_to(top, total.shape)

    return emit


def local_kernel(g, blk_ref, kv_ref, q_ref, *refs):
    @pl.when(blk_ref[0] > 0)
    def _():
        local_pass(g, q_ref, kv_ref, refs[3], lambda h: None, keep_in(refs[:3]))


def local_attention(blk, kv, g, query):
    rows = kv.shape[0]
    return list(
        pl.pallas_call(
            functools.partial(local_kernel, g),
            out_shape=[pltpu.VMEM((rows, GROUP * HD), jnp.float32)] * 3,
            in_specs=[SMEM, VMEM, VMEM],
            out_specs=[VMEM] * 3,
            scratch_shapes=[pltpu.VMEM((rows, 2 * HD), jnp.bfloat16)],
            compiler_params=params(6),
            cost_estimate=cost(1000000000),
            name="local_attention",
        )(blk, kv, query)
    )


def anchor_kernel(g, count, prior, blk_ref, q_ref, kv_ref, acc_ref, top_ref, sum_ref, *refs):
    cand, (o_ref, token, ka, vae, out, sem) = refs[:count], refs[count + prior :]
    rows = q_ref.shape[0]
    blk = blk_ref[0]
    token[...] = jnp.zeros(token.shape, jnp.float32)

    def leave(h):
        return pltpu.make_async_copy(out.at[h], o_ref.at[:, head_columns(g * GROUP + h)], sem.at[h])

    def take(ref):
        ka[...] = ref[:, :HD]
        vae[:, :HD] = ref[:, HD:]

    def scores(h):
        return nt(q_ref[:, head_columns(g * GROUP + h)], ka[...])

    def finish(h, s):
        held = (slice(None), head_columns(h))
        before = top_ref[held]
        top = jnp.maximum(jnp.max(s, axis=1, keepdims=True) * C2, before)
        p = [jnp.exp2(s[:, at : at + HD] * C2 - top).astype(jnp.bfloat16) for at in range(0, rows, HD)]
        total = nn(jnp.concatenate(p, axis=1), vae[...])
        w = jnp.exp2(before - top)
        o = (total[:, :HD] + w * acc_ref[held]) * inverse(total[:, HD:] + w * sum_ref[held])
        out[h] = o.astype(jnp.bfloat16)
        leave(h).start()

    @pl.when(blk > 0)
    def _():
        if count == 1:
            take(cand[0])
        else:
            for i, ref in enumerate(cand):
                pl.when(blk == i + 1)(functools.partial(take, ref))
        vae[:, HD:] = jnp.ones((rows, HD), jnp.bfloat16)
        pipelined(list(range(GROUP)), scores, finish)

    def emit(here, h, total, z, top):
        out[h, here, :] = (total * inverse(z)).astype(jnp.bfloat16)
        if here.stop == rows:
            leave(h).start()

    @pl.when(blk == 0)
    def _():
        local_pass(g, q_ref, kv_ref, vae, lambda first: None, emit)

    for h in range(GROUP):
        leave(h).wait()


def inverse(x):
    guess = pl.reciprocal(x, approx=True)
    return guess * (2.0 - x * guess)


def anchor_attention(blk, query, kv, state, cands, g, prior):
    rows = query.shape[0]
    args = [blk, query, kv, *state, *cands]
    specs = [SMEM] + [VMEM] * (5 + len(cands))
    alias = {}
    if prior is not None:
        alias = {len(args): 0}
        args.append(prior)
        specs.append(ANY)
    return pl.pallas_call(
        functools.partial(anchor_kernel, g, len(cands), len(alias)),
        out_shape=[jax.ShapeDtypeStruct(query.shape, query.dtype), jax.ShapeDtypeStruct((8, HD), jnp.float32)],
        in_specs=specs,
        out_specs=[ANY, VMEM],
        scratch_shapes=[
            pltpu.VMEM((rows, HD), jnp.bfloat16),
            pltpu.VMEM((rows, 2 * HD), jnp.bfloat16),
            pltpu.VMEM((GROUP, rows, HD), jnp.bfloat16),
            pltpu.SemaphoreType.DMA((GROUP,)),
        ],
        input_output_aliases=alias,
        compiler_params=params(6),
        cost_estimate=cost(1000000000),
        name="anchor_attention",
    )(*args)


def fold_order(n):
    bits = n.bit_length() - 1
    return sorted(range(n), key=lambda x: int(format(x, "0%db" % bits)[::-1], 2))


def join_kernel(*refs):
    at = 0
    for ref in refs[:-1]:
        refs[-1][at : at + ref.shape[0], :] = ref[...]
        at += ref.shape[0]


def join(arrays):
    height, width = sum(x.shape[0] for x in arrays), arrays[0].shape[1]
    return pl.pallas_call(
        join_kernel,
        out_shape=pltpu.VMEM((height, width), arrays[0].dtype),
        in_specs=[VMEM] * len(arrays),
        out_specs=VMEM,
        compiler_params=params(2),
        cost_estimate=BRIEF,
        name="join",
    )(*arrays)


def option_kernel(masks, heads, blk_ref, owner_ref, slot_ref, length_ref, *refs):
    n = len(masks)
    kv_heads = heads // GROUP
    count = len(refs) - kv_heads - 5
    kv, queries = refs[:kv_heads], refs[kv_heads : kv_heads + count]
    keep, send, q_all, part = refs[kv_heads + count + 1 :]
    blk = blk_ref[0]
    rows = kv[0].shape[0]
    half = queries[0].shape[0]
    options, each = 2 * half, 2 * half // n

    def place(ref, masks, flip):
        for i, mask in enumerate(masks):
            at = jnp.bitwise_xor(blk, jnp.bitwise_xor(mask, flip)) * each
            q_all[pl.ds(pl.multiple_of(at, each), each), :] = ref[i * each : (i + 1) * each, :]

    place(queries[0], masks[: n // 2], 0)
    if count == 2:
        place(queries[1], masks[n // 2 :], 0)
    else:
        pl.when(blk < 3)(lambda: place(queries[1], masks[n // 2 :], jnp.where(blk == 1, 2, 0)))
        pl.when(blk == 3)(lambda: place(queries[2], masks[n // 2 :], 0))
    eye = lax.broadcasted_iota(jnp.int32, (options, options), 0) == lax.broadcasted_iota(jnp.int32, (options, options), 1)
    length = jnp.sum(jnp.where(eye, length_ref[...].astype(jnp.float32), 0.0), axis=1, keepdims=True)
    seen = length - (blk * rows).astype(jnp.float32)
    lane = lax.broadcasted_iota(jnp.int32, (options, HD), 1)
    logs = jnp.zeros((options, HD), jnp.float32)
    stack = max(1, min(GROUP, 512 // options))
    spots = lax.broadcasted_iota(jnp.int32, (options * stack, rows), 1).astype(jnp.float32)
    seen_all = jnp.concatenate([seen] * stack, axis=0)
    for first in range(0, heads, stack):
        g = first // GROUP
        q = jnp.concatenate([q_all[:, h * HD : (h + 1) * HD] for h in range(first, first + stack)], axis=0)
        s = nt(q, kv[g][:, :HD])
        s = jnp.where(spots < seen_all, s, NEG)
        top = jnp.max(s, axis=1, keepdims=True)
        e = jnp.exp2((s - top) * C2)
        z = jnp.sum(e, axis=1, keepdims=True)
        o = nn(e.astype(jnp.bfloat16), kv[g][:, HD:]) / z
        live = seen_all > 0
        o = jnp.where(live, o, 0.0).astype(jnp.bfloat16)
        log = jnp.where(live, top * SCALE + jnp.log(z), NEG)
        for j in range(stack):
            h = first + j
            part[:, h * HD : (h + 1) * HD] = o[j * options : (j + 1) * options]
            logs = jnp.where(lax.rem(lane, heads) == h, log[j * options : (j + 1) * options], logs)
    part[:, heads * HD :] = summands(logs, heads)
    slot = lax.broadcasted_iota(jnp.int32, (CAP, options), 0)
    order = fold_order(n)
    for half, out in ((order[: n // 2], keep), (order[n // 2 :], send)):
        for i, mask in enumerate(half):
            pick = (owner_ref[...] == jnp.bitwise_xor(blk, mask)) & (slot_ref[...] == slot)
            pick = jnp.where(pick, 1.0, 0.0).astype(jnp.bfloat16)
            out[i * CAP : (i + 1) * CAP, :] = nn(pick, part[...]).astype(jnp.bfloat16)


def summands(logs, heads):
    lane = lax.broadcasted_iota(jnp.int32, logs.shape, 1)
    high = logs.astype(jnp.bfloat16).astype(jnp.float32)
    rest = logs - high
    mid = rest.astype(jnp.bfloat16).astype(jnp.float32)
    low = rest - mid
    low = jnp.where(lane < 3 * heads, low, 0.0)
    return jnp.where(lane < heads, high, jnp.where(lane < 2 * heads, mid, low)).astype(jnp.bfloat16)


def option_partials(blk, owner, slot, length, kvs, masks, queries, after):
    n, heads = len(masks), queries[0].shape[1] // HD
    options = 2 * queries[0].shape[0]
    width = (heads + 1) * HD
    rows = kvs[0].shape[0]
    return pl.pallas_call(
        functools.partial(option_kernel, masks, heads),
        out_shape=[jax.ShapeDtypeStruct((n // 2 * CAP, width), jnp.bfloat16)] * 2,
        in_specs=[SMEM] + [VMEM] * (3 + len(kvs) + len(queries)) + [ANY],
        out_specs=[VMEM] * 2,
        scratch_shapes=[
            pltpu.VMEM((options, heads * HD), jnp.bfloat16),
            pltpu.VMEM((options, width), jnp.bfloat16),
        ],
        compiler_params=params(4 + options // 32),
        cost_estimate=cost(1),
        name="option_partials",
    )(blk, owner, slot, length, *kvs, *queries, after)


def merge_kernel(heads, a, b, after, *outs):
    width = heads * HD
    lane = lax.broadcasted_iota(jnp.int32, (HD, width), 0)
    head = lax.broadcasted_iota(jnp.int32, (HD, width), 1) // HD
    pick = jnp.where((lax.rem(lane, heads) == head) & (lane < 3 * heads), 1.0, 0.0).astype(jnp.bfloat16)
    logs = [nn(x[:, width:], pick) for x in (a, b)]
    top = jnp.maximum(*logs)
    weights = [jnp.exp(log - top) for log in logs]
    total = weights[0] + weights[1]
    merged = (weights[0] * a[:, :width].astype(jnp.float32) + weights[1] * b[:, :width].astype(jnp.float32)) / total
    merged = merged.astype(jnp.bfloat16)
    if len(outs) == 1:
        outs[0][...] = merged
        return
    log = top + jnp.log(total)
    lane = lax.broadcasted_iota(jnp.int32, (a.shape[0], HD), 1)
    packed = jnp.zeros((a.shape[0], HD), jnp.float32)
    for h in range(heads):
        packed = jnp.where(lax.rem(lane, heads) == h, log[:, h * HD : (h + 1) * HD], packed)
    packed = summands(packed, heads)
    half = a.shape[0] // 2
    for i, out in enumerate(outs):
        out[:, :width] = merged[i * half : (i + 1) * half]
        out[:, width:] = packed[i * half : (i + 1) * half]


def merge(a, b, last, after):
    rows, width = a.shape
    heads = width // HD - 1
    if last:
        shapes = [jax.ShapeDtypeStruct((rows, heads * HD), jnp.bfloat16)]
    else:
        shapes = [jax.ShapeDtypeStruct((rows // 2, width), jnp.bfloat16)] * 2
    return pl.pallas_call(
        functools.partial(merge_kernel, heads),
        out_shape=shapes,
        in_specs=[VMEM] * 2 + [ANY],
        out_specs=[VMEM] * len(shapes),
        compiler_params=params(6),
        cost_estimate=BRIEF,
        name="merge",
    )(a, b, after)


def swap(x, n, mask):
    return lax.ppermute(x, "blk", [(i, i ^ mask) for i in range(n)])


def from_root(x, blk):
    return lax.psum(jnp.where(blk == 0, x, jnp.zeros_like(x)), "blk")


def body(ctx_query, ctx_key, ctx_value, opt_query, opt_owner, opt_slot, opt_length):
    n = lax.axis_size("blk")
    blk = lax.axis_index("blk")
    blk_arr = blk.astype(jnp.int32).reshape(1)
    options = opt_owner.shape[0]
    rounds = n.bit_length() - 1

    hold = lax.optimization_barrier
    row = lambda x: x.reshape(1, options)

    blk_arr, ctx_key = hold((blk_arr, ctx_key))
    kvs = parts(ctx_key, ctx_value)
    shards = [opt_query]
    masks = [0]
    for bit in reversed(range(1, rounds)):
        mine = shards[0] if len(shards) == 1 else jnp.concatenate(shards, axis=0)
        shards = [mine, swap(mine, n, 1 << bit)]
        masks = masks + [mask | 1 << bit for mask in masks]
    masks = masks + [mask | 1 for mask in masks]
    if n == 4:
        first = [lax.ppermute(kvs[0], "blk", [(0, 2)])]
    small = [row(opt_owner), row(opt_slot), row(opt_length), shards[0]]
    state, (ctx_query, *small, own) = first_attention(blk_arr, kvs[0], ctx_query, small)
    kvs, state, shards = hold((kvs, state, shards))
    mine = join([own, *shards[1:]])
    states = [state]
    if n == 4:
        first += [lax.ppermute(x, "blk", [(0, 2)]) for x in kvs[1:]]
    states += [local_attention(blk_arr, kv, g, ctx_query) for g, kv in enumerate(kvs) if g]
    mine, states = hold((mine, states))
    queries = [mine]
    if n == 4:
        queries += [lax.ppermute(mine, "blk", pairs) for pairs in ([(2, 1), (1, 0), (3, 2)], [(2, 3)])]
    else:
        queries.append(swap(mine, n, 1))
    if n == 4:
        first[0], states = hold((first[0], states))
    keep, send = option_partials(blk_arr, *small, kvs, masks, queries, states[-1][1])
    if n == 4:
        near = [lax.ppermute(first[0], "blk", [(2, 1)])]
        kvs, keep = hold((kvs, keep))
        near += [lax.ppermute(x, "blk", [(0, 1)]) for x in kvs[1:]]
        first[1:], keep = hold((first[1:], keep))
        anchors = [[x, y, lax.ppermute(y, "blk", [(2, 3)])] for x, y in zip(near, first)]
        anchors[0], first = hold((anchors[0], first))
    else:
        anchors = [[from_root(x, blk)] for x in kvs]
    ctx_out, tokens = None, []
    for g, state in enumerate(states):
        ctx_out, token = anchor_attention(blk_arr, ctx_query, kvs[g], state, anchors[g], g, ctx_out)
        tokens.append(token)
    for bit in range(rounds):
        got = swap(send, n, 1 << bit)
        last = bit == rounds - 1
        outs = merge(keep, got, last, tokens[-1 if last else 0])
        if last:
            opt_out = outs[0]
        else:
            keep, send = outs
    return (ctx_out, opt_out)


def solution(mesh):
    spread = P(("groups", "blk"), "head")
    return jax.shard_map(
        body,
        mesh=mesh,
        in_specs=(spread, spread, spread, spread, P("groups"), P("groups"), P("groups")),
        out_specs=(spread, spread),
        check_vma=False,
    )
```

```python
import functools
import math

import jax
import jax.numpy as jnp
from jax import lax
from jax.experimental import pallas as pl
from jax.experimental.pallas import tpu as pltpu
from jax.sharding import PartitionSpec as P

HD = 128
HQ = 64
KVH = 8
CAP = 32
GROUP = HQ // KVH
SCALE = HD ** (-0.5)
C2 = SCALE * math.log2(math.e)
NEG = -1e30
TILE = 256
PAIR = 2
VMEM = pl.BlockSpec(memory_space=pltpu.VMEM)
SMEM = pl.BlockSpec(memory_space=pltpu.SMEM)
HBM = pl.BlockSpec(memory_space=pltpu.HBM)
ANY = pl.BlockSpec(memory_space=pl.ANY)


def cost(flops):
    return pl.CostEstimate(flops=flops, bytes_accessed=1, transcendentals=0)


BRIEF = cost(1)


def nt(a, b):
    return lax.dot_general(a, b, (((1,), (1,)), ((), ())), preferred_element_type=jnp.float32)


def nn(a, b):
    return jnp.dot(a, b, preferred_element_type=jnp.float32)


def params(mib):
    return pltpu.CompilerParams(vmem_limit_bytes=mib * 1024 * 1024)


def fold(op, items):
    return functools.reduce(op, items)


def start_all(copies, sem):
    started = [pltpu.make_async_copy(a, b, sem.at[i]) for i, (a, b) in enumerate(copies)]
    for copy in started:
        copy.start()
    return started


def in_hbm(x):
    return pltpu.with_memory_space_constraint(x, pltpu.HBM)


def beside(heads, k_ref, v_ref, kv):
    copies = []
    for g in range(heads):
        for ref, at in ((k_ref, 0), (v_ref, HD)):
            copies.append((ref.at[:, g * HD : (g + 1) * HD], kv[g].at[:, at : at + HD]))
    return copies


def parts_kernel(heads, k_ref, v_ref, *refs):
    kv, sem = refs[:heads], refs[heads]
    for copy in start_all(beside(heads, k_ref, v_ref, kv), sem):
        copy.wait()


def parts(key, value):
    rows, heads = key.shape[0], key.shape[1] // HD
    outs = pl.pallas_call(
        functools.partial(parts_kernel, heads),
        out_shape=[pltpu.VMEM((rows, 2 * HD), key.dtype)] * heads,
        in_specs=[HBM] * 2,
        out_specs=[VMEM] * heads,
        scratch_shapes=[pltpu.SemaphoreType.DMA((2 * heads,))],
        compiler_params=params(2),
        cost_estimate=BRIEF,
        name="parts",
    )(in_hbm(key), in_hbm(value))
    return list(outs)


def pipelined(tasks, scores, finish):
    ahead = scores(tasks[0])
    for i, task in enumerate(tasks):
        now = ahead
        if i + 1 < len(tasks):
            ahead = scores(tasks[i + 1])
        finish(task, now)


def head_columns(h):
    return slice(h * HD, (h + 1) * HD)


def local_pass(g, q_ref, kv_ref, ve, arrived, emit):
    rows = kv_ref.shape[0]
    ve[:, :HD] = kv_ref[:, HD:]
    ve[:, HD:] = jnp.ones((rows, HD), jnp.bfloat16)
    row = lax.broadcasted_iota(jnp.int32, (PAIR * TILE, TILE), 0)
    seen = (row & (TILE - 1)) >= lax.broadcasted_iota(jnp.int32, (PAIR * TILE, TILE), 1)

    def scores(task):
        first, at = task
        if at == 0:
            arrived(first)
        q = jnp.concatenate([q_ref[at : at + TILE, head_columns(g * GROUP + first + j)] for j in range(PAIR)], axis=0)
        parts = [nt(q, kv_ref[:at, :HD])] if at else []
        parts.append(jnp.where(seen, nt(q, kv_ref[at : at + TILE, :HD]), NEG))
        return parts

    def finish(task, parts):
        first, at = task
        top = fold(jnp.maximum, [jnp.max(s, axis=1, keepdims=True) for s in parts])
        total = None
        for s, start in zip(parts, [0, at] if at else [at]):
            p = jnp.exp2((s - top) * C2).astype(jnp.bfloat16)
            part = nn(p, ve[start : start + s.shape[1], :])
            total = part if total is None else total + part
        for j in range(PAIR):
            mine = slice(j * TILE, (j + 1) * TILE)
            emit(slice(at, at + TILE), first + j, total[mine, :HD], total[mine, HD:], top[mine] * C2)

    pipelined([(h, at) for h in range(0, GROUP, PAIR) for at in range(0, rows, TILE)], scores, finish)


def first_kernel(blk_ref, kv_ref, *refs):
    count = (len(refs) - 5) // 2
    sources, state, held, (ve, sem) = refs[:count], refs[count : count + 3], refs[count + 3 : -2], refs[-2:]
    q_ref = held[0]
    spots = [slice(h * HD, (h + PAIR) * HD) for h in range(0, q_ref.shape[1] // HD, PAIR)]
    copies = [(sources[0].at[:, x], q_ref.at[:, x]) for x in spots] + list(zip(sources[1:], held[1:]))
    copies = start_all(copies, sem)
    ahead = GROUP // PAIR

    @pl.when(blk_ref[0] > 0)
    def _():
        local_pass(0, q_ref, kv_ref, ve, lambda h: copies[h // PAIR].wait(), keep_in(state))

    @pl.when(blk_ref[0] == 0)
    def _():
        for copy in copies[:ahead]:
            copy.wait()

    for copy in copies[ahead:]:
        copy.wait()


def first_attention(blk, kv, query, others):
    rows = kv.shape[0]
    sources = [query, *others]
    outs = pl.pallas_call(
        first_kernel,
        out_shape=[pltpu.VMEM((rows, GROUP * HD), jnp.float32)] * 3 + [pltpu.VMEM(x.shape, x.dtype) for x in sources],
        in_specs=[SMEM, VMEM] + [HBM] * len(sources),
        out_specs=[VMEM] * (3 + len(sources)),
        scratch_shapes=[
            pltpu.VMEM((rows, 2 * HD), jnp.bfloat16),
            pltpu.SemaphoreType.DMA((query.shape[1] // HD // PAIR + len(others),)),
        ],
        compiler_params=params(6),
        cost_estimate=cost(2 * 10**9),
        name="local_attention",
    )(blk, kv, *[in_hbm(x) for x in sources])
    return list(outs[:3]), list(outs[3:])


def keep_in(state):
    acc_ref, top_ref, sum_ref = state

    def emit(rows, h, total, z, top):
        here = (rows, head_columns(h))
        acc_ref[here], sum_ref[here], top_ref[here] = total, z, jnp.broadcast_to(top, total.shape)

    return emit


def local_kernel(g, blk_ref, kv_ref, q_ref, *refs):
    @pl.when(blk_ref[0] > 0)
    def _():
        local_pass(g, q_ref, kv_ref, refs[3], lambda h: None, keep_in(refs[:3]))


def local_attention(blk, kv, g, query):
    rows = kv.shape[0]
    return list(
        pl.pallas_call(
            functools.partial(local_kernel, g),
            out_shape=[pltpu.VMEM((rows, GROUP * HD), jnp.float32)] * 3,
            in_specs=[SMEM, VMEM, VMEM],
            out_specs=[VMEM] * 3,
            scratch_shapes=[pltpu.VMEM((rows, 2 * HD), jnp.bfloat16)],
            compiler_params=params(6),
            cost_estimate=cost(10**9),
            name="local_attention",
        )(blk, kv, query)
    )


def anchor_kernel(g, count, prior, blk_ref, q_ref, kv_ref, acc_ref, top_ref, sum_ref, *refs):
    cand, (o_ref, token, ka, vae, out, sem) = refs[:count], refs[count + prior :]
    rows = q_ref.shape[0]
    blk = blk_ref[0]
    token[...] = jnp.zeros(token.shape, jnp.float32)

    def leave(h):
        return pltpu.make_async_copy(out.at[h], o_ref.at[:, head_columns(g * GROUP + h)], sem.at[h])

    def take(ref):
        ka[...] = ref[:, :HD]
        vae[:, :HD] = ref[:, HD:]

    def scores(h):
        return nt(q_ref[:, head_columns(g * GROUP + h)], ka[...])

    def weigh(h, s):
        before = top_ref[:, head_columns(h)]
        top = jnp.maximum(jnp.max(s, axis=1, keepdims=True) * C2, before)
        p = [jnp.exp2(s[:, at : at + HD] * C2 - top).astype(jnp.bfloat16) for at in range(0, rows, HD)]
        return jnp.concatenate(p, axis=1), jnp.exp2(before - top)

    def finish(h, total, w):
        held = (slice(None), head_columns(h))
        o = (total[:, :HD] + w * acc_ref[held]) * inverse(total[:, HD:] + w * sum_ref[held])
        out[h] = o.astype(jnp.bfloat16)
        leave(h).start()

    @pl.when(blk > 0)
    def _():
        if count == 1:
            take(cand[0])
        else:
            for i, ref in enumerate(cand):
                pl.when(blk == i + 1)(functools.partial(take, ref))
        vae[:, HD:] = jnp.ones((rows, HD), jnp.bfloat16)
        ahead, weighed = scores(0), None
        for h in range(GROUP + 1):
            s = ahead
            if h + 1 < GROUP:
                ahead = scores(h + 1)
            if weighed is not None:
                total, w = nn(weighed[0], vae[...]), weighed[1]
            if h < GROUP:
                weighed = weigh(h, s)
            if h:
                finish(h - 1, total, w)

    def emit(here, h, total, z, top):
        out[h, here, :] = (total * inverse(z)).astype(jnp.bfloat16)
        if here.stop == rows:
            leave(h).start()

    @pl.when(blk == 0)
    def _():
        local_pass(g, q_ref, kv_ref, vae, lambda first: None, emit)

    for h in range(GROUP):
        leave(h).wait()


def inverse(x):
    guess = pl.reciprocal(x, approx=True)
    return guess * (2.0 - x * guess)


def anchor_attention(blk, query, kv, state, cands, g, prior):
    rows = query.shape[0]
    args = [blk, query, kv, *state, *cands]
    specs = [SMEM] + [VMEM] * (5 + len(cands))
    alias = {}
    if prior is not None:
        alias = {len(args): 0}
        args.append(prior)
        specs.append(ANY)
    return pl.pallas_call(
        functools.partial(anchor_kernel, g, len(cands), len(alias)),
        out_shape=[jax.ShapeDtypeStruct(query.shape, query.dtype), jax.ShapeDtypeStruct((8, HD), jnp.float32)],
        in_specs=specs,
        out_specs=[ANY, VMEM],
        scratch_shapes=[
            pltpu.VMEM((rows, HD), jnp.bfloat16),
            pltpu.VMEM((rows, 2 * HD), jnp.bfloat16),
            pltpu.VMEM((GROUP, rows, HD), jnp.bfloat16),
            pltpu.SemaphoreType.DMA((GROUP,)),
        ],
        input_output_aliases=alias,
        compiler_params=params(6),
        cost_estimate=cost(1000000000),
        name="anchor_attention",
    )(*args)


def fold_order(n):
    bits = n.bit_length() - 1
    return sorted(range(n), key=lambda x: int(format(x, "0%db" % bits)[::-1], 2))


def join_kernel(*refs):
    at = 0
    for ref in refs[:-1]:
        refs[-1][at : at + ref.shape[0], :] = ref[...]
        at += ref.shape[0]


def join(arrays):
    height, width = sum(x.shape[0] for x in arrays), arrays[0].shape[1]
    return pl.pallas_call(
        join_kernel,
        out_shape=pltpu.VMEM((height, width), arrays[0].dtype),
        in_specs=[VMEM] * len(arrays),
        out_specs=VMEM,
        compiler_params=params(2),
        cost_estimate=BRIEF,
        name="join",
    )(*arrays)


def option_kernel(masks, heads, blk_ref, owner_ref, slot_ref, length_ref, *refs):
    n = len(masks)
    kv_heads = heads // GROUP
    kv, queries = refs[:kv_heads], refs[kv_heads : kv_heads + 2]
    keep, send, q_all, part = refs[kv_heads + 3 :]
    blk = blk_ref[0]
    rows = kv[0].shape[0]
    half = queries[0].shape[0]
    options, each = 2 * half, 2 * half // n
    for i, mask in enumerate(masks):
        at = jnp.bitwise_xor(blk, mask) * each
        here = queries[i * each // half].at[i * each % half : i * each % half + each]
        q_all[pl.ds(pl.multiple_of(at, each), each), :] = here[...]
    eye = lax.broadcasted_iota(jnp.int32, (options, options), 0) == lax.broadcasted_iota(jnp.int32, (options, options), 1)
    length = jnp.sum(jnp.where(eye, length_ref[...].astype(jnp.float32), 0.0), axis=1, keepdims=True)
    seen = length - (blk * rows).astype(jnp.float32)
    lane = lax.broadcasted_iota(jnp.int32, (options, HD), 1)
    logs = jnp.zeros((options, HD), jnp.float32)
    home = head_of(lane, heads)
    stack = max(1, min(GROUP, 512 // options))
    spots = lax.broadcasted_iota(jnp.int32, (options * stack, rows), 1).astype(jnp.float32)
    seen_all = jnp.concatenate([seen] * stack, axis=0)
    for first in range(0, heads, stack):
        g = first // GROUP
        q = jnp.concatenate([q_all[:, h * HD : (h + 1) * HD] for h in range(first, first + stack)], axis=0)
        s = nt(q, kv[g][:, :HD])
        s = jnp.where(spots < seen_all, s, NEG)
        top = jnp.max(s, axis=1, keepdims=True)
        e = jnp.exp2((s - top) * C2)
        z = jnp.sum(e, axis=1, keepdims=True)
        o = nn(e.astype(jnp.bfloat16), kv[g][:, HD:]) / z
        live = seen_all > 0
        o = jnp.where(live, o, 0.0).astype(jnp.bfloat16)
        log = jnp.where(live, top * SCALE + jnp.log(z), NEG)
        for j in range(stack):
            h = first + j
            part[:, h * HD : (h + 1) * HD] = o[j * options : (j + 1) * options]
            logs = jnp.where(home == h, log[j * options : (j + 1) * options], logs)
    part[:, heads * HD :] = summands(logs, heads)
    slot = lax.broadcasted_iota(jnp.int32, (CAP, options), 0)
    order = fold_order(n)
    for half, out in ((order[: n // 2], keep), (order[n // 2 :], send)):
        for i, mask in enumerate(half):
            pick = (owner_ref[...] == jnp.bitwise_xor(blk, mask)) & (slot_ref[...] == slot)
            pick = jnp.where(pick, 1.0, 0.0).astype(jnp.bfloat16)
            out[i * CAP : (i + 1) * CAP, :] = nn(pick, part[...]).astype(jnp.bfloat16)


def summands(logs, heads):
    lane = lax.broadcasted_iota(jnp.int32, logs.shape, 1)
    high = logs.astype(jnp.bfloat16).astype(jnp.float32)
    rest = logs - high
    mid = rest.astype(jnp.bfloat16).astype(jnp.float32)
    low = rest - mid
    low = jnp.where(lane < 3 * heads, low, 0.0)
    return jnp.where(lane < heads, high, jnp.where(lane < 2 * heads, mid, low)).astype(jnp.bfloat16)


def option_partials(blk, owner, slot, length, kvs, masks, queries, after):
    n, heads = len(masks), queries[0].shape[1] // HD
    options = 2 * queries[0].shape[0]
    width = (heads + 1) * HD
    rows = kvs[0].shape[0]
    return pl.pallas_call(
        functools.partial(option_kernel, masks, heads),
        out_shape=[jax.ShapeDtypeStruct((n // 2 * CAP, width), jnp.bfloat16)] * 2,
        in_specs=[SMEM] + [VMEM] * (5 + len(kvs)) + [ANY],
        out_specs=[VMEM] * 2,
        scratch_shapes=[
            pltpu.VMEM((options, heads * HD), jnp.bfloat16),
            pltpu.VMEM((options, width), jnp.bfloat16),
        ],
        compiler_params=params(4 + options // 32),
        cost_estimate=cost(1000000000),
        name="option_partials",
    )(blk, owner, slot, length, *kvs, *queries, after)


def head_of(lane, heads):
    return lane & (heads - 1) if heads & (heads - 1) == 0 else lax.rem(lane, heads)


def merge_kernel(heads, a, b, after, *outs):
    width = heads * HD
    home = head_of(lax.broadcasted_iota(jnp.int32, (HD, HD), 0), heads)
    home = jnp.where(lax.broadcasted_iota(jnp.int32, (HD, HD), 0) < 3 * heads, home, heads)
    pick = jnp.concatenate([jnp.where(home == h, 1.0, 0.0).astype(jnp.bfloat16) for h in range(heads)], axis=1)
    logs = [nn(x[:, width:], pick) for x in (a, b)]
    top = jnp.maximum(*logs)
    weights = [jnp.exp(log - top) for log in logs]
    total = weights[0] + weights[1]
    merged = (weights[0] * a[:, :width].astype(jnp.float32) + weights[1] * b[:, :width].astype(jnp.float32)) / total
    merged = merged.astype(jnp.bfloat16)
    if len(outs) == 1:
        outs[0][...] = merged
        return
    log = top + jnp.log(total)
    lane = lax.broadcasted_iota(jnp.int32, (a.shape[0], HD), 1)
    packed = jnp.zeros((a.shape[0], HD), jnp.float32)
    home = head_of(lane, heads)
    for h in range(heads):
        packed = jnp.where(home == h, log[:, h * HD : (h + 1) * HD], packed)
    packed = summands(packed, heads)
    half = a.shape[0] // 2
    for i, out in enumerate(outs):
        out[:, :width] = merged[i * half : (i + 1) * half]
        out[:, width:] = packed[i * half : (i + 1) * half]


def merge(a, b, last, after):
    rows, width = a.shape
    heads = width // HD - 1
    if last:
        shapes = [jax.ShapeDtypeStruct((rows, heads * HD), jnp.bfloat16)]
    else:
        shapes = [jax.ShapeDtypeStruct((rows // 2, width), jnp.bfloat16)] * 2
    return pl.pallas_call(
        functools.partial(merge_kernel, heads),
        out_shape=shapes,
        in_specs=[VMEM] * 2 + [ANY],
        out_specs=[VMEM] * len(shapes),
        compiler_params=params(6),
        cost_estimate=BRIEF,
        name="merge",
    )(a, b, after)


def swap(x, n, mask):
    return lax.ppermute(x, "blk", [(i, i ^ mask) for i in range(n)])


def from_root(x, blk):
    return lax.psum(jnp.where(blk == 0, x, jnp.zeros_like(x)), "blk")


def body(ctx_query, ctx_key, ctx_value, opt_query, opt_owner, opt_slot, opt_length):
    n = lax.axis_size("blk")
    blk = lax.axis_index("blk")
    blk_arr = blk.astype(jnp.int32).reshape(1)
    options = opt_owner.shape[0]
    rounds = n.bit_length() - 1

    hold = lax.optimization_barrier
    row = lambda x: x.reshape(1, options)

    blk_arr, ctx_key = hold((blk_arr, ctx_key))
    kvs = parts(ctx_key, ctx_value)
    shards = [opt_query]
    masks = [0]
    for bit in reversed(range(1, rounds)):
        mine = shards[0] if len(shards) == 1 else jnp.concatenate(shards, axis=0)
        shards = [mine, swap(mine, n, 1 << bit)]
        masks = masks + [mask | 1 << bit for mask in masks]
    masks = masks + [mask | 1 for mask in masks]
    if n == 4:
        first = [lax.ppermute(kvs[0], "blk", [(0, 2)])]
    small = [row(opt_owner), row(opt_slot), row(opt_length), shards[0]]
    state, (ctx_query, *small, own) = first_attention(blk_arr, kvs[0], ctx_query, small)
    kvs, state, shards = hold((kvs, state, shards))
    mine = join([own, *shards[1:]])
    queries = [mine, swap(mine, n, 1)]
    states = [state]
    if n == 4:
        first += [lax.ppermute(x, "blk", [(0, 2)]) for x in kvs[1:]]
    states += [local_attention(blk_arr, kv, g, ctx_query) for g, kv in enumerate(kvs) if g]
    if n == 4:
        first[0], states = hold((first[0], states))
    keep, send = option_partials(blk_arr, *small, kvs, masks, queries, states[-1][1])
    if n == 4:
        near = [lax.ppermute(first[0], "blk", [(2, 1)])]
        kvs, keep = hold((kvs, keep))
        near += [lax.ppermute(x, "blk", [(0, 1)]) for x in kvs[1:]]
        first[1:], keep = hold((first[1:], keep))
        anchors = [[x, y, lax.ppermute(y, "blk", [(2, 3)])] for x, y in zip(near, first)]
        anchors[0], first = hold((anchors[0], first))
    else:
        anchors = [[from_root(x, blk)] for x in kvs]
    ctx_out, tokens = None, []
    for g, state in enumerate(states):
        ctx_out, token = anchor_attention(blk_arr, ctx_query, kvs[g], state, anchors[g], g, ctx_out)
        tokens.append(token)
    for bit in range(rounds):
        got = swap(send, n, 1 << bit)
        last = bit == rounds - 1
        outs = merge(keep, got, last, tokens[-1 if last else 0])
        if last:
            opt_out = outs[0]
        else:
            keep, send = outs
    return (ctx_out, opt_out)


def solution(mesh):
    spread = P(("groups", "blk"), "head")
    return jax.shard_map(
        body,
        mesh=mesh,
        in_specs=(spread, spread, spread, spread, P("groups"), P("groups"), P("groups")),
        out_specs=(spread, spread),
        check_vma=False,
    )
```

```python
import functools
import math

import jax
import jax.numpy as jnp
from jax import lax
from jax.experimental import pallas as pl
from jax.experimental.pallas import tpu as pltpu
from jax.sharding import PartitionSpec as P

HD = 128
HQ = 64
KVH = 8
CAP = 32
GROUP = HQ // KVH
SCALE = HD ** (-0.5)
C2 = SCALE * math.log2(math.e)
NEG = -1e30
TILE = 256
PAIR = 2
VMEM = pl.BlockSpec(memory_space=pltpu.VMEM)
SMEM = pl.BlockSpec(memory_space=pltpu.SMEM)
HBM = pl.BlockSpec(memory_space=pltpu.HBM)
ANY = pl.BlockSpec(memory_space=pl.ANY)


def cost(flops):
    return pl.CostEstimate(flops=flops, bytes_accessed=1, transcendentals=0)


BRIEF = cost(1)


def nt(a, b):
    return lax.dot_general(a, b, (((1,), (1,)), ((), ())), preferred_element_type=jnp.float32)


def nn(a, b):
    return jnp.dot(a, b, preferred_element_type=jnp.float32)


def params(mib):
    return pltpu.CompilerParams(vmem_limit_bytes=mib * 1024 * 1024)


def fold(op, items):
    return functools.reduce(op, items)


def start_all(copies, sem):
    started = [pltpu.make_async_copy(a, b, sem.at[i]) for i, (a, b) in enumerate(copies)]
    for copy in started:
        copy.start()
    return started


def in_hbm(x):
    return pltpu.with_memory_space_constraint(x, pltpu.HBM)


def beside(heads, k_ref, v_ref, kv):
    copies = []
    for g in range(heads):
        for ref, at in ((k_ref, 0), (v_ref, HD)):
            copies.append((ref.at[:, g * HD : (g + 1) * HD], kv[g].at[:, at : at + HD]))
    return copies


def parts_kernel(heads, k_ref, v_ref, *refs):
    kv, sem = refs[:heads], refs[heads]
    for copy in start_all(beside(heads, k_ref, v_ref, kv), sem):
        copy.wait()


def parts(key, value):
    rows, heads = key.shape[0], key.shape[1] // HD
    outs = pl.pallas_call(
        functools.partial(parts_kernel, heads),
        out_shape=[pltpu.VMEM((rows, 2 * HD), key.dtype)] * heads,
        in_specs=[HBM] * 2,
        out_specs=[VMEM] * heads,
        scratch_shapes=[pltpu.SemaphoreType.DMA((2 * heads,))],
        compiler_params=params(2),
        cost_estimate=BRIEF,
        name="parts",
    )(in_hbm(key), in_hbm(value))
    return list(outs)


def pipelined(tasks, scores, finish):
    ahead = scores(tasks[0])
    for i, task in enumerate(tasks):
        now = ahead
        if i + 1 < len(tasks):
            ahead = scores(tasks[i + 1])
        finish(task, now)


def head_columns(h):
    return slice(h * HD, (h + 1) * HD)


def local_pass(g, q_ref, kv_ref, ve, arrived, emit):
    rows = kv_ref.shape[0]
    ve[:, :HD] = kv_ref[:, HD:]
    ve[:, HD:] = jnp.ones((rows, HD), jnp.bfloat16)
    row = lax.broadcasted_iota(jnp.int32, (PAIR * TILE, TILE), 0)
    seen = (row & (TILE - 1)) >= lax.broadcasted_iota(jnp.int32, (PAIR * TILE, TILE), 1)

    def scores(task):
        first, at = task
        if at == 0:
            arrived(first)
        q = jnp.concatenate([q_ref[at : at + TILE, head_columns(g * GROUP + first + j)] for j in range(PAIR)], axis=0)
        parts = [nt(q, kv_ref[:at, :HD])] if at else []
        parts.append(jnp.where(seen, nt(q, kv_ref[at : at + TILE, :HD]), NEG))
        return parts

    def finish(task, parts):
        first, at = task
        top = fold(jnp.maximum, [jnp.max(s, axis=1, keepdims=True) for s in parts])
        total = None
        for s, start in zip(parts, [0, at] if at else [at]):
            p = jnp.exp2((s - top) * C2).astype(jnp.bfloat16)
            part = nn(p, ve[start : start + s.shape[1], :])
            total = part if total is None else total + part
        for j in range(PAIR):
            mine = slice(j * TILE, (j + 1) * TILE)
            emit(slice(at, at + TILE), first + j, total[mine, :HD], total[mine, HD:], top[mine] * C2)

    pipelined([(h, at) for h in range(0, GROUP, PAIR) for at in range(0, rows, TILE)], scores, finish)


def first_kernel(blk_ref, kv_ref, *refs):
    count = (len(refs) - 5) // 2
    sources, state, held, (ve, sem) = refs[:count], refs[count : count + 3], refs[count + 3 : -2], refs[-2:]
    q_ref = held[0]
    spots = [slice(h * HD, (h + PAIR) * HD) for h in range(0, q_ref.shape[1] // HD, PAIR)]
    copies = [(sources[0].at[:, x], q_ref.at[:, x]) for x in spots] + list(zip(sources[1:], held[1:]))
    copies = start_all(copies, sem)
    ahead = GROUP // PAIR

    @pl.when(blk_ref[0] > 0)
    def _():
        local_pass(0, q_ref, kv_ref, ve, lambda h: copies[h // PAIR].wait(), keep_in(state))

    @pl.when(blk_ref[0] == 0)
    def _():
        for copy in copies[:ahead]:
            copy.wait()

    for copy in copies[ahead:]:
        copy.wait()


def first_attention(blk, kv, query, others):
    rows = kv.shape[0]
    sources = [query, *others]
    outs = pl.pallas_call(
        first_kernel,
        out_shape=[pltpu.VMEM((rows, GROUP * HD), jnp.float32)] * 3 + [pltpu.VMEM(x.shape, x.dtype) for x in sources],
        in_specs=[SMEM, VMEM] + [HBM] * len(sources),
        out_specs=[VMEM] * (3 + len(sources)),
        scratch_shapes=[
            pltpu.VMEM((rows, 2 * HD), jnp.bfloat16),
            pltpu.SemaphoreType.DMA((query.shape[1] // HD // PAIR + len(others),)),
        ],
        compiler_params=params(6),
        cost_estimate=cost(2 * 10**9),
        name="local_attention",
    )(blk, kv, *[in_hbm(x) for x in sources])
    return list(outs[:3]), list(outs[3:])


def keep_in(state):
    acc_ref, top_ref, sum_ref = state

    def emit(rows, h, total, z, top):
        here = (rows, head_columns(h))
        acc_ref[here], sum_ref[here], top_ref[here] = total, z, jnp.broadcast_to(top, total.shape)

    return emit


def local_kernel(g, blk_ref, kv_ref, q_ref, *refs):
    @pl.when(blk_ref[0] > 0)
    def _():
        local_pass(g, q_ref, kv_ref, refs[3], lambda h: None, keep_in(refs[:3]))


def local_attention(blk, kv, g, query):
    rows = kv.shape[0]
    return list(
        pl.pallas_call(
            functools.partial(local_kernel, g),
            out_shape=[pltpu.VMEM((rows, GROUP * HD), jnp.float32)] * 3,
            in_specs=[SMEM, VMEM, VMEM],
            out_specs=[VMEM] * 3,
            scratch_shapes=[pltpu.VMEM((rows, 2 * HD), jnp.bfloat16)],
            compiler_params=params(6),
            cost_estimate=cost(1000000000),
            name="local_attention",
        )(blk, kv, query)
    )


def anchor_kernel(g, groups, prior, blk_ref, q_ref, kv_ref, acc_ref, top_ref, sum_ref, *refs):
    count = sum(groups)
    cand, (o_ref, token, ka, vae, out, sem) = refs[:count], refs[count + prior :]
    rows = q_ref.shape[0]
    blk = blk_ref[0]
    token[...] = jnp.zeros(token.shape, jnp.float32)

    def leave(h):
        return pltpu.make_async_copy(out.at[h], o_ref.at[:, head_columns(g * GROUP + h)], sem.at[h])

    def take(refs):
        at = 0
        for ref in refs:
            here = slice(at, at + ref.shape[0])
            ka[here, :] = ref[:, :HD]
            vae[here, :HD] = ref[:, HD:]
            at = here.stop

    def scores(h):
        return nt(q_ref[:, head_columns(g * GROUP + h)], ka[...])

    def weigh(h, s):
        before = top_ref[:, head_columns(h)]
        top = jnp.maximum(jnp.max(s, axis=1, keepdims=True) * C2, before)
        p = [jnp.exp2(s[:, at : at + HD] * C2 - top).astype(jnp.bfloat16) for at in range(0, rows, HD)]
        return jnp.concatenate(p, axis=1), jnp.exp2(before - top)

    def finish(h, total, w):
        held = (slice(None), head_columns(h))
        o = (total[:, :HD] + w * acc_ref[held]) * inverse(total[:, HD:] + w * sum_ref[held])
        out[h] = o.astype(jnp.bfloat16)
        leave(h).start()

    @pl.when(blk > 0)
    def _():
        if len(groups) == 1:
            take(cand)
        else:
            at = 0
            for i, size in enumerate(groups):
                pl.when(blk == i + 1)(functools.partial(take, cand[at : at + size]))
                at += size
        vae[:, HD:] = jnp.ones((rows, HD), jnp.bfloat16)
        ahead, weighed = scores(0), None
        for h in range(GROUP + 1):
            s = ahead
            if h + 1 < GROUP:
                ahead = scores(h + 1)
            if weighed is not None:
                total, w = nn(weighed[0], vae[...]), weighed[1]
            if h < GROUP:
                weighed = weigh(h, s)
            if h:
                finish(h - 1, total, w)

    def emit(here, h, total, z, top):
        out[h, here, :] = (total * inverse(z)).astype(jnp.bfloat16)
        if here.stop == rows:
            leave(h).start()

    @pl.when(blk == 0)
    def _():
        local_pass(g, q_ref, kv_ref, vae, lambda first: None, emit)

    for h in range(GROUP):
        leave(h).wait()


def inverse(x):
    guess = pl.reciprocal(x, approx=True)
    return guess * (2.0 - x * guess)


def anchor_attention(blk, query, kv, state, cands, g, prior):
    rows = query.shape[0]
    flat = [x for group in cands for x in group]
    args = [blk, query, kv, *state, *flat]
    specs = [SMEM] + [VMEM] * (5 + len(flat))
    alias = {}
    if prior is not None:
        alias = {len(args): 0}
        args.append(prior)
        specs.append(ANY)
    return pl.pallas_call(
        functools.partial(anchor_kernel, g, [len(group) for group in cands], len(alias)),
        out_shape=[jax.ShapeDtypeStruct(query.shape, query.dtype), jax.ShapeDtypeStruct((8, HD), jnp.float32)],
        in_specs=specs,
        out_specs=[ANY, VMEM],
        scratch_shapes=[
            pltpu.VMEM((rows, HD), jnp.bfloat16),
            pltpu.VMEM((rows, 2 * HD), jnp.bfloat16),
            pltpu.VMEM((GROUP, rows, HD), jnp.bfloat16),
            pltpu.SemaphoreType.DMA((GROUP,)),
        ],
        input_output_aliases=alias,
        compiler_params=params(6),
        cost_estimate=cost(1000000000),
        name="anchor_attention",
    )(*args)


def fold_order(n):
    bits = n.bit_length() - 1
    return sorted(range(n), key=lambda x: int(format(x, "0%db" % bits)[::-1], 2))


def join_kernel(*refs):
    at = 0
    for ref in refs[:-1]:
        refs[-1][at : at + ref.shape[0], :] = ref[...]
        at += ref.shape[0]


def join(arrays):
    height, width = sum(x.shape[0] for x in arrays), arrays[0].shape[1]
    return pl.pallas_call(
        join_kernel,
        out_shape=pltpu.VMEM((height, width), arrays[0].dtype),
        in_specs=[VMEM] * len(arrays),
        out_specs=VMEM,
        compiler_params=params(2),
        cost_estimate=BRIEF,
        name="join",
    )(*arrays)


def half_kernel(which, x_ref, o_ref):
    rows = o_ref.shape[0]
    o_ref[...] = x_ref[which * rows : (which + 1) * rows, :]


def half_rows(x, which):
    return pl.pallas_call(
        functools.partial(half_kernel, which),
        out_shape=pltpu.VMEM((x.shape[0] // 2, x.shape[1]), x.dtype),
        in_specs=[VMEM],
        out_specs=VMEM,
        compiler_params=params(2),
        cost_estimate=BRIEF,
        name="half_rows",
    )(x)


def option_kernel(masks, heads, blk_ref, owner_ref, slot_ref, length_ref, *refs):
    n = len(masks)
    kv_heads = heads // GROUP
    kv, queries = refs[:kv_heads], refs[kv_heads : kv_heads + 2]
    keep, send, q_all, part = refs[kv_heads + 3 :]
    blk = blk_ref[0]
    rows = kv[0].shape[0]
    half = queries[0].shape[0]
    options, each = 2 * half, 2 * half // n
    for i, mask in enumerate(masks):
        at = jnp.bitwise_xor(blk, mask) * each
        here = queries[i * each // half].at[i * each % half : i * each % half + each]
        q_all[pl.ds(pl.multiple_of(at, each), each), :] = here[...]
    eye = lax.broadcasted_iota(jnp.int32, (options, options), 0) == lax.broadcasted_iota(jnp.int32, (options, options), 1)
    length = jnp.sum(jnp.where(eye, length_ref[...].astype(jnp.float32), 0.0), axis=1, keepdims=True)
    seen = length - (blk * rows).astype(jnp.float32)
    lane = lax.broadcasted_iota(jnp.int32, (options, HD), 1)
    logs = jnp.zeros((options, HD), jnp.float32)
    home = head_of(lane, heads)
    stack = max(1, min(GROUP, 512 // options))
    spots = lax.broadcasted_iota(jnp.int32, (options * stack, rows), 1).astype(jnp.float32)
    seen_all = jnp.concatenate([seen] * stack, axis=0)
    for first in range(0, heads, stack):
        g = first // GROUP
        q = jnp.concatenate([q_all[:, h * HD : (h + 1) * HD] for h in range(first, first + stack)], axis=0)
        s = nt(q, kv[g][:, :HD])
        s = jnp.where(spots < seen_all, s, NEG)
        top = jnp.max(s, axis=1, keepdims=True)
        e = jnp.exp2((s - top) * C2)
        z = jnp.sum(e, axis=1, keepdims=True)
        o = nn(e.astype(jnp.bfloat16), kv[g][:, HD:]) / z
        live = seen_all > 0
        o = jnp.where(live, o, 0.0).astype(jnp.bfloat16)
        log = jnp.where(live, top * SCALE + jnp.log(z), NEG)
        for j in range(stack):
            h = first + j
            part[:, h * HD : (h + 1) * HD] = o[j * options : (j + 1) * options]
            logs = jnp.where(home == h, log[j * options : (j + 1) * options], logs)
    part[:, heads * HD :] = summands(logs, heads)
    slot = lax.broadcasted_iota(jnp.int32, (CAP, options), 0)
    order = fold_order(n)
    for half, out in ((order[: n // 2], keep), (order[n // 2 :], send)):
        for i, mask in enumerate(half):
            pick = (owner_ref[...] == jnp.bitwise_xor(blk, mask)) & (slot_ref[...] == slot)
            pick = jnp.where(pick, 1.0, 0.0).astype(jnp.bfloat16)
            out[i * CAP : (i + 1) * CAP, :] = nn(pick, part[...]).astype(jnp.bfloat16)


def summands(logs, heads):
    lane = lax.broadcasted_iota(jnp.int32, logs.shape, 1)
    high = logs.astype(jnp.bfloat16).astype(jnp.float32)
    rest = logs - high
    mid = rest.astype(jnp.bfloat16).astype(jnp.float32)
    low = rest - mid
    low = jnp.where(lane < 3 * heads, low, 0.0)
    return jnp.where(lane < heads, high, jnp.where(lane < 2 * heads, mid, low)).astype(jnp.bfloat16)


def option_partials(blk, owner, slot, length, kvs, masks, queries, after):
    n, heads = len(masks), queries[0].shape[1] // HD
    options = 2 * queries[0].shape[0]
    width = (heads + 1) * HD
    rows = kvs[0].shape[0]
    return pl.pallas_call(
        functools.partial(option_kernel, masks, heads),
        out_shape=[jax.ShapeDtypeStruct((n // 2 * CAP, width), jnp.bfloat16)] * 2,
        in_specs=[SMEM] + [VMEM] * (5 + len(kvs)) + [ANY],
        out_specs=[VMEM] * 2,
        scratch_shapes=[
            pltpu.VMEM((options, heads * HD), jnp.bfloat16),
            pltpu.VMEM((options, width), jnp.bfloat16),
        ],
        compiler_params=params(4 + options // 32),
        cost_estimate=cost(1),
        name="option_partials",
    )(blk, owner, slot, length, *kvs, *queries, after)


def head_of(lane, heads):
    return lane & (heads - 1) if heads & (heads - 1) == 0 else lax.rem(lane, heads)


def merge_kernel(heads, a, b, after, *outs):
    width = heads * HD
    home = head_of(lax.broadcasted_iota(jnp.int32, (HD, HD), 0), heads)
    home = jnp.where(lax.broadcasted_iota(jnp.int32, (HD, HD), 0) < 3 * heads, home, heads)
    pick = jnp.concatenate([jnp.where(home == h, 1.0, 0.0).astype(jnp.bfloat16) for h in range(heads)], axis=1)
    logs = [nn(x[:, width:], pick) for x in (a, b)]
    top = jnp.maximum(*logs)
    weights = [jnp.exp(log - top) for log in logs]
    total = weights[0] + weights[1]
    merged = (weights[0] * a[:, :width].astype(jnp.float32) + weights[1] * b[:, :width].astype(jnp.float32)) / total
    merged = merged.astype(jnp.bfloat16)
    if len(outs) == 1:
        outs[0][...] = merged
        return
    log = top + jnp.log(total)
    lane = lax.broadcasted_iota(jnp.int32, (a.shape[0], HD), 1)
    packed = jnp.zeros((a.shape[0], HD), jnp.float32)
    home = head_of(lane, heads)
    for h in range(heads):
        packed = jnp.where(home == h, log[:, h * HD : (h + 1) * HD], packed)
    packed = summands(packed, heads)
    half = a.shape[0] // 2
    for i, out in enumerate(outs):
        out[:, :width] = merged[i * half : (i + 1) * half]
        out[:, width:] = packed[i * half : (i + 1) * half]


def merge(a, b, last, after):
    rows, width = a.shape
    heads = width // HD - 1
    if last:
        shapes = [jax.ShapeDtypeStruct((rows, heads * HD), jnp.bfloat16)]
    else:
        shapes = [jax.ShapeDtypeStruct((rows // 2, width), jnp.bfloat16)] * 2
    return pl.pallas_call(
        functools.partial(merge_kernel, heads),
        out_shape=shapes,
        in_specs=[VMEM] * 2 + [ANY],
        out_specs=[VMEM] * len(shapes),
        compiler_params=params(6),
        cost_estimate=BRIEF,
        name="merge",
    )(a, b, after)


def swap(x, n, mask):
    return lax.ppermute(x, "blk", [(i, i ^ mask) for i in range(n)])


def from_root(x, blk):
    return lax.psum(jnp.where(blk == 0, x, jnp.zeros_like(x)), "blk")


def body(ctx_query, ctx_key, ctx_value, opt_query, opt_owner, opt_slot, opt_length):
    n = lax.axis_size("blk")
    blk = lax.axis_index("blk")
    blk_arr = blk.astype(jnp.int32).reshape(1)
    options = opt_owner.shape[0]
    rounds = n.bit_length() - 1

    hold = lax.optimization_barrier
    row = lambda x: x.reshape(1, options)

    blk_arr, ctx_key = hold((blk_arr, ctx_key))
    kvs = parts(ctx_key, ctx_value)
    shards = [opt_query]
    masks = [0]
    for bit in reversed(range(1, rounds)):
        mine = shards[0] if len(shards) == 1 else jnp.concatenate(shards, axis=0)
        shards = [mine, swap(mine, n, 1 << bit)]
        masks = masks + [mask | 1 << bit for mask in masks]
    masks = masks + [mask | 1 for mask in masks]
    if n == 4:
        first = [lax.ppermute(kvs[0], "blk", [(0, 2)])]
    small = [row(opt_owner), row(opt_slot), row(opt_length), shards[0]]
    state, (ctx_query, *small, own) = first_attention(blk_arr, kvs[0], ctx_query, small)
    kvs, state, shards = hold((kvs, state, shards))
    mine = join([own, *shards[1:]])
    queries = [mine, swap(mine, n, 1)]
    states = [state]
    if n == 4:
        first += [lax.ppermute(x, "blk", [(0, 2)]) for x in kvs[1:]]
    states += [local_attention(blk_arr, kv, g, ctx_query) for g, kv in enumerate(kvs) if g]
    if n == 4:
        first[0], states = hold((first[0], states))
    keep, send = option_partials(blk_arr, *small, kvs, masks, queries, states[-1][1])
    if n == 4:
        near = [[lax.ppermute(first[0], "blk", [(2, 1)])]]
        kvs, keep = hold((kvs, keep))
        tops = [half_rows(x, 0) for x in kvs[1:]]
        near += [[lax.ppermute(x, "blk", [(0, 1)])] for x in tops]
        first[1:], keep, tops = hold((first[1:], keep, tops))
        for x, y in zip(near[1:], first[1:]):
            x.append(lax.ppermute(half_rows(y, 1), "blk", [(2, 1)]))
        anchors = [[x, [y], [lax.ppermute(y, "blk", [(2, 3)])]] for x, y in zip(near, first)]
        anchors[0], first = hold((anchors[0], first))
    else:
        anchors = [[[from_root(x, blk)]] for x in kvs]
    ctx_out, tokens = None, []
    for g, state in enumerate(states):
        ctx_out, token = anchor_attention(blk_arr, ctx_query, kvs[g], state, anchors[g], g, ctx_out)
        tokens.append(token)
    for bit in range(rounds):
        got = swap(send, n, 1 << bit)
        last = bit == rounds - 1
        outs = merge(keep, got, last, tokens[-1 if last else 0])
        if last:
            opt_out = outs[0]
        else:
            keep, send = outs
    return (ctx_out, opt_out)


def solution(mesh):
    spread = P(("groups", "blk"), "head")
    return jax.shard_map(
        body,
        mesh=mesh,
        in_specs=(spread, spread, spread, spread, P("groups"), P("groups"), P("groups")),
        out_specs=(spread, spread),
        check_vma=False,
    )
```

```python
import functools
import math

import jax
import jax.numpy as jnp
from jax import lax
from jax.experimental import pallas as pl
from jax.experimental.pallas import tpu as pltpu
from jax.sharding import PartitionSpec as P

HD = 128
HQ = 64
KVH = 8
CAP = 32
GROUP = HQ // KVH
SCALE = HD ** (-0.5)
C2 = SCALE * math.log2(math.e)
NEG = -1e30
TILE = 256
PAIR = 2
VMEM = pl.BlockSpec(memory_space=pltpu.VMEM)
SMEM = pl.BlockSpec(memory_space=pltpu.SMEM)
HBM = pl.BlockSpec(memory_space=pltpu.HBM)
ANY = pl.BlockSpec(memory_space=pl.ANY)


def cost(flops):
    return pl.CostEstimate(flops=flops, bytes_accessed=1, transcendentals=0)


BRIEF = cost(1)


def nt(a, b):
    return lax.dot_general(a, b, (((1,), (1,)), ((), ())), preferred_element_type=jnp.float32)


def nn(a, b):
    return jnp.dot(a, b, preferred_element_type=jnp.float32)


def params(mib):
    return pltpu.CompilerParams(vmem_limit_bytes=mib * 1024 * 1024)


def fold(op, items):
    return functools.reduce(op, items)


def start_all(copies, sem):
    started = [pltpu.make_async_copy(a, b, sem.at[i]) for i, (a, b) in enumerate(copies)]
    for copy in started:
        copy.start()
    return started


def in_hbm(x):
    return pltpu.with_memory_space_constraint(x, pltpu.HBM)


def beside(heads, k_ref, v_ref, kv):
    copies = []
    for g in range(heads):
        for ref, at in ((k_ref, 0), (v_ref, HD)):
            copies.append((ref.at[:, g * HD : (g + 1) * HD], kv[g].at[:, at : at + HD]))
    return copies


def parts_kernel(heads, k_ref, v_ref, *refs):
    kv, sem = refs[:heads], refs[heads]
    for copy in start_all(beside(heads, k_ref, v_ref, kv), sem):
        copy.wait()


def parts(key, value):
    rows, heads = key.shape[0], key.shape[1] // HD
    outs = pl.pallas_call(
        functools.partial(parts_kernel, heads),
        out_shape=[pltpu.VMEM((rows, 2 * HD), key.dtype)] * heads,
        in_specs=[HBM] * 2,
        out_specs=[VMEM] * heads,
        scratch_shapes=[pltpu.SemaphoreType.DMA((2 * heads,))],
        compiler_params=params(2),
        cost_estimate=BRIEF,
        name="parts",
    )(in_hbm(key), in_hbm(value))
    return list(outs)


def pipelined(tasks, scores, finish):
    ahead = scores(tasks[0])
    for i, task in enumerate(tasks):
        now = ahead
        if i + 1 < len(tasks):
            ahead = scores(tasks[i + 1])
        finish(task, now)


def head_columns(h):
    return slice(h * HD, (h + 1) * HD)


def local_pass(g, q_ref, kv_ref, ve, arrived, emit):
    rows = kv_ref.shape[0]
    ve[:, :HD] = kv_ref[:, HD:]
    ve[:, HD:] = jnp.ones((rows, HD), jnp.bfloat16)
    row = lax.broadcasted_iota(jnp.int32, (PAIR * TILE, TILE), 0)
    seen = (row & (TILE - 1)) >= lax.broadcasted_iota(jnp.int32, (PAIR * TILE, TILE), 1)

    def scores(task):
        first, at = task
        if at == 0:
            arrived(first)
        q = jnp.concatenate([q_ref[at : at + TILE, head_columns(g * GROUP + first + j)] for j in range(PAIR)], axis=0)
        parts = [nt(q, kv_ref[:at, :HD])] if at else []
        parts.append(jnp.where(seen, nt(q, kv_ref[at : at + TILE, :HD]), NEG))
        return parts

    def finish(task, parts):
        first, at = task
        top = fold(jnp.maximum, [jnp.max(s, axis=1, keepdims=True) for s in parts])
        total = None
        for s, start in zip(parts, [0, at] if at else [at]):
            p = jnp.exp2((s - top) * C2).astype(jnp.bfloat16)
            part = nn(p, ve[start : start + s.shape[1], :])
            total = part if total is None else total + part
        for j in range(PAIR):
            mine = slice(j * TILE, (j + 1) * TILE)
            emit(slice(at, at + TILE), first + j, total[mine, :HD], total[mine, HD:], top[mine] * C2)

    pipelined([(h, at) for h in range(0, GROUP, PAIR) for at in range(0, rows, TILE)], scores, finish)


def first_kernel(blk_ref, kv_ref, *refs):
    count = (len(refs) - 5) // 2
    sources, state, held, (ve, sem) = refs[:count], refs[count : count + 3], refs[count + 3 : -2], refs[-2:]
    q_ref = held[0]
    spots = [slice(h * HD, (h + PAIR) * HD) for h in range(0, q_ref.shape[1] // HD, PAIR)]
    copies = [(sources[0].at[:, x], q_ref.at[:, x]) for x in spots] + list(zip(sources[1:], held[1:]))
    copies = start_all(copies, sem)
    ahead = GROUP // PAIR

    @pl.when(blk_ref[0] > 0)
    def _():
        local_pass(0, q_ref, kv_ref, ve, lambda h: copies[h // PAIR].wait(), keep_in(state))

    @pl.when(blk_ref[0] == 0)
    def _():
        for copy in copies[:ahead]:
            copy.wait()

    for copy in copies[ahead:]:
        copy.wait()


def first_attention(blk, kv, query, others):
    rows = kv.shape[0]
    sources = [query, *others]
    outs = pl.pallas_call(
        first_kernel,
        out_shape=[pltpu.VMEM((rows, GROUP * HD), jnp.float32)] * 3 + [pltpu.VMEM(x.shape, x.dtype) for x in sources],
        in_specs=[SMEM, VMEM] + [HBM] * len(sources),
        out_specs=[VMEM] * (3 + len(sources)),
        scratch_shapes=[
            pltpu.VMEM((rows, 2 * HD), jnp.bfloat16),
            pltpu.SemaphoreType.DMA((query.shape[1] // HD // PAIR + len(others),)),
        ],
        compiler_params=params(6),
        cost_estimate=cost(2 * 10**9),
        name="local_attention",
    )(blk, kv, *[in_hbm(x) for x in sources])
    return list(outs[:3]), list(outs[3:])


def keep_in(state):
    acc_ref, top_ref, sum_ref = state

    def emit(rows, h, total, z, top):
        here = (rows, head_columns(h))
        acc_ref[here], sum_ref[here], top_ref[here] = total, z, jnp.broadcast_to(top, total.shape)

    return emit


def local_kernel(g, blk_ref, kv_ref, q_ref, *refs):
    @pl.when(blk_ref[0] > 0)
    def _():
        local_pass(g, q_ref, kv_ref, refs[3], lambda h: None, keep_in(refs[:3]))


def local_attention(blk, kv, g, query):
    rows = kv.shape[0]
    return list(
        pl.pallas_call(
            functools.partial(local_kernel, g),
            out_shape=[pltpu.VMEM((rows, GROUP * HD), jnp.float32)] * 3,
            in_specs=[SMEM, VMEM, VMEM],
            out_specs=[VMEM] * 3,
            scratch_shapes=[pltpu.VMEM((rows, 2 * HD), jnp.bfloat16)],
            compiler_params=params(6),
            cost_estimate=cost(1000000000),
            name="local_attention",
        )(blk, kv, query)
    )


def anchor_kernel(g, groups, prior, blk_ref, q_ref, kv_ref, acc_ref, top_ref, sum_ref, *refs):
    count = sum(groups)
    cand, (o_ref, token, ka, vae, out, sem) = refs[:count], refs[count + prior :]
    rows = q_ref.shape[0]
    blk = blk_ref[0]
    token[...] = jnp.zeros(token.shape, jnp.float32)

    def leave(h):
        return pltpu.make_async_copy(out.at[h], o_ref.at[:, head_columns(g * GROUP + h)], sem.at[h])

    def take(refs):
        at = 0
        for ref in refs:
            here = slice(at, at + ref.shape[0])
            ka[here, :] = ref[:, :HD]
            vae[here, :HD] = ref[:, HD:]
            at = here.stop

    def scores(h):
        return nt(q_ref[:, head_columns(g * GROUP + h)], ka[...])

    def weigh(h, s):
        before = top_ref[:, head_columns(h)]
        top = jnp.maximum(jnp.max(s, axis=1, keepdims=True) * C2, before)
        p = [jnp.exp2(s[:, at : at + HD] * C2 - top).astype(jnp.bfloat16) for at in range(0, rows, HD)]
        return jnp.concatenate(p, axis=1), jnp.exp2(before - top)

    def finish(h, total, w):
        held = (slice(None), head_columns(h))
        o = (total[:, :HD] + w * acc_ref[held]) * inverse(total[:, HD:] + w * sum_ref[held])
        out[h] = o.astype(jnp.bfloat16)
        leave(h).start()

    @pl.when(blk > 0)
    def _():
        if len(groups) == 1:
            take(cand)
        else:
            at = 0
            for i, size in enumerate(groups):
                pl.when(blk == i + 1)(functools.partial(take, cand[at : at + size]))
                at += size
        vae[:, HD:] = jnp.ones((rows, HD), jnp.bfloat16)
        ahead, weighed = scores(0), None
        for h in range(GROUP + 1):
            s = ahead
            if h + 1 < GROUP:
                ahead = scores(h + 1)
            if weighed is not None:
                total, w = nn(weighed[0], vae[...]), weighed[1]
            if h < GROUP:
                weighed = weigh(h, s)
            if h:
                finish(h - 1, total, w)

    def emit(here, h, total, z, top):
        out[h, here, :] = (total * inverse(z)).astype(jnp.bfloat16)
        if here.stop == rows:
            leave(h).start()

    @pl.when(blk == 0)
    def _():
        local_pass(g, q_ref, kv_ref, vae, lambda first: None, emit)

    for h in range(GROUP):
        leave(h).wait()


def inverse(x):
    guess = pl.reciprocal(x, approx=True)
    return guess * (2.0 - x * guess)


def anchor_attention(blk, query, kv, state, cands, g, prior):
    rows = query.shape[0]
    flat = [x for group in cands for x in group]
    args = [blk, query, kv, *state, *flat]
    specs = [SMEM] + [VMEM] * (5 + len(flat))
    alias = {}
    if prior is not None:
        alias = {len(args): 0}
        args.append(prior)
        specs.append(ANY)
    return pl.pallas_call(
        functools.partial(anchor_kernel, g, [len(group) for group in cands], len(alias)),
        out_shape=[jax.ShapeDtypeStruct(query.shape, query.dtype), jax.ShapeDtypeStruct((8, HD), jnp.float32)],
        in_specs=specs,
        out_specs=[ANY, VMEM],
        scratch_shapes=[
            pltpu.VMEM((rows, HD), jnp.bfloat16),
            pltpu.VMEM((rows, 2 * HD), jnp.bfloat16),
            pltpu.VMEM((GROUP, rows, HD), jnp.bfloat16),
            pltpu.SemaphoreType.DMA((GROUP,)),
        ],
        input_output_aliases=alias,
        compiler_params=params(6),
        cost_estimate=cost(1000000000),
        name="anchor_attention",
    )(*args)


def fold_order(n):
    bits = n.bit_length() - 1
    return sorted(range(n), key=lambda x: int(format(x, "0%db" % bits)[::-1], 2))


def join_kernel(*refs):
    at = 0
    for ref in refs[:-1]:
        refs[-1][at : at + ref.shape[0], :] = ref[...]
        at += ref.shape[0]


def join(arrays):
    height, width = sum(x.shape[0] for x in arrays), arrays[0].shape[1]
    return pl.pallas_call(
        join_kernel,
        out_shape=pltpu.VMEM((height, width), arrays[0].dtype),
        in_specs=[VMEM] * len(arrays),
        out_specs=VMEM,
        compiler_params=params(2),
        cost_estimate=BRIEF,
        name="join",
    )(*arrays)


def half_kernel(which, x_ref, o_ref):
    rows = o_ref.shape[0]
    o_ref[...] = x_ref[which * rows : (which + 1) * rows, :]


def half_rows(x, which):
    return pl.pallas_call(
        functools.partial(half_kernel, which),
        out_shape=pltpu.VMEM((x.shape[0] // 2, x.shape[1]), x.dtype),
        in_specs=[VMEM],
        out_specs=VMEM,
        compiler_params=params(2),
        cost_estimate=BRIEF,
        name="half_rows",
    )(x)


def option_kernel(masks, heads, blk_ref, owner_ref, slot_ref, length_ref, *refs):
    n = len(masks)
    kv_heads = heads // GROUP
    kv, queries = refs[:kv_heads], refs[kv_heads : kv_heads + 2]
    keep, send, q_all, part = refs[kv_heads + 3 :]
    blk = blk_ref[0]
    rows = kv[0].shape[0]
    half = queries[0].shape[0]
    options, each = 2 * half, 2 * half // n
    for i, mask in enumerate(masks):
        at = jnp.bitwise_xor(blk, mask) * each
        here = queries[i * each // half].at[i * each % half : i * each % half + each]
        q_all[pl.ds(pl.multiple_of(at, each), each), :] = here[...]
    eye = lax.broadcasted_iota(jnp.int32, (options, options), 0) == lax.broadcasted_iota(jnp.int32, (options, options), 1)
    length = jnp.sum(jnp.where(eye, length_ref[...].astype(jnp.float32), 0.0), axis=1, keepdims=True)
    seen = length - (blk * rows).astype(jnp.float32)
    lane = lax.broadcasted_iota(jnp.int32, (options, HD), 1)
    logs = jnp.zeros((options, HD), jnp.float32)
    home = head_of(lane, heads)
    stack = max(1, min(GROUP, 512 // options))
    spots = lax.broadcasted_iota(jnp.int32, (options * stack, rows), 1).astype(jnp.float32)
    seen_all = jnp.concatenate([seen] * stack, axis=0)
    for first in range(0, heads, stack):
        g = first // GROUP
        q = jnp.concatenate([q_all[:, h * HD : (h + 1) * HD] for h in range(first, first + stack)], axis=0)
        s = nt(q, kv[g][:, :HD])
        s = jnp.where(spots < seen_all, s, NEG)
        top = jnp.max(s, axis=1, keepdims=True)
        e = jnp.exp2((s - top) * C2)
        z = jnp.sum(e, axis=1, keepdims=True)
        o = nn(e.astype(jnp.bfloat16), kv[g][:, HD:]) / z
        live = seen_all > 0
        o = jnp.where(live, o, 0.0).astype(jnp.bfloat16)
        log = jnp.where(live, top * SCALE + jnp.log(z), NEG)
        for j in range(stack):
            h = first + j
            part[:, h * HD : (h + 1) * HD] = o[j * options : (j + 1) * options]
            logs = jnp.where(home == h, log[j * options : (j + 1) * options], logs)
    part[:, heads * HD :] = summands(logs, heads)
    slot = lax.broadcasted_iota(jnp.int32, (CAP, options), 0)
    order = fold_order(n)
    for half, out in ((order[: n // 2], keep), (order[n // 2 :], send)):
        for i, mask in enumerate(half):
            pick = (owner_ref[...] == jnp.bitwise_xor(blk, mask)) & (slot_ref[...] == slot)
            pick = jnp.where(pick, 1.0, 0.0).astype(jnp.bfloat16)
            out[i * CAP : (i + 1) * CAP, :] = nn(pick, part[...]).astype(jnp.bfloat16)


def summands(logs, heads):
    lane = lax.broadcasted_iota(jnp.int32, logs.shape, 1)
    high = logs.astype(jnp.bfloat16).astype(jnp.float32)
    rest = logs - high
    mid = rest.astype(jnp.bfloat16).astype(jnp.float32)
    low = rest - mid
    low = jnp.where(lane < 3 * heads, low, 0.0)
    return jnp.where(lane < heads, high, jnp.where(lane < 2 * heads, mid, low)).astype(jnp.bfloat16)


def option_partials(blk, owner, slot, length, kvs, masks, queries, after):
    n, heads = len(masks), queries[0].shape[1] // HD
    options = 2 * queries[0].shape[0]
    width = (heads + 1) * HD
    rows = kvs[0].shape[0]
    return pl.pallas_call(
        functools.partial(option_kernel, masks, heads),
        out_shape=[jax.ShapeDtypeStruct((n // 2 * CAP, width), jnp.bfloat16)] * 2,
        in_specs=[SMEM] + [VMEM] * (5 + len(kvs)) + [ANY],
        out_specs=[VMEM] * 2,
        scratch_shapes=[
            pltpu.VMEM((options, heads * HD), jnp.bfloat16),
            pltpu.VMEM((options, width), jnp.bfloat16),
        ],
        compiler_params=params(4 + options // 32),
        cost_estimate=cost(1000000000),
        name="option_partials",
    )(blk, owner, slot, length, *kvs, *queries, after)


def head_of(lane, heads):
    return lane & (heads - 1) if heads & (heads - 1) == 0 else lax.rem(lane, heads)


def merge_kernel(heads, a, b, after, *outs):
    width = heads * HD
    home = head_of(lax.broadcasted_iota(jnp.int32, (HD, HD), 0), heads)
    home = jnp.where(lax.broadcasted_iota(jnp.int32, (HD, HD), 0) < 3 * heads, home, heads)
    pick = jnp.concatenate([jnp.where(home == h, 1.0, 0.0).astype(jnp.bfloat16) for h in range(heads)], axis=1)
    logs = [nn(x[:, width:], pick) for x in (a, b)]
    top = jnp.maximum(*logs)
    weights = [jnp.exp(log - top) for log in logs]
    total = weights[0] + weights[1]
    merged = (weights[0] * a[:, :width].astype(jnp.float32) + weights[1] * b[:, :width].astype(jnp.float32)) / total
    merged = merged.astype(jnp.bfloat16)
    if len(outs) == 1:
        outs[0][...] = merged
        return
    log = top + jnp.log(total)
    lane = lax.broadcasted_iota(jnp.int32, (a.shape[0], HD), 1)
    packed = jnp.zeros((a.shape[0], HD), jnp.float32)
    home = head_of(lane, heads)
    for h in range(heads):
        packed = jnp.where(home == h, log[:, h * HD : (h + 1) * HD], packed)
    packed = summands(packed, heads)
    half = a.shape[0] // 2
    for i, out in enumerate(outs):
        out[:, :width] = merged[i * half : (i + 1) * half]
        out[:, width:] = packed[i * half : (i + 1) * half]


def merge(a, b, last, after):
    rows, width = a.shape
    heads = width // HD - 1
    if last:
        shapes = [jax.ShapeDtypeStruct((rows, heads * HD), jnp.bfloat16)]
    else:
        shapes = [jax.ShapeDtypeStruct((rows // 2, width), jnp.bfloat16)] * 2
    return pl.pallas_call(
        functools.partial(merge_kernel, heads),
        out_shape=shapes,
        in_specs=[VMEM] * 2 + [ANY],
        out_specs=[VMEM] * len(shapes),
        compiler_params=params(6),
        cost_estimate=BRIEF,
        name="merge",
    )(a, b, after)


def swap(x, n, mask):
    return lax.ppermute(x, "blk", [(i, i ^ mask) for i in range(n)])


def from_root(x, blk):
    return lax.psum(jnp.where(blk == 0, x, jnp.zeros_like(x)), "blk")


def body(ctx_query, ctx_key, ctx_value, opt_query, opt_owner, opt_slot, opt_length):
    n = lax.axis_size("blk")
    blk = lax.axis_index("blk")
    blk_arr = blk.astype(jnp.int32).reshape(1)
    options = opt_owner.shape[0]
    rounds = n.bit_length() - 1

    hold = lax.optimization_barrier
    row = lambda x: x.reshape(1, options)

    blk_arr, ctx_key = hold((blk_arr, ctx_key))
    kvs = parts(ctx_key, ctx_value)
    shards = [opt_query]
    masks = [0]
    for bit in reversed(range(1, rounds)):
        mine = shards[0] if len(shards) == 1 else jnp.concatenate(shards, axis=0)
        shards = [mine, swap(mine, n, 1 << bit)]
        masks = masks + [mask | 1 << bit for mask in masks]
    masks = masks + [mask | 1 for mask in masks]
    if n == 4:
        first = [lax.ppermute(kvs[0], "blk", [(0, 2)])]
    small = [row(opt_owner), row(opt_slot), row(opt_length), shards[0]]
    state, (ctx_query, *small, own) = first_attention(blk_arr, kvs[0], ctx_query, small)
    kvs, state, shards = hold((kvs, state, shards))
    mine = join([own, *shards[1:]])
    queries = [mine, swap(mine, n, 1)]
    states = [state]
    if n == 4:
        first += [lax.ppermute(x, "blk", [(0, 2)]) for x in kvs[1:]]
    states += [local_attention(blk_arr, kv, g, ctx_query) for g, kv in enumerate(kvs) if g]
    if n == 4:
        first[0], states = hold((first[0], states))
    keep, send = option_partials(blk_arr, *small, kvs, masks, queries, states[-1][1])
    if n == 4:
        near = [[lax.ppermute(first[0], "blk", [(2, 1)])]]
        kvs, keep = hold((kvs, keep))
        tops = [half_rows(x, 0) for x in kvs[1:]]
        near += [[lax.ppermute(x, "blk", [(0, 1)])] for x in tops]
        first[1:], keep, tops = hold((first[1:], keep, tops))
        for x, y in zip(near[1:], first[1:]):
            x.append(lax.ppermute(half_rows(y, 1), "blk", [(2, 1)]))
        anchors = [[x, [y], [lax.ppermute(y, "blk", [(2, 3)])]] for x, y in zip(near, first)]
        anchors[0], first = hold((anchors[0], first))
    else:
        anchors = [[[from_root(x, blk)]] for x in kvs]
    ctx_out, tokens = None, []
    for g, state in enumerate(states):
        ctx_out, token = anchor_attention(blk_arr, ctx_query, kvs[g], state, anchors[g], g, ctx_out)
        tokens.append(token)
    for bit in range(rounds):
        got = swap(send, n, 1 << bit)
        last = bit == rounds - 1
        outs = merge(keep, got, last, tokens[-1 if last else 0])
        if last:
            opt_out = outs[0]
        else:
            keep, send = outs
    return (ctx_out, opt_out)


def solution(mesh):
    spread = P(("groups", "blk"), "head")
    return jax.shard_map(
        body,
        mesh=mesh,
        in_specs=(spread, spread, spread, spread, P("groups"), P("groups"), P("groups")),
        out_specs=(spread, spread),
        check_vma=False,
    )
```

```python
import functools
import math

import jax
import jax.numpy as jnp
from jax import lax
from jax.experimental import pallas as pl
from jax.experimental.pallas import tpu as pltpu
from jax.sharding import PartitionSpec as P

HD = 128
HQ = 64
KVH = 8
CAP = 32
GROUP = HQ // KVH
SCALE = HD ** (-0.5)
C2 = SCALE * math.log2(math.e)
NEG = -1e30
TILE = 256
PAIR = 2
VMEM = pl.BlockSpec(memory_space=pltpu.VMEM)
SMEM = pl.BlockSpec(memory_space=pltpu.SMEM)
HBM = pl.BlockSpec(memory_space=pltpu.HBM)
ANY = pl.BlockSpec(memory_space=pl.ANY)


def cost(flops):
    return pl.CostEstimate(flops=flops, bytes_accessed=1, transcendentals=0)


BRIEF = cost(1)


def nt(a, b):
    return lax.dot_general(a, b, (((1,), (1,)), ((), ())), preferred_element_type=jnp.float32)


def nn(a, b):
    return jnp.dot(a, b, preferred_element_type=jnp.float32)


def params(mib):
    return pltpu.CompilerParams(vmem_limit_bytes=mib * 1024 * 1024)


def fold(op, items):
    return functools.reduce(op, items)


def start_all(copies, sem):
    started = [pltpu.make_async_copy(a, b, sem.at[i]) for i, (a, b) in enumerate(copies)]
    for copy in started:
        copy.start()
    return started


def in_hbm(x):
    return pltpu.with_memory_space_constraint(x, pltpu.HBM)


def beside(heads, k_ref, v_ref, kv):
    copies = []
    for g in range(heads):
        for ref, at in ((k_ref, 0), (v_ref, HD)):
            copies.append((ref.at[:, g * HD : (g + 1) * HD], kv[g].at[:, at : at + HD]))
    return copies


def parts_kernel(heads, k_ref, v_ref, *refs):
    kv, sem = refs[:heads], refs[heads]
    for copy in start_all(beside(heads, k_ref, v_ref, kv), sem):
        copy.wait()


def parts(key, value):
    rows, heads = key.shape[0], key.shape[1] // HD
    outs = pl.pallas_call(
        functools.partial(parts_kernel, heads),
        out_shape=[pltpu.VMEM((rows, 2 * HD), key.dtype)] * heads,
        in_specs=[HBM] * 2,
        out_specs=[VMEM] * heads,
        scratch_shapes=[pltpu.SemaphoreType.DMA((2 * heads,))],
        compiler_params=params(2),
        cost_estimate=BRIEF,
        name="parts",
    )(in_hbm(key), in_hbm(value))
    return list(outs)


def pipelined(tasks, scores, finish):
    ahead = scores(tasks[0])
    for i, task in enumerate(tasks):
        now = ahead
        if i + 1 < len(tasks):
            ahead = scores(tasks[i + 1])
        finish(task, now)


def head_columns(h):
    return slice(h * HD, (h + 1) * HD)


def local_pass(g, q_ref, kv_ref, ve, arrived, emit):
    rows = kv_ref.shape[0]
    ve[:, :HD] = kv_ref[:, HD:]
    ve[:, HD:] = jnp.ones((rows, HD), jnp.bfloat16)
    row = lax.broadcasted_iota(jnp.int32, (PAIR * TILE, TILE), 0)
    seen = (row & (TILE - 1)) >= lax.broadcasted_iota(jnp.int32, (PAIR * TILE, TILE), 1)

    def scores(task):
        first, at = task
        if at == 0:
            arrived(first)
        q = jnp.concatenate([q_ref[at : at + TILE, head_columns(g * GROUP + first + j)] for j in range(PAIR)], axis=0)
        parts = [nt(q, kv_ref[:at, :HD])] if at else []
        parts.append(jnp.where(seen, nt(q, kv_ref[at : at + TILE, :HD]), NEG))
        return parts

    def finish(task, parts):
        first, at = task
        top = fold(jnp.maximum, [jnp.max(s, axis=1, keepdims=True) for s in parts])
        total = None
        for s, start in zip(parts, [0, at] if at else [at]):
            p = jnp.exp2((s - top) * C2).astype(jnp.bfloat16)
            part = nn(p, ve[start : start + s.shape[1], :])
            total = part if total is None else total + part
        for j in range(PAIR):
            mine = slice(j * TILE, (j + 1) * TILE)
            emit(slice(at, at + TILE), first + j, total[mine, :HD], total[mine, HD:], top[mine] * C2)

    pipelined([(h, at) for h in range(0, GROUP, PAIR) for at in range(0, rows, TILE)], scores, finish)


def first_kernel(blk_ref, kv_ref, *refs):
    count = (len(refs) - 5) // 2
    sources, state, held, (ve, sem) = refs[:count], refs[count : count + 3], refs[count + 3 : -2], refs[-2:]
    q_ref = held[0]
    spots = [slice(h * HD, (h + PAIR) * HD) for h in range(0, q_ref.shape[1] // HD, PAIR)]
    copies = [(sources[0].at[:, x], q_ref.at[:, x]) for x in spots] + list(zip(sources[1:], held[1:]))
    copies = start_all(copies, sem)
    ahead = GROUP // PAIR

    @pl.when(blk_ref[0] > 0)
    def _():
        local_pass(0, q_ref, kv_ref, ve, lambda h: copies[h // PAIR].wait(), keep_in(state))

    @pl.when(blk_ref[0] == 0)
    def _():
        for copy in copies[:ahead]:
            copy.wait()

    for copy in copies[ahead:]:
        copy.wait()


def first_attention(blk, kv, query, others):
    rows = kv.shape[0]
    sources = [query, *others]
    outs = pl.pallas_call(
        first_kernel,
        out_shape=[pltpu.VMEM((rows, GROUP * HD), jnp.float32)] * 3 + [pltpu.VMEM(x.shape, x.dtype) for x in sources],
        in_specs=[SMEM, VMEM] + [HBM] * len(sources),
        out_specs=[VMEM] * (3 + len(sources)),
        scratch_shapes=[
            pltpu.VMEM((rows, 2 * HD), jnp.bfloat16),
            pltpu.SemaphoreType.DMA((query.shape[1] // HD // PAIR + len(others),)),
        ],
        compiler_params=params(6),
        cost_estimate=cost(2 * 10**9),
        name="local_attention",
    )(blk, kv, *[in_hbm(x) for x in sources])
    return list(outs[:3]), list(outs[3:])


def keep_in(state):
    acc_ref, top_ref, sum_ref = state

    def emit(rows, h, total, z, top):
        here = (rows, head_columns(h))
        acc_ref[here], sum_ref[here], top_ref[here] = total, z, jnp.broadcast_to(top, total.shape)

    return emit


def local_kernel(g, blk_ref, kv_ref, q_ref, *refs):
    @pl.when(blk_ref[0] > 0)
    def _():
        local_pass(g, q_ref, kv_ref, refs[3], lambda h: None, keep_in(refs[:3]))


def local_attention(blk, kv, g, query):
    rows = kv.shape[0]
    return list(
        pl.pallas_call(
            functools.partial(local_kernel, g),
            out_shape=[pltpu.VMEM((rows, GROUP * HD), jnp.float32)] * 3,
            in_specs=[SMEM, VMEM, VMEM],
            out_specs=[VMEM] * 3,
            scratch_shapes=[pltpu.VMEM((rows, 2 * HD), jnp.bfloat16)],
            compiler_params=params(6),
            cost_estimate=cost(10**9),
            name="local_attention",
        )(blk, kv, query)
    )


def anchor_kernel(g, count, prior, blk_ref, q_ref, kv_ref, acc_ref, top_ref, sum_ref, *refs):
    cand, (o_ref, token, ka, vae, out, sem) = refs[:count], refs[count + prior :]
    rows = q_ref.shape[0]
    blk = blk_ref[0]
    token[...] = jnp.zeros(token.shape, jnp.float32)

    def leave(h):
        return pltpu.make_async_copy(out.at[h], o_ref.at[:, head_columns(g * GROUP + h)], sem.at[h])

    def take(ref):
        ka[...] = ref[:, :HD]
        vae[:, :HD] = ref[:, HD:]

    def stacked(ref, first):
        return jnp.concatenate([ref[:, head_columns(first + j)] for j in range(PAIR)], axis=0)

    def scores(h):
        return nt(stacked(q_ref, g * GROUP + h), ka[...])

    def weigh(h, s):
        before = stacked(top_ref, h)
        top = jnp.maximum(jnp.max(s, axis=1, keepdims=True) * C2, before)
        p = [jnp.exp2(s[:, at : at + HD] * C2 - top).astype(jnp.bfloat16) for at in range(0, rows, HD)]
        return jnp.concatenate(p, axis=1), jnp.exp2(before - top)

    def finish(first, total, w):
        for j in range(PAIR):
            h, mine = first + j, slice(j * rows, (j + 1) * rows)
            held = (slice(None), head_columns(h))
            o = (total[mine, :HD] + w[mine] * acc_ref[held]) * inverse(total[mine, HD:] + w[mine] * sum_ref[held])
            out[h] = o.astype(jnp.bfloat16)
            leave(h).start()

    @pl.when(blk > 0)
    def _():
        if count == 1:
            take(cand[0])
        else:
            for i, ref in enumerate(cand):
                pl.when(blk == i + 1)(functools.partial(take, ref))
        vae[:, HD:] = jnp.ones((rows, HD), jnp.bfloat16)
        ahead, weighed = scores(0), None
        for h in range(0, GROUP + PAIR, PAIR):
            s = ahead
            if h + PAIR < GROUP:
                ahead = scores(h + PAIR)
            if weighed is not None:
                total, w = nn(weighed[0], vae[...]), weighed[1]
            if h < GROUP:
                weighed = weigh(h, s)
            if h:
                finish(h - PAIR, total, w)

    def emit(here, h, total, z, top):
        out[h, here, :] = (total * inverse(z)).astype(jnp.bfloat16)
        if here.stop == rows:
            leave(h).start()

    @pl.when(blk == 0)
    def _():
        local_pass(g, q_ref, kv_ref, vae, lambda first: None, emit)

    for h in range(GROUP):
        leave(h).wait()


def inverse(x):
    guess = pl.reciprocal(x, approx=True)
    return guess * (2.0 - x * guess)


def anchor_attention(blk, query, kv, state, cands, g, prior):
    rows = query.shape[0]
    args = [blk, query, kv, *state, *cands]
    specs = [SMEM] + [VMEM] * (5 + len(cands))
    alias = {}
    if prior is not None:
        alias = {len(args): 0}
        args.append(prior)
        specs.append(ANY)
    return pl.pallas_call(
        functools.partial(anchor_kernel, g, len(cands), len(alias)),
        out_shape=[jax.ShapeDtypeStruct(query.shape, query.dtype), jax.ShapeDtypeStruct((8, HD), jnp.float32)],
        in_specs=specs,
        out_specs=[ANY, VMEM],
        scratch_shapes=[
            pltpu.VMEM((rows, HD), jnp.bfloat16),
            pltpu.VMEM((rows, 2 * HD), jnp.bfloat16),
            pltpu.VMEM((GROUP, rows, HD), jnp.bfloat16),
            pltpu.SemaphoreType.DMA((GROUP,)),
        ],
        input_output_aliases=alias,
        compiler_params=params(12),
        cost_estimate=cost(1000000000),
        name="anchor_attention",
    )(*args)


def fold_order(n):
    bits = n.bit_length() - 1
    return sorted(range(n), key=lambda x: int(format(x, "0%db" % bits)[::-1], 2))


def join_kernel(*refs):
    at = 0
    for ref in refs[:-1]:
        refs[-1][at : at + ref.shape[0], :] = ref[...]
        at += ref.shape[0]


def join(arrays):
    height, width = sum(x.shape[0] for x in arrays), arrays[0].shape[1]
    return pl.pallas_call(
        join_kernel,
        out_shape=pltpu.VMEM((height, width), arrays[0].dtype),
        in_specs=[VMEM] * len(arrays),
        out_specs=VMEM,
        compiler_params=params(2),
        cost_estimate=BRIEF,
        name="join",
    )(*arrays)


def option_kernel(masks, heads, blk_ref, owner_ref, slot_ref, length_ref, *refs):
    n = len(masks)
    kv_heads = heads // GROUP
    kv, queries = refs[:kv_heads], refs[kv_heads : kv_heads + 2]
    keep, send, q_all, part = refs[kv_heads + 3 :]
    blk = blk_ref[0]
    rows = kv[0].shape[0]
    half = queries[0].shape[0]
    options, each = 2 * half, 2 * half // n
    for i, mask in enumerate(masks):
        at = jnp.bitwise_xor(blk, mask) * each
        here = queries[i * each // half].at[i * each % half : i * each % half + each]
        q_all[pl.ds(pl.multiple_of(at, each), each), :] = here[...]
    eye = lax.broadcasted_iota(jnp.int32, (options, options), 0) == lax.broadcasted_iota(jnp.int32, (options, options), 1)
    length = jnp.sum(jnp.where(eye, length_ref[...].astype(jnp.float32), 0.0), axis=1, keepdims=True)
    seen = length - (blk * rows).astype(jnp.float32)
    lane = lax.broadcasted_iota(jnp.int32, (options, HD), 1)
    logs = jnp.zeros((options, HD), jnp.float32)
    home = head_of(lane, heads)
    stack = max(1, min(GROUP, 512 // options))
    spots = lax.broadcasted_iota(jnp.int32, (options * stack, rows), 1).astype(jnp.float32)
    seen_all = jnp.concatenate([seen] * stack, axis=0)
    for first in range(0, heads, stack):
        g = first // GROUP
        q = jnp.concatenate([q_all[:, h * HD : (h + 1) * HD] for h in range(first, first + stack)], axis=0)
        s = nt(q, kv[g][:, :HD])
        s = jnp.where(spots < seen_all, s, NEG)
        top = jnp.max(s, axis=1, keepdims=True)
        e = jnp.exp2((s - top) * C2)
        z = jnp.sum(e, axis=1, keepdims=True)
        o = nn(e.astype(jnp.bfloat16), kv[g][:, HD:]) / z
        live = seen_all > 0
        o = jnp.where(live, o, 0.0).astype(jnp.bfloat16)
        log = jnp.where(live, top * SCALE + jnp.log(z), NEG)
        for j in range(stack):
            h = first + j
            part[:, h * HD : (h + 1) * HD] = o[j * options : (j + 1) * options]
            logs = jnp.where(home == h, log[j * options : (j + 1) * options], logs)
    part[:, heads * HD :] = summands(logs, heads)
    slot = lax.broadcasted_iota(jnp.int32, (CAP, options), 0)
    order = fold_order(n)
    for half, out in ((order[: n // 2], keep), (order[n // 2 :], send)):
        for i, mask in enumerate(half):
            pick = (owner_ref[...] == jnp.bitwise_xor(blk, mask)) & (slot_ref[...] == slot)
            pick = jnp.where(pick, 1.0, 0.0).astype(jnp.bfloat16)
            out[i * CAP : (i + 1) * CAP, :] = nn(pick, part[...]).astype(jnp.bfloat16)


def summands(logs, heads):
    lane = lax.broadcasted_iota(jnp.int32, logs.shape, 1)
    high = logs.astype(jnp.bfloat16).astype(jnp.float32)
    rest = logs - high
    mid = rest.astype(jnp.bfloat16).astype(jnp.float32)
    low = rest - mid
    low = jnp.where(lane < 3 * heads, low, 0.0)
    return jnp.where(lane < heads, high, jnp.where(lane < 2 * heads, mid, low)).astype(jnp.bfloat16)


def option_partials(blk, owner, slot, length, kvs, masks, queries, after):
    n, heads = len(masks), queries[0].shape[1] // HD
    options = 2 * queries[0].shape[0]
    width = (heads + 1) * HD
    rows = kvs[0].shape[0]
    return pl.pallas_call(
        functools.partial(option_kernel, masks, heads),
        out_shape=[jax.ShapeDtypeStruct((n // 2 * CAP, width), jnp.bfloat16)] * 2,
        in_specs=[SMEM] + [VMEM] * (5 + len(kvs)) + [ANY],
        out_specs=[VMEM] * 2,
        scratch_shapes=[
            pltpu.VMEM((options, heads * HD), jnp.bfloat16),
            pltpu.VMEM((options, width), jnp.bfloat16),
        ],
        compiler_params=params(4 + options // 32),
        cost_estimate=cost(1000000000),
        name="option_partials",
    )(blk, owner, slot, length, *kvs, *queries, after)


def head_of(lane, heads):
    return lane & (heads - 1) if heads & (heads - 1) == 0 else lax.rem(lane, heads)


def merge_kernel(heads, a, b, after, *outs):
    width = heads * HD
    home = head_of(lax.broadcasted_iota(jnp.int32, (HD, HD), 0), heads)
    home = jnp.where(lax.broadcasted_iota(jnp.int32, (HD, HD), 0) < 3 * heads, home, heads)
    pick = jnp.concatenate([jnp.where(home == h, 1.0, 0.0).astype(jnp.bfloat16) for h in range(heads)], axis=1)
    logs = [nn(x[:, width:], pick) for x in (a, b)]
    top = jnp.maximum(*logs)
    weights = [jnp.exp(log - top) for log in logs]
    total = weights[0] + weights[1]
    merged = (weights[0] * a[:, :width].astype(jnp.float32) + weights[1] * b[:, :width].astype(jnp.float32)) / total
    merged = merged.astype(jnp.bfloat16)
    if len(outs) == 1:
        outs[0][...] = merged
        return
    log = top + jnp.log(total)
    lane = lax.broadcasted_iota(jnp.int32, (a.shape[0], HD), 1)
    packed = jnp.zeros((a.shape[0], HD), jnp.float32)
    home = head_of(lane, heads)
    for h in range(heads):
        packed = jnp.where(home == h, log[:, h * HD : (h + 1) * HD], packed)
    packed = summands(packed, heads)
    half = a.shape[0] // 2
    for i, out in enumerate(outs):
        out[:, :width] = merged[i * half : (i + 1) * half]
        out[:, width:] = packed[i * half : (i + 1) * half]


def merge(a, b, last, after):
    rows, width = a.shape
    heads = width // HD - 1
    if last:
        shapes = [jax.ShapeDtypeStruct((rows, heads * HD), jnp.bfloat16)]
    else:
        shapes = [jax.ShapeDtypeStruct((rows // 2, width), jnp.bfloat16)] * 2
    return pl.pallas_call(
        functools.partial(merge_kernel, heads),
        out_shape=shapes,
        in_specs=[VMEM] * 2 + [ANY],
        out_specs=[VMEM] * len(shapes),
        compiler_params=params(6),
        cost_estimate=BRIEF,
        name="merge",
    )(a, b, after)


def swap(x, n, mask):
    return lax.ppermute(x, "blk", [(i, i ^ mask) for i in range(n)])


def from_root(x, blk):
    return lax.psum(jnp.where(blk == 0, x, jnp.zeros_like(x)), "blk")


def body(ctx_query, ctx_key, ctx_value, opt_query, opt_owner, opt_slot, opt_length):
    n = lax.axis_size("blk")
    blk = lax.axis_index("blk")
    blk_arr = blk.astype(jnp.int32).reshape(1)
    options = opt_owner.shape[0]
    rounds = n.bit_length() - 1

    hold = lax.optimization_barrier
    row = lambda x: x.reshape(1, options)

    blk_arr, ctx_key = hold((blk_arr, ctx_key))
    kvs = parts(ctx_key, ctx_value)
    shards = [opt_query]
    masks = [0]
    for bit in reversed(range(1, rounds)):
        mine = shards[0] if len(shards) == 1 else jnp.concatenate(shards, axis=0)
        shards = [mine, swap(mine, n, 1 << bit)]
        masks = masks + [mask | 1 << bit for mask in masks]
    masks = masks + [mask | 1 for mask in masks]
    if n == 4:
        first = [lax.ppermute(kvs[0], "blk", [(0, 2)])]
    small = [row(opt_owner), row(opt_slot), row(opt_length), shards[0]]
    state, (ctx_query, *small, own) = first_attention(blk_arr, kvs[0], ctx_query, small)
    kvs, state, shards = hold((kvs, state, shards))
    mine = join([own, *shards[1:]])
    queries = [mine, swap(mine, n, 1)]
    states = [state]
    if n == 4:
        first += [lax.ppermute(x, "blk", [(0, 2)]) for x in kvs[1:]]
    states += [local_attention(blk_arr, kv, g, ctx_query) for g, kv in enumerate(kvs) if g]
    if n == 4:
        first[0], states = hold((first[0], states))
    keep, send = option_partials(blk_arr, *small, kvs, masks, queries, states[-1][1])
    if n == 4:
        near = [lax.ppermute(first[0], "blk", [(2, 1)])]
        kvs, keep = hold((kvs, keep))
        near += [lax.ppermute(x, "blk", [(0, 1)]) for x in kvs[1:]]
        first[1:], keep = hold((first[1:], keep))
        anchors = [[x, y, lax.ppermute(y, "blk", [(2, 3)])] for x, y in zip(near, first)]
        anchors[0], first = hold((anchors[0], first))
    else:
        anchors = [[from_root(x, blk)] for x in kvs]
    ctx_out, tokens = None, []
    for g, state in enumerate(states):
        ctx_out, token = anchor_attention(blk_arr, ctx_query, kvs[g], state, anchors[g], g, ctx_out)
        tokens.append(token)
    for bit in range(rounds):
        got = swap(send, n, 1 << bit)
        last = bit == rounds - 1
        outs = merge(keep, got, last, tokens[-1 if last else 0])
        if last:
            opt_out = outs[0]
        else:
            keep, send = outs
    return (ctx_out, opt_out)


def solution(mesh):
    spread = P(("groups", "blk"), "head")
    return jax.shard_map(
        body,
        mesh=mesh,
        in_specs=(spread, spread, spread, spread, P("groups"), P("groups"), P("groups")),
        out_specs=(spread, spread),
        check_vma=False,
    )
```
